32 devices in a mesh: seq: 8 (over z, x), tp: 4 (over y, core).
Axes of the slice: x: 2, y: 2, z: 4, core: 2. Of those that a mesh axis runs over, the one named last changes fastest.
Arguments:
- tokens: bfloat16 [4096, 4096], P('seq', 'tp'), may hold values from -6 to 6
- log_decay: float32 [4096, 16], P('seq', 'tp'), may hold values from -2 to 0
- w_query: bfloat16 [4096, 2048], P(None, 'tp'), may hold values from -0.09375 to 0.09375
- w_key: bfloat16 [4096, 512], P(None, 'tp'), may hold values from -0.09375 to 0.09375
- w_value: bfloat16 [4096, 512], P(None, 'tp'), may hold values from -0.09375 to 0.09375
- w_level: bfloat16 [4096, 96], P(None, 'tp'), may hold values from -0.09375 to 0.09375
- w_out: bfloat16 [2048, 4096], P('tp'), may hold values from -0.125 to 0.125
Outputs:
- mixed: bfloat16 [4096, 4096], P('seq', 'tp')
The draws below stay inside these ranges and needn't reach their ends.
All inputs are finite; a program needn't handle non-finite values.
Results may differ from the reference program's by a relative error of at most 0.02.
Values may be sent and summed in bfloat16 or wider, within the bound.
No kernel may reach another device: no remote copies, remote signals or barrier semaphores. Data moves between devices by JAX's collectives and lax.ppermute only.
A program may use at most 128 MiB of HBM per device.

```python
import jax
import jax.numpy as jnp
from jax import lax

D = 4096
HEAD_GROUP = 16
KV_HEADS = 4
DH = 128
BLOCK = 128
TOKEN_COUNT = 4096
LEVELS = 6
N_TP = 4


def draw_log_decay(key, part):
    key = jax.random.fold_in(key, 11)
    sequence_flows = jax.random.split(key, 7)
    slow_count = HEAD_GROUP // 2
    middle_count = HEAD_GROUP // 4
    ranking = jax.random.permutation(sequence_flows[0], HEAD_GROUP)
    fast_rate = jnp.exp(jax.random.uniform(sequence_flows[1], (HEAD_GROUP,), jnp.float32, jnp.log(1.0 / 50.0), jnp.log(1.0 / 30.0)))
    middle_rate = jnp.exp(jax.random.uniform(sequence_flows[6], (HEAD_GROUP,), jnp.float32, jnp.log(1.0 / 1000.0), jnp.log(1.0 / 200.0)))
    slow_rate = 0.3 / TOKEN_COUNT
    baseline_rate = jnp.where(ranking < slow_count, slow_rate, jnp.where(ranking < slow_count + middle_count, middle_rate, fast_rate))
    block_multiplier = jnp.exp(jax.random.uniform(sequence_flows[2], (TOKEN_COUNT // BLOCK, HEAD_GROUP), jnp.float32, -0.69, 0.69))
    block_multiplier = jnp.repeat(block_multiplier, BLOCK, axis=0, total_repeat_length=TOKEN_COUNT)
    random_offset = jax.random.uniform(sequence_flows[3], (TOKEN_COUNT, HEAD_GROUP), jnp.float32, 0.7, 1.3)
    spike_positions = jax.random.randint(sequence_flows[4], (2, HEAD_GROUP), 0, TOKEN_COUNT)
    spike_lengths = jax.random.uniform(sequence_flows[5], (2, HEAD_GROUP), jnp.float32, jnp.log(0.6), jnp.log(0.8))
    token_positions = jnp.arange(TOKEN_COUNT)[:, None]
    spike_runs = jnp.where(token_positions == spike_positions[0][None, :], spike_lengths[0][None, :], 0.0)
    spike_runs = spike_runs + jnp.where(token_positions == spike_positions[1][None, :], spike_lengths[1][None, :], 0.0)
    return (spike_runs - baseline_rate[None, :] * block_multiplier * random_offset).astype(jnp.float32)


def levels(rng, dims, pieces, low, top_value):
    level = 1.0
    for position, shards_of in pieces:
        draws = jax.random.uniform(jax.random.fold_in(jax.random.fold_in(rng, 6), position), (shards_of,), jnp.float32, low / len(pieces), top_value / len(pieces))
        level = level * jnp.repeat(jnp.exp(draws), dims[position] // shards_of).reshape((-1,) + (1,) * (len(dims) - 1 - position))
    return level


def bell_draw(stream_key, shape, deviation, bound, pieces=(), held_as=jnp.bfloat16):
    entries = deviation * jax.random.normal(stream_key, shape, jnp.float32)
    if pieces:
        entries = entries * levels(stream_key, shape, pieces, -0.22, 0.18)
    return jnp.clip(entries, -bound, bound).astype(held_as)


def setup_inputs(seed: int = 0) -> dict:
    key_of = jax.random.split(jax.random.key(seed), 8)
    tokens = bell_draw(key_of[0], (TOKEN_COUNT, D), 1.0, 6.0, ((0, 8), (1, 4)))
    log_decay = draw_log_decay(jax.random.fold_in(key_of[7], 71), 0)
    w_query = bell_draw(key_of[2], (D, HEAD_GROUP * DH), D ** -0.5, 0.09375, ((1, 4),))
    w_key = bell_draw(key_of[3], (D, KV_HEADS * DH), D ** -0.5, 0.09375, ((1, 4),))
    w_value = bell_draw(key_of[4], (D, KV_HEADS * DH), D ** -0.5, 0.09375, ((1, 4),))
    w_level = bell_draw(key_of[5], (D, HEAD_GROUP * LEVELS), D ** -0.5, 0.09375, ((1, 4),))
    w_out = bell_draw(key_of[6], (HEAD_GROUP * DH, D), (HEAD_GROUP * DH) ** -0.5, 0.125, ((0, 4),))
    return {"tokens": tokens, "log_decay": log_decay, "w_query": w_query, "w_key": w_key, "w_value": w_value, "w_level": w_level, "w_out": w_out}


def head_output(inputs):
    query, keys, values, weights, decay = inputs
    count = TOKEN_COUNT // BLOCK
    highest = lax.Precision.HIGHEST
    query_blocks = query.astype(jnp.float32).reshape(count, BLOCK, DH)
    key_blocks = keys.astype(jnp.float32).reshape(count, BLOCK, DH)
    value_blocks = values.astype(jnp.float32).reshape(count, BLOCK, DH)
    decay_blocks = decay.reshape(count, BLOCK)
    level_blocks = weights.reshape(count, BLOCK, LEVELS)
    inside = jnp.arange(BLOCK, dtype=jnp.int32)
    causal = inside[:, None] >= inside[None, :]
    scores = jnp.einsum('cik,cjk->cij', query_blocks, key_blocks, precision=highest)
    gaps = jnp.where(causal[None], decay_blocks[:, :, None] - decay_blocks[:, None, :], -jnp.inf)
    mixing = level_blocks[:, :, 0:1] * jnp.exp(gaps) * scores
    result = jnp.einsum('cij,cjv->civ', mixing, value_blocks, precision=highest)
    block_ends = decay_blocks[:, BLOCK - 1]
    weighted_keys = jnp.exp(block_ends[:, None] - decay_blocks)[:, :, None] * key_blocks
    block_states = jnp.einsum('cjk,cjv->ckv', weighted_keys, value_blocks, precision=highest)
    block_index = jnp.arange(count, dtype=jnp.int32)
    for bit in range(count.bit_length() - 1):
        upper = jnp.bitwise_and(jnp.right_shift(block_index, bit), 1) == 1
        sibling = jnp.maximum(jnp.right_shift(block_index, bit) - 1, 0).astype(jnp.int32)
        picked = block_states[sibling]
        sibling_end = block_ends[sibling]
        gap = jnp.where(upper[:, None], decay_blocks - sibling_end[:, None], -jnp.inf)
        factor = level_blocks[:, :, 1 + bit] * jnp.exp(gap)
        result = result + factor[:, :, None] * jnp.einsum('cik,ckv->civ', query_blocks, picked, precision=highest)
        paired = block_states.reshape(-1, 2, DH, DH)
        paired_ends = block_ends.reshape(-1, 2)
        fade = jnp.exp(paired_ends[:, 1] - paired_ends[:, 0])
        block_states = paired[:, 1] + fade[:, None, None] * paired[:, 0]
        block_ends = paired_ends[:, 1]
    return result.reshape(TOKEN_COUNT, DH)

def reference(tokens, log_decay, w_query, w_key, w_value, w_level, w_out):
    query = jnp.dot(tokens, w_query, preferred_element_type=jnp.float32).astype(jnp.bfloat16).reshape(TOKEN_COUNT, HEAD_GROUP, DH)
    keys = jnp.dot(tokens, w_key, preferred_element_type=jnp.float32).astype(jnp.bfloat16).reshape(TOKEN_COUNT, KV_HEADS, DH)
    values = jnp.dot(tokens, w_value, preferred_element_type=jnp.float32).astype(jnp.bfloat16).reshape(TOKEN_COUNT, KV_HEADS, DH)
    weights = jax.nn.softplus(jnp.dot(tokens, w_level, preferred_element_type=jnp.float32)).reshape(TOKEN_COUNT, HEAD_GROUP, LEVELS)
    decay = jnp.cumsum(log_decay.astype(jnp.float32), axis=0)
    group_size = HEAD_GROUP // KV_HEADS
    keys_heads = jnp.repeat(keys, group_size, axis=1)
    values_heads = jnp.repeat(values, group_size, axis=1)
    outputs = lax.map(head_output, (jnp.transpose(query, (1, 0, 2)), jnp.transpose(keys_heads, (1, 0, 2)), jnp.transpose(values_heads, (1, 0, 2)), jnp.transpose(weights, (1, 0, 2)), decay.T))
    normed = (outputs * lax.rsqrt(lax.optimization_barrier(jnp.mean(outputs * outputs, axis=-1, keepdims=True)) + 1e-05)).astype(jnp.bfloat16)
    per_group = HEAD_GROUP // N_TP
    out_rows = w_out.reshape(HEAD_GROUP, DH, D)
    mixed = jnp.zeros((TOKEN_COUNT, D), jnp.float32)
    for index in range(N_TP):
        lower = index * per_group
        partial_sum = jnp.einsum('htd,hde->te', normed[lower:lower + per_group].astype(jnp.float32), out_rows[lower:lower + per_group].astype(jnp.float32), precision=lax.Precision.HIGHEST)
        rounded = lax.optimization_barrier(partial_sum.astype(jnp.bfloat16))
        mixed = mixed + rounded.astype(jnp.float32)
    return mixed.astype(jnp.bfloat16)
```

```python
import functools

import jax
import jax.numpy as jnp
from jax import lax
from jax.experimental import pallas as pl
from jax.experimental.pallas import tpu as pltpu
from jax.sharding import PartitionSpec as P

BLOCK = 128
VMEM_LIMIT = 40 * 1024 * 1024
F32 = jnp.float32
BF16 = jnp.bfloat16


def dot(a, b):
    return jnp.dot(a, b, preferred_element_type=F32)


def dot_dims(a, b, left, right):
    return lax.dot_general(a, b, (((left,), (right,)), ((), ())), preferred_element_type=F32)


def whole(shape):
    return pl.BlockSpec(shape, lambda *_: (0,) * len(shape))


def project_kernel(n_x, first, final, widths, place, *refs):
    xs, refs = refs[:n_x], refs[n_x:]
    ws, refs = refs[: 4 * n_x], refs[4 * n_x :]
    if not first:
        total_in, refs = refs[0], refs[1:]
    if final:
        keep_ref, refs = refs[0], refs[1:]
        q_out, k_out, v_out, l_out, s_out, total = refs
    else:
        (total,) = refs
    step = pl.program_id(0)
    bounds = [0]
    for width in widths:
        bounds.append(bounds[-1] + width)

    @pl.when(step == 0)
    def _():
        if first:
            total[...] = jnp.zeros_like(total)
        else:
            total[...] = total_in[...]

    for which in range(4):
        add = dot(xs[0][...], ws[which][...])
        for other in range(1, n_x):
            add = add + dot(xs[other][...], ws[4 * other + which][...])
        total[:, bounds[which] : bounds[which + 1]] += add

    if final:

        @pl.when(step == pl.num_programs(0) - 1)
        def _():
            keys = total[:, bounds[1] : bounds[2]].astype(BF16)
            values = total[:, bounds[2] : bounds[3]].astype(BF16)
            k_out[...] = keys
            v_out[...] = values
            heads = keep_ref.shape[1]
            head_size = s_out.shape[1]
            kv_local = keys.shape[1] // head_size
            group = heads // kv_local
            for g in range(kv_local):
                kf = keys[:, g * head_size : (g + 1) * head_size].astype(F32)
                vg = values[:, g * head_size : (g + 1) * head_size]
                for h in range(g * group, (g + 1) * group):
                    weighted = (kf * keep_ref[:, h : h + 1]).astype(BF16)
                    s_out[h * head_size : (h + 1) * head_size, :] = dot_dims(
                        weighted, vg, 0, 0
                    ).astype(BF16)
            q_out[...] = total[:, : bounds[1]].astype(BF16)
            raw = total[:, bounds[3] : bounds[4]]
            l_out[...] = jnp.maximum(raw, 0.0) + jnp.log1p(jnp.exp(-jnp.abs(raw)))


def project(xs, places, ws, offset, tile, total, keep, head_size):
    rows, depth = xs[0].shape
    n_x = len(xs)
    shard = ws[0].shape[0] // 4
    widths = tuple(w.shape[1] for w in ws)
    columns = sum(widths)
    first, final = total is None, keep is not None
    per_shard, skip = shard // tile, offset // tile
    in_specs = [pl.BlockSpec((rows, tile), lambda s, p: (0, s)) for _ in xs]
    for i in range(n_x):
        for width in widths:
            in_specs.append(
                pl.BlockSpec((tile, width), lambda s, p, i=i: (p[i] * per_shard + skip + s, 0))
            )
    operands = list(xs) + list(ws) * n_x
    if not first:
        in_specs.append(whole((rows, columns)))
        operands.append(total)
    scratch = []
    if final:
        heads = keep.shape[1]
        in_specs.append(whole(keep.shape))
        operands.append(keep)
        shapes = [
            ((rows, widths[0]), BF16),
            ((rows, widths[1]), BF16),
            ((rows, widths[2]), BF16),
            ((rows, widths[3]), F32),
            ((heads * head_size, head_size), BF16),
        ]
        out_shape = [jax.ShapeDtypeStruct(s, t) for s, t in shapes]
        out_specs = [whole(s) for s, _ in shapes]
        scratch = [pltpu.VMEM((rows, columns), F32)]
    else:
        out_shape = jax.ShapeDtypeStruct((rows, columns), F32)
        out_specs = whole((rows, columns))
    return pl.pallas_call(
        functools.partial(project_kernel, n_x, first, final, widths),
        grid_spec=pltpu.PrefetchScalarGridSpec(
            num_scalar_prefetch=1,
            grid=(depth // tile,),
            in_specs=in_specs,
            out_specs=out_specs,
            scratch_shapes=scratch,
        ),
        out_shape=out_shape,
        compiler_params=pltpu.CompilerParams(vmem_limit_bytes=VMEM_LIMIT),
        cost_estimate=pl.CostEstimate(
            flops=2 * rows * depth * n_x * columns,
            bytes_accessed=depth * n_x * (rows + columns) * 2,
            transcendentals=0,
        ),
    )(places, *operands)


def level_of(differ):
    return differ.bit_length()


def local_kernel(head_size, group, level_count, q_ref, k_ref, v_ref, l_ref, dcol_ref, drow_ref, o_ref):
    rows = q_ref.shape[0]
    heads = q_ref.shape[1] // head_size
    row_id = lax.broadcasted_iota(jnp.int32, (BLOCK, BLOCK), 0)
    col_id = lax.broadcasted_iota(jnp.int32, (BLOCK, BLOCK), 1)
    causal = row_id >= col_id
    for h in range(heads):
        g = h // group
        cols = slice(h * head_size, (h + 1) * head_size)
        kv = slice(g * head_size, (g + 1) * head_size)
        for i in range(rows // BLOCK):
            here = slice(i * BLOCK, (i + 1) * BLOCK)
            width = (i + 1) * BLOCK
            scores = dot_dims(q_ref[here, cols], k_ref[:width, kv], 1, 1)
            d_here = jnp.broadcast_to(dcol_ref[here, h : h + 1], (BLOCK, BLOCK))
            weights = {}
            mixed = []
            for j in range(i + 1):
                level = level_of(i ^ j)
                if level not in weights:
                    column = h * level_count + level
                    weights[level] = jnp.broadcast_to(
                        l_ref[here, column : column + 1], (BLOCK, BLOCK)
                    )
                there = slice(j * BLOCK, (j + 1) * BLOCK)
                gap = d_here - drow_ref[h : h + 1, there]
                if i == j:
                    gap = jnp.where(causal, gap, -jnp.inf)
                mixed.append((weights[level] * jnp.exp(gap) * scores[:, there]).astype(BF16))
            mixing = mixed[0] if i == 0 else jnp.concatenate(mixed, axis=1)
            o_ref[here, cols] = dot(mixing, v_ref[:width, kv])


def local_attention(q, k, v, level, dcol, drow, head_size, group, level_count):
    rows, width = q.shape
    args = (q, k, v, level, dcol, drow)
    return pl.pallas_call(
        functools.partial(local_kernel, head_size, group, level_count),
        grid=(1,),
        in_specs=[whole(a.shape) for a in args],
        out_specs=whole((rows, width)),
        out_shape=jax.ShapeDtypeStruct((rows, width), F32),
        compiler_params=pltpu.CompilerParams(vmem_limit_bytes=VMEM_LIMIT),
        cost_estimate=pl.CostEstimate(
            flops=4 * rows * rows * width, bytes_accessed=rows * width * 8, transcendentals=rows * rows * 4
        ),
    )(*args)


def finish_kernel(head_size, bits, o_ref, q_ref, c_ref, *refs):
    states, n_ref = refs[:bits], refs[bits]
    heads = q_ref.shape[1] // head_size
    for h in range(heads):
        cols = slice(h * head_size, (h + 1) * head_size)
        total = o_ref[:, cols]
        q = q_ref[:, cols]
        for b in range(bits):
            column = h * bits + b
            total = total + c_ref[:, column : column + 1] * dot(q, states[b][cols, :])
        mean = jnp.mean(total * total, axis=-1, keepdims=True)
        n_ref[:, cols] = (total * lax.rsqrt(mean + 1e-05)).astype(BF16)


def finish(local, q, coef, states, head_size):
    rows, width = q.shape
    bits = len(states)
    args = (local, q, coef, *states)
    return pl.pallas_call(
        functools.partial(finish_kernel, head_size, bits),
        grid=(1,),
        in_specs=[whole(a.shape) for a in args],
        out_specs=whole((rows, width)),
        out_shape=jax.ShapeDtypeStruct((rows, width), BF16),
        compiler_params=pltpu.CompilerParams(vmem_limit_bytes=VMEM_LIMIT),
        cost_estimate=pl.CostEstimate(
            flops=2 * rows * width * head_size * bits, bytes_accessed=rows * width * 8, transcendentals=0
        ),
    )(*args)


def out_kernel(place, n0_ref, n1_ref, w0_ref, w1_ref, o_ref):
    o_ref[...] = (dot(n0_ref[...], w0_ref[...]) + dot(n1_ref[...], w1_ref[...])).astype(o_ref.dtype)


def out_block(n0, n1, w_out, w1, place, dtype, tile=256):
    rows, depth = n0.shape
    columns = w1.shape[1]
    steps = columns // tile
    return pl.pallas_call(
        out_kernel,
        grid_spec=pltpu.PrefetchScalarGridSpec(
            num_scalar_prefetch=1,
            grid=(steps,),
            in_specs=[
                whole((rows, depth)),
                whole((rows, depth)),
                pl.BlockSpec((depth, tile), lambda s, p: (0, p[0] * steps + s)),
                pl.BlockSpec((depth, tile), lambda s, p: (0, s)),
            ],
            out_specs=pl.BlockSpec((rows, tile), lambda s, p: (0, s)),
        ),
        out_shape=jax.ShapeDtypeStruct((rows, columns), dtype),
        compiler_params=pltpu.CompilerParams(vmem_limit_bytes=VMEM_LIMIT),
        cost_estimate=pl.CostEstimate(
            flops=4 * rows * columns * depth, bytes_accessed=(rows + depth) * columns * 4, transcendentals=0
        ),
    )(place, n0, n1, w_out, w1)


def body(tokens, log_decay, w_query, w_key, w_value, w_level, w_out):
    rows, shard = tokens.shape
    heads = log_decay.shape[1]
    head_size = w_out.shape[0] // heads
    level_count = w_level.shape[1] // heads
    group = heads // (w_key.shape[1] // head_size)
    seq_size = lax.axis_size("seq")
    seq_bits = seq_size.bit_length() - 1
    local_levels = level_count - seq_bits
    me = lax.axis_index("tp")
    slab = lax.axis_index("seq")
    ws = (w_query, w_key, w_value, w_level)

    def swap_tp(x, bit):
        return lax.ppermute(x, "tp", [(i, i ^ bit) for i in range(4)])

    def swap_seq(x, bit):
        return lax.ppermute(x, "seq", [(i, i ^ bit) for i in range(seq_size)])

    parts = 2
    depth = shard // parts
    far = [swap_tp(tokens[:, p * depth : (p + 1) * depth], 2) for p in range(parts)]
    near = swap_tp(tokens, 1)
    far_near = [swap_tp(x, 1) for x in far]

    dcol = jnp.cumsum(log_decay, axis=0)
    drow = dcol.T
    slab_total = dcol[rows - 1]
    keep = jnp.exp(slab_total[None, :] - dcol)
    group_total, before = slab_total, jnp.zeros_like(slab_total)
    fades, spans = [], []
    for b in range(seq_bits):
        upper = (jnp.right_shift(slab, b) & 1) == 1
        other_total = swap_seq(group_total, 1 << b)
        spans.append(jnp.where(upper, before, -jnp.inf))
        fades.append((upper, jnp.exp(jnp.where(upper, group_total, other_total))))
        before = before + jnp.where(upper, other_total, 0.0)
        group_total = group_total + other_total
    span = jnp.exp(dcol[:, :, None] + jnp.stack(spans, axis=-1)[None])

    mine = me.astype(jnp.int32)
    near_places = jnp.stack([mine, mine ^ 1])
    far_places = jnp.stack([mine ^ 2, mine ^ 3])
    total = project((tokens, near), near_places, ws, 0, 256, None, None, head_size)
    for p in range(parts):
        last = p == parts - 1
        total = project(
            (far[p], far_near[p]), far_places, ws, p * depth, 256, total, keep if last else None, head_size
        )
    q, k, v, level, state = total

    earlier = []
    for b in range(seq_bits):
        other = swap_seq(state, 1 << b)
        earlier.append(other)
        if b < seq_bits - 1:
            upper, fade = fades[b]
            rows_fade = jnp.repeat(fade, head_size)[:, None]
            last = jnp.where(upper, state, other).astype(F32)
            first = jnp.where(upper, other, state).astype(F32)
            state = (last + rows_fade * first).astype(BF16)

    local = local_attention(q, k, v, level, dcol, drow, head_size, group, level_count)
    remote_level = level.reshape(rows, heads, level_count)[:, :, local_levels:]
    coef = (remote_level * span).reshape(rows, heads * seq_bits)
    normed = finish(local, q, coef, earlier, head_size)

    def columns_of(place):
        return lax.dynamic_slice_in_dim(w_out, place * shard, shard, axis=1)

    w_far = swap_tp(columns_of(mine ^ 3), 1)
    w_here = swap_tp(columns_of(mine ^ 1), 1)
    normed_near = swap_tp(normed, 1)
    for_far = out_block(normed, normed_near, w_out, w_far, (mine ^ 2)[None], BF16)
    arrived = swap_tp(for_far, 2)
    here = out_block(normed, normed_near, w_out, w_here, mine[None], F32)
    return (here + arrived.astype(F32)).astype(BF16)


def solution(mesh):
    in_specs = (
        P("seq", "tp"),
        P("seq", "tp"),
        P(None, "tp"),
        P(None, "tp"),
        P(None, "tp"),
        P(None, "tp"),
        P("tp", None),
    )
    out_specs = P("seq", "tp")
    return jax.shard_map(body, mesh=mesh, in_specs=in_specs, out_specs=out_specs, check_vma=False)
```

```python
import functools

import jax
import jax.numpy as jnp
from jax import lax
from jax.experimental import pallas as pl
from jax.experimental.pallas import tpu as pltpu
from jax.sharding import PartitionSpec as P

BLOCK = 128
F32 = jnp.float32
BF16 = jnp.bfloat16
VMEM = pl.BlockSpec(memory_space=pltpu.VMEM)
SMEM = pl.BlockSpec(memory_space=pltpu.SMEM)
ANY = pl.BlockSpec(memory_space=pl.ANY)


def dot(a, b):
    return jnp.dot(a, b, preferred_element_type=F32)


def dot_dims(a, b, left, right):
    return lax.dot_general(a, b, (((left,), (right,)), ((), ())), preferred_element_type=F32)


def shape(dims, dtype):
    return jax.ShapeDtypeStruct(dims, dtype)


def call(kernel, ins, outs, flops, after=(), smem=0, aliases=None, megabytes=8):
    count = len(ins)

    def run(*refs):
        kernel(*refs[:count], *refs[count + len(after) :])

    nbytes = sum(x.size * x.dtype.itemsize for x in (*ins, *outs)) if flops else 0
    return pl.pallas_call(
        run,
        in_specs=[SMEM] * smem + [VMEM] * (count - smem) + [ANY] * len(after),
        out_specs=[VMEM] * len(outs),
        out_shape=list(outs),
        input_output_aliases=aliases or {},
        compiler_params=pltpu.CompilerParams(vmem_limit_bytes=megabytes * 1024 * 1024),
        cost_estimate=pl.CostEstimate(flops=flops, bytes_accessed=nbytes, transcendentals=0),
    )(*ins, *after)


def gate(x, *after):
    def run(*refs):
        pass

    return pl.pallas_call(
        run,
        in_specs=[ANY] * (1 + len(after)),
        out_specs=ANY,
        out_shape=shape(x.shape, x.dtype),
        input_output_aliases={0: 0},
        compiler_params=pltpu.CompilerParams(vmem_limit_bytes=1024 * 1024),
        cost_estimate=pl.CostEstimate(flops=0, bytes_accessed=0, transcendentals=0),
    )(x, *after)


def rows_of(w_ref, start, depth):
    return w_ref[pl.ds(pl.multiple_of(start, 128), depth), :]


def add_products(places, xs, w_ref, offset):
    shard = w_ref.shape[0] // 4
    total = None
    for i, x_ref in enumerate(xs):
        depth = x_ref.shape[1]
        add = dot(x_ref[...], rows_of(w_ref, places[i] * shard + offset, depth))
        total = add if total is None else total + add
    return total


def add_keys_values(places, xs, wk_ref, wv_ref, offset):
    shard = wk_ref.shape[0] // 4
    total = None
    for i, x_ref in enumerate(xs):
        depth = x_ref.shape[1]
        start = places[i] * shard + offset
        w = jnp.concatenate([rows_of(wk_ref, start, depth), rows_of(wv_ref, start, depth)], axis=1)
        add = dot(x_ref[...], w)
        total = add if total is None else total + add
    return total


def project(places, xs, ws, offset, totals, after=()):
    rows = xs[0].shape[0]
    n_x = len(xs)
    wq, wk, wv, wl = ws
    widths = (wq.shape[1], wk.shape[1] + wv.shape[1], wl.shape[1])

    def kernel(p, *refs):
        x, (q_ref, k_ref, v_ref, l_ref), rest = refs[:n_x], refs[n_x : n_x + 4], refs[n_x + 4 :]
        ins, outs = (rest[:3], rest[3:]) if totals is not None else (None, rest)
        kv = add_keys_values(p, x, k_ref, v_ref, offset)
        outs[1][...] = kv if ins is None else ins[1][...] + kv
        q = add_products(p, x, q_ref, offset)
        outs[0][...] = q if ins is None else ins[0][...] + q
        level = add_products(p, x, l_ref, offset)
        outs[2][...] = level if ins is None else ins[2][...] + level

    ins = [places, *xs, *ws]
    aliases = {}
    if totals is not None:
        aliases = {len(ins) + i: i for i in range(3)}
        ins += list(totals)
    outs = [shape((rows, w), F32) for w in widths]
    return call(kernel, ins, outs, 0, after, smem=1, aliases=aliases)


def project_state(places, xs, wk, wv, offset, total_kv, keep, head_size):
    rows, depth = xs[0].shape
    n_x = len(xs)
    heads = keep.shape[1]
    kv_width = wk.shape[1]
    group = heads // (kv_width // head_size)

    def kernel(p, *refs):
        x, (wk_ref, wv_ref, total_ref, keep_ref, k_out, v_out, s_out) = refs[:n_x], refs[n_x:]
        total = total_ref[...] + add_keys_values(p, x, wk_ref, wv_ref, offset)
        keys = total[:, :kv_width].astype(BF16)
        values = total[:, kv_width:].astype(BF16)
        k_out[...] = keys
        v_out[...] = values
        for g in range(kv_width // head_size):
            cols = slice(g * head_size, (g + 1) * head_size)
            kf = keys[:, cols].astype(F32)
            weighted = jnp.concatenate(
                [(kf * keep_ref[:, h : h + 1]).astype(BF16) for h in range(g * group, (g + 1) * group)],
                axis=1,
            )
            wide = slice(g * group * head_size, (g + 1) * group * head_size)
            s_out[:, wide] = dot_dims(values[:, cols], weighted, 0, 0).astype(BF16)

    outs = [
        shape((rows, kv_width), BF16),
        shape((rows, kv_width), BF16),
        shape((head_size, heads * head_size), BF16),
    ]
    flops = 4 * rows * depth * n_x * kv_width + 2 * rows * heads * head_size**2
    return call(kernel, [places, *xs, wk, wv, total_kv, keep], outs, flops, smem=1)


def attend(places, xs, wq, wl, offset, total_q, total_l, k, v, dcol, drow, head_size, level_count):
    rows, width = total_q.shape
    n_x = len(xs)
    heads = width // head_size
    group = heads // (k.shape[1] // head_size)

    def kernel(p, *refs):
        x, refs = refs[:n_x], refs[n_x:]
        wq_ref, wl_ref, tq_ref, tl_ref, k_ref, v_ref, dcol_ref, drow_ref, q_ref, l_ref, o_ref = refs
        raw = tl_ref[...] + add_products(p, x, wl_ref, offset)
        l_ref[...] = jnp.maximum(raw, 0.0) + jnp.log1p(jnp.exp(-jnp.abs(raw)))
        q_ref[...] = (tq_ref[...] + add_products(p, x, wq_ref, offset)).astype(BF16)
        row_id = lax.broadcasted_iota(jnp.int32, (BLOCK, BLOCK), 0)
        col_id = lax.broadcasted_iota(jnp.int32, (BLOCK, BLOCK), 1)
        causal = row_id >= col_id
        for h in range(heads):
            g = h // group
            cols = slice(h * head_size, (h + 1) * head_size)
            kv = slice(g * head_size, (g + 1) * head_size)
            for i in range(rows // BLOCK):
                here = slice(i * BLOCK, (i + 1) * BLOCK)
                span = (i + 1) * BLOCK
                scores = dot_dims(q_ref[here, cols], k_ref[:span, kv], 1, 1)
                d_here = jnp.broadcast_to(dcol_ref[here, h : h + 1], (BLOCK, BLOCK))
                weights = {}
                mixed = []
                for j in range(i + 1):
                    level = (i ^ j).bit_length()
                    if level not in weights:
                        column = h * level_count + level
                        weights[level] = jnp.broadcast_to(
                            l_ref[here, column : column + 1], (BLOCK, BLOCK)
                        )
                    there = slice(j * BLOCK, (j + 1) * BLOCK)
                    gap = d_here - drow_ref[h : h + 1, there]
                    if i == j:
                        gap = jnp.where(causal, gap, -jnp.inf)
                    mixed.append((weights[level] * jnp.exp(gap) * scores[:, there]).astype(BF16))
                mixing = mixed[0] if i == 0 else jnp.concatenate(mixed, axis=1)
                o_ref[here, cols] = dot(mixing, v_ref[:span, kv])

    ins = [places, *xs, wq, wl, total_q, total_l, k, v, dcol, drow]
    outs = [shape((rows, width), BF16), shape(total_l.shape, F32), shape((rows, width), F32)]
    flops = 2 * rows * xs[0].shape[1] * n_x * width + 4 * rows * rows * width
    return call(kernel, ins, outs, flops, smem=1)


def finish(local, q, level, span, states, rows, head_size, level_count, after=()):
    width = q.shape[1]
    heads = width // head_size
    bits = len(states)
    own_levels = level_count - bits

    def kernel(o_ref, q_ref, l_ref, c_ref, *refs):
        state_refs, n_ref = refs[:bits], refs[bits]
        for h in range(heads):
            cols = slice(h * head_size, (h + 1) * head_size)
            total = o_ref[rows, cols]
            query = q_ref[rows, cols]
            for b in range(bits):
                at = h * level_count + own_levels + b
                factor = l_ref[rows, at : at + 1] * c_ref[rows, h * bits + b : h * bits + b + 1]
                total = total + factor * dot_dims(query, state_refs[b][:, cols], 1, 1)
            mean = jnp.mean(total * total, axis=-1, keepdims=True)
            n_ref[:, cols] = (total * lax.rsqrt(mean + 1e-05)).astype(BF16)

    count = rows.stop - rows.start
    outs = [shape((count, width), BF16)]
    flops = 2 * count * width * head_size * bits
    return call(kernel, [local, q, level, span, *states], outs, flops, after)[0]


def out_block(n0s, n1s, w0, w1, dtype, after=()):
    columns = w0.shape[1]
    count = len(n0s)
    rows = sum(n.shape[0] for n in n0s)
    tile = min(columns, 512)

    def kernel(*refs):
        first, second = refs[:count], refs[count : 2 * count]
        w0_ref, w1_ref, o_ref = refs[2 * count :]
        at = 0
        for a_ref, b_ref in zip(first, second):
            here = slice(at, at + a_ref.shape[0])
            at += a_ref.shape[0]
            for c in range(0, columns, tile):
                cols = slice(c, c + tile)
                o_ref[here, cols] = (
                    dot(a_ref[...], w0_ref[:, cols]) + dot(b_ref[...], w1_ref[:, cols])
                ).astype(o_ref.dtype)

    flops = 4 * rows * columns * w0.shape[0]
    return call(kernel, [*n0s, *n1s, w0, w1], [shape((rows, columns), dtype)], flops, after)[0]


def add_rows(here, arrived, out, start):
    count, columns = arrived.shape
    block = start // count

    def kernel(h_ref, a_ref, *refs):
        o_ref = refs[-1]
        o_ref[...] = (h_ref[...] + a_ref[...].astype(F32)).astype(BF16)

    spec = pl.BlockSpec((count, columns), lambda s: (block, 0))
    ins, specs, aliases = [here, arrived], [spec, pl.BlockSpec((count, columns), lambda s: (0, 0))], {}
    if out is not None:
        ins, specs, aliases = ins + [out], specs + [ANY], {2: 0}
    return pl.pallas_call(
        kernel,
        grid=(1,),
        in_specs=specs,
        out_specs=spec,
        out_shape=shape(here.shape, BF16),
        input_output_aliases=aliases,
        compiler_params=pltpu.CompilerParams(vmem_limit_bytes=8 * 1024 * 1024),
        cost_estimate=pl.CostEstimate(flops=count * columns, bytes_accessed=count * columns * 8, transcendentals=0),
    )(*ins)


def body(tokens, log_decay, w_query, w_key, w_value, w_level, w_out):
    rows, shard = tokens.shape
    heads = log_decay.shape[1]
    head_size = w_out.shape[0] // heads
    level_count = w_level.shape[1] // heads
    seq_size = lax.axis_size("seq")
    seq_bits = seq_size.bit_length() - 1
    me = lax.axis_index("tp").astype(jnp.int32)
    slab = lax.axis_index("seq")
    ws = (w_query, w_key, w_value, w_level)

    def swap_tp(x, bit):
        return lax.ppermute(x, "tp", [(i, i ^ bit) for i in range(4)])

    def swap_seq(x, bit):
        return lax.ppermute(x, "seq", [(i, i ^ bit) for i in range(seq_size)])

    parts = 4
    depth = shard // parts
    piece = tokens[:, :depth]
    piece, tokens_later = lax.optimization_barrier((piece, tokens))
    pieces = [piece] + [tokens_later[:, p * depth : (p + 1) * depth] for p in range(1, parts)]
    far = [swap_tp(x, 2) for x in pieces]
    near = swap_tp(tokens, 1)

    dcol = jnp.cumsum(log_decay, axis=0)
    drow = dcol.T
    slab_total = dcol[rows - 1]
    keep = jnp.exp(slab_total[None, :] - dcol)
    group_total, before = slab_total, jnp.zeros_like(slab_total)
    fades, spans = [], []
    for b in range(seq_bits):
        upper = (jnp.right_shift(slab, b) & 1) == 1
        spans.append(jnp.where(upper, before, -jnp.inf))
        if b < seq_bits - 1:
            other_total = swap_seq(group_total, 1 << b)
            fade = jnp.exp(jnp.where(upper, group_total, other_total))
            fades.append((upper, jnp.repeat(fade, head_size)[None, :]))
            before = before + jnp.where(upper, other_total, 0.0)
            group_total = group_total + other_total
    span = jnp.exp(dcol[:, :, None] + jnp.stack(spans, axis=-1)[None]).reshape(rows, heads * seq_bits)

    near_places = jnp.stack([me, me ^ 1])
    far_places = jnp.stack([me ^ 2, me ^ 3])
    totals = project(near_places, (tokens, near), ws, 0, None)

    def columns_of(place):
        return lax.dynamic_slice_in_dim(w_out, place * shard, shard, axis=1)

    w_far = swap_tp(columns_of(me ^ 3), 1)
    w_here = swap_tp(columns_of(me ^ 1), 1)
    w_far_own, w_here_own = columns_of(me ^ 2), columns_of(me)

    for p in range(parts):
        arrived = gate(far[p], totals[0])
        pair = (arrived, swap_tp(arrived, 1))
        if p < parts - 1:
            after = {0: (span, keep, fades[-1][1]), 2: (w_far, w_here, w_far_own, w_here_own)}.get(p, ())
            totals = project(far_places, pair, ws, p * depth, totals, after)
    total_q, total_kv, total_l = totals
    last = (parts - 1) * depth
    k, v, state = project_state(far_places, pair, w_key, w_value, last, total_kv, keep, head_size)

    earlier = []
    for b in range(seq_bits):
        other = swap_seq(state, 1 << b)
        earlier.append(other)
        if b < seq_bits - 1:
            upper, fade = fades[b]
            later = jnp.where(upper, state, other).astype(F32)
            sooner = jnp.where(upper, other, state).astype(F32)
            state = (later + fade * sooner).astype(BF16)

    q, level, local = attend(
        far_places, pair, w_query, w_level, last, total_q, total_l, k, v, dcol, drow, head_size, level_count
    )

    step = rows // 4
    cuts = [slice(r, r + step) for r in range(0, rows, step)]
    own, near_normed, crossing = [], [], []
    for r, cut in enumerate(cuts):
        after = (own[-1],) if r else ()
        if r >= 2:
            after += (crossing[r - 2],)
        normed = finish(local, q, level, span, earlier, cut, head_size, level_count, after)
        own.append(normed)
        near_normed.append(swap_tp(normed, 1))
        if r:
            crossing.append(out_block(own[r - 1 : r], near_normed[r - 1 : r], w_far_own, w_far, BF16))
    crossing.append(out_block(own[-1:], near_normed[-1:], w_far_own, w_far, BF16))
    here = out_block(own, near_normed, w_here_own, w_here, F32, (crossing[-1],))
    out = None
    for cut, x in zip(cuts, crossing):
        out = add_rows(here, swap_tp(x, 2), out, cut.start)
    return out


def solution(mesh):
    in_specs = (
        P("seq", "tp"),
        P("seq", "tp"),
        P(None, "tp"),
        P(None, "tp"),
        P(None, "tp"),
        P(None, "tp"),
        P("tp", None),
    )
    out_specs = P("seq", "tp")
    return jax.shard_map(body, mesh=mesh, in_specs=in_specs, out_specs=out_specs, check_vma=False)
```

```python
import functools

import jax
import jax.numpy as jnp
from jax import lax
from jax.experimental import pallas as pl
from jax.experimental.pallas import tpu as pltpu
from jax.sharding import PartitionSpec as P

BLOCK = 128
F32 = jnp.float32
BF16 = jnp.bfloat16
VMEM = pl.BlockSpec(memory_space=pltpu.VMEM)
SMEM = pl.BlockSpec(memory_space=pltpu.SMEM)
ANY = pl.BlockSpec(memory_space=pl.ANY)


def dot(a, b):
    return jnp.dot(a, b, preferred_element_type=F32)


def dot_dims(a, b, left, right):
    return lax.dot_general(a, b, (((left,), (right,)), ((), ())), preferred_element_type=F32)


def shape(dims, dtype):
    return jax.ShapeDtypeStruct(dims, dtype)


def call(kernel, ins, outs, flops, after=(), smem=0, aliases=None, megabytes=8):
    count = len(ins)

    def run(*refs):
        kernel(*refs[:count], *refs[count + len(after) :])

    nbytes = sum(x.size * x.dtype.itemsize for x in (*ins, *outs)) if flops else 0
    return pl.pallas_call(
        run,
        in_specs=[SMEM] * smem + [VMEM] * (count - smem) + [ANY] * len(after),
        out_specs=[VMEM] * len(outs),
        out_shape=list(outs),
        input_output_aliases=aliases or {},
        compiler_params=pltpu.CompilerParams(vmem_limit_bytes=megabytes * 1024 * 1024),
        cost_estimate=pl.CostEstimate(flops=flops, bytes_accessed=nbytes, transcendentals=0),
    )(*ins, *after)


def gate(x, *after):
    def run(*refs):
        pass

    return pl.pallas_call(
        run,
        in_specs=[ANY] * (1 + len(after)),
        out_specs=ANY,
        out_shape=shape(x.shape, x.dtype),
        input_output_aliases={0: 0},
        compiler_params=pltpu.CompilerParams(vmem_limit_bytes=1024 * 1024),
        cost_estimate=pl.CostEstimate(flops=0, bytes_accessed=0, transcendentals=0),
    )(x, *after)


def cut_columns(tokens, ways):
    rows, columns = tokens.shape
    depth = columns // ways

    def kernel(t_ref, first_ref, second_ref):
        first_ref[...] = t_ref[:, :depth]
        second_ref[0] = t_ref[:, depth : depth + depth // 2]
        second_ref[1] = t_ref[:, depth + depth // 2 :]

    outs = [shape((rows, depth), tokens.dtype), shape((2, rows, depth // 2), tokens.dtype)]
    return call(kernel, [tokens], outs, 0)


def upper_half(slab_ref, bit):
    return ((slab_ref[0] >> bit) & 1) == 1


def decays(slab, log_decay_rows, head_size):
    heads, rows = log_decay_rows.shape

    def kernel(slab_ref, x_ref, row_ref, col_ref, keep_ref, total_ref, span_ref):
        x = x_ref[...]
        x = jnp.concatenate([x, jnp.zeros((-heads % 8, rows), F32)], axis=0) if heads % 8 else x
        place = lax.broadcasted_iota(jnp.int32, x.shape, 1)
        shift = 1
        while shift < rows:
            x = x + jnp.where(place >= shift, pltpu.roll(x, shift, 1), 0.0)
            shift *= 2
        total = x[:, rows - 1 : rows]
        row_ref[...] = x[:heads]
        col_ref[...] = jnp.transpose(x)[:, :heads]
        keep_ref[...] = jnp.transpose(jnp.exp(total - x))[:, :heads]
        for h in range(heads):
            total_ref[:, h * head_size : (h + 1) * head_size] = jnp.broadcast_to(
                total[h : h + 1], (8, head_size)
            )
        span_ref[...] = jnp.full(span_ref.shape, jnp.where(upper_half(slab_ref, 0), 0.0, -jnp.inf), F32)

    wide = shape((8, heads * head_size), F32)
    outs = [shape((heads, rows), F32), shape((rows, heads), F32), shape((rows, heads), F32), wide, wide]
    return call(kernel, [slab, log_decay_rows], outs, 0, smem=1)


def link(slab, bit, total, other, before):
    def kernel(slab_ref, *refs):
        total_ref, other_ref = refs[:2]
        total_out, before_out, own_out, other_out, span_out = refs[-5:]
        upper = upper_half(slab_ref, bit)
        here, there = total_ref[...], other_ref[...]
        total_out[...] = here + there
        so_far = jnp.where(upper, there, 0.0)
        if before is not None:
            so_far = so_far + refs[2][...]
        before_out[...] = so_far
        own_out[...] = jnp.where(upper, 1.0, jnp.exp(there))
        other_out[...] = jnp.where(upper, jnp.exp(here), 1.0)
        span_out[...] = jnp.where(upper_half(slab_ref, bit + 1), so_far, -jnp.inf)

    ins = [slab, total, other] + ([] if before is None else [before])
    return call(kernel, ins, [shape(total.shape, F32)] * 5, 0, smem=1)


def combine(state, other, own_factor, other_factor):
    def kernel(s_ref, o_ref, a_ref, b_ref, out_ref):
        out_ref[...] = (
            a_ref[0:1, :] * s_ref[...].astype(F32) + b_ref[0:1, :] * o_ref[...].astype(F32)
        ).astype(BF16)

    return call(kernel, [state, other, own_factor, other_factor], [shape(state.shape, BF16)], 0)[0]


def pad_widths(width):
    return -(-width // 128) * 128


def project_first(me, tokens, near, ws, after=(), tile=256):
    rows, shard = tokens.shape
    wq, wk, wv, wl = ws
    q_width, kv_width, l_width = wq.shape[1], wk.shape[1], wl.shape[0]
    steps = shard // tile
    n_after = len(after)

    def kernel(me_ref, *refs):
        x_refs, w_refs = refs[:2], refs[2:18]
        total_q, total_kv, total_l, q_out, kv_out, l_out = refs[18 + n_after :]
        step = pl.program_id(0)

        @pl.when(step == 0)
        def _():
            total_q[...] = jnp.zeros_like(total_q)
            total_kv[...] = jnp.zeros_like(total_kv)
            total_l[...] = jnp.zeros_like(total_l)

        def joined(i):
            return jnp.concatenate([w_refs[4 * i + 1][...], w_refs[4 * i + 2][...]], axis=1)

        x0, x1 = x_refs[0][...], x_refs[1][...]
        total_q[...] += dot(x0, w_refs[0][...]) + dot(x1, w_refs[4][...])
        total_kv[...] += dot(x0, joined(0)) + dot(x1, joined(1))
        total_l[...] += dot_dims(x0, w_refs[3][...], 1, 1) + dot_dims(x1, w_refs[7][...], 1, 1)
        for i in (2, 3):
            q_out[i - 2] = w_refs[4 * i][...]
            kv_out[i - 2] = joined(i)
            l_out[i - 2] = w_refs[4 * i + 3][...]

    x_spec = pl.BlockSpec((rows, tile), lambda s, m: (0, s))
    w_specs, operands = [], []
    for i in range(4):
        for w in (wq, wk, wv):
            w_specs.append(pl.BlockSpec((tile, w.shape[1]), lambda s, m, i=i: ((m[0] ^ i) * steps + s, 0)))
        w_specs.append(pl.BlockSpec((l_width, tile), lambda s, m, i=i: (0, (m[0] ^ i) * steps + s)))
        operands += [wq, wk, wv, wl]
    out_shape = [
        shape((rows, q_width), F32),
        shape((rows, 2 * kv_width), F32),
        shape((rows, l_width), F32),
        shape((2, shard, q_width), BF16),
        shape((2, shard, 2 * kv_width), BF16),
        shape((2, l_width, shard), BF16),
    ]
    out_specs = [pl.BlockSpec(o.shape, lambda s, m: (0, 0)) for o in out_shape[:3]]
    out_specs += [
        pl.BlockSpec((2, tile, q_width), lambda s, m: (0, s, 0)),
        pl.BlockSpec((2, tile, 2 * kv_width), lambda s, m: (0, s, 0)),
        pl.BlockSpec((2, l_width, tile), lambda s, m: (0, 0, s)),
    ]
    outs = pl.pallas_call(
        kernel,
        grid_spec=pltpu.PrefetchScalarGridSpec(
            num_scalar_prefetch=1,
            grid=(steps,),
            in_specs=[x_spec, x_spec, *w_specs] + [ANY] * n_after,
            out_specs=out_specs,
        ),
        out_shape=out_shape,
        compiler_params=pltpu.CompilerParams(vmem_limit_bytes=16 * 1024 * 1024),
        cost_estimate=pl.CostEstimate(flops=0, bytes_accessed=0, transcendentals=0),
    )(me, tokens, near, *operands, *after)
    return outs[:3], outs[3:]


def add_products(xs, w_ref, offset):
    total = None
    for i, x_ref in enumerate(xs):
        add = dot(x_ref[...], w_ref[i, offset : offset + x_ref.shape[1], :])
        total = add if total is None else total + add
    return total


def add_levels(xs, wl_ref, offset):
    total = None
    for i, x_ref in enumerate(xs):
        add = dot_dims(x_ref[...], wl_ref[i, :, offset : offset + x_ref.shape[1]], 1, 1)
        total = add if total is None else total + add
    return total


def project(xs, ws, offset, totals, after=()):
    n_x = len(xs)

    def kernel(*refs):
        x, (q_ref, kv_ref, l_ref), ins, outs = refs[:n_x], refs[n_x : n_x + 3], refs[-6:-3], refs[-3:]
        outs[1][...] = ins[1][...] + add_products(x, kv_ref, offset)
        outs[0][...] = ins[0][...] + add_products(x, q_ref, offset)
        outs[2][...] = ins[2][...] + add_levels(x, l_ref, offset)

    ins = [*xs, *ws, *totals]
    aliases = {n_x + 3 + i: i for i in range(3)}
    outs = [shape(t.shape, F32) for t in totals]
    return call(kernel, ins, outs, 0, after, aliases=aliases)


def project_state(xs, wkv, offset, total_kv, keep, head_size):
    rows, depth = xs[0].shape
    n_x = len(xs)
    heads = keep.shape[1]
    kv_width = wkv.shape[2] // 2
    group = heads // (kv_width // head_size)

    def kernel(*refs):
        x, (w_ref, total_ref, keep_ref, k_out, v_out, s_out) = refs[:n_x], refs[n_x:]
        total = total_ref[...] + add_products(x, w_ref, offset)
        keys = total[:, :kv_width].astype(BF16)
        values = total[:, kv_width:].astype(BF16)
        k_out[...] = keys
        v_out[...] = values
        for g in range(kv_width // head_size):
            cols = slice(g * head_size, (g + 1) * head_size)
            kf = keys[:, cols].astype(F32)
            weighted = jnp.concatenate(
                [(kf * keep_ref[:, h : h + 1]).astype(BF16) for h in range(g * group, (g + 1) * group)],
                axis=1,
            )
            wide = slice(g * group * head_size, (g + 1) * group * head_size)
            s_out[:, wide] = dot_dims(values[:, cols], weighted, 0, 0).astype(BF16)

    outs = [
        shape((rows, kv_width), BF16),
        shape((rows, kv_width), BF16),
        shape((head_size, heads * head_size), BF16),
    ]
    return call(kernel, [*xs, wkv, total_kv, keep], outs, 0)


def attend(xs, wq, wl, offset, total_q, total_l, k, v, dcol, drow, spans, states, head_size, level_count):
    rows, width = total_q.shape
    n_x = len(xs)
    bits = len(spans)
    heads = width // head_size
    group = heads // (k.shape[1] // head_size)
    own_levels = level_count - bits

    def kernel(*refs):
        x, refs = refs[:n_x], refs[n_x:]
        wq_ref, wl_ref, tq_ref, tl_ref, k_ref, v_ref, dcol_ref, drow_ref = refs[:8]
        span_refs, state_refs = refs[8 : 8 + bits], refs[8 + bits : 7 + 2 * bits]
        o_ref, s_ref, q_ref, l_ref = refs[-4:]
        raw = tl_ref[...] + add_levels(x, wl_ref, offset)
        l_ref[...] = jnp.maximum(raw, 0.0) + jnp.log1p(jnp.exp(-jnp.abs(raw)))
        q_ref[...] = (tq_ref[...] + add_products(x, wq_ref, offset)).astype(BF16)
        row_id = lax.broadcasted_iota(jnp.int32, (BLOCK, BLOCK), 0)
        col_id = lax.broadcasted_iota(jnp.int32, (BLOCK, BLOCK), 1)
        causal = row_id >= col_id
        for h in range(heads):
            g = h // group
            cols = slice(h * head_size, (h + 1) * head_size)
            kv = slice(g * head_size, (g + 1) * head_size)
            for i in range(rows // BLOCK):
                here = slice(i * BLOCK, (i + 1) * BLOCK)
                span = (i + 1) * BLOCK
                query = q_ref[here, cols]
                scores = dot_dims(query, k_ref[:span, kv], 1, 1)
                d_here = jnp.broadcast_to(dcol_ref[here, h : h + 1], (BLOCK, BLOCK))

                def weight(level):
                    column = h * level_count + level
                    return jnp.broadcast_to(l_ref[here, column : column + 1], (BLOCK, BLOCK))

                weights = {}
                mixed = []
                for j in range(i + 1):
                    level = (i ^ j).bit_length()
                    if level not in weights:
                        weights[level] = weight(level)
                    there = slice(j * BLOCK, (j + 1) * BLOCK)
                    gap = d_here - drow_ref[h : h + 1, there]
                    if i == j:
                        gap = jnp.where(causal, gap, -jnp.inf)
                    mixed.append((weights[level] * jnp.exp(gap) * scores[:, there]).astype(BF16))
                mixing = mixed[0] if i == 0 else jnp.concatenate(mixed, axis=1)
                total = dot(mixing, v_ref[:span, kv])
                wide = query.astype(F32)
                for b in range(bits):
                    factor = weight(own_levels + b) * jnp.exp(d_here + span_refs[b][0:1, cols])
                    scaled = (wide * factor).astype(BF16)
                    if b == bits - 1:
                        s_ref[here, cols] = scaled
                    else:
                        total = total + dot_dims(scaled, state_refs[b][:, cols], 1, 1)
                o_ref[here, cols] = total

    ins = [*xs, wq, wl, total_q, total_l, k, v, dcol, drow, *spans, *states]
    wide = shape((rows, width), BF16)
    outs = [shape((rows, width), F32), wide, wide, shape(total_l.shape, F32)]
    flops = 2 * rows * xs[0].shape[1] * n_x * width + 4 * rows * rows * width
    return call(kernel, ins, outs, flops)[:2]


def finish(local, scaled, state, rows, head_size, after=()):
    width = local.shape[1]

    def kernel(o_ref, q_ref, s_ref, n_ref):
        for c in range(0, width, head_size):
            cols = slice(c, c + head_size)
            total = o_ref[rows, cols] + dot_dims(q_ref[rows, cols], s_ref[:, cols], 1, 1)
            mean = jnp.mean(total * total, axis=-1, keepdims=True)
            n_ref[:, cols] = (total * lax.rsqrt(mean + 1e-05)).astype(BF16)

    outs = [shape((rows.stop - rows.start, width), BF16)]
    return call(kernel, [local, scaled, state], outs, 0, after)[0]


def cut_blocks(me, w_out, after, tile=256):
    depth, columns = w_out.shape
    block = columns // 4
    steps = block // tile

    def kernel(me_ref, *refs):
        for w_ref, o_ref in zip(refs[:4], refs[-4:]):
            o_ref[...] = w_ref[...]

    in_specs = [
        pl.BlockSpec((depth, tile), lambda s, m, i=i: (0, (m[0] ^ i) * steps + s)) for i in range(4)
    ]
    return pl.pallas_call(
        kernel,
        grid_spec=pltpu.PrefetchScalarGridSpec(
            num_scalar_prefetch=1,
            grid=(steps,),
            in_specs=in_specs + [ANY] * len(after),
            out_specs=[pl.BlockSpec((depth, tile), lambda s, m: (0, s))] * 4,
        ),
        out_shape=[shape((depth, block), w_out.dtype)] * 4,
        compiler_params=pltpu.CompilerParams(vmem_limit_bytes=8 * 1024 * 1024),
        cost_estimate=pl.CostEstimate(flops=0, bytes_accessed=0, transcendentals=0),
    )(me, *[w_out] * 4, *after)


def out_far(n0, n1, w0, w1, rows_own, rows_near):
    rows, columns = rows_own.stop - rows_own.start, w1.shape[1]
    tile = min(columns, 512)

    def kernel(n0_ref, n1_ref, w0_ref, w1_ref, o_ref):
        for c in range(0, columns, tile):
            cols = slice(c, c + tile)
            o_ref[:, cols] = (
                dot(n0_ref[rows_own, :], w0_ref[:, cols]) + dot(n1_ref[rows_near, :], w1_ref[:, cols])
            ).astype(BF16)

    return call(kernel, [n0, n1, w0, w1], [shape((rows, columns), BF16)], 0)[0]


def out_here(n0, n1, w0, w1, rows_own, rows_near, arrived, out, total_rows, start_row):
    rows, columns = arrived.shape
    block = start_row // rows
    tile = min(columns, 512)

    def kernel(n0_ref, n1_ref, w0_ref, w1_ref, a_ref, *refs):
        o_ref = refs[-1]
        for c in range(0, columns, tile):
            cols = slice(c, c + tile)
            here = dot(n0_ref[rows_own, :], w0_ref[:, cols]) + dot(n1_ref[rows_near, :], w1_ref[:, cols])
            o_ref[:, cols] = (here + a_ref[:, cols].astype(F32)).astype(BF16)

    ins, specs, aliases = [n0, n1, w0, w1, arrived], [VMEM] * 5, {}
    if out is not None:
        ins, specs, aliases = ins + [out], specs + [ANY], {5: 0}
    return pl.pallas_call(
        kernel,
        grid=(1,),
        in_specs=specs,
        out_specs=pl.BlockSpec((rows, columns), lambda s: (block, 0)),
        out_shape=shape((total_rows, columns), BF16),
        input_output_aliases=aliases,
        compiler_params=pltpu.CompilerParams(vmem_limit_bytes=8 * 1024 * 1024),
        cost_estimate=pl.CostEstimate(
            flops=4 * rows * columns * w0.shape[0], bytes_accessed=rows * columns * 16, transcendentals=0
        ),
    )(*ins)


def body(tokens, log_decay, w_query, w_key, w_value, w_level, w_out):
    rows, shard = tokens.shape
    heads = log_decay.shape[1]
    head_size = w_out.shape[0] // heads
    level_count = w_level.shape[1] // heads
    seq_size = lax.axis_size("seq")
    seq_bits = seq_size.bit_length() - 1
    me = jnp.full((1,), lax.axis_index("tp"), jnp.int32)
    slab = jnp.full((1,), lax.axis_index("seq"), jnp.int32)

    def swap_tp(x, bit):
        return lax.ppermute(x, "tp", [(i, i ^ bit) for i in range(4)])

    def swap_seq(x, bit, both=True):
        return lax.ppermute(x, "seq", [(i, i ^ bit) for i in range(seq_size) if both or not i & bit])

    half = shard // 2
    first, second = cut_columns(tokens, 2)
    far_first, far_second = swap_tp(first, 2), swap_tp(second, 2)
    near = swap_tp(tokens, 1)

    drow, dcol, keep, total, span = decays(slab, log_decay.T, head_size)
    spans, factors, before = [span], [], None
    for b in range(seq_bits - 1):
        total, before, own, other, span = link(slab, b, total, swap_seq(total, 1 << b), before)
        spans.append(span)
        factors.append((own, other))

    totals, ws = project_first(me, tokens, near, (w_query, w_key, w_value, w_level.T))
    w_here_own, w_here_send, w_far_own, w_far_send = cut_blocks(me, w_out, (totals[0],))
    w_here, w_far = swap_tp(w_here_send, 1), swap_tp(w_far_send, 1)
    arrived = gate(far_first, total, w_here_send)
    later = gate(far_second, totals[0])
    totals = project((arrived, swap_tp(arrived, 1)), ws, 0, totals, (w_far, w_here))
    arrived = later
    pair = (arrived[0], swap_tp(arrived[0], 1))
    totals = project(pair, ws, half, totals)
    pair = (arrived[1], swap_tp(arrived[1], 1))
    last = half + half // 2
    wq, wkv, wl = ws
    total_q, total_kv, total_l = totals
    k, v, state = project_state(pair, wkv, last, total_kv, keep, head_size)

    earlier = []
    for b in range(seq_bits):
        other = swap_seq(state, 1 << b, b < seq_bits - 1)
        earlier.append(other)
        if b < seq_bits - 1:
            state = combine(state, other, *factors[b])

    local, scaled = attend(
        pair, wq, wl, last, total_q, total_l, k, v, dcol, drow, spans, earlier[:-1], head_size, level_count
    )

    step = rows // 4
    normed = []
    for cut in (slice(0, step), slice(step, rows)):
        after = (normed[0][0],) if normed else ()
        own = finish(local, scaled, earlier[-1], cut, head_size, after)
        normed.append((own, swap_tp(own, 1)))
    pieces = [(normed[0], 0, 0)] + [(normed[1], r, r + step) for r in range(0, rows - step, step)]
    crossing = []
    for pair, r, _ in pieces:
        cut = slice(r, r + step)
        crossing.append(out_far(*pair, w_far_own, w_far, cut, cut))
    out = None
    for (pair, r, start), x in zip(pieces, crossing):
        cut = slice(r, r + step)
        out = out_here(*pair, w_here_own, w_here, cut, cut, swap_tp(x, 2), out, rows, start)
    return out


def solution(mesh):
    in_specs = (
        P("seq", "tp"),
        P("seq", "tp"),
        P(None, "tp"),
        P(None, "tp"),
        P(None, "tp"),
        P(None, "tp"),
        P("tp", None),
    )
    out_specs = P("seq", "tp")
    return jax.shard_map(body, mesh=mesh, in_specs=in_specs, out_specs=out_specs, check_vma=False)
```

```python
import functools

import jax
import jax.numpy as jnp
from jax import lax
from jax.experimental import pallas as pl
from jax.experimental.pallas import tpu as pltpu
from jax.sharding import PartitionSpec as P

BLOCK = 128
F32 = jnp.float32
BF16 = jnp.bfloat16
VMEM = pl.BlockSpec(memory_space=pltpu.VMEM)
SMEM = pl.BlockSpec(memory_space=pltpu.SMEM)
ANY = pl.BlockSpec(memory_space=pl.ANY)
HBM = pl.BlockSpec(memory_space=pltpu.HBM)


def dot(a, b):
    return jnp.dot(a, b, preferred_element_type=F32)


def dot_dims(a, b, left, right):
    return lax.dot_general(a, b, (((left,), (right,)), ((), ())), preferred_element_type=F32)


def shape(dims, dtype):
    return jax.ShapeDtypeStruct(dims, dtype)


def call(kernel, ins, outs, flops, after=(), smem=0, hbm=0, aliases=None, scratch=(), megabytes=8):
    count = len(ins)
    ins = list(ins)
    for i in range(smem, smem + hbm):
        ins[i] = pltpu.with_memory_space_constraint(ins[i], pltpu.HBM)

    def run(*refs):
        kernel(*refs[:count], *refs[count + len(after) :])

    nbytes = sum(x.size * x.dtype.itemsize for x in (*ins, *outs)) if flops else 0
    return pl.pallas_call(
        run,
        in_specs=[SMEM] * smem + [HBM] * hbm + [VMEM] * (count - smem - hbm) + [ANY] * len(after),
        out_specs=[VMEM] * len(outs),
        out_shape=list(outs),
        input_output_aliases=aliases or {},
        scratch_shapes=list(scratch),
        compiler_params=pltpu.CompilerParams(vmem_limit_bytes=megabytes * 1024 * 1024),
        cost_estimate=pl.CostEstimate(flops=flops, bytes_accessed=nbytes, transcendentals=0),
    )(*ins, *after)


def gate(x, *after):
    def run(*refs):
        pass

    return pl.pallas_call(
        run,
        in_specs=[ANY] * (1 + len(after)),
        out_specs=ANY,
        out_shape=shape(x.shape, x.dtype),
        input_output_aliases={0: 0},
        compiler_params=pltpu.CompilerParams(vmem_limit_bytes=1024 * 1024),
        cost_estimate=pl.CostEstimate(flops=0, bytes_accessed=0, transcendentals=0),
    )(x, *after)


def copies(pairs, sems):
    started = [pltpu.make_async_copy(src, dst, sems.at[i]) for i, (src, dst) in enumerate(pairs)]
    for copy in started:
        copy.start()
    return started


def cut_columns(tokens, cuts):
    def kernel(t_ref, *refs):
        for copy in copies([(t_ref.at[:, cut], o_ref) for cut, o_ref in zip(cuts, refs)], refs[-1]):
            copy.wait()

    outs = [shape((tokens.shape[0], cut.stop - cut.start), tokens.dtype) for cut in cuts]
    return call(kernel, [tokens], outs, 0, hbm=1, scratch=[pltpu.SemaphoreType.DMA((len(cuts),))])


def split(x, after):
    rows, columns = x.shape

    def kernel(x_ref, a_ref, b_ref):
        a_ref[...] = x_ref[:, : columns // 2]
        b_ref[...] = x_ref[:, columns // 2 :]

    return call(kernel, [x], [shape((rows, columns // 2), x.dtype)] * 2, 0, after)


def upper_half(slab_ref, bit):
    return ((slab_ref[0] >> bit) & 1) == 1


def decays(slab_ref, x_ref, row_ref, col_ref, keep_ref, total_ref, span_ref):
    heads, rows = x_ref.shape
    head_size = total_ref.shape[1] // heads
    x = x_ref[...]
    x = jnp.concatenate([x, jnp.zeros((-heads % 8, rows), F32)], axis=0) if heads % 8 else x
    place = lax.broadcasted_iota(jnp.int32, x.shape, 1)
    shift = 1
    while shift < rows:
        x = x + jnp.where(place >= shift, pltpu.roll(x, shift, 1), 0.0)
        shift *= 2
    total = x[:, rows - 1 : rows]
    row_ref[...] = x[:heads]
    col_ref[...] = jnp.transpose(x)[:, :heads]
    keep_ref[...] = jnp.transpose(jnp.exp(total - x))[:, :heads]
    for h in range(heads):
        total_ref[:, h * head_size : (h + 1) * head_size] = jnp.broadcast_to(
            total[h : h + 1], (8, head_size)
        )
    span_ref[...] = jnp.full(span_ref.shape, jnp.where(upper_half(slab_ref, 0), 0.0, -jnp.inf), F32)


def link(slab, bit, total, other, before):
    def kernel(slab_ref, *refs):
        total_ref, other_ref = refs[:2]
        total_out, before_out, own_out, other_out, span_out = refs[-5:]
        upper = upper_half(slab_ref, bit)
        here, there = total_ref[...], other_ref[...]
        total_out[...] = here + there
        so_far = jnp.where(upper, there, 0.0)
        if before is not None:
            so_far = so_far + refs[2][...]
        before_out[...] = so_far
        own_out[...] = jnp.where(upper, 1.0, jnp.exp(there))
        other_out[...] = jnp.where(upper, jnp.exp(here), 1.0)
        span_out[...] = jnp.where(upper_half(slab_ref, bit + 1), so_far, -jnp.inf)

    ins = [slab, total, other] + ([] if before is None else [before])
    return call(kernel, ins, [shape(total.shape, F32)] * 5, 0, smem=1)


def combine(state, other, own_factor, other_factor):
    def kernel(s_ref, o_ref, a_ref, b_ref, out_ref):
        out_ref[...] = (
            a_ref[0:1, :] * s_ref[...].astype(F32) + b_ref[0:1, :] * o_ref[...].astype(F32)
        ).astype(BF16)

    return call(kernel, [state, other, own_factor, other_factor], [shape(state.shape, BF16)], 0)[0]


def begin(me, slab, tokens, cuts, near, log_decay_rows, ws, w_out, head_size):
    wq, wk, wv, wl = ws
    n_x = len(tokens)
    shard = near.shape[1]
    rows = near.shape[0]
    q_width, kv_width = wq.shape[1], wk.shape[1]
    heads = log_decay_rows.shape[0]
    block = w_out.shape[1] // 4

    def kernel(me_ref, slab_ref, wq_ref, wk_ref, wv_ref, wl_ref, wo_ref, *refs):
        x_refs, near_ref, decay_ref, refs = refs[:n_x], refs[n_x], refs[n_x + 1], refs[n_x + 2 :]
        total_q, total_kv, total_l, far_q, far_kv, all_l = refs[:6]
        decay_outs, blocks, (own_q, own_kv, sems) = refs[6:11], refs[11:15], refs[15:]

        def pairs(i, q_dst, kv_dst):
            here = pl.ds(pl.multiple_of((me_ref[0] ^ i) * shard, 128), shard)
            return [
                (wk_ref.at[here, :], kv_dst.at[:, :kv_width]),
                (wv_ref.at[here, :], kv_dst.at[:, kv_width:]),
                (wq_ref.at[here, :], q_dst),
            ]

        def columns(i):
            return wo_ref.at[:, pl.ds(pl.multiple_of((me_ref[0] ^ i) * block, 128), block)]

        moves = pairs(0, own_q.at[0], own_kv.at[0]) + [(wl_ref, all_l)]
        moves += pairs(1, own_q.at[1], own_kv.at[1])
        moves += pairs(2, far_q.at[0], far_kv.at[0]) + pairs(3, far_q.at[1], far_kv.at[1])
        moves += [(columns(i), blocks[i]) for i in range(4)]
        started = copies(moves, sems)
        decays(slab_ref, decay_ref, *decay_outs)
        for copy in started[:4]:
            copy.wait()
        lanes = pl.ds(pl.multiple_of(me_ref[0] * shard, 128), shard)
        own = jnp.concatenate([x_ref[...] for x_ref in x_refs], axis=1)
        total_kv[...] = dot(own, own_kv[0])
        total_q[...] = dot(own, own_q[0])
        total_l[...] = dot_dims(own, all_l[:, lanes], 1, 1)
        for copy in started[4:7]:
            copy.wait()
        lanes = pl.ds(pl.multiple_of((me_ref[0] ^ 1) * shard, 128), shard)
        total_kv[...] += dot(near_ref[...], own_kv[1])
        total_q[...] += dot(near_ref[...], own_q[1])
        total_l[...] += dot_dims(near_ref[...], all_l[:, lanes], 1, 1)
        for copy in started[7:]:
            copy.wait()

    wide = shape((8, heads * head_size), F32)
    outs = [
        shape((rows, q_width), F32),
        shape((rows, 2 * kv_width), F32),
        shape((rows, wl.shape[0]), F32),
        shape((2, shard, q_width), BF16),
        shape((2, shard, 2 * kv_width), BF16),
        shape(wl.shape, BF16),
        shape((heads, rows), F32),
        shape((rows, heads), F32),
        shape((rows, heads), F32),
        wide,
        wide,
    ] + [shape((w_out.shape[0], block), BF16)] * 4
    scratch = [
        pltpu.VMEM((2, shard, q_width), BF16),
        pltpu.VMEM((2, shard, 2 * kv_width), BF16),
        pltpu.SemaphoreType.DMA((17,)),
    ]
    ins = [me, slab, wq, wk, wv, wl, w_out, *tokens, near, log_decay_rows]
    outs = call(kernel, ins, outs, 0, smem=2, hbm=5, scratch=scratch, megabytes=14)
    return outs[:3], outs[3:6], outs[6:11], outs[11:]


def add_products(xs, w_ref, offset):
    total = None
    for i, x_ref in enumerate(xs):
        add = dot(x_ref[...], w_ref[i, offset : offset + x_ref.shape[1], :])
        total = add if total is None else total + add
    return total


def add_levels(me_ref, xs, wl_ref, offset):
    shard = wl_ref.shape[1] // 4
    total = None
    for i, x_ref in enumerate(xs):
        start = pl.multiple_of((me_ref[0] ^ (2 + i)) * shard + offset, 128)
        add = dot_dims(x_ref[...], wl_ref[:, pl.ds(start, x_ref.shape[1])], 1, 1)
        total = add if total is None else total + add
    return total


def project(me, xs, ws, offset, totals, after=()):
    n_x = len(xs)

    def kernel(me_ref, *refs):
        x, (q_ref, kv_ref, l_ref), ins, outs = refs[:n_x], refs[n_x : n_x + 3], refs[-6:-3], refs[-3:]
        outs[1][...] = ins[1][...] + add_products(x, kv_ref, offset)
        outs[0][...] = ins[0][...] + add_products(x, q_ref, offset)
        outs[2][...] = ins[2][...] + add_levels(me_ref, x, l_ref, offset)

    ins = [me, *xs, *ws, *totals]
    aliases = {n_x + 4 + i: i for i in range(3)}
    outs = [shape(t.shape, F32) for t in totals]
    return call(kernel, ins, outs, 0, after, smem=1, aliases=aliases)


def project_state(xs, wkv, offset, total_kv, keep, head_size):
    rows, depth = xs[0].shape
    n_x = len(xs)
    heads = keep.shape[1]
    kv_width = wkv.shape[2] // 2
    group = heads // (kv_width // head_size)

    def kernel(*refs):
        x, (w_ref, total_ref, keep_ref, k_out, v_out, s_out) = refs[:n_x], refs[n_x:]
        total = total_ref[...] + add_products(x, w_ref, offset)
        keys = total[:, :kv_width].astype(BF16)
        values = total[:, kv_width:].astype(BF16)
        k_out[...] = keys
        v_out[...] = values
        for g in range(kv_width // head_size):
            cols = slice(g * head_size, (g + 1) * head_size)
            kf = keys[:, cols].astype(F32)
            weighted = jnp.concatenate(
                [(kf * keep_ref[:, h : h + 1]).astype(BF16) for h in range(g * group, (g + 1) * group)],
                axis=1,
            )
            wide = slice(g * group * head_size, (g + 1) * group * head_size)
            s_out[:, wide] = dot_dims(values[:, cols], weighted, 0, 0).astype(BF16)

    outs = [
        shape((rows, kv_width), BF16),
        shape((rows, kv_width), BF16),
        shape((head_size, heads * head_size), BF16),
    ]
    return call(kernel, [*xs, wkv, total_kv, keep], outs, 0)


def attend(me, xs, wq, wl, offset, total_q, total_l, k, v, dcol, drow, spans, states, head_size, level_count):
    rows, width = total_q.shape
    n_x = len(xs)
    bits = len(spans)
    heads = width // head_size
    group = heads // (k.shape[1] // head_size)
    own_levels = level_count - bits

    def kernel(me_ref, *refs):
        x, refs = refs[:n_x], refs[n_x:]
        wq_ref, wl_ref, tq_ref, tl_ref, k_ref, v_ref, dcol_ref, drow_ref = refs[:8]
        span_refs, state_refs = refs[8 : 8 + bits], refs[8 + bits : 7 + 2 * bits]
        o_ref, s_ref, q_ref, l_ref = refs[-4:]
        raw = tl_ref[...] + add_levels(me_ref, x, wl_ref, offset)
        l_ref[...] = jnp.maximum(raw, 0.0) + jnp.log1p(jnp.exp(-jnp.abs(raw)))
        q_ref[...] = (tq_ref[...] + add_products(x, wq_ref, offset)).astype(BF16)
        row_id = lax.broadcasted_iota(jnp.int32, (BLOCK, BLOCK), 0)
        col_id = lax.broadcasted_iota(jnp.int32, (BLOCK, BLOCK), 1)
        causal = row_id >= col_id
        for h in range(heads):
            g = h // group
            cols = slice(h * head_size, (h + 1) * head_size)
            kv = slice(g * head_size, (g + 1) * head_size)
            for i in range(rows // BLOCK):
                here = slice(i * BLOCK, (i + 1) * BLOCK)
                span = (i + 1) * BLOCK
                query = q_ref[here, cols]
                scores = dot_dims(query, k_ref[:span, kv], 1, 1)
                d_here = jnp.broadcast_to(dcol_ref[here, h : h + 1], (BLOCK, BLOCK))

                def weight(level):
                    column = h * level_count + level
                    return jnp.broadcast_to(l_ref[here, column : column + 1], (BLOCK, BLOCK))

                weights = {}
                mixed = []
                for j in range(i + 1):
                    level = (i ^ j).bit_length()
                    if level not in weights:
                        weights[level] = weight(level)
                    there = slice(j * BLOCK, (j + 1) * BLOCK)
                    gap = d_here - drow_ref[h : h + 1, there]
                    if i == j:
                        gap = jnp.where(causal, gap, -jnp.inf)
                    mixed.append((weights[level] * jnp.exp(gap) * scores[:, there]).astype(BF16))
                mixing = mixed[0] if i == 0 else jnp.concatenate(mixed, axis=1)
                total = dot(mixing, v_ref[:span, kv])
                wide = query.astype(F32)
                for b in range(bits):
                    factor = weight(own_levels + b) * jnp.exp(d_here + span_refs[b][0:1, cols])
                    scaled = (wide * factor).astype(BF16)
                    if b == bits - 1:
                        s_ref[here, cols] = scaled
                    else:
                        total = total + dot_dims(scaled, state_refs[b][:, cols], 1, 1)
                o_ref[here, cols] = total

    ins = [me, *xs, wq, wl, total_q, total_l, k, v, dcol, drow, *spans, *states]
    wide = shape((rows, width), BF16)
    outs = [shape((rows, width), F32), wide, wide, shape(total_l.shape, F32)]
    flops = 2 * rows * xs[0].shape[1] * n_x * width + 4 * rows * rows * width
    return call(kernel, ins, outs, flops, smem=1)[:2]


def finish(local, scaled, state, rows, head_size, after=()):
    width = local.shape[1]

    def kernel(o_ref, q_ref, s_ref, n_ref):
        for c in range(0, width, head_size):
            cols = slice(c, c + head_size)
            total = o_ref[rows, cols] + dot_dims(q_ref[rows, cols], s_ref[:, cols], 1, 1)
            mean = jnp.mean(total * total, axis=-1, keepdims=True)
            n_ref[:, cols] = (total * lax.rsqrt(mean + 1e-05)).astype(BF16)

    outs = [shape((rows.stop - rows.start, width), BF16)]
    return call(kernel, [local, scaled, state], outs, 0, after)[0]


def out_far(n0, n1, w0, w1, rows_own, rows_near):
    rows, columns = rows_own.stop - rows_own.start, w1.shape[1]
    tile = min(columns, 512)

    def kernel(n0_ref, n1_ref, w0_ref, w1_ref, o_ref):
        for c in range(0, columns, tile):
            cols = slice(c, c + tile)
            o_ref[:, cols] = (
                dot(n0_ref[rows_own, :], w0_ref[:, cols]) + dot(n1_ref[rows_near, :], w1_ref[:, cols])
            ).astype(BF16)

    return call(kernel, [n0, n1, w0, w1], [shape((rows, columns), BF16)], 0)[0]


def out_here(n0, n1, w0, w1, rows_own, rows_near, arrived, out, total_rows, start_row):
    rows, columns = arrived.shape
    block = start_row // rows
    tile = min(columns, 512)

    def kernel(n0_ref, n1_ref, w0_ref, w1_ref, a_ref, *refs):
        o_ref = refs[-1]
        for c in range(0, columns, tile):
            cols = slice(c, c + tile)
            here = dot(n0_ref[rows_own, :], w0_ref[:, cols]) + dot(n1_ref[rows_near, :], w1_ref[:, cols])
            o_ref[:, cols] = (here + a_ref[:, cols].astype(F32)).astype(BF16)

    ins, specs, aliases = [n0, n1, w0, w1, arrived], [VMEM] * 5, {}
    if out is not None:
        ins, specs, aliases = ins + [out], specs + [ANY], {5: 0}
    return pl.pallas_call(
        kernel,
        grid=(1,),
        in_specs=specs,
        out_specs=pl.BlockSpec((rows, columns), lambda s: (block, 0)),
        out_shape=shape((total_rows, columns), BF16),
        input_output_aliases=aliases,
        compiler_params=pltpu.CompilerParams(vmem_limit_bytes=8 * 1024 * 1024),
        cost_estimate=pl.CostEstimate(
            flops=4 * rows * columns * w0.shape[0], bytes_accessed=rows * columns * 16, transcendentals=0
        ),
    )(*ins)


def body(tokens, log_decay, w_query, w_key, w_value, w_level, w_out):
    rows, shard = tokens.shape
    heads = log_decay.shape[1]
    head_size = w_out.shape[0] // heads
    level_count = w_level.shape[1] // heads
    seq_size = lax.axis_size("seq")
    seq_bits = seq_size.bit_length() - 1
    me = jnp.full((1,), lax.axis_index("tp"), jnp.int32)
    slab = jnp.full((1,), lax.axis_index("seq"), jnp.int32)

    def swap_tp(x, bit):
        return lax.ppermute(x, "tp", [(i, i ^ bit) for i in range(4)])

    def swap_seq(x, bit):
        return lax.ppermute(x, "seq", [(i, i ^ bit) for i in range(seq_size)])

    half, quarter = shard // 2, shard // 4
    cuts = [slice(0, half), slice(half, shard)]
    pieces = cut_columns(tokens, cuts)
    far = [swap_tp(x, 2) for x in pieces]
    near = swap_tp(tokens, 1)

    weights = (w_query, w_key, w_value, w_level.T)
    totals, ws, (drow, dcol, keep, total, span), blocks = begin(
        me, slab, pieces, cuts, near, log_decay.T, weights, w_out, head_size
    )
    w_here_own, w_here_send, w_far_own, w_far_send = blocks
    w_here, w_far = swap_tp(w_here_send, 1), swap_tp(w_far_send, 1)

    spans, factors, before = [span], [], None
    for b in range(seq_bits - 1):
        total, before, own, other, span = link(slab, b, total, swap_seq(total, 1 << b), before)
        spans.append(span)
        factors.append((own, other))

    wq, wkv, wl = ws
    arrived = gate(far[0], total, totals[0])
    pair = (arrived, swap_tp(arrived, 1))
    later = split(far[1], (totals[0],))
    totals = project(me, pair, ws, 0, totals, (w_far, w_here))
    pair = (later[0], swap_tp(later[0], 1))
    totals = project(me, pair, ws, half, totals)
    pair = (later[1], swap_tp(later[1], 1))
    total_q, total_kv, total_l = totals
    last = half + quarter
    k, v, state = project_state(pair, wkv, last, total_kv, keep, head_size)

    earlier = []
    for b in range(seq_bits):
        other = swap_seq(state, 1 << b)
        earlier.append(other)
        if b < seq_bits - 1:
            state = combine(state, other, *factors[b])

    local, scaled = attend(
        me, pair, wq, wl, last, total_q, total_l, k, v, dcol, drow, spans, earlier[:-1], head_size, level_count
    )

    step = rows // 4
    normed = []
    for cut in (slice(0, step), slice(step, rows)):
        after = (normed[0][0],) if normed else ()
        own = finish(local, scaled, earlier[-1], cut, head_size, after)
        normed.append((own, swap_tp(own, 1)))
    pieces = [(normed[0], 0, 0)] + [(normed[1], r, r + step) for r in range(0, rows - step, step)]
    crossing = []
    for pair, r, _ in pieces:
        cut = slice(r, r + step)
        crossing.append(out_far(*pair, w_far_own, w_far, cut, cut))
    out = None
    for (pair, r, start), x in zip(pieces, crossing):
        cut = slice(r, r + step)
        out = out_here(*pair, w_here_own, w_here, cut, cut, swap_tp(x, 2), out, rows, start)
    return out


def solution(mesh):
    in_specs = (
        P("seq", "tp"),
        P("seq", "tp"),
        P(None, "tp"),
        P(None, "tp"),
        P(None, "tp"),
        P(None, "tp"),
        P("tp", None),
    )
    out_specs = P("seq", "tp")
    return jax.shard_map(body, mesh=mesh, in_specs=in_specs, out_specs=out_specs, check_vma=False)
```

```python
import functools

import jax
import jax.numpy as jnp
from jax import lax
from jax.experimental import pallas as pl
from jax.experimental.pallas import tpu as pltpu
from jax.sharding import PartitionSpec as P

BLOCK = 128
F32 = jnp.float32
BF16 = jnp.bfloat16
VMEM = pl.BlockSpec(memory_space=pltpu.VMEM)
SMEM = pl.BlockSpec(memory_space=pltpu.SMEM)
ANY = pl.BlockSpec(memory_space=pl.ANY)
HBM = pl.BlockSpec(memory_space=pltpu.HBM)


def dot(a, b):
    return jnp.dot(a, b, preferred_element_type=F32)


def dot_dims(a, b, left, right):
    return lax.dot_general(a, b, (((left,), (right,)), ((), ())), preferred_element_type=F32)


def shape(dims, dtype):
    return jax.ShapeDtypeStruct(dims, dtype)


def call(kernel, ins, outs, flops, after=(), smem=0, hbm=0, aliases=None, scratch=(), megabytes=8):
    count = len(ins)
    ins = list(ins)
    for i in range(smem, smem + hbm):
        ins[i] = pltpu.with_memory_space_constraint(ins[i], pltpu.HBM)

    def run(*refs):
        kernel(*refs[:count], *refs[count + len(after) :])

    nbytes = sum(x.size * x.dtype.itemsize for x in (*ins, *outs)) if flops else 0
    return pl.pallas_call(
        run,
        in_specs=[SMEM] * smem + [HBM] * hbm + [VMEM] * (count - smem - hbm) + [ANY] * len(after),
        out_specs=[VMEM] * len(outs),
        out_shape=list(outs),
        input_output_aliases=aliases or {},
        scratch_shapes=list(scratch),
        compiler_params=pltpu.CompilerParams(vmem_limit_bytes=megabytes * 1024 * 1024),
        cost_estimate=pl.CostEstimate(flops=flops, bytes_accessed=nbytes, transcendentals=0),
    )(*ins, *after)


def gate(x, *after):
    def run(*refs):
        pass

    return pl.pallas_call(
        run,
        in_specs=[ANY] * (1 + len(after)),
        out_specs=ANY,
        out_shape=shape(x.shape, x.dtype),
        input_output_aliases={0: 0},
        compiler_params=pltpu.CompilerParams(vmem_limit_bytes=1024 * 1024),
        cost_estimate=pl.CostEstimate(flops=0, bytes_accessed=0, transcendentals=0),
    )(x, *after)


def copies(pairs, sems):
    started = [pltpu.make_async_copy(src, dst, sems.at[i]) for i, (src, dst) in enumerate(pairs)]
    for copy in started:
        copy.start()
    return started


def upper_half(slab_ref, bit):
    return ((slab_ref[0] >> bit) & 1) == 1


def decays(slab_ref, x_ref, row_ref, col_ref, keep_ref, total_ref, span_ref):
    heads, rows = x_ref.shape
    head_size = total_ref.shape[1] // heads
    x = x_ref[...]
    x = jnp.concatenate([x, jnp.zeros((-heads % 8, rows), F32)], axis=0) if heads % 8 else x
    place = lax.broadcasted_iota(jnp.int32, x.shape, 1)
    shift = 1
    while shift < rows:
        x = x + jnp.where(place >= shift, pltpu.roll(x, shift, 1), 0.0)
        shift *= 2
    total = x[:, rows - 1 : rows]
    row_ref[...] = x[:heads]
    col_ref[...] = jnp.transpose(x)[:, :heads]
    keep_ref[...] = jnp.transpose(jnp.exp(total - x))[:, :heads]
    for h in range(heads):
        total_ref[:, h * head_size : (h + 1) * head_size] = jnp.broadcast_to(
            total[h : h + 1], (8, head_size)
        )
    span_ref[...] = jnp.full(span_ref.shape, jnp.where(upper_half(slab_ref, 0), 0.0, -jnp.inf), F32)


def link(slab, bit, total, other, before):
    def kernel(slab_ref, *refs):
        total_ref, other_ref = refs[:2]
        total_out, before_out, own_out, other_out, span_out = refs[-5:]
        upper = upper_half(slab_ref, bit)
        here, there = total_ref[...], other_ref[...]
        total_out[...] = here + there
        so_far = jnp.where(upper, there, 0.0)
        if before is not None:
            so_far = so_far + refs[2][...]
        before_out[...] = so_far
        own_out[...] = jnp.where(upper, 1.0, jnp.exp(there))
        other_out[...] = jnp.where(upper, jnp.exp(here), 1.0)
        span_out[...] = jnp.where(upper_half(slab_ref, bit + 1), so_far, -jnp.inf)

    ins = [slab, total, other] + ([] if before is None else [before])
    return call(kernel, ins, [shape(total.shape, F32)] * 5, 0, smem=1)


def pair_totals(total, other):
    def kernel(t_ref, o_ref, out_ref):
        out_ref[0:4, :] = t_ref[0:4, :]
        out_ref[4:8, :] = o_ref[0:4, :]

    return call(kernel, [total, other], [shape(total.shape, F32)], 0)[0]


def link_four(slab, here, there):
    def kernel(slab_ref, h_ref, t_ref, total_out, before_out, factors_out, span1_out, span2_out):
        upper, above = upper_half(slab_ref, 0), upper_half(slab_ref, 1)
        mine, beside = h_ref[0:1, :], h_ref[4:5, :]
        across, diagonal = t_ref[0:1, :], t_ref[4:5, :]
        own_pair, other_pair = mine + beside, across + diagonal
        first = jnp.where(upper, beside, 0.0)
        second = first + jnp.where(above, other_pair, 0.0)
        own_scale = jnp.where(above, 0.0, other_pair)
        other_scale = jnp.where(above, own_pair, 0.0)
        by_mine = jnp.where(upper, 0.0, beside)
        by_beside = jnp.where(upper, mine, 0.0)
        by_across = jnp.where(upper, 0.0, diagonal)
        by_diagonal = jnp.where(upper, across, 0.0)
        factors_out[0:1, :] = jnp.exp(by_mine + own_scale)
        factors_out[1:2, :] = jnp.exp(by_beside + own_scale)
        factors_out[2:3, :] = jnp.exp(by_across + other_scale)
        factors_out[3:4, :] = jnp.exp(by_diagonal + other_scale)
        factors_out[4:5, :] = jnp.exp(by_across)
        factors_out[5:6, :] = jnp.exp(by_diagonal)
        factors_out[6:8, :] = jnp.zeros((2, h_ref.shape[1]), F32)
        wide = h_ref.shape
        total_out[...] = jnp.broadcast_to(own_pair + other_pair, wide)
        before_out[...] = jnp.broadcast_to(second, wide)
        span1_out[...] = jnp.broadcast_to(jnp.where(above, first, -jnp.inf), wide)
        span2_out[...] = jnp.broadcast_to(jnp.where(upper_half(slab_ref, 2), second, -jnp.inf), wide)

    return call(kernel, [slab, here, there], [shape(here.shape, F32)] * 5, 0, smem=1)


def join_four(mine, beside, across, diagonal, factors):
    def kernel(m_ref, b_ref, a_ref, d_ref, f_ref, four_ref, pair_ref):
        m, b = m_ref[...].astype(F32), b_ref[...].astype(F32)
        a, d = a_ref[...].astype(F32), d_ref[...].astype(F32)
        f = [f_ref[i : i + 1, :] for i in range(6)]
        four_ref[...] = (f[0] * m + f[1] * b + f[2] * a + f[3] * d).astype(BF16)
        pair_ref[...] = (f[4] * a + f[5] * d).astype(BF16)

    outs = [shape(mine.shape, BF16)] * 2
    return call(kernel, [mine, beside, across, diagonal, factors], outs, 0)


def combine(state, other, own_factor, other_factor):
    def kernel(s_ref, o_ref, a_ref, b_ref, out_ref):
        out_ref[...] = (
            a_ref[0:1, :] * s_ref[...].astype(F32) + b_ref[0:1, :] * o_ref[...].astype(F32)
        ).astype(BF16)

    return call(kernel, [state, other, own_factor, other_factor], [shape(state.shape, BF16)], 0)[0]


def begin(me, slab, tokens, near, log_decay_rows, ws, w_out, head_size):
    wq, wk, wv, wl = ws
    rows, shard = near.shape
    q_width, kv_width = wq.shape[1], wk.shape[1]
    heads = log_decay_rows.shape[0]
    block = w_out.shape[1] // 4

    def kernel(me_ref, slab_ref, t_ref, wq_ref, wk_ref, wv_ref, wl_ref, wo_ref, near_ref, decay_ref, *refs):
        total_q, total_kv, total_l, far_q, far_kv, all_l = refs[:6]
        decay_outs, blocks, (own_x, own_q, own_kv, sems) = refs[6:11], refs[11:15], refs[15:]

        def pairs(i, q_dst, kv_dst):
            here = pl.ds(pl.multiple_of((me_ref[0] ^ i) * shard, 128), shard)
            return [
                (wk_ref.at[here, :], kv_dst.at[:, :kv_width]),
                (wv_ref.at[here, :], kv_dst.at[:, kv_width:]),
                (wq_ref.at[here, :], q_dst),
            ]

        def columns(i):
            return wo_ref.at[:, pl.ds(pl.multiple_of((me_ref[0] ^ i) * block, 128), block)]

        moves = pairs(0, own_q.at[0], own_kv.at[0]) + [(wl_ref, all_l), (t_ref, own_x)]
        moves += pairs(1, own_q.at[1], own_kv.at[1])
        moves += pairs(2, far_q.at[0], far_kv.at[0]) + pairs(3, far_q.at[1], far_kv.at[1])
        moves += [(columns(i), blocks[i]) for i in range(4)]
        started = copies(moves, sems)
        decays(slab_ref, decay_ref, *decay_outs)
        for copy in started[:5]:
            copy.wait()
        lanes = pl.ds(pl.multiple_of(me_ref[0] * shard, 128), shard)
        own = own_x[...]
        total_kv[...] = dot(own, own_kv[0])
        total_q[...] = dot(own, own_q[0])
        total_l[...] = dot_dims(own, all_l[:, lanes], 1, 1)
        for copy in started[5:8]:
            copy.wait()
        lanes = pl.ds(pl.multiple_of((me_ref[0] ^ 1) * shard, 128), shard)
        total_kv[...] += dot(near_ref[...], own_kv[1])
        total_q[...] += dot(near_ref[...], own_q[1])
        total_l[...] += dot_dims(near_ref[...], all_l[:, lanes], 1, 1)
        for copy in started[8:]:
            copy.wait()

    wide = shape((8, heads * head_size), F32)
    outs = [
        shape((rows, q_width), F32),
        shape((rows, 2 * kv_width), F32),
        shape((rows, wl.shape[0]), F32),
        shape((2, shard, q_width), BF16),
        shape((2, shard, 2 * kv_width), BF16),
        shape(wl.shape, BF16),
        shape((heads, rows), F32),
        shape((rows, heads), F32),
        shape((rows, heads), F32),
        wide,
        wide,
    ] + [shape((w_out.shape[0], block), BF16)] * 4
    scratch = [
        pltpu.VMEM((rows, shard), BF16),
        pltpu.VMEM((2, shard, q_width), BF16),
        pltpu.VMEM((2, shard, 2 * kv_width), BF16),
        pltpu.SemaphoreType.DMA((18,)),
    ]
    ins = [me, slab, tokens, wq, wk, wv, wl, w_out, near, log_decay_rows]
    outs = call(kernel, ins, outs, 0, smem=2, hbm=6, scratch=scratch, megabytes=14)
    return outs[:3], outs[3:6], outs[6:11], outs[11:]


def add_levels(me_ref, place, x_ref, wl_ref):
    shard = wl_ref.shape[1] // 4
    start = pl.multiple_of((me_ref[0] ^ place) * shard, 128)
    return dot_dims(x_ref[...], wl_ref[:, pl.ds(start, shard)], 1, 1)


def project(me, place, x, ws, totals, after=()):
    def kernel(me_ref, x_ref, q_ref, kv_ref, l_ref, *refs):
        ins, outs = refs[:3], refs[3:]
        outs[1][...] = ins[1][...] + dot(x_ref[...], kv_ref[place - 2])
        outs[0][...] = ins[0][...] + dot(x_ref[...], q_ref[place - 2])
        outs[2][...] = ins[2][...] + add_levels(me_ref, place, x_ref, l_ref)

    outs = [shape(t.shape, F32) for t in totals]
    return call(kernel, [me, x, *ws, *totals], outs, 0, after, smem=1, aliases={5: 0, 6: 1, 7: 2})


def project_state(x, wkv, total_kv, keep, head_size):
    rows = x.shape[0]
    heads = keep.shape[1]
    kv_width = wkv.shape[2] // 2
    group = heads // (kv_width // head_size)

    def kernel(x_ref, w_ref, total_ref, keep_ref, k_out, v_out, s_out):
        total = total_ref[...] + dot(x_ref[...], w_ref[1])
        keys = total[:, :kv_width].astype(BF16)
        values = total[:, kv_width:].astype(BF16)
        k_out[...] = keys
        v_out[...] = values
        for g in range(kv_width // head_size):
            cols = slice(g * head_size, (g + 1) * head_size)
            kf = keys[:, cols].astype(F32)
            weighted = jnp.concatenate(
                [(kf * keep_ref[:, h : h + 1]).astype(BF16) for h in range(g * group, (g + 1) * group)],
                axis=1,
            )
            wide = slice(g * group * head_size, (g + 1) * group * head_size)
            s_out[:, wide] = dot_dims(values[:, cols], weighted, 0, 0).astype(BF16)

    outs = [
        shape((rows, kv_width), BF16),
        shape((rows, kv_width), BF16),
        shape((head_size, heads * head_size), BF16),
    ]
    return call(kernel, [x, wkv, total_kv, keep], outs, 0)


def attend(me, place, x, wq, wl, total_q, total_l, k, v, dcol, drow, spans, states, head_size, level_count):
    rows, width = total_q.shape
    bits = len(spans)
    heads = width // head_size
    group = heads // (k.shape[1] // head_size)
    own_levels = level_count - bits

    def kernel(me_ref, x_ref, *refs):
        wq_ref, wl_ref, tq_ref, tl_ref, k_ref, v_ref, dcol_ref, drow_ref = refs[:8]
        span_refs, state_refs = refs[8 : 8 + bits], refs[8 + bits : 7 + 2 * bits]
        o_ref, s_ref, q_ref, l_ref = refs[-4:]
        raw = tl_ref[...] + add_levels(me_ref, place, x_ref, wl_ref)
        l_ref[...] = jnp.maximum(raw, 0.0) + jnp.log1p(jnp.exp(-jnp.abs(raw)))
        q_ref[...] = (tq_ref[...] + dot(x_ref[...], wq_ref[place - 2])).astype(BF16)
        row_id = lax.broadcasted_iota(jnp.int32, (BLOCK, BLOCK), 0)
        col_id = lax.broadcasted_iota(jnp.int32, (BLOCK, BLOCK), 1)
        causal = row_id >= col_id
        for h in range(heads):
            g = h // group
            cols = slice(h * head_size, (h + 1) * head_size)
            kv = slice(g * head_size, (g + 1) * head_size)
            for i in range(rows // BLOCK):
                here = slice(i * BLOCK, (i + 1) * BLOCK)
                span = (i + 1) * BLOCK
                query = q_ref[here, cols]
                scores = dot_dims(query, k_ref[:span, kv], 1, 1)
                d_here = jnp.broadcast_to(dcol_ref[here, h : h + 1], (BLOCK, BLOCK))

                def weight(level):
                    column = h * level_count + level
                    return jnp.broadcast_to(l_ref[here, column : column + 1], (BLOCK, BLOCK))

                weights = {}
                mixed = []
                for j in range(i + 1):
                    level = (i ^ j).bit_length()
                    if level not in weights:
                        weights[level] = weight(level)
                    there = slice(j * BLOCK, (j + 1) * BLOCK)
                    gap = d_here - drow_ref[h : h + 1, there]
                    if i == j:
                        gap = jnp.where(causal, gap, -jnp.inf)
                    mixed.append((weights[level] * jnp.exp(gap) * scores[:, there]).astype(BF16))
                mixing = mixed[0] if i == 0 else jnp.concatenate(mixed, axis=1)
                total = dot(mixing, v_ref[:span, kv])
                wide = query.astype(F32)
                for b in range(bits):
                    factor = weight(own_levels + b) * jnp.exp(d_here + span_refs[b][0:1, cols])
                    scaled = (wide * factor).astype(BF16)
                    if b == bits - 1:
                        s_ref[here, cols] = scaled
                    else:
                        total = total + dot_dims(scaled, state_refs[b][:, cols], 1, 1)
                o_ref[here, cols] = total

    ins = [me, x, wq, wl, total_q, total_l, k, v, dcol, drow, *spans, *states]
    wide = shape((rows, width), BF16)
    outs = [shape((rows, width), F32), wide, wide, shape(total_l.shape, F32)]
    flops = 2 * rows * x.shape[1] * width + 4 * rows * rows * width
    return call(kernel, ins, outs, flops, smem=1)[:2]


def finish(local, scaled, state, rows, head_size, after=()):
    width = local.shape[1]

    def kernel(o_ref, q_ref, s_ref, n_ref):
        for c in range(0, width, head_size):
            cols = slice(c, c + head_size)
            total = o_ref[rows, cols] + dot_dims(q_ref[rows, cols], s_ref[:, cols], 1, 1)
            mean = jnp.mean(total * total, axis=-1, keepdims=True)
            n_ref[:, cols] = (total * lax.rsqrt(mean + 1e-05)).astype(BF16)

    outs = [shape((rows.stop - rows.start, width), BF16)]
    return call(kernel, [local, scaled, state], outs, 0, after)[0]


def out_block(n0s, n1s, cuts, w0, w1, dtype, after=()):
    columns = w1.shape[1]
    count = len(n0s)
    rows = sum(cut.stop - cut.start for cut in cuts)
    tile = min(columns, 512)

    def kernel(*refs):
        w0_ref, w1_ref, o_ref = refs[2 * count :]
        start = 0
        for a_ref, b_ref, cut in zip(refs[:count], refs[count : 2 * count], cuts):
            here = slice(start, start + cut.stop - cut.start)
            start = here.stop
            for c in range(0, columns, tile):
                cols = slice(c, c + tile)
                o_ref[here, cols] = (
                    dot(a_ref[cut, :], w0_ref[:, cols]) + dot(b_ref[cut, :], w1_ref[:, cols])
                ).astype(dtype)

    return call(kernel, [*n0s, *n1s, w0, w1], [shape((rows, columns), dtype)], 0, after)[0]


def add_rows(here, arrived, out, start):
    rows, columns = arrived.shape
    block = start // rows

    def kernel(h_ref, a_ref, *refs):
        refs[-1][...] = (h_ref[start : start + rows, :] + a_ref[...].astype(F32)).astype(BF16)

    ins, specs, aliases = [here, arrived], [VMEM] * 2, {}
    if out is not None:
        ins, specs, aliases = ins + [out], specs + [ANY], {2: 0}
    return pl.pallas_call(
        kernel,
        grid=(1,),
        in_specs=specs,
        out_specs=pl.BlockSpec((rows, columns), lambda s: (block, 0)),
        out_shape=shape(here.shape, BF16),
        input_output_aliases=aliases,
        compiler_params=pltpu.CompilerParams(vmem_limit_bytes=8 * 1024 * 1024),
        cost_estimate=pl.CostEstimate(flops=0, bytes_accessed=rows * columns * 8, transcendentals=0),
    )(*ins)


def body(tokens, log_decay, w_query, w_key, w_value, w_level, w_out):
    rows, shard = tokens.shape
    heads = log_decay.shape[1]
    head_size = w_out.shape[0] // heads
    level_count = w_level.shape[1] // heads
    seq_size = lax.axis_size("seq")
    seq_bits = seq_size.bit_length() - 1
    me = jnp.full((1,), lax.axis_index("tp"), jnp.int32)
    slab = jnp.full((1,), lax.axis_index("seq"), jnp.int32)

    def swap_tp(x, bit):
        return lax.ppermute(x, "tp", [(i, i ^ bit) for i in range(4)])

    def swap_seq(x, bit):
        return lax.ppermute(x, "seq", [(i, i ^ bit) for i in range(seq_size)])

    far = swap_tp(tokens, 2)
    near = swap_tp(tokens, 1)

    weights = (w_query, w_key, w_value, w_level.T)
    totals, ws, (drow, dcol, keep, total, span), blocks = begin(
        me, slab, tokens, near, log_decay.T, weights, w_out, head_size
    )
    w_here_own, w_here_send, w_far_own, w_far_send = blocks
    w_here, w_far = swap_tp(w_here_send, 1), swap_tp(w_far_send, 1)

    here = pair_totals(total, swap_seq(total, 1))
    group_total, before, four_factors, *later_spans = link_four(slab, here, swap_seq(here, 2))
    spans, factors = [span, *later_spans], []
    for b in range(2, seq_bits - 1):
        group_total, before, own, other, span = link(slab, b, group_total, swap_seq(group_total, 1 << b), before)
        spans.append(span)
        factors.append((own, other))

    wq, wkv, wl = ws
    arrived = gate(far, group_total, w_far, w_here)
    arrived_near = swap_tp(arrived, 1)
    total_q, total_kv, total_l = project(me, 2, arrived, ws, totals)
    k, v, state = project_state(arrived_near, wkv, total_kv, keep, head_size)

    beside, across, diagonal = (swap_seq(state, bits) for bits in (1, 2, 3))
    state, other_pair = join_four(state, beside, across, diagonal, four_factors)
    earlier = [beside, other_pair]
    for b in range(2, seq_bits):
        other = swap_seq(state, 1 << b)
        earlier.append(other)
        if b < seq_bits - 1:
            state = combine(state, other, *factors[b - 2])

    local, scaled = attend(
        me, 3, arrived_near, wq, wl, total_q, total_l, k, v, dcol, drow, spans, earlier[:-1], head_size, level_count
    )

    step = rows // 4
    own = finish(local, scaled, earlier[-1], slice(0, step), head_size)
    near_own = swap_tp(own, 1)
    rest = finish(local, scaled, earlier[-1], slice(step, rows), head_size, (near_own,))
    near_rest = swap_tp(rest, 1)
    crossing = [out_block([own], [near_own], [slice(0, step)], w_far_own, w_far, BF16)]
    for r in range(0, rows - step, step):
        crossing.append(out_block([rest], [near_rest], [slice(r, r + step)], w_far_own, w_far, BF16))
    both = [slice(0, step), slice(0, rows - step)]
    own_block = out_block([own, rest], [near_own, near_rest], both, w_here_own, w_here, F32, (crossing[-1],))
    out = None
    for r, x in enumerate(crossing):
        out = add_rows(own_block, swap_tp(x, 2), out, r * step)
    return out


def solution(mesh):
    in_specs = (
        P("seq", "tp"),
        P("seq", "tp"),
        P(None, "tp"),
        P(None, "tp"),
        P(None, "tp"),
        P(None, "tp"),
        P("tp", None),
    )
    out_specs = P("seq", "tp")
    return jax.shard_map(body, mesh=mesh, in_specs=in_specs, out_specs=out_specs, check_vma=False)
```

```python
import functools

import jax
import jax.numpy as jnp
from jax import lax
from jax.experimental import pallas as pl
from jax.experimental.pallas import tpu as pltpu
from jax.sharding import PartitionSpec as P

BLOCK = 128
F32 = jnp.float32
BF16 = jnp.bfloat16
VMEM = pl.BlockSpec(memory_space=pltpu.VMEM)
SMEM = pl.BlockSpec(memory_space=pltpu.SMEM)
ANY = pl.BlockSpec(memory_space=pl.ANY)
HBM = pl.BlockSpec(memory_space=pltpu.HBM)


def dot(a, b):
    return jnp.dot(a, b, preferred_element_type=F32)


def dot_dims(a, b, left, right):
    return lax.dot_general(a, b, (((left,), (right,)), ((), ())), preferred_element_type=F32)


def shape(dims, dtype):
    return jax.ShapeDtypeStruct(dims, dtype)


def call(kernel, ins, outs, flops, after=(), smem=0, hbm=0, aliases=None, scratch=(), megabytes=8):
    count = len(ins)
    ins = list(ins)
    for i in range(smem, smem + hbm):
        ins[i] = pltpu.with_memory_space_constraint(ins[i], pltpu.HBM)

    def run(*refs):
        kernel(*refs[:count], *refs[count + len(after) :])

    nbytes = sum(x.size * x.dtype.itemsize for x in (*ins, *outs)) if flops else 0
    return pl.pallas_call(
        run,
        in_specs=[SMEM] * smem + [HBM] * hbm + [VMEM] * (count - smem - hbm) + [ANY] * len(after),
        out_specs=[VMEM] * len(outs),
        out_shape=list(outs),
        input_output_aliases=aliases or {},
        scratch_shapes=list(scratch),
        compiler_params=pltpu.CompilerParams(vmem_limit_bytes=megabytes * 1024 * 1024),
        cost_estimate=pl.CostEstimate(flops=flops, bytes_accessed=nbytes, transcendentals=0),
    )(*ins, *after)


def gate(x, *after):
    def run(*refs):
        pass

    return pl.pallas_call(
        run,
        in_specs=[ANY] * (1 + len(after)),
        out_specs=ANY,
        out_shape=shape(x.shape, x.dtype),
        input_output_aliases={0: 0},
        compiler_params=pltpu.CompilerParams(vmem_limit_bytes=1024 * 1024),
        cost_estimate=pl.CostEstimate(flops=0, bytes_accessed=0, transcendentals=0),
    )(x, *after)


def copies(pairs, sems):
    started = [pltpu.make_async_copy(src, dst, sems.at[i]) for i, (src, dst) in enumerate(pairs)]
    for copy in started:
        copy.start()
    return started


def upper_half(slab_ref, bit):
    return ((slab_ref[0] >> bit) & 1) == 1


def decays(slab_ref, x_ref, row_ref, col_ref, keep_ref, total_ref, span_ref):
    heads, rows = x_ref.shape
    head_size = total_ref.shape[1] // heads
    x = x_ref[...]
    x = jnp.concatenate([x, jnp.zeros((-heads % 8, rows), F32)], axis=0) if heads % 8 else x
    place = lax.broadcasted_iota(jnp.int32, x.shape, 1)
    shift = 1
    while shift < rows:
        x = x + jnp.where(place >= shift, pltpu.roll(x, shift, 1), 0.0)
        shift *= 2
    total = x[:, rows - 1 : rows]
    row_ref[...] = x[:heads]
    col_ref[...] = jnp.transpose(x)[:, :heads]
    keep_ref[...] = jnp.transpose(jnp.exp(total - x))[:, :heads]
    for h in range(heads):
        total_ref[:, h * head_size : (h + 1) * head_size] = jnp.broadcast_to(
            total[h : h + 1], (8, head_size)
        )
    span_ref[...] = jnp.full(span_ref.shape, jnp.where(upper_half(slab_ref, 0), 0.0, -jnp.inf), F32)


def link(slab, bit, total, other, before):
    def kernel(slab_ref, *refs):
        total_ref, other_ref = refs[:2]
        total_out, before_out, own_out, other_out, span_out = refs[-5:]
        upper = upper_half(slab_ref, bit)
        here, there = total_ref[...], other_ref[...]
        total_out[...] = here + there
        so_far = jnp.where(upper, there, 0.0)
        if before is not None:
            so_far = so_far + refs[2][...]
        before_out[...] = so_far
        own_out[...] = jnp.where(upper, 1.0, jnp.exp(there))
        other_out[...] = jnp.where(upper, jnp.exp(here), 1.0)
        span_out[...] = jnp.where(upper_half(slab_ref, bit + 1), so_far, -jnp.inf)

    ins = [slab, total, other] + ([] if before is None else [before])
    return call(kernel, ins, [shape(total.shape, F32)] * 5, 0, smem=1)


def combine(state, other, own_factor, other_factor, after):
    def kernel(s_ref, o_ref, a_ref, b_ref, out_ref):
        out_ref[...] = (
            a_ref[0:1, :] * s_ref[...].astype(F32) + b_ref[0:1, :] * o_ref[...].astype(F32)
        ).astype(BF16)

    return call(kernel, [state, other, own_factor, other_factor], [shape(state.shape, BF16)], 0, after)[0]


def begin(me, slab, tokens, near, log_decay_rows, ws, w_out, head_size):
    wq, wk, wv, wl = ws
    rows, shard = near.shape
    q_width, kv_width = wq.shape[1], wk.shape[1]
    heads = log_decay_rows.shape[0]
    block = w_out.shape[1] // 4

    def kernel(me_ref, slab_ref, t_ref, wq_ref, wk_ref, wv_ref, wl_ref, wo_ref, near_ref, decay_ref, *refs):
        total_q, total_kv, total_l, far_q, far_kv, send_kv, all_l = refs[:7]
        decay_outs, blocks, (own_x, own_q, own_kv, sems) = refs[7:12], refs[12:16], refs[16:]

        def pairs(i, q_dst, kv_dst):
            here = pl.ds(pl.multiple_of((me_ref[0] ^ i) * shard, 128), shard)
            return [
                (wk_ref.at[here, :], kv_dst.at[:, :kv_width]),
                (wv_ref.at[here, :], kv_dst.at[:, kv_width:]),
                (wq_ref.at[here, :], q_dst),
            ]

        def columns(i):
            return wo_ref.at[:, pl.ds(pl.multiple_of((me_ref[0] ^ i) * block, 128), block)]

        moves = pairs(0, own_q.at[0], own_kv.at[0]) + [(wl_ref, all_l), (t_ref, own_x)]
        moves += pairs(1, own_q.at[1], own_kv.at[1])
        moves += pairs(2, far_q.at[0], far_kv) + pairs(3, far_q.at[1], send_kv)
        moves += [(columns(i), blocks[i]) for i in range(4)]
        started = copies(moves, sems)
        decays(slab_ref, decay_ref, *decay_outs)
        for copy in started[:5]:
            copy.wait()
        lanes = pl.ds(pl.multiple_of(me_ref[0] * shard, 128), shard)
        own = own_x[...]
        total_kv[...] = dot(own, own_kv[0])
        total_q[...] = dot(own, own_q[0])
        total_l[...] = dot_dims(own, all_l[:, lanes], 1, 1)
        for copy in started[5:8]:
            copy.wait()
        lanes = pl.ds(pl.multiple_of((me_ref[0] ^ 1) * shard, 128), shard)
        total_kv[...] += dot(near_ref[...], own_kv[1])
        total_q[...] += dot(near_ref[...], own_q[1])
        total_l[...] += dot_dims(near_ref[...], all_l[:, lanes], 1, 1)
        for copy in started[8:]:
            copy.wait()

    wide = shape((8, heads * head_size), F32)
    outs = [
        shape((rows, q_width), F32),
        shape((rows, 2 * kv_width), F32),
        shape((rows, wl.shape[0]), F32),
        shape((2, shard, q_width), BF16),
        shape((shard, 2 * kv_width), BF16),
        shape((shard, 2 * kv_width), BF16),
        shape(wl.shape, BF16),
        shape((heads, rows), F32),
        shape((rows, heads), F32),
        shape((rows, heads), F32),
        wide,
        wide,
    ] + [shape((w_out.shape[0], block), BF16)] * 4
    scratch = [
        pltpu.VMEM((rows, shard), BF16),
        pltpu.VMEM((2, shard, q_width), BF16),
        pltpu.VMEM((2, shard, 2 * kv_width), BF16),
        pltpu.SemaphoreType.DMA((18,)),
    ]
    ins = [me, slab, tokens, wq, wk, wv, wl, w_out, near, log_decay_rows]
    outs = call(kernel, ins, outs, 0, smem=2, hbm=6, scratch=scratch, megabytes=14)
    return outs[:3], outs[3:7], outs[7:12], outs[12:]


def add_levels(me_ref, place, x, wl_ref):
    shard = wl_ref.shape[1] // 4
    start = pl.multiple_of((me_ref[0] ^ place) * shard, 128)
    return dot_dims(x, wl_ref[:, pl.ds(start, shard)], 1, 1)


def project(me, place, x, wq, wl, total_q, total_l, after):
    def kernel(me_ref, x_ref, wq_ref, wl_ref, q_ref, l_ref, q_out, l_out):
        q_out[...] = q_ref[...] + dot(x_ref[...], wq_ref[place - 2])
        l_out[...] = l_ref[...] + add_levels(me_ref, place, x_ref[...], wl_ref)

    outs = [shape(t.shape, F32) for t in (total_q, total_l)]
    flops = 2 * x.size * (total_q.shape[1] + total_l.shape[1])
    return call(kernel, [me, x, wq, wl, total_q, total_l], outs, flops, after, smem=1, aliases={4: 0, 5: 1})


def split(x, ways, after):
    rows, columns = x.shape
    part = columns // ways

    def kernel(x_ref, *outs):
        for i, o_ref in enumerate(outs):
            o_ref[...] = x_ref[:, i * part : (i + 1) * part]

    return call(kernel, [x], [shape((rows, part), x.dtype)] * ways, 0, after)


def partial(x, w):
    def kernel(x_ref, w_ref, o_ref):
        o_ref[...] = dot(x_ref[...], w_ref[...]).astype(BF16)

    return call(kernel, [x, w], [shape((x.shape[0], w.shape[1]), BF16)], 0)[0]


def project_state(x, wkv, total_kv, from_near, keep, head_size):
    rows = x.shape[0]
    heads = keep.shape[1]
    kv_width = wkv.shape[1] // 2
    group = heads // (kv_width // head_size)

    def kernel(x_ref, w_ref, total_ref, near_ref, keep_ref, k_out, v_out, s_out):
        total = total_ref[...] + near_ref[...].astype(F32) + dot(x_ref[...], w_ref[...])
        keys = total[:, :kv_width].astype(BF16)
        values = total[:, kv_width:].astype(BF16)
        k_out[...] = keys
        v_out[...] = values
        for g in range(kv_width // head_size):
            cols = slice(g * head_size, (g + 1) * head_size)
            kf = keys[:, cols].astype(F32)
            weighted = jnp.concatenate(
                [(kf * keep_ref[:, h : h + 1]).astype(BF16) for h in range(g * group, (g + 1) * group)],
                axis=1,
            )
            wide = slice(g * group * head_size, (g + 1) * group * head_size)
            s_out[:, wide] = dot_dims(values[:, cols], weighted, 0, 0).astype(BF16)

    outs = [
        shape((rows, kv_width), BF16),
        shape((rows, kv_width), BF16),
        shape((head_size, heads * head_size), BF16),
    ]
    return call(kernel, [x, wkv, total_kv, from_near, keep], outs, 0)


def attend(me, place, xs, wq, wl, total_q, total_l, k, v, dcol, drow, spans, states, head_size, level_count):
    rows, width = total_q.shape
    bits = len(spans)
    heads = width // head_size
    group = heads // (k.shape[1] // head_size)
    own_levels = level_count - bits

    def kernel(me_ref, *refs):
        x = jnp.concatenate([x_ref[...] for x_ref in refs[: len(xs)]], axis=1)
        refs = refs[len(xs) :]
        wq_ref, wl_ref, tq_ref, tl_ref, k_ref, v_ref, dcol_ref, drow_ref = refs[:8]
        span_refs, state_refs = refs[8 : 8 + bits], refs[8 + bits : 7 + 2 * bits]
        o_ref, s_ref, q_ref, l_ref = refs[-4:]
        raw = tl_ref[...] + add_levels(me_ref, place, x, wl_ref)
        l_ref[...] = jnp.maximum(raw, 0.0) + jnp.log1p(jnp.exp(-jnp.abs(raw)))
        q_ref[...] = (tq_ref[...] + dot(x, wq_ref[place - 2])).astype(BF16)
        row_id = lax.broadcasted_iota(jnp.int32, (BLOCK, BLOCK), 0)
        col_id = lax.broadcasted_iota(jnp.int32, (BLOCK, BLOCK), 1)
        causal = row_id >= col_id
        for h in range(heads):
            g = h // group
            cols = slice(h * head_size, (h + 1) * head_size)
            kv = slice(g * head_size, (g + 1) * head_size)
            for i in range(rows // BLOCK):
                here = slice(i * BLOCK, (i + 1) * BLOCK)
                span = (i + 1) * BLOCK
                query = q_ref[here, cols]
                scores = dot_dims(query, k_ref[:span, kv], 1, 1)
                d_here = jnp.broadcast_to(dcol_ref[here, h : h + 1], (BLOCK, BLOCK))

                def weight(level):
                    column = h * level_count + level
                    return jnp.broadcast_to(l_ref[here, column : column + 1], (BLOCK, BLOCK))

                weights = {}
                mixed = []
                for j in range(i + 1):
                    level = (i ^ j).bit_length()
                    if level not in weights:
                        weights[level] = weight(level)
                    there = slice(j * BLOCK, (j + 1) * BLOCK)
                    gap = d_here - drow_ref[h : h + 1, there]
                    if i == j:
                        gap = jnp.where(causal, gap, -jnp.inf)
                    mixed.append((weights[level] * jnp.exp(gap) * scores[:, there]).astype(BF16))
                mixing = mixed[0] if i == 0 else jnp.concatenate(mixed, axis=1)
                total = dot(mixing, v_ref[:span, kv])
                wide = query.astype(F32)
                for b in range(bits):
                    factor = weight(own_levels + b) * jnp.exp(d_here + span_refs[b][0:1, cols])
                    scaled = (wide * factor).astype(BF16)
                    if b == bits - 1:
                        s_ref[here, cols] = scaled
                    else:
                        total = total + dot_dims(scaled, state_refs[b][:, cols], 1, 1)
                o_ref[here, cols] = total

    ins = [me, *xs, wq, wl, total_q, total_l, k, v, dcol, drow, *spans, *states]
    wide = shape((rows, width), BF16)
    outs = [shape((rows, width), F32), wide, wide, shape(total_l.shape, F32)]
    flops = 2 * rows * wq.shape[1] * width + 4 * rows * rows * width
    return call(kernel, ins, outs, flops, smem=1)[:2]


def finish(local, scaled, state, rows, head_size, after=()):
    width = local.shape[1]

    def kernel(o_ref, q_ref, s_ref, n_ref):
        for c in range(0, width, head_size):
            cols = slice(c, c + head_size)
            total = o_ref[rows, cols] + dot_dims(q_ref[rows, cols], s_ref[:, cols], 1, 1)
            mean = jnp.mean(total * total, axis=-1, keepdims=True)
            n_ref[:, cols] = (total * lax.rsqrt(mean + 1e-05)).astype(BF16)

    outs = [shape((rows.stop - rows.start, width), BF16)]
    return call(kernel, [local, scaled, state], outs, 0, after)[0]


def out_block(n0s, n1s, cuts, w0, w1, dtype, after=()):
    columns = w1.shape[1]
    count = len(n0s)
    rows = sum(cut.stop - cut.start for cut in cuts)
    tile = min(columns, 512)

    def kernel(*refs):
        w0_ref, w1_ref, o_ref = refs[2 * count :]
        start = 0
        for a_ref, b_ref, cut in zip(refs[:count], refs[count : 2 * count], cuts):
            here = slice(start, start + cut.stop - cut.start)
            start = here.stop
            for c in range(0, columns, tile):
                cols = slice(c, c + tile)
                o_ref[here, cols] = (
                    dot(a_ref[cut, :], w0_ref[:, cols]) + dot(b_ref[cut, :], w1_ref[:, cols])
                ).astype(dtype)

    return call(kernel, [*n0s, *n1s, w0, w1], [shape((rows, columns), dtype)], 0, after)[0]


def add_rows(here, arrived, out, start):
    rows, columns = arrived.shape
    block = start // rows

    def kernel(h_ref, a_ref, *refs):
        refs[-1][...] = (h_ref[start : start + rows, :] + a_ref[...].astype(F32)).astype(BF16)

    ins, specs, aliases = [here, arrived], [VMEM] * 2, {}
    if out is not None:
        ins, specs, aliases = ins + [out], specs + [ANY], {2: 0}
    return pl.pallas_call(
        kernel,
        grid=(1,),
        in_specs=specs,
        out_specs=pl.BlockSpec((rows, columns), lambda s: (block, 0)),
        out_shape=shape(here.shape, BF16),
        input_output_aliases=aliases,
        compiler_params=pltpu.CompilerParams(vmem_limit_bytes=8 * 1024 * 1024),
        cost_estimate=pl.CostEstimate(flops=0, bytes_accessed=rows * columns * 8, transcendentals=0),
    )(*ins)


def body(tokens, log_decay, w_query, w_key, w_value, w_level, w_out):
    rows, shard = tokens.shape
    heads = log_decay.shape[1]
    head_size = w_out.shape[0] // heads
    level_count = w_level.shape[1] // heads
    seq_size = lax.axis_size("seq")
    seq_bits = seq_size.bit_length() - 1
    me = jnp.full((1,), lax.axis_index("tp"), jnp.int32)
    slab = jnp.full((1,), lax.axis_index("seq"), jnp.int32)

    def swap_tp(x, bit):
        return lax.ppermute(x, "tp", [(i, i ^ bit) for i in range(4)])

    def swap_seq(x, bit):
        return lax.ppermute(x, "seq", [(i, i ^ bit) for i in range(seq_size)])

    far = swap_tp(tokens, 2)
    near = swap_tp(tokens, 1)

    weights = (w_query, w_key, w_value, w_level.T)
    totals, ws, (drow, dcol, keep, total, span), blocks = begin(
        me, slab, tokens, near, log_decay.T, weights, w_out, head_size
    )
    w_here_own, w_here_send, w_far_own, w_far_send = blocks
    w_here, w_far = swap_tp(w_here_send, 1), swap_tp(w_far_send, 1)

    spans, factors, before = [span], [], None
    for b in range(seq_bits - 1):
        total, before, own, other, span = link(slab, b, total, swap_seq(total, 1 << b), before)
        spans.append(span)
        factors.append((own, other))

    wq, wkv, wkv_send, wl = ws
    wkv_near = swap_tp(wkv_send, 1)
    arrived = gate(far, total, w_far, w_here)
    from_near = swap_tp(partial(arrived, wkv_near), 1)
    total_q, total_kv, total_l = totals
    k, v, state = project_state(arrived, wkv, total_kv, from_near, keep, head_size)
    total_q, total_l = project(me, 2, arrived, wq, wl, total_q, total_l, (k,))
    arrived_near = [swap_tp(x, 1) for x in split(arrived, 4, (total_l,))]

    earlier = []
    for b in range(seq_bits):
        other = swap_seq(state, 1 << b)
        earlier.append(other)
        if b < seq_bits - 1:
            after = () if b else (total_l,)
            state = combine(state, other, *factors[b], after)

    local, scaled = attend(
        me, 3, arrived_near, wq, wl, total_q, total_l, k, v, dcol, drow, spans, earlier[:-1], head_size, level_count
    )

    step = rows // 4
    own = finish(local, scaled, earlier[-1], slice(0, step), head_size)
    near_own = swap_tp(own, 1)
    crossing = [out_block([own], [near_own], [slice(0, step)], w_far_own, w_far, BF16)]
    rest = finish(local, scaled, earlier[-1], slice(step, rows), head_size, (crossing[0],))
    near_rest = swap_tp(rest, 1)
    for r in range(0, rows - step, step):
        crossing.append(out_block([rest], [near_rest], [slice(r, r + step)], w_far_own, w_far, BF16))
    both = [slice(0, step), slice(0, rows - step)]
    own_block = out_block([own, rest], [near_own, near_rest], both, w_here_own, w_here, F32, (crossing[-1],))
    out = None
    for r, x in enumerate(crossing):
        out = add_rows(own_block, swap_tp(x, 2), out, r * step)
    return out


def solution(mesh):
    in_specs = (
        P("seq", "tp"),
        P("seq", "tp"),
        P(None, "tp"),
        P(None, "tp"),
        P(None, "tp"),
        P(None, "tp"),
        P("tp", None),
    )
    out_specs = P("seq", "tp")
    return jax.shard_map(body, mesh=mesh, in_specs=in_specs, out_specs=out_specs, check_vma=False)
```

```python
import functools

import jax
import jax.numpy as jnp
from jax import lax
from jax.experimental import pallas as pl
from jax.experimental.pallas import tpu as pltpu
from jax.sharding import PartitionSpec as P

BLOCK = 128
F32 = jnp.float32
BF16 = jnp.bfloat16
VMEM = pl.BlockSpec(memory_space=pltpu.VMEM)
SMEM = pl.BlockSpec(memory_space=pltpu.SMEM)
ANY = pl.BlockSpec(memory_space=pl.ANY)
HBM = pl.BlockSpec(memory_space=pltpu.HBM)


def dot(a, b):
    return jnp.dot(a, b, preferred_element_type=F32)


def dot_dims(a, b, left, right):
    return lax.dot_general(a, b, (((left,), (right,)), ((), ())), preferred_element_type=F32)


def shape(dims, dtype):
    return jax.ShapeDtypeStruct(dims, dtype)


def call(kernel, ins, outs, flops, after=(), smem=0, hbm=0, aliases=None, scratch=(), megabytes=8):
    count = len(ins)
    ins = list(ins)
    for i in range(smem, smem + hbm):
        ins[i] = pltpu.with_memory_space_constraint(ins[i], pltpu.HBM)

    def run(*refs):
        kernel(*refs[:count], *refs[count + len(after) :])

    nbytes = sum(x.size * x.dtype.itemsize for x in (*ins, *outs)) if flops else 0
    return pl.pallas_call(
        run,
        in_specs=[SMEM] * smem + [HBM] * hbm + [VMEM] * (count - smem - hbm) + [ANY] * len(after),
        out_specs=[VMEM] * len(outs),
        out_shape=list(outs),
        input_output_aliases=aliases or {},
        scratch_shapes=list(scratch),
        compiler_params=pltpu.CompilerParams(vmem_limit_bytes=megabytes * 1024 * 1024),
        cost_estimate=pl.CostEstimate(flops=flops, bytes_accessed=nbytes, transcendentals=0),
    )(*ins, *after)


def gate(x, *after):
    def run(*refs):
        pass

    return pl.pallas_call(
        run,
        in_specs=[ANY] * (1 + len(after)),
        out_specs=ANY,
        out_shape=shape(x.shape, x.dtype),
        input_output_aliases={0: 0},
        compiler_params=pltpu.CompilerParams(vmem_limit_bytes=1024 * 1024),
        cost_estimate=pl.CostEstimate(flops=0, bytes_accessed=0, transcendentals=0),
    )(x, *after)


def copies(pairs, sems):
    started = [pltpu.make_async_copy(src, dst, sems.at[i]) for i, (src, dst) in enumerate(pairs)]
    for copy in started:
        copy.start()
    return started


def upper_half(slab_ref, bit):
    return ((slab_ref[0] >> bit) & 1) == 1


def decays(slab_ref, x_ref, row_ref, col_ref, keep_ref, total_ref, span_ref):
    heads, rows = x_ref.shape
    head_size = total_ref.shape[1] // heads
    x = x_ref[...]
    x = jnp.concatenate([x, jnp.zeros((-heads % 8, rows), F32)], axis=0) if heads % 8 else x
    place = lax.broadcasted_iota(jnp.int32, x.shape, 1)
    shift = 1
    while shift < rows:
        x = x + jnp.where(place >= shift, pltpu.roll(x, shift, 1), 0.0)
        shift *= 2
    total = x[:, rows - 1 : rows]
    row_ref[...] = x[:heads]
    col_ref[...] = jnp.transpose(x)[:, :heads]
    keep_ref[...] = jnp.transpose(jnp.exp(total - x))[:, :heads]
    for h in range(heads):
        total_ref[:, h * head_size : (h + 1) * head_size] = jnp.broadcast_to(
            total[h : h + 1], (8, head_size)
        )
    span_ref[...] = jnp.full(span_ref.shape, jnp.where(upper_half(slab_ref, 0), 0.0, -jnp.inf), F32)


def link(slab, bit, total, other, before):
    def kernel(slab_ref, *refs):
        total_ref, other_ref = refs[:2]
        total_out, before_out, own_out, other_out, span_out = refs[-5:]
        upper = upper_half(slab_ref, bit)
        here, there = total_ref[...], other_ref[...]
        total_out[...] = here + there
        so_far = jnp.where(upper, there, 0.0)
        if before is not None:
            so_far = so_far + refs[2][...]
        before_out[...] = so_far
        own_out[...] = jnp.where(upper, 1.0, jnp.exp(there))
        other_out[...] = jnp.where(upper, jnp.exp(here), 1.0)
        span_out[...] = jnp.where(upper_half(slab_ref, bit + 1), so_far, -jnp.inf)

    ins = [slab, total, other] + ([] if before is None else [before])
    return call(kernel, ins, [shape(total.shape, F32)] * 5, 0, smem=1)


def combine(state, other, own_factor, other_factor, after):
    def kernel(s_ref, o_ref, a_ref, b_ref, out_ref):
        out_ref[...] = (
            a_ref[0:1, :] * s_ref[...].astype(F32) + b_ref[0:1, :] * o_ref[...].astype(F32)
        ).astype(BF16)

    return call(kernel, [state, other, own_factor, other_factor], [shape(state.shape, BF16)], 0, after)[0]


def begin(me, slab, tokens, near, log_decay_rows, ws, w_out, head_size):
    wq, wk, wv, wl = ws
    rows, shard = near.shape
    q_width, kv_width = wq.shape[1], wk.shape[1]
    heads = log_decay_rows.shape[0]
    block = w_out.shape[1] // 4

    def kernel(me_ref, slab_ref, t_ref, wq_ref, wk_ref, wv_ref, wl_ref, wo_ref, near_ref, decay_ref, *refs):
        total_q, total_kv, total_l, far_q, far_kv, send_kv, all_l = refs[:7]
        decay_outs, blocks, (own_x, own_q, own_kv, sems) = refs[7:12], refs[12:16], refs[16:]

        def pairs(i, q_dst, kv_dst):
            here = pl.ds(pl.multiple_of((me_ref[0] ^ i) * shard, 128), shard)
            return [
                (wk_ref.at[here, :], kv_dst.at[:, :kv_width]),
                (wv_ref.at[here, :], kv_dst.at[:, kv_width:]),
                (wq_ref.at[here, :], q_dst),
            ]

        def columns(i):
            return wo_ref.at[:, pl.ds(pl.multiple_of((me_ref[0] ^ i) * block, 128), block)]

        moves = pairs(0, own_q.at[0], own_kv.at[0]) + [(wl_ref, all_l), (t_ref, own_x)]
        moves += pairs(1, own_q.at[1], own_kv.at[1])
        moves += pairs(2, far_q.at[0], far_kv) + pairs(3, far_q.at[1], send_kv)
        moves += [(columns(i), blocks[i]) for i in range(4)]
        started = copies(moves, sems)
        decays(slab_ref, decay_ref, *decay_outs)
        for copy in started[:5]:
            copy.wait()
        lanes = pl.ds(pl.multiple_of(me_ref[0] * shard, 128), shard)
        own = own_x[...]
        total_kv[...] = dot(own, own_kv[0])
        total_q[...] = dot(own, own_q[0])
        total_l[...] = dot_dims(own, all_l[:, lanes], 1, 1)
        for copy in started[5:8]:
            copy.wait()
        lanes = pl.ds(pl.multiple_of((me_ref[0] ^ 1) * shard, 128), shard)
        total_kv[...] += dot(near_ref[...], own_kv[1])
        total_q[...] += dot(near_ref[...], own_q[1])
        total_l[...] += dot_dims(near_ref[...], all_l[:, lanes], 1, 1)
        for copy in started[8:]:
            copy.wait()

    wide = shape((8, heads * head_size), F32)
    outs = [
        shape((rows, q_width), F32),
        shape((rows, 2 * kv_width), F32),
        shape((rows, wl.shape[0]), F32),
        shape((2, shard, q_width), BF16),
        shape((shard, 2 * kv_width), BF16),
        shape((shard, 2 * kv_width), BF16),
        shape(wl.shape, BF16),
        shape((heads, rows), F32),
        shape((rows, heads), F32),
        shape((rows, heads), F32),
        wide,
        wide,
    ] + [shape((w_out.shape[0], block), BF16)] * 4
    scratch = [
        pltpu.VMEM((rows, shard), BF16),
        pltpu.VMEM((2, shard, q_width), BF16),
        pltpu.VMEM((2, shard, 2 * kv_width), BF16),
        pltpu.SemaphoreType.DMA((18,)),
    ]
    ins = [me, slab, tokens, wq, wk, wv, wl, w_out, near, log_decay_rows]
    outs = call(kernel, ins, outs, 0, smem=2, hbm=6, scratch=scratch, megabytes=14)
    return outs[:3], outs[3:7], outs[7:12], outs[12:]


def add_levels(me_ref, place, x, wl_ref):
    shard = wl_ref.shape[1] // 4
    start = pl.multiple_of((me_ref[0] ^ place) * shard, 128)
    return dot_dims(x, wl_ref[:, pl.ds(start, shard)], 1, 1)


def project(me, place, x, wq, wl, total_q, total_l, after):
    def kernel(me_ref, x_ref, wq_ref, wl_ref, q_ref, l_ref, q_out, l_out):
        q_out[...] = q_ref[...] + dot(x_ref[...], wq_ref[place - 2])
        l_out[...] = l_ref[...] + add_levels(me_ref, place, x_ref[...], wl_ref)

    outs = [shape(t.shape, F32) for t in (total_q, total_l)]
    flops = 2 * x.size * (total_q.shape[1] + total_l.shape[1])
    return call(kernel, [me, x, wq, wl, total_q, total_l], outs, flops, after, smem=1, aliases={4: 0, 5: 1})


def split(x, ways, after):
    rows, columns = x.shape
    part = columns // ways

    def kernel(x_ref, *outs):
        for i, o_ref in enumerate(outs):
            o_ref[...] = x_ref[:, i * part : (i + 1) * part]

    return call(kernel, [x], [shape((rows, part), x.dtype)] * ways, 0, after)


def partial(x, w):
    def kernel(x_ref, w_ref, o_ref):
        o_ref[...] = dot(x_ref[...], w_ref[...]).astype(BF16)

    return call(kernel, [x, w], [shape((x.shape[0], w.shape[1]), BF16)], 0)[0]


def project_state(x, wkv, total_kv, from_near, keep, head_size):
    rows = x.shape[0]
    heads = keep.shape[1]
    kv_width = wkv.shape[1] // 2
    group = heads // (kv_width // head_size)

    def kernel(x_ref, w_ref, total_ref, near_ref, keep_ref, k_out, v_out, s_out):
        total = total_ref[...] + near_ref[...].astype(F32) + dot(x_ref[...], w_ref[...])
        keys = total[:, :kv_width].astype(BF16)
        values = total[:, kv_width:].astype(BF16)
        k_out[...] = keys
        v_out[...] = values
        for g in range(kv_width // head_size):
            cols = slice(g * head_size, (g + 1) * head_size)
            kf = keys[:, cols].astype(F32)
            weighted = jnp.concatenate(
                [(kf * keep_ref[:, h : h + 1]).astype(BF16) for h in range(g * group, (g + 1) * group)],
                axis=1,
            )
            wide = slice(g * group * head_size, (g + 1) * group * head_size)
            s_out[:, wide] = dot_dims(values[:, cols], weighted, 0, 0).astype(BF16)

    outs = [
        shape((rows, kv_width), BF16),
        shape((rows, kv_width), BF16),
        shape((head_size, heads * head_size), BF16),
    ]
    return call(kernel, [x, wkv, total_kv, from_near, keep], outs, 0)


def attend(me, place, xs, wq, wl, total_q, total_l, k, v, dcol, drow, spans, states, head_size, level_count):
    rows, width = total_q.shape
    bits = len(spans)
    heads = width // head_size
    group = heads // (k.shape[1] // head_size)
    own_levels = level_count - bits

    def kernel(me_ref, *refs):
        x = jnp.concatenate([x_ref[...] for x_ref in refs[: len(xs)]], axis=1)
        refs = refs[len(xs) :]
        wq_ref, wl_ref, tq_ref, tl_ref, k_ref, v_ref, dcol_ref, drow_ref = refs[:8]
        span_refs, state_refs = refs[8 : 8 + bits], refs[8 + bits : 7 + 2 * bits]
        o_ref, s_ref, q_ref, l_ref = refs[-4:]
        raw = tl_ref[...] + add_levels(me_ref, place, x, wl_ref)
        l_ref[...] = jnp.maximum(raw, 0.0) + jnp.log1p(jnp.exp(-jnp.abs(raw)))
        q_ref[...] = (tq_ref[...] + dot(x, wq_ref[place - 2])).astype(BF16)
        row_id = lax.broadcasted_iota(jnp.int32, (BLOCK, BLOCK), 0)
        col_id = lax.broadcasted_iota(jnp.int32, (BLOCK, BLOCK), 1)
        causal = row_id >= col_id
        for h in range(heads):
            g = h // group
            cols = slice(h * head_size, (h + 1) * head_size)
            kv = slice(g * head_size, (g + 1) * head_size)
            for i in range(rows // BLOCK):
                here = slice(i * BLOCK, (i + 1) * BLOCK)
                span = (i + 1) * BLOCK
                query = q_ref[here, cols]
                scores = dot_dims(query, k_ref[:span, kv], 1, 1)
                d_here = jnp.broadcast_to(dcol_ref[here, h : h + 1], (BLOCK, BLOCK))

                def weight(level):
                    column = h * level_count + level
                    return jnp.broadcast_to(l_ref[here, column : column + 1], (BLOCK, BLOCK))

                weights = {}
                mixed = []
                for j in range(i + 1):
                    level = (i ^ j).bit_length()
                    if level not in weights:
                        weights[level] = weight(level)
                    there = slice(j * BLOCK, (j + 1) * BLOCK)
                    gap = d_here - drow_ref[h : h + 1, there]
                    if i == j:
                        gap = jnp.where(causal, gap, -jnp.inf)
                    mixed.append((weights[level] * jnp.exp(gap) * scores[:, there]).astype(BF16))
                mixing = mixed[0] if i == 0 else jnp.concatenate(mixed, axis=1)
                total = dot(mixing, v_ref[:span, kv])
                wide = query.astype(F32)
                for b in range(bits):
                    factor = weight(own_levels + b) * jnp.exp(d_here + span_refs[b][0:1, cols])
                    scaled = (wide * factor).astype(BF16)
                    if b == bits - 1:
                        s_ref[here, cols] = scaled
                    else:
                        total = total + dot_dims(scaled, state_refs[b][:, cols], 1, 1)
                o_ref[here, cols] = total

    ins = [me, *xs, wq, wl, total_q, total_l, k, v, dcol, drow, *spans, *states]
    wide = shape((rows, width), BF16)
    outs = [shape((rows, width), F32), wide, wide, shape(total_l.shape, F32)]
    flops = 2 * rows * wq.shape[1] * width + 4 * rows * rows * width
    return call(kernel, ins, outs, flops, smem=1)[:2]


def finish(local, scaled, state, cuts, head_size, after=()):
    width = local.shape[1]

    def kernel(o_ref, q_ref, s_ref, *outs):
        for rows, n_ref in zip(cuts, outs):
            for c in range(0, width, head_size):
                cols = slice(c, c + head_size)
                total = o_ref[rows, cols] + dot_dims(q_ref[rows, cols], s_ref[:, cols], 1, 1)
                mean = jnp.mean(total * total, axis=-1, keepdims=True)
                n_ref[:, cols] = (total * lax.rsqrt(mean + 1e-05)).astype(BF16)

    outs = [shape((cut.stop - cut.start, width), BF16) for cut in cuts]
    return call(kernel, [local, scaled, state], outs, 0, after)


def out_block(pairs, w0, w1, dtype, after=()):
    columns = w1.shape[1]
    count = len(pairs)
    rows = sum(own.shape[0] for own, _ in pairs)
    tile = min(columns, 512)

    def kernel(*refs):
        w0_ref, w1_ref, o_ref = refs[2 * count :]
        start = 0
        for i in range(count):
            a_ref, b_ref = refs[2 * i], refs[2 * i + 1]
            here = slice(start, start + a_ref.shape[0])
            start = here.stop
            for c in range(0, columns, tile):
                cols = slice(c, c + tile)
                o_ref[here, cols] = (
                    dot(a_ref[...], w0_ref[:, cols]) + dot(b_ref[...], w1_ref[:, cols])
                ).astype(dtype)

    ins = [x for pair in pairs for x in pair] + [w0, w1]
    return call(kernel, ins, [shape((rows, columns), dtype)], 0, after)[0]


def add_rows(here, arrived, out, start, unit):
    rows, columns = arrived.shape

    def kernel(h_ref, a_ref, *refs):
        place = pl.ds(pl.multiple_of(start + pl.program_id(0) * unit, unit), unit)
        refs[-1][...] = (h_ref[place, :] + a_ref[...].astype(F32)).astype(BF16)

    block = (unit, columns)
    ins, specs, aliases = [here, arrived], [VMEM, pl.BlockSpec(block, lambda s: (s, 0))], {}
    if out is not None:
        ins, specs, aliases = ins + [out], specs + [ANY], {2: 0}
    return pl.pallas_call(
        kernel,
        grid=(rows // unit,),
        in_specs=specs,
        out_specs=pl.BlockSpec(block, lambda s: (start // unit + s, 0)),
        out_shape=shape(here.shape, BF16),
        input_output_aliases=aliases,
        compiler_params=pltpu.CompilerParams(vmem_limit_bytes=8 * 1024 * 1024),
        cost_estimate=pl.CostEstimate(flops=0, bytes_accessed=rows * columns * 8, transcendentals=0),
    )(*ins)


def body(tokens, log_decay, w_query, w_key, w_value, w_level, w_out):
    rows, shard = tokens.shape
    heads = log_decay.shape[1]
    head_size = w_out.shape[0] // heads
    level_count = w_level.shape[1] // heads
    seq_size = lax.axis_size("seq")
    seq_bits = seq_size.bit_length() - 1
    me = jnp.full((1,), lax.axis_index("tp"), jnp.int32)
    slab = jnp.full((1,), lax.axis_index("seq"), jnp.int32)

    def swap_tp(x, bit):
        return lax.ppermute(x, "tp", [(i, i ^ bit) for i in range(4)])

    def swap_seq(x, bit):
        return lax.ppermute(x, "seq", [(i, i ^ bit) for i in range(seq_size)])

    far = swap_tp(tokens, 2)
    near = swap_tp(tokens, 1)

    weights = (w_query, w_key, w_value, w_level.T)
    totals, ws, (drow, dcol, keep, total, span), blocks = begin(
        me, slab, tokens, near, log_decay.T, weights, w_out, head_size
    )
    w_here_own, w_here_send, w_far_own, w_far_send = blocks
    w_here, w_far = swap_tp(w_here_send, 1), swap_tp(w_far_send, 1)

    spans, factors, before = [span], [], None
    for b in range(seq_bits - 1):
        total, before, own, other, span = link(slab, b, total, swap_seq(total, 1 << b), before)
        spans.append(span)
        factors.append((own, other))

    wq, wkv, wkv_send, wl = ws
    wkv_near = swap_tp(wkv_send, 1)
    arrived = gate(far, total, w_far, w_here)
    from_near = swap_tp(partial(arrived, wkv_near), 1)
    total_q, total_kv, total_l = totals
    k, v, state = project_state(arrived, wkv, total_kv, from_near, keep, head_size)
    total_q, total_l = project(me, 2, arrived, wq, wl, total_q, total_l, (k,))
    arrived_near = [swap_tp(x, 1) for x in split(arrived, 4, (total_l,))]

    earlier = []
    for b in range(seq_bits):
        other = swap_seq(state, 1 << b)
        earlier.append(other)
        if b < seq_bits - 1:
            after = () if b else (total_l,)
            state = combine(state, other, *factors[b], after)

    local, scaled = attend(
        me, 3, arrived_near, wq, wl, total_q, total_l, k, v, dcol, drow, spans, earlier[:-1], head_size, level_count
    )

    unit = rows // 8
    ends = (0, 2, 4, 6, 7, 8)
    cuts = [slice(start * unit, stop * unit) for start, stop in zip(ends, ends[1:])]
    pieces = finish(local, scaled, earlier[-1], cuts[:1], head_size)
    pieces += finish(local, scaled, earlier[-1], cuts[1:], head_size, pieces)
    pairs = [(x, swap_tp(x, 1)) for x in pieces]
    crossing = [out_block([pair], w_far_own, w_far, BF16) for pair in pairs]
    own_block = out_block(pairs, w_here_own, w_here, F32, (crossing[-1],))
    out = None
    for cut, x in zip(cuts, crossing):
        out = add_rows(own_block, swap_tp(x, 2), out, cut.start, unit)
    return out


def solution(mesh):
    in_specs = (
        P("seq", "tp"),
        P("seq", "tp"),
        P(None, "tp"),
        P(None, "tp"),
        P(None, "tp"),
        P(None, "tp"),
        P("tp", None),
    )
    out_specs = P("seq", "tp")
    return jax.shard_map(body, mesh=mesh, in_specs=in_specs, out_specs=out_specs, check_vma=False)
```

```python
import functools

import jax
import jax.numpy as jnp
from jax import lax
from jax.experimental import pallas as pl
from jax.experimental.pallas import tpu as pltpu
from jax.sharding import PartitionSpec as P

BLOCK = 128
F32 = jnp.float32
BF16 = jnp.bfloat16
VMEM = pl.BlockSpec(memory_space=pltpu.VMEM)
SMEM = pl.BlockSpec(memory_space=pltpu.SMEM)
ANY = pl.BlockSpec(memory_space=pl.ANY)
HBM = pl.BlockSpec(memory_space=pltpu.HBM)


def dot(a, b):
    return jnp.dot(a, b, preferred_element_type=F32)


def dot_dims(a, b, left, right):
    return lax.dot_general(a, b, (((left,), (right,)), ((), ())), preferred_element_type=F32)


def shape(dims, dtype):
    return jax.ShapeDtypeStruct(dims, dtype)


def call(kernel, ins, outs, flops, after=(), smem=0, hbm=0, aliases=None, scratch=(), megabytes=8):
    count = len(ins)
    ins = list(ins)
    for i in range(smem, smem + hbm):
        ins[i] = pltpu.with_memory_space_constraint(ins[i], pltpu.HBM)

    def run(*refs):
        kernel(*refs[:count], *refs[count + len(after) :])

    nbytes = sum(x.size * x.dtype.itemsize for x in (*ins, *outs)) if flops else 0
    return pl.pallas_call(
        run,
        in_specs=[SMEM] * smem + [HBM] * hbm + [VMEM] * (count - smem - hbm) + [ANY] * len(after),
        out_specs=[VMEM] * len(outs),
        out_shape=list(outs),
        input_output_aliases=aliases or {},
        scratch_shapes=list(scratch),
        compiler_params=pltpu.CompilerParams(vmem_limit_bytes=megabytes * 1024 * 1024),
        cost_estimate=pl.CostEstimate(flops=flops, bytes_accessed=nbytes, transcendentals=0),
    )(*ins, *after)


def gate(x, *after):
    def run(*refs):
        pass

    return pl.pallas_call(
        run,
        in_specs=[ANY] * (1 + len(after)),
        out_specs=ANY,
        out_shape=shape(x.shape, x.dtype),
        input_output_aliases={0: 0},
        compiler_params=pltpu.CompilerParams(vmem_limit_bytes=1024 * 1024),
        cost_estimate=pl.CostEstimate(flops=0, bytes_accessed=0, transcendentals=0),
    )(x, *after)


def copies(pairs, sems):
    started = [pltpu.make_async_copy(src, dst, sems.at[i]) for i, (src, dst) in enumerate(pairs)]
    for copy in started:
        copy.start()
    return started


def upper_half(slab_ref, bit):
    return ((slab_ref[0] >> bit) & 1) == 1


def decays(slab_ref, x_ref, row_ref, col_ref, keep_ref, total_ref, span_ref):
    heads, rows = x_ref.shape
    head_size = total_ref.shape[1] // heads
    x = x_ref[...]
    x = jnp.concatenate([x, jnp.zeros((-heads % 8, rows), F32)], axis=0) if heads % 8 else x
    place = lax.broadcasted_iota(jnp.int32, x.shape, 1)
    shift = 1
    while shift < rows:
        x = x + jnp.where(place >= shift, pltpu.roll(x, shift, 1), 0.0)
        shift *= 2
    total = x[:, rows - 1 : rows]
    row_ref[...] = x[:heads]
    col_ref[...] = jnp.transpose(x)[:, :heads]
    keep_ref[...] = jnp.transpose(jnp.exp(total - x))[:, :heads]
    for h in range(heads):
        total_ref[:, h * head_size : (h + 1) * head_size] = jnp.broadcast_to(
            total[h : h + 1], (8, head_size)
        )
    span_ref[...] = jnp.full(span_ref.shape, jnp.where(upper_half(slab_ref, 0), 0.0, -jnp.inf), F32)


def link(slab, bit, total, other, before):
    def kernel(slab_ref, *refs):
        total_ref, other_ref = refs[:2]
        total_out, before_out, own_out, other_out, span_out = refs[-5:]
        upper = upper_half(slab_ref, bit)
        here, there = total_ref[...], other_ref[...]
        total_out[...] = here + there
        so_far = jnp.where(upper, there, 0.0)
        if before is not None:
            so_far = so_far + refs[2][...]
        before_out[...] = so_far
        own_out[...] = jnp.where(upper, 1.0, jnp.exp(there))
        other_out[...] = jnp.where(upper, jnp.exp(here), 1.0)
        span_out[...] = jnp.where(upper_half(slab_ref, bit + 1), so_far, -jnp.inf)

    ins = [slab, total, other] + ([] if before is None else [before])
    return call(kernel, ins, [shape(total.shape, F32)] * 5, 0, smem=1)


def pair_totals(total, other):
    def kernel(t_ref, o_ref, out_ref):
        out_ref[0:4, :] = t_ref[0:4, :]
        out_ref[4:8, :] = o_ref[0:4, :]

    return call(kernel, [total, other], [shape(total.shape, F32)], 0)[0]


def link_four(slab, here, there):
    def kernel(slab_ref, h_ref, t_ref, total_out, before_out, factors_out, span1_out, span2_out):
        upper, above = upper_half(slab_ref, 0), upper_half(slab_ref, 1)
        mine, beside = h_ref[0:1, :], h_ref[4:5, :]
        across, diagonal = t_ref[0:1, :], t_ref[4:5, :]
        own_pair, other_pair = mine + beside, across + diagonal
        first = jnp.where(upper, beside, 0.0)
        second = first + jnp.where(above, other_pair, 0.0)
        own_scale = jnp.where(above, 0.0, other_pair)
        other_scale = jnp.where(above, own_pair, 0.0)
        by_mine = jnp.where(upper, 0.0, beside)
        by_beside = jnp.where(upper, mine, 0.0)
        by_across = jnp.where(upper, 0.0, diagonal)
        by_diagonal = jnp.where(upper, across, 0.0)
        factors_out[0:1, :] = jnp.exp(by_mine + own_scale)
        factors_out[1:2, :] = jnp.exp(by_beside + own_scale)
        factors_out[2:3, :] = jnp.exp(by_across + other_scale)
        factors_out[3:4, :] = jnp.exp(by_diagonal + other_scale)
        factors_out[4:5, :] = jnp.exp(by_across)
        factors_out[5:6, :] = jnp.exp(by_diagonal)
        factors_out[6:8, :] = jnp.zeros((2, h_ref.shape[1]), F32)
        wide = h_ref.shape
        total_out[...] = jnp.broadcast_to(own_pair + other_pair, wide)
        before_out[...] = jnp.broadcast_to(second, wide)
        span1_out[...] = jnp.broadcast_to(jnp.where(above, first, -jnp.inf), wide)
        span2_out[...] = jnp.broadcast_to(jnp.where(upper_half(slab_ref, 2), second, -jnp.inf), wide)

    return call(kernel, [slab, here, there], [shape(here.shape, F32)] * 5, 0, smem=1)


def join_four(me, mine, first, second, diagonal, factors, after):
    rows = mine.shape[0]

    def kernel(me_ref, m_ref, x_ref, y_ref, d_ref, f_ref, four_ref, pair_ref, beside_ref):
        even = (me_ref[0] & 1) == 0
        m, d = m_ref[...].astype(F32), d_ref[...].astype(F32)
        x, y = x_ref[...].astype(F32), y_ref[0:rows, :].astype(F32)
        b, a = jnp.where(even, x, y), jnp.where(even, y, x)
        beside_ref[...] = b.astype(BF16)
        f = [f_ref[i : i + 1, :] for i in range(6)]
        four_ref[...] = (f[0] * m + f[1] * b + f[2] * a + f[3] * d).astype(BF16)
        pair_ref[...] = (f[4] * a + f[5] * d).astype(BF16)

    outs = [shape(mine.shape, BF16)] * 3
    return call(kernel, [me, mine, first, second, diagonal, factors], outs, 0, after, smem=1)


def combine(state, other, own_factor, other_factor, after):
    def kernel(s_ref, o_ref, a_ref, b_ref, out_ref):
        out_ref[...] = (
            a_ref[0:1, :] * s_ref[...].astype(F32) + b_ref[0:1, :] * o_ref[...].astype(F32)
        ).astype(BF16)

    return call(kernel, [state, other, own_factor, other_factor], [shape(state.shape, BF16)], 0, after)[0]


def begin(me, slab, tokens, near, log_decay_rows, ws, w_out, head_size):
    wq, wk, wv, wl = ws
    rows, shard = near.shape
    q_width, kv_width = wq.shape[1], wk.shape[1]
    heads = log_decay_rows.shape[0]
    block = w_out.shape[1] // 4

    def kernel(me_ref, slab_ref, t_ref, wq_ref, wk_ref, wv_ref, wl_ref, wo_ref, near_ref, decay_ref, *refs):
        total_q, total_kv, total_l, far_q, far_kv, send_kv, all_l = refs[:7]
        decay_outs, blocks, (own_x, own_q, own_kv, sems) = refs[7:12], refs[12:16], refs[16:]

        def pairs(i, q_dst, kv_dst):
            here = pl.ds(pl.multiple_of((me_ref[0] ^ i) * shard, 128), shard)
            return [
                (wk_ref.at[here, :], kv_dst.at[:, :kv_width]),
                (wv_ref.at[here, :], kv_dst.at[:, kv_width:]),
                (wq_ref.at[here, :], q_dst),
            ]

        def columns(i):
            return wo_ref.at[:, pl.ds(pl.multiple_of((me_ref[0] ^ i) * block, 128), block)]

        moves = pairs(0, own_q.at[0], own_kv.at[0]) + [(wl_ref, all_l), (t_ref, own_x)]
        moves += pairs(1, own_q.at[1], own_kv.at[1])
        moves += pairs(2, far_q.at[0], far_kv) + pairs(3, far_q.at[1], send_kv)
        moves += [(columns(i), blocks[i]) for i in range(4)]
        started = copies(moves, sems)
        decays(slab_ref, decay_ref, *decay_outs)
        for copy in started[:5]:
            copy.wait()
        lanes = pl.ds(pl.multiple_of(me_ref[0] * shard, 128), shard)
        own = own_x[...]
        total_kv[...] = dot(own, own_kv[0])
        total_q[...] = dot(own, own_q[0])
        total_l[...] = dot_dims(own, all_l[:, lanes], 1, 1)
        for copy in started[5:8]:
            copy.wait()
        lanes = pl.ds(pl.multiple_of((me_ref[0] ^ 1) * shard, 128), shard)
        total_kv[...] += dot(near_ref[...], own_kv[1])
        total_q[...] += dot(near_ref[...], own_q[1])
        total_l[...] += dot_dims(near_ref[...], all_l[:, lanes], 1, 1)
        for copy in started[8:]:
            copy.wait()

    wide = shape((8, heads * head_size), F32)
    outs = [
        shape((rows, q_width), F32),
        shape((rows, 2 * kv_width), F32),
        shape((rows, wl.shape[0]), F32),
        shape((2, shard, q_width), BF16),
        shape((shard, 2 * kv_width), BF16),
        shape((shard, 2 * kv_width), BF16),
        shape(wl.shape, BF16),
        shape((heads, rows), F32),
        shape((rows, heads), F32),
        shape((rows, heads), F32),
        wide,
        wide,
    ] + [shape((w_out.shape[0], block), BF16)] * 4
    scratch = [
        pltpu.VMEM((rows, shard), BF16),
        pltpu.VMEM((2, shard, q_width), BF16),
        pltpu.VMEM((2, shard, 2 * kv_width), BF16),
        pltpu.SemaphoreType.DMA((18,)),
    ]
    ins = [me, slab, tokens, wq, wk, wv, wl, w_out, near, log_decay_rows]
    outs = call(kernel, ins, outs, 0, smem=2, hbm=6, scratch=scratch, megabytes=14)
    return outs[:3], outs[3:7], outs[7:12], outs[12:]


def add_levels(me_ref, place, x, wl_ref):
    shard = wl_ref.shape[1] // 4
    start = pl.multiple_of((me_ref[0] ^ place) * shard, 128)
    return dot_dims(x, wl_ref[:, pl.ds(start, shard)], 1, 1)


def project(me, place, x, wq, wl, total_q, total_l, after):
    def kernel(me_ref, x_ref, wq_ref, wl_ref, q_ref, l_ref, q_out, l_out):
        q_out[...] = q_ref[...] + dot(x_ref[...], wq_ref[place - 2])
        l_out[...] = l_ref[...] + add_levels(me_ref, place, x_ref[...], wl_ref)

    outs = [shape(t.shape, F32) for t in (total_q, total_l)]
    flops = 2 * x.size * (total_q.shape[1] + total_l.shape[1])
    return call(kernel, [me, x, wq, wl, total_q, total_l], outs, flops, after, smem=1, aliases={4: 0, 5: 1})


def partial(x, w):
    def kernel(x_ref, w_ref, o_ref):
        o_ref[...] = dot(x_ref[...], w_ref[...]).astype(BF16)

    return call(kernel, [x, w], [shape((x.shape[0], w.shape[1]), BF16)], 0)[0]


def project_state(x, wkv, total_kv, from_near, keep, head_size):
    rows = x.shape[0]
    heads = keep.shape[1]
    kv_width = wkv.shape[1] // 2
    group = heads // (kv_width // head_size)

    def kernel(x_ref, w_ref, total_ref, near_ref, keep_ref, k_out, v_out, s_out, wide_out):
        total = total_ref[...] + near_ref[...].astype(F32) + dot(x_ref[...], w_ref[...])
        keys = total[:, :kv_width].astype(BF16)
        values = total[:, kv_width:].astype(BF16)
        k_out[...] = keys
        v_out[...] = values
        for g in range(kv_width // head_size):
            cols = slice(g * head_size, (g + 1) * head_size)
            kf = keys[:, cols].astype(F32)
            weighted = jnp.concatenate(
                [(kf * keep_ref[:, h : h + 1]).astype(BF16) for h in range(g * group, (g + 1) * group)],
                axis=1,
            )
            wide = slice(g * group * head_size, (g + 1) * group * head_size)
            state = dot_dims(values[:, cols], weighted, 0, 0).astype(BF16)
            s_out[:, wide] = state
            wide_out[0:head_size, wide] = state
        wide_out[head_size:, :] = jnp.zeros((16, wide_out.shape[1]), BF16)

    outs = [
        shape((rows, kv_width), BF16),
        shape((rows, kv_width), BF16),
        shape((head_size, heads * head_size), BF16),
        shape((head_size + 16, heads * head_size), BF16),
    ]
    return call(kernel, [x, wkv, total_kv, from_near, keep], outs, 0)


def attend(me, place, xs, wq, wl, total_q, total_l, k, v, dcol, drow, spans, states, head_size, level_count):
    rows, width = total_q.shape
    bits = len(spans)
    heads = width // head_size
    group = heads // (k.shape[1] // head_size)
    own_levels = level_count - bits

    def kernel(me_ref, *refs):
        x = jnp.concatenate([x_ref[...] for x_ref in refs[: len(xs)]], axis=1)
        refs = refs[len(xs) :]
        wq_ref, wl_ref, tq_ref, tl_ref, k_ref, v_ref, dcol_ref, drow_ref = refs[:8]
        span_refs, state_refs = refs[8 : 8 + bits], refs[8 + bits : 7 + 2 * bits]
        o_ref, s_ref, q_ref, l_ref = refs[-4:]
        raw = tl_ref[...] + add_levels(me_ref, place, x, wl_ref)
        l_ref[...] = jnp.maximum(raw, 0.0) + jnp.log1p(jnp.exp(-jnp.abs(raw)))
        q_ref[...] = (tq_ref[...] + dot(x, wq_ref[place - 2])).astype(BF16)
        row_id = lax.broadcasted_iota(jnp.int32, (BLOCK, BLOCK), 0)
        col_id = lax.broadcasted_iota(jnp.int32, (BLOCK, BLOCK), 1)
        causal = row_id >= col_id
        for h in range(heads):
            g = h // group
            cols = slice(h * head_size, (h + 1) * head_size)
            kv = slice(g * head_size, (g + 1) * head_size)
            for i in range(rows // BLOCK):
                here = slice(i * BLOCK, (i + 1) * BLOCK)
                span = (i + 1) * BLOCK
                query = q_ref[here, cols]
                scores = dot_dims(query, k_ref[:span, kv], 1, 1)
                d_here = jnp.broadcast_to(dcol_ref[here, h : h + 1], (BLOCK, BLOCK))

                def weight(level):
                    column = h * level_count + level
                    return jnp.broadcast_to(l_ref[here, column : column + 1], (BLOCK, BLOCK))

                weights = {}
                mixed = []
                for j in range(i + 1):
                    level = (i ^ j).bit_length()
                    if level not in weights:
                        weights[level] = weight(level)
                    there = slice(j * BLOCK, (j + 1) * BLOCK)
                    gap = d_here - drow_ref[h : h + 1, there]
                    if i == j:
                        gap = jnp.where(causal, gap, -jnp.inf)
                    mixed.append((weights[level] * jnp.exp(gap) * scores[:, there]).astype(BF16))
                mixing = mixed[0] if i == 0 else jnp.concatenate(mixed, axis=1)
                total = dot(mixing, v_ref[:span, kv])
                wide = query.astype(F32)
                for b in range(bits):
                    factor = weight(own_levels + b) * jnp.exp(d_here + span_refs[b][0:1, cols])
                    scaled = (wide * factor).astype(BF16)
                    if b == bits - 1:
                        s_ref[here, cols] = scaled
                    else:
                        total = total + dot_dims(scaled, state_refs[b][:, cols], 1, 1)
                o_ref[here, cols] = total

    ins = [me, *xs, wq, wl, total_q, total_l, k, v, dcol, drow, *spans, *states]
    wide = shape((rows, width), BF16)
    outs = [shape((rows, width), F32), wide, wide, shape(total_l.shape, F32)]
    flops = 2 * rows * wq.shape[1] * width + 4 * rows * rows * width
    return call(kernel, ins, outs, flops, smem=1)[:2]


def finish(local, scaled, state, cuts, head_size, after=()):
    width = local.shape[1]

    def kernel(o_ref, q_ref, s_ref, *outs):
        for rows, n_ref in zip(cuts, outs):
            for c in range(0, width, head_size):
                cols = slice(c, c + head_size)
                total = o_ref[rows, cols] + dot_dims(q_ref[rows, cols], s_ref[:, cols], 1, 1)
                mean = jnp.mean(total * total, axis=-1, keepdims=True)
                n_ref[:, cols] = (total * lax.rsqrt(mean + 1e-05)).astype(BF16)

    outs = [shape((cut.stop - cut.start, width), BF16) for cut in cuts]
    return call(kernel, [local, scaled, state], outs, 0, after)


def out_block(pairs, w0, w1, dtype, after=()):
    columns = w1.shape[1]
    count = len(pairs)
    rows = sum(own.shape[0] for own, _ in pairs)
    tile = min(columns, 512)

    def kernel(*refs):
        w0_ref, w1_ref, o_ref = refs[2 * count :]
        start = 0
        for i in range(count):
            a_ref, b_ref = refs[2 * i], refs[2 * i + 1]
            here = slice(start, start + a_ref.shape[0])
            start = here.stop
            for c in range(0, columns, tile):
                cols = slice(c, c + tile)
                o_ref[here, cols] = (
                    dot(a_ref[...], w0_ref[:, cols]) + dot(b_ref[...], w1_ref[:, cols])
                ).astype(dtype)

    ins = [x for pair in pairs for x in pair] + [w0, w1]
    return call(kernel, ins, [shape((rows, columns), dtype)], 0, after)[0]


def add_rows(here, arrived, out, start, unit):
    rows, columns = arrived.shape

    def kernel(h_ref, a_ref, *refs):
        place = pl.ds(pl.multiple_of(start + pl.program_id(0) * unit, unit), unit)
        refs[-1][...] = (h_ref[place, :] + a_ref[...].astype(F32)).astype(BF16)

    block = (unit, columns)
    ins, specs, aliases = [here, arrived], [VMEM, pl.BlockSpec(block, lambda s: (s, 0))], {}
    if out is not None:
        ins, specs, aliases = ins + [out], specs + [ANY], {2: 0}
    return pl.pallas_call(
        kernel,
        grid=(rows // unit,),
        in_specs=specs,
        out_specs=pl.BlockSpec(block, lambda s: (start // unit + s, 0)),
        out_shape=shape(here.shape, BF16),
        input_output_aliases=aliases,
        compiler_params=pltpu.CompilerParams(vmem_limit_bytes=8 * 1024 * 1024),
        cost_estimate=pl.CostEstimate(flops=0, bytes_accessed=rows * columns * 8, transcendentals=0),
    )(*ins)


def body(tokens, log_decay, w_query, w_key, w_value, w_level, w_out):
    rows, shard = tokens.shape
    heads = log_decay.shape[1]
    head_size = w_out.shape[0] // heads
    level_count = w_level.shape[1] // heads
    seq_size = lax.axis_size("seq")
    seq_bits = seq_size.bit_length() - 1
    me = jnp.full((1,), lax.axis_index("tp"), jnp.int32)
    slab = jnp.full((1,), lax.axis_index("seq"), jnp.int32)

    def swap_tp(x, bit):
        return lax.ppermute(x, "tp", [(i, i ^ bit) for i in range(4)])

    def swap_seq(x, bit):
        return lax.ppermute(x, "seq", [(i, i ^ bit) for i in range(seq_size)])

    far = swap_tp(tokens, 2)
    near = swap_tp(tokens, 1)

    weights = (w_query, w_key, w_value, w_level.T)
    totals, ws, (drow, dcol, keep, total, span), blocks = begin(
        me, slab, tokens, near, log_decay.T, weights, w_out, head_size
    )
    w_here_own, w_here_send, w_far_own, w_far_send = blocks
    w_here, w_far = swap_tp(w_here_send, 1), swap_tp(w_far_send, 1)

    here = pair_totals(total, swap_seq(total, 1))
    total, before, four_factors, *later_spans = link_four(slab, here, swap_seq(here, 2))
    spans, factors = [span, *later_spans], []
    for b in range(2, seq_bits - 1):
        total, before, own, other, span = link(slab, b, total, swap_seq(total, 1 << b), before)
        spans.append(span)
        factors.append((own, other))

    wq, wkv, wkv_send, wl = ws
    wkv_near = swap_tp(wkv_send, 1)
    arrived = gate(far, total, w_far, w_here)
    from_near = swap_tp(partial(arrived, wkv_near), 1)
    arrived = gate(arrived, from_near)
    arrived_near = [swap_tp(arrived, 1)]
    total_q, total_kv, total_l = totals
    k, v, state, state_wide = project_state(arrived, wkv, total_kv, from_near, keep, head_size)

    def swap_group(x, bits):
        tp_size = lax.axis_size("tp")
        pairs = [
            (i * tp_size + j, (i ^ bits[j & 1]) * tp_size + j)
            for i in range(seq_size)
            for j in range(tp_size)
        ]
        return lax.ppermute(x, ("seq", "tp"), pairs)

    first = swap_group(state, (1, 2))
    second = swap_group(state_wide, (2, 1))
    diagonal = swap_group(first, (2, 1))
    total_q, total_l = project(me, 2, arrived, wq, wl, total_q, total_l, (k, first))
    state, other_pair, beside = join_four(me, state, first, second, diagonal, four_factors, (total_l,))
    earlier = [beside, other_pair]
    for b in range(2, seq_bits):
        other = swap_seq(state, 1 << b)
        earlier.append(other)
        if b < seq_bits - 1:
            state = combine(state, other, *factors[b - 2], ())

    local, scaled = attend(
        me, 3, arrived_near, wq, wl, total_q, total_l, k, v, dcol, drow, spans, earlier[:-1], head_size, level_count
    )

    unit = rows // 8
    ends = (0, 2, 4, 6, 7, 8)
    cuts = [slice(start * unit, stop * unit) for start, stop in zip(ends, ends[1:])]
    pieces = finish(local, scaled, earlier[-1], cuts[:1], head_size)
    pieces += finish(local, scaled, earlier[-1], cuts[1:], head_size, pieces)
    pairs = [(x, swap_tp(x, 1)) for x in pieces]
    crossing = [out_block([pair], w_far_own, w_far, BF16) for pair in pairs]
    own_block = out_block(pairs, w_here_own, w_here, F32, (crossing[-1],))
    out = None
    for cut, x in zip(cuts, crossing):
        out = add_rows(own_block, swap_tp(x, 2), out, cut.start, unit)
    return out


def solution(mesh):
    in_specs = (
        P("seq", "tp"),
        P("seq", "tp"),
        P(None, "tp"),
        P(None, "tp"),
        P(None, "tp"),
        P(None, "tp"),
        P("tp", None),
    )
    out_specs = P("seq", "tp")
    return jax.shard_map(body, mesh=mesh, in_specs=in_specs, out_specs=out_specs, check_vma=False)
```

```python
import functools

import jax
import jax.numpy as jnp
from jax import lax
from jax.experimental import pallas as pl
from jax.experimental.pallas import tpu as pltpu
from jax.sharding import PartitionSpec as P

BLOCK = 128
F32 = jnp.float32
BF16 = jnp.bfloat16
VMEM = pl.BlockSpec(memory_space=pltpu.VMEM)
SMEM = pl.BlockSpec(memory_space=pltpu.SMEM)
ANY = pl.BlockSpec(memory_space=pl.ANY)
HBM = pl.BlockSpec(memory_space=pltpu.HBM)


def dot(a, b):
    return jnp.dot(a, b, preferred_element_type=F32)


def dot_dims(a, b, left, right):
    return lax.dot_general(a, b, (((left,), (right,)), ((), ())), preferred_element_type=F32)


def shape(dims, dtype):
    return jax.ShapeDtypeStruct(dims, dtype)


def call(kernel, ins, outs, flops, after=(), smem=0, hbm=0, aliases=None, scratch=(), megabytes=8):
    count = len(ins)
    ins = list(ins)
    for i in range(smem, smem + hbm):
        ins[i] = pltpu.with_memory_space_constraint(ins[i], pltpu.HBM)

    def run(*refs):
        kernel(*refs[:count], *refs[count + len(after) :])

    nbytes = sum(x.size * x.dtype.itemsize for x in (*ins, *outs)) if flops else 0
    return pl.pallas_call(
        run,
        in_specs=[SMEM] * smem + [HBM] * hbm + [VMEM] * (count - smem - hbm) + [ANY] * len(after),
        out_specs=[VMEM] * len(outs),
        out_shape=list(outs),
        input_output_aliases=aliases or {},
        scratch_shapes=list(scratch),
        compiler_params=pltpu.CompilerParams(vmem_limit_bytes=megabytes * 1024 * 1024),
        cost_estimate=pl.CostEstimate(flops=flops, bytes_accessed=nbytes, transcendentals=0),
    )(*ins, *after)


def gate(x, *after):
    def run(*refs):
        pass

    return pl.pallas_call(
        run,
        in_specs=[ANY] * (1 + len(after)),
        out_specs=ANY,
        out_shape=shape(x.shape, x.dtype),
        input_output_aliases={0: 0},
        compiler_params=pltpu.CompilerParams(vmem_limit_bytes=1024 * 1024),
        cost_estimate=pl.CostEstimate(flops=0, bytes_accessed=0, transcendentals=0),
    )(x, *after)


def copies(pairs, sems):
    started = [pltpu.make_async_copy(src, dst, sems.at[i]) for i, (src, dst) in enumerate(pairs)]
    for copy in started:
        copy.start()
    return started


def upper_half(slab_ref, bit):
    return ((slab_ref[0] >> bit) & 1) == 1


def decays(slab_ref, x_ref, row_ref, col_ref, keep_ref, total_ref, span_ref):
    heads, rows = x_ref.shape
    head_size = total_ref.shape[1] // heads
    x = x_ref[...]
    x = jnp.concatenate([x, jnp.zeros((-heads % 8, rows), F32)], axis=0) if heads % 8 else x
    place = lax.broadcasted_iota(jnp.int32, x.shape, 1)
    shift = 1
    while shift < rows:
        x = x + jnp.where(place >= shift, pltpu.roll(x, shift, 1), 0.0)
        shift *= 2
    total = x[:, rows - 1 : rows]
    row_ref[...] = x[:heads]
    col_ref[...] = jnp.transpose(x)[:, :heads]
    keep_ref[...] = jnp.transpose(jnp.exp(total - x))[:, :heads]
    for h in range(heads):
        total_ref[:, h * head_size : (h + 1) * head_size] = jnp.broadcast_to(
            total[h : h + 1], (8, head_size)
        )
    span_ref[...] = jnp.full(span_ref.shape, jnp.where(upper_half(slab_ref, 0), 0.0, -jnp.inf), F32)


def link(slab, bit, total, other, before):
    def kernel(slab_ref, *refs):
        total_ref, other_ref = refs[:2]
        total_out, before_out, own_out, other_out, span_out = refs[-5:]
        upper = upper_half(slab_ref, bit)
        here, there = total_ref[...], other_ref[...]
        total_out[...] = here + there
        so_far = jnp.where(upper, there, 0.0)
        if before is not None:
            so_far = so_far + refs[2][...]
        before_out[...] = so_far
        own_out[...] = jnp.where(upper, 1.0, jnp.exp(there))
        other_out[...] = jnp.where(upper, jnp.exp(here), 1.0)
        span_out[...] = jnp.where(upper_half(slab_ref, bit + 1), so_far, -jnp.inf)

    ins = [slab, total, other] + ([] if before is None else [before])
    return call(kernel, ins, [shape(total.shape, F32)] * 5, 0, smem=1)


def pair_totals(total, other):
    def kernel(t_ref, o_ref, out_ref):
        out_ref[0:4, :] = t_ref[0:4, :]
        out_ref[4:8, :] = o_ref[0:4, :]

    return call(kernel, [total, other], [shape(total.shape, F32)], 0)[0]


def link_four(slab, here, there):
    def kernel(slab_ref, h_ref, t_ref, total_out, before_out, factors_out, span1_out, span2_out):
        upper, above = upper_half(slab_ref, 0), upper_half(slab_ref, 1)
        mine, beside = h_ref[0:1, :], h_ref[4:5, :]
        across, diagonal = t_ref[0:1, :], t_ref[4:5, :]
        own_pair, other_pair = mine + beside, across + diagonal
        first = jnp.where(upper, beside, 0.0)
        second = first + jnp.where(above, other_pair, 0.0)
        own_scale = jnp.where(above, 0.0, other_pair)
        other_scale = jnp.where(above, own_pair, 0.0)
        by_mine = jnp.where(upper, 0.0, beside)
        by_beside = jnp.where(upper, mine, 0.0)
        by_across = jnp.where(upper, 0.0, diagonal)
        by_diagonal = jnp.where(upper, across, 0.0)
        factors_out[0:1, :] = jnp.exp(by_mine + own_scale)
        factors_out[1:2, :] = jnp.exp(by_beside + own_scale)
        factors_out[2:3, :] = jnp.exp(by_across + other_scale)
        factors_out[3:4, :] = jnp.exp(by_diagonal + other_scale)
        factors_out[4:5, :] = jnp.exp(by_across)
        factors_out[5:6, :] = jnp.exp(by_diagonal)
        factors_out[6:8, :] = jnp.zeros((2, h_ref.shape[1]), F32)
        wide = h_ref.shape
        total_out[...] = jnp.broadcast_to(own_pair + other_pair, wide)
        before_out[...] = jnp.broadcast_to(second, wide)
        span1_out[...] = jnp.broadcast_to(jnp.where(above, first, -jnp.inf), wide)
        span2_out[...] = jnp.broadcast_to(jnp.where(upper_half(slab_ref, 2), second, -jnp.inf), wide)

    return call(kernel, [slab, here, there], [shape(here.shape, F32)] * 5, 0, smem=1)


def join_four(me, mine, first, second, diagonal, factors):
    rows = mine.shape[0]

    def kernel(me_ref, m_ref, x_ref, y_ref, d_ref, f_ref, four_ref, pair_ref, beside_ref):
        even = (me_ref[0] & 1) == 0
        m, d = m_ref[...].astype(F32), d_ref[...].astype(F32)
        x, y = x_ref[...].astype(F32), y_ref[0:rows, :].astype(F32)
        b, a = jnp.where(even, x, y), jnp.where(even, y, x)
        beside_ref[...] = b.astype(BF16)
        f = [f_ref[i : i + 1, :] for i in range(6)]
        four_ref[...] = (f[0] * m + f[1] * b + f[2] * a + f[3] * d).astype(BF16)
        pair_ref[...] = (f[4] * a + f[5] * d).astype(BF16)

    outs = [shape(mine.shape, BF16)] * 3
    return call(kernel, [me, mine, first, second, diagonal, factors], outs, 0, smem=1)


def combine(state, other, own_factor, other_factor, after):
    def kernel(s_ref, o_ref, a_ref, b_ref, out_ref):
        out_ref[...] = (
            a_ref[0:1, :] * s_ref[...].astype(F32) + b_ref[0:1, :] * o_ref[...].astype(F32)
        ).astype(BF16)

    return call(kernel, [state, other, own_factor, other_factor], [shape(state.shape, BF16)], 0, after)[0]


def begin(me, slab, tokens, near, log_decay_rows, ws, w_out, head_size):
    wq, wk, wv, wl = ws
    rows, shard = near.shape
    q_width, kv_width = wq.shape[1], wk.shape[1]
    heads = log_decay_rows.shape[0]
    block = w_out.shape[1] // 4

    def kernel(me_ref, slab_ref, t_ref, wq_ref, wk_ref, wv_ref, wl_ref, wo_ref, near_ref, decay_ref, *refs):
        total_q, total_kv, total_l, far_q, far_kv, send_kv, all_l = refs[:7]
        decay_outs, blocks, (own_x, own_q, own_kv, sems) = refs[7:12], refs[12:16], refs[16:]

        def pairs(i, q_dst, kv_dst):
            here = pl.ds(pl.multiple_of((me_ref[0] ^ i) * shard, 128), shard)
            return [
                (wk_ref.at[here, :], kv_dst.at[:, :kv_width]),
                (wv_ref.at[here, :], kv_dst.at[:, kv_width:]),
                (wq_ref.at[here, :], q_dst),
            ]

        def columns(i):
            return wo_ref.at[:, pl.ds(pl.multiple_of((me_ref[0] ^ i) * block, 128), block)]

        moves = pairs(0, own_q.at[0], own_kv.at[0]) + [(wl_ref, all_l), (t_ref, own_x)]
        moves += pairs(1, own_q.at[1], own_kv.at[1])
        moves += pairs(2, far_q.at[0], far_kv) + pairs(3, far_q.at[1], send_kv)
        moves += [(columns(i), blocks[i]) for i in range(4)]
        started = copies(moves, sems)
        decays(slab_ref, decay_ref, *decay_outs)
        for copy in started[:5]:
            copy.wait()
        lanes = pl.ds(pl.multiple_of(me_ref[0] * shard, 128), shard)
        own = own_x[...]
        total_kv[...] = dot(own, own_kv[0])
        total_q[...] = dot(own, own_q[0])
        total_l[...] = dot_dims(own, all_l[:, lanes], 1, 1)
        for copy in started[5:8]:
            copy.wait()
        lanes = pl.ds(pl.multiple_of((me_ref[0] ^ 1) * shard, 128), shard)
        total_kv[...] += dot(near_ref[...], own_kv[1])
        total_q[...] += dot(near_ref[...], own_q[1])
        total_l[...] += dot_dims(near_ref[...], all_l[:, lanes], 1, 1)
        for copy in started[8:]:
            copy.wait()

    wide = shape((8, heads * head_size), F32)
    outs = [
        shape((rows, q_width), F32),
        shape((rows, 2 * kv_width), F32),
        shape((rows, wl.shape[0]), F32),
        shape((2, shard, q_width), BF16),
        shape((shard, 2 * kv_width), BF16),
        shape((shard, 2 * kv_width), BF16),
        shape(wl.shape, BF16),
        shape((heads, rows), F32),
        shape((rows, heads), F32),
        shape((rows, heads), F32),
        wide,
        wide,
    ] + [shape((w_out.shape[0], block), BF16)] * 4
    scratch = [
        pltpu.VMEM((rows, shard), BF16),
        pltpu.VMEM((2, shard, q_width), BF16),
        pltpu.VMEM((2, shard, 2 * kv_width), BF16),
        pltpu.SemaphoreType.DMA((18,)),
    ]
    ins = [me, slab, tokens, wq, wk, wv, wl, w_out, near, log_decay_rows]
    outs = call(kernel, ins, outs, 0, smem=2, hbm=6, scratch=scratch, megabytes=14)
    return outs[:3], outs[3:7], outs[7:12], outs[12:]


def add_levels(me_ref, place, x, wl_ref):
    shard = wl_ref.shape[1] // 4
    start = pl.multiple_of((me_ref[0] ^ place) * shard, 128)
    return dot_dims(x, wl_ref[:, pl.ds(start, shard)], 1, 1)


def project(me, place, x, wq, wkv, wl, totals, after=()):
    def kernel(me_ref, x_ref, q_ref, kv_ref, l_ref, *refs):
        ins, outs = refs[:3], refs[3:]
        outs[1][...] = ins[1][...] + dot(x_ref[...], kv_ref[...])
        outs[0][...] = ins[0][...] + dot(x_ref[...], q_ref[place - 2])
        outs[2][...] = ins[2][...] + add_levels(me_ref, place, x_ref[...], l_ref)

    outs = [shape(t.shape, F32) for t in totals]
    return call(kernel, [me, x, wq, wkv, wl, *totals], outs, 0, after, smem=1, aliases={5: 0, 6: 1, 7: 2})


def project_state(x, wkv, total_kv, keep, head_size):
    rows = x.shape[0]
    heads = keep.shape[1]
    kv_width = wkv.shape[1] // 2
    group = heads // (kv_width // head_size)

    def kernel(x_ref, w_ref, total_ref, keep_ref, k_out, v_out, s_out, wide_out):
        total = total_ref[...] + dot(x_ref[...], w_ref[...])
        keys = total[:, :kv_width].astype(BF16)
        values = total[:, kv_width:].astype(BF16)
        k_out[...] = keys
        v_out[...] = values
        for g in range(kv_width // head_size):
            cols = slice(g * head_size, (g + 1) * head_size)
            kf = keys[:, cols].astype(F32)
            weighted = jnp.concatenate(
                [(kf * keep_ref[:, h : h + 1]).astype(BF16) for h in range(g * group, (g + 1) * group)],
                axis=1,
            )
            wide = slice(g * group * head_size, (g + 1) * group * head_size)
            state = dot_dims(values[:, cols], weighted, 0, 0).astype(BF16)
            s_out[:, wide] = state
            wide_out[0:head_size, wide] = state
        wide_out[head_size:, :] = jnp.zeros((16, wide_out.shape[1]), BF16)

    outs = [
        shape((rows, kv_width), BF16),
        shape((rows, kv_width), BF16),
        shape((head_size, heads * head_size), BF16),
        shape((head_size + 16, heads * head_size), BF16),
    ]
    return call(kernel, [x, wkv, total_kv, keep], outs, 0)


def attend(me, place, x, wq, wl, total_q, total_l, k, v, dcol, drow, spans, states, head_size, level_count):
    rows, width = total_q.shape
    bits = len(spans)
    heads = width // head_size
    group = heads // (k.shape[1] // head_size)
    own_levels = level_count - bits

    def kernel(me_ref, x_ref, wq_ref, wl_ref, *refs):
        x = x_ref[...]
        tq_ref, tl_ref, k_ref, v_ref, dcol_ref, drow_ref = refs[:6]
        span_refs, state_refs = refs[6 : 6 + bits], refs[6 + bits : 5 + 2 * bits]
        o_ref, s_ref, q_ref, l_ref = refs[-4:]
        raw = tl_ref[...] + add_levels(me_ref, place, x, wl_ref)
        l_ref[...] = jnp.maximum(raw, 0.0) + jnp.log1p(jnp.exp(-jnp.abs(raw)))
        q_ref[...] = (tq_ref[...] + dot(x, wq_ref[place - 2])).astype(BF16)
        row_id = lax.broadcasted_iota(jnp.int32, (BLOCK, BLOCK), 0)
        col_id = lax.broadcasted_iota(jnp.int32, (BLOCK, BLOCK), 1)
        causal = row_id >= col_id
        for h in range(heads):
            g = h // group
            cols = slice(h * head_size, (h + 1) * head_size)
            kv = slice(g * head_size, (g + 1) * head_size)
            for i in range(rows // BLOCK):
                here = slice(i * BLOCK, (i + 1) * BLOCK)
                span = (i + 1) * BLOCK
                query = q_ref[here, cols]
                scores = dot_dims(query, k_ref[:span, kv], 1, 1)
                d_here = jnp.broadcast_to(dcol_ref[here, h : h + 1], (BLOCK, BLOCK))

                def weight(level):
                    column = h * level_count + level
                    return jnp.broadcast_to(l_ref[here, column : column + 1], (BLOCK, BLOCK))

                weights = {}
                mixed = []
                for j in range(i + 1):
                    level = (i ^ j).bit_length()
                    if level not in weights:
                        weights[level] = weight(level)
                    there = slice(j * BLOCK, (j + 1) * BLOCK)
                    gap = d_here - drow_ref[h : h + 1, there]
                    if i == j:
                        gap = jnp.where(causal, gap, -jnp.inf)
                    mixed.append((weights[level] * jnp.exp(gap) * scores[:, there]).astype(BF16))
                mixing = mixed[0] if i == 0 else jnp.concatenate(mixed, axis=1)
                total = dot(mixing, v_ref[:span, kv])
                wide = query.astype(F32)
                for b in range(bits):
                    factor = weight(own_levels + b) * jnp.exp(d_here + span_refs[b][0:1, cols])
                    scaled = (wide * factor).astype(BF16)
                    if b == bits - 1:
                        s_ref[here, cols] = scaled
                    else:
                        total = total + dot_dims(scaled, state_refs[b][:, cols], 1, 1)
                o_ref[here, cols] = total

    ins = [me, x, wq, wl, total_q, total_l, k, v, dcol, drow, *spans, *states]
    wide = shape((rows, width), BF16)
    outs = [shape((rows, width), F32), wide, wide, shape(total_l.shape, F32)]
    flops = 2 * rows * wq.shape[1] * width + 4 * rows * rows * width
    return call(kernel, ins, outs, flops, smem=1)[:2]


def finish(local, scaled, state, cuts, head_size, after=()):
    width = local.shape[1]

    def kernel(o_ref, q_ref, s_ref, *outs):
        for rows, n_ref in zip(cuts, outs):
            for c in range(0, width, head_size):
                cols = slice(c, c + head_size)
                total = o_ref[rows, cols] + dot_dims(q_ref[rows, cols], s_ref[:, cols], 1, 1)
                mean = jnp.mean(total * total, axis=-1, keepdims=True)
                n_ref[:, cols] = (total * lax.rsqrt(mean + 1e-05)).astype(BF16)

    outs = [shape((cut.stop - cut.start, width), BF16) for cut in cuts]
    return call(kernel, [local, scaled, state], outs, 0, after)


def out_block(pairs, w0, w1, dtype, after=()):
    columns = w1.shape[1]
    count = len(pairs)
    rows = sum(own.shape[0] for own, _ in pairs)
    tile = min(columns, 512)

    def kernel(*refs):
        w0_ref, w1_ref, o_ref = refs[2 * count :]
        start = 0
        for i in range(count):
            a_ref, b_ref = refs[2 * i], refs[2 * i + 1]
            here = slice(start, start + a_ref.shape[0])
            start = here.stop
            for c in range(0, columns, tile):
                cols = slice(c, c + tile)
                o_ref[here, cols] = (
                    dot(a_ref[...], w0_ref[:, cols]) + dot(b_ref[...], w1_ref[:, cols])
                ).astype(dtype)

    ins = [x for pair in pairs for x in pair] + [w0, w1]
    return call(kernel, ins, [shape((rows, columns), dtype)], 0, after)[0]


def add_rows(here, arrived, out, start, unit):
    rows, columns = arrived.shape

    def kernel(h_ref, a_ref, *refs):
        place = pl.ds(pl.multiple_of(start + pl.program_id(0) * unit, unit), unit)
        refs[-1][...] = (h_ref[place, :] + a_ref[...].astype(F32)).astype(BF16)

    block = (unit, columns)
    ins, specs, aliases = [here, arrived], [VMEM, pl.BlockSpec(block, lambda s: (s, 0))], {}
    if out is not None:
        ins, specs, aliases = ins + [out], specs + [ANY], {2: 0}
    return pl.pallas_call(
        kernel,
        grid=(rows // unit,),
        in_specs=specs,
        out_specs=pl.BlockSpec(block, lambda s: (start // unit + s, 0)),
        out_shape=shape(here.shape, BF16),
        input_output_aliases=aliases,
        compiler_params=pltpu.CompilerParams(vmem_limit_bytes=8 * 1024 * 1024),
        cost_estimate=pl.CostEstimate(flops=0, bytes_accessed=rows * columns * 8, transcendentals=0),
    )(*ins)


def body(tokens, log_decay, w_query, w_key, w_value, w_level, w_out):
    rows, shard = tokens.shape
    heads = log_decay.shape[1]
    head_size = w_out.shape[0] // heads
    level_count = w_level.shape[1] // heads
    seq_size = lax.axis_size("seq")
    seq_bits = seq_size.bit_length() - 1
    me = jnp.full((1,), lax.axis_index("tp"), jnp.int32)
    slab = jnp.full((1,), lax.axis_index("seq"), jnp.int32)

    def swap_tp(x, bit):
        return lax.ppermute(x, "tp", [(i, i ^ bit) for i in range(4)])

    def swap_seq(x, bit):
        return lax.ppermute(x, "seq", [(i, i ^ bit) for i in range(seq_size)])

    far = swap_tp(tokens, 2)
    near = swap_tp(tokens, 1)

    weights = (w_query, w_key, w_value, w_level.T)
    totals, ws, (drow, dcol, keep, total, span), blocks = begin(
        me, slab, tokens, near, log_decay.T, weights, w_out, head_size
    )
    w_here_own, w_here_send, w_far_own, w_far_send = blocks
    w_here, w_far = swap_tp(w_here_send, 1), swap_tp(w_far_send, 1)

    here = pair_totals(total, swap_seq(total, 1))
    total, before, four_factors, *later_spans = link_four(slab, here, swap_seq(here, 2))
    spans, factors = [span, *later_spans], []
    for b in range(2, seq_bits - 1):
        total, before, own, other, span = link(slab, b, total, swap_seq(total, 1 << b), before)
        spans.append(span)
        factors.append((own, other))

    wq, wkv, wkv_near, wl = ws
    arrived = gate(far, total, w_far, w_here)
    arrived_near = swap_tp(arrived, 1)
    total_q, total_kv, total_l = project(me, 2, arrived, wq, wkv, wl, totals)
    k, v, state, state_wide = project_state(arrived_near, wkv_near, total_kv, keep, head_size)

    def swap_group(x, bits):
        tp_size = lax.axis_size("tp")
        pairs = [
            (i * tp_size + j, (i ^ bits[j & 1]) * tp_size + j)
            for i in range(seq_size)
            for j in range(tp_size)
        ]
        return lax.ppermute(x, ("seq", "tp"), pairs)

    first = swap_group(state, (1, 2))
    second = swap_group(state_wide, (2, 1))
    diagonal = swap_group(first, (2, 1))
    state, other_pair, beside = join_four(me, state, first, second, diagonal, four_factors)
    earlier = [beside, other_pair]
    for b in range(2, seq_bits):
        other = swap_seq(state, 1 << b)
        earlier.append(other)
        if b < seq_bits - 1:
            state = combine(state, other, *factors[b - 2], ())

    local, scaled = attend(
        me, 3, arrived_near, wq, wl, total_q, total_l, k, v, dcol, drow, spans, earlier[:-1], head_size, level_count
    )

    unit = rows // 8
    ends = (0, 2, 4, 6, 7, 8)
    cuts = [slice(start * unit, stop * unit) for start, stop in zip(ends, ends[1:])]
    pieces = finish(local, scaled, earlier[-1], cuts[:1], head_size)
    pieces += finish(local, scaled, earlier[-1], cuts[1:], head_size, pieces)
    pairs = [(x, swap_tp(x, 1)) for x in pieces]
    crossing = [out_block([pair], w_far_own, w_far, BF16) for pair in pairs]
    own_block = out_block(pairs, w_here_own, w_here, F32, (crossing[-1],))
    out = None
    for cut, x in zip(cuts, crossing):
        out = add_rows(own_block, swap_tp(x, 2), out, cut.start, unit)
    return out


def solution(mesh):
    in_specs = (
        P("seq", "tp"),
        P("seq", "tp"),
        P(None, "tp"),
        P(None, "tp"),
        P(None, "tp"),
        P(None, "tp"),
        P("tp", None),
    )
    out_specs = P("seq", "tp")
    return jax.shard_map(body, mesh=mesh, in_specs=in_specs, out_specs=out_specs, check_vma=False)
```

```python
import functools

import jax
import jax.numpy as jnp
from jax import lax
from jax.experimental import pallas as pl
from jax.experimental.pallas import tpu as pltpu
from jax.sharding import PartitionSpec as P

BLOCK = 128
F32 = jnp.float32
BF16 = jnp.bfloat16
VMEM = pl.BlockSpec(memory_space=pltpu.VMEM)
SMEM = pl.BlockSpec(memory_space=pltpu.SMEM)
ANY = pl.BlockSpec(memory_space=pl.ANY)
HBM = pl.BlockSpec(memory_space=pltpu.HBM)


def dot(a, b):
    return jnp.dot(a, b, preferred_element_type=F32)


def dot_dims(a, b, left, right):
    return lax.dot_general(a, b, (((left,), (right,)), ((), ())), preferred_element_type=F32)


def shape(dims, dtype):
    return jax.ShapeDtypeStruct(dims, dtype)


def call(kernel, ins, outs, flops, after=(), smem=0, hbm=0, aliases=None, scratch=(), megabytes=8):
    count = len(ins)
    ins = list(ins)
    for i in range(smem, smem + hbm):
        ins[i] = pltpu.with_memory_space_constraint(ins[i], pltpu.HBM)

    def run(*refs):
        kernel(*refs[:count], *refs[count + len(after) :])

    nbytes = sum(x.size * x.dtype.itemsize for x in (*ins, *outs)) if flops else 0
    return pl.pallas_call(
        run,
        in_specs=[SMEM] * smem + [HBM] * hbm + [VMEM] * (count - smem - hbm) + [ANY] * len(after),
        out_specs=[VMEM] * len(outs),
        out_shape=list(outs),
        input_output_aliases=aliases or {},
        scratch_shapes=list(scratch),
        compiler_params=pltpu.CompilerParams(vmem_limit_bytes=megabytes * 1024 * 1024),
        cost_estimate=pl.CostEstimate(flops=flops, bytes_accessed=nbytes, transcendentals=0),
    )(*ins, *after)


def gate(x, *after):
    def run(*refs):
        pass

    return pl.pallas_call(
        run,
        in_specs=[ANY] * (1 + len(after)),
        out_specs=ANY,
        out_shape=shape(x.shape, x.dtype),
        input_output_aliases={0: 0},
        compiler_params=pltpu.CompilerParams(vmem_limit_bytes=1024 * 1024),
        cost_estimate=pl.CostEstimate(flops=0, bytes_accessed=0, transcendentals=0),
    )(x, *after)


def copies(pairs, sems):
    started = [pltpu.make_async_copy(src, dst, sems.at[i]) for i, (src, dst) in enumerate(pairs)]
    for copy in started:
        copy.start()
    return started


def upper_half(slab_ref, bit):
    return ((slab_ref[0] >> bit) & 1) == 1


def decays(slab_ref, x_ref, row_ref, col_ref, keep_ref, total_ref, span_ref):
    heads, rows = x_ref.shape
    head_size = total_ref.shape[1] // heads
    x = x_ref[...]
    x = jnp.concatenate([x, jnp.zeros((-heads % 8, rows), F32)], axis=0) if heads % 8 else x
    place = lax.broadcasted_iota(jnp.int32, x.shape, 1)
    shift = 1
    while shift < rows:
        x = x + jnp.where(place >= shift, pltpu.roll(x, shift, 1), 0.0)
        shift *= 2
    total = x[:, rows - 1 : rows]
    row_ref[...] = x[:heads]
    col_ref[...] = jnp.transpose(x)[:, :heads]
    keep_ref[...] = jnp.transpose(jnp.exp(total - x))[:, :heads]
    for h in range(heads):
        total_ref[:, h * head_size : (h + 1) * head_size] = jnp.broadcast_to(
            total[h : h + 1], (8, head_size)
        )
    span_ref[...] = jnp.full(span_ref.shape, jnp.where(upper_half(slab_ref, 0), 0.0, -jnp.inf), F32)


def link(slab, bit, total, other, before):
    def kernel(slab_ref, *refs):
        total_ref, other_ref = refs[:2]
        total_out, before_out, own_out, other_out, span_out = refs[-5:]
        upper = upper_half(slab_ref, bit)
        here, there = total_ref[...], other_ref[...]
        total_out[...] = here + there
        so_far = jnp.where(upper, there, 0.0)
        if before is not None:
            so_far = so_far + refs[2][...]
        before_out[...] = so_far
        own_out[...] = jnp.where(upper, 1.0, jnp.exp(there))
        other_out[...] = jnp.where(upper, jnp.exp(here), 1.0)
        span_out[...] = jnp.where(upper_half(slab_ref, bit + 1), so_far, -jnp.inf)

    ins = [slab, total, other] + ([] if before is None else [before])
    return call(kernel, ins, [shape(total.shape, F32)] * 5, 0, smem=1)


def combine(state, other, own_factor, other_factor, after):
    def kernel(s_ref, o_ref, a_ref, b_ref, out_ref):
        out_ref[...] = (
            a_ref[0:1, :] * s_ref[...].astype(F32) + b_ref[0:1, :] * o_ref[...].astype(F32)
        ).astype(BF16)

    return call(kernel, [state, other, own_factor, other_factor], [shape(state.shape, BF16)], 0, after)[0]


def begin(me, slab, tokens, near, log_decay_rows, ws, w_out, head_size):
    wq, wk, wv, wl = ws
    rows, shard = near.shape
    q_width, kv_width = wq.shape[1], wk.shape[1]
    heads = log_decay_rows.shape[0]
    block = w_out.shape[1] // 4

    def kernel(me_ref, slab_ref, t_ref, wq_ref, wk_ref, wv_ref, wl_ref, wo_ref, near_ref, decay_ref, *refs):
        total_q, total_kv, total_l, far_q, far_kv, send_kv, all_l = refs[:7]
        decay_outs, blocks, (own_x, own_q, own_kv, sems) = refs[7:12], refs[12:16], refs[16:]

        def pairs(i, q_dst, kv_dst):
            here = pl.ds(pl.multiple_of((me_ref[0] ^ i) * shard, 128), shard)
            return [
                (wk_ref.at[here, :], kv_dst.at[:, :kv_width]),
                (wv_ref.at[here, :], kv_dst.at[:, kv_width:]),
                (wq_ref.at[here, :], q_dst),
            ]

        def columns(i):
            return wo_ref.at[:, pl.ds(pl.multiple_of((me_ref[0] ^ i) * block, 128), block)]

        moves = pairs(0, own_q.at[0], own_kv.at[0]) + [(wl_ref, all_l), (t_ref, own_x)]
        moves += pairs(1, own_q.at[1], own_kv.at[1])
        moves += pairs(2, far_q.at[0], far_kv) + pairs(3, far_q.at[1], send_kv)
        moves += [(columns(i), blocks[i]) for i in range(4)]
        started = copies(moves, sems)
        decays(slab_ref, decay_ref, *decay_outs)
        for copy in started[:5]:
            copy.wait()
        lanes = pl.ds(pl.multiple_of(me_ref[0] * shard, 128), shard)
        own = own_x[...]
        total_kv[...] = dot(own, own_kv[0])
        total_q[...] = dot(own, own_q[0])
        total_l[...] = dot_dims(own, all_l[:, lanes], 1, 1)
        for copy in started[5:8]:
            copy.wait()
        lanes = pl.ds(pl.multiple_of((me_ref[0] ^ 1) * shard, 128), shard)
        total_kv[...] += dot(near_ref[...], own_kv[1])
        total_q[...] += dot(near_ref[...], own_q[1])
        total_l[...] += dot_dims(near_ref[...], all_l[:, lanes], 1, 1)
        for copy in started[8:]:
            copy.wait()

    wide = shape((8, heads * head_size), F32)
    outs = [
        shape((rows, q_width), F32),
        shape((rows, 2 * kv_width), F32),
        shape((rows, wl.shape[0]), F32),
        shape((2, shard, q_width), BF16),
        shape((shard, 2 * kv_width), BF16),
        shape((shard, 2 * kv_width), BF16),
        shape(wl.shape, BF16),
        shape((heads, rows), F32),
        shape((rows, heads), F32),
        shape((rows, heads), F32),
        wide,
        wide,
    ] + [shape((w_out.shape[0], block), BF16)] * 4
    scratch = [
        pltpu.VMEM((rows, shard), BF16),
        pltpu.VMEM((2, shard, q_width), BF16),
        pltpu.VMEM((2, shard, 2 * kv_width), BF16),
        pltpu.SemaphoreType.DMA((18,)),
    ]
    ins = [me, slab, tokens, wq, wk, wv, wl, w_out, near, log_decay_rows]
    outs = call(kernel, ins, outs, 0, smem=2, hbm=6, scratch=scratch, megabytes=14)
    return outs[:3], outs[3:7], outs[7:12], outs[12:]


def add_levels(me_ref, place, x, wl_ref):
    shard = wl_ref.shape[1] // 4
    start = pl.multiple_of((me_ref[0] ^ place) * shard, 128)
    return dot_dims(x, wl_ref[:, pl.ds(start, shard)], 1, 1)


def project(me, place, x, wq, wl, total_q, total_l, after):
    def kernel(me_ref, x_ref, wq_ref, wl_ref, q_ref, l_ref, q_out, l_out):
        q_out[...] = q_ref[...] + dot(x_ref[...], wq_ref[place - 2])
        l_out[...] = l_ref[...] + add_levels(me_ref, place, x_ref[...], wl_ref)

    outs = [shape(t.shape, F32) for t in (total_q, total_l)]
    flops = 2 * x.size * (total_q.shape[1] + total_l.shape[1])
    return call(kernel, [me, x, wq, wl, total_q, total_l], outs, flops, after, smem=1, aliases={4: 0, 5: 1})


def split(x, ways, after):
    rows, columns = x.shape
    part = columns // ways

    def kernel(x_ref, *outs):
        for i, o_ref in enumerate(outs):
            o_ref[...] = x_ref[:, i * part : (i + 1) * part]

    return call(kernel, [x], [shape((rows, part), x.dtype)] * ways, 0, after)


def partial(x, w, after):
    def kernel(x_ref, w_ref, o_ref):
        o_ref[...] = dot(x_ref[...], w_ref[...]).astype(BF16)

    return call(kernel, [x, w], [shape((x.shape[0], w.shape[1]), BF16)], 0, after)[0]


def add_product(x, w, total, after):
    def kernel(x_ref, w_ref, t_ref, o_ref):
        o_ref[...] = t_ref[...] + dot(x_ref[...], w_ref[...])

    return call(kernel, [x, w, total], [shape(total.shape, F32)], 0, after, aliases={2: 0})[0]


def project_state(total_kv, from_near, keep, head_size):
    rows = total_kv.shape[0]
    heads = keep.shape[1]
    kv_width = total_kv.shape[1] // 2
    group = heads // (kv_width // head_size)

    def kernel(total_ref, near_ref, keep_ref, k_out, v_out, s_out):
        total = total_ref[...] + near_ref[...].astype(F32)
        keys = total[:, :kv_width].astype(BF16)
        values = total[:, kv_width:].astype(BF16)
        k_out[...] = keys
        v_out[...] = values
        for g in range(kv_width // head_size):
            cols = slice(g * head_size, (g + 1) * head_size)
            kf = keys[:, cols].astype(F32)
            weighted = jnp.concatenate(
                [(kf * keep_ref[:, h : h + 1]).astype(BF16) for h in range(g * group, (g + 1) * group)],
                axis=1,
            )
            wide = slice(g * group * head_size, (g + 1) * group * head_size)
            s_out[:, wide] = dot_dims(values[:, cols], weighted, 0, 0).astype(BF16)

    outs = [
        shape((rows, kv_width), BF16),
        shape((rows, kv_width), BF16),
        shape((head_size, heads * head_size), BF16),
    ]
    return call(kernel, [total_kv, from_near, keep], outs, 0)


def attend(me, place, xs, wq, wl, total_q, total_l, k, v, dcol, drow, spans, states, head_size, level_count):
    rows, width = total_q.shape
    bits = len(spans)
    heads = width // head_size
    group = heads // (k.shape[1] // head_size)
    own_levels = level_count - bits

    def kernel(me_ref, *refs):
        x = jnp.concatenate([x_ref[...] for x_ref in refs[: len(xs)]], axis=1)
        refs = refs[len(xs) :]
        wq_ref, wl_ref, tq_ref, tl_ref, k_ref, v_ref, dcol_ref, drow_ref = refs[:8]
        span_refs, state_refs = refs[8 : 8 + bits], refs[8 + bits : 7 + 2 * bits]
        o_ref, s_ref, q_ref, l_ref = refs[-4:]
        raw = tl_ref[...] + add_levels(me_ref, place, x, wl_ref)
        l_ref[...] = jnp.maximum(raw, 0.0) + jnp.log1p(jnp.exp(-jnp.abs(raw)))
        q_ref[...] = (tq_ref[...] + dot(x, wq_ref[place - 2])).astype(BF16)
        row_id = lax.broadcasted_iota(jnp.int32, (BLOCK, BLOCK), 0)
        col_id = lax.broadcasted_iota(jnp.int32, (BLOCK, BLOCK), 1)
        causal = row_id >= col_id
        for h in range(heads):
            g = h // group
            cols = slice(h * head_size, (h + 1) * head_size)
            kv = slice(g * head_size, (g + 1) * head_size)
            for i in range(rows // BLOCK):
                here = slice(i * BLOCK, (i + 1) * BLOCK)
                span = (i + 1) * BLOCK
                query = q_ref[here, cols]
                scores = dot_dims(query, k_ref[:span, kv], 1, 1)
                d_here = jnp.broadcast_to(dcol_ref[here, h : h + 1], (BLOCK, BLOCK))

                def weight(level):
                    column = h * level_count + level
                    return jnp.broadcast_to(l_ref[here, column : column + 1], (BLOCK, BLOCK))

                weights = {}
                mixed = []
                for j in range(i + 1):
                    level = (i ^ j).bit_length()
                    if level not in weights:
                        weights[level] = weight(level)
                    there = slice(j * BLOCK, (j + 1) * BLOCK)
                    gap = d_here - drow_ref[h : h + 1, there]
                    if i == j:
                        gap = jnp.where(causal, gap, -jnp.inf)
                    mixed.append((weights[level] * jnp.exp(gap) * scores[:, there]).astype(BF16))
                mixing = mixed[0] if i == 0 else jnp.concatenate(mixed, axis=1)
                total = dot(mixing, v_ref[:span, kv])
                wide = query.astype(F32)
                for b in range(bits):
                    factor = weight(own_levels + b) * jnp.exp(d_here + span_refs[b][0:1, cols])
                    scaled = (wide * factor).astype(BF16)
                    if b == bits - 1:
                        s_ref[here, cols] = scaled
                    else:
                        total = total + dot_dims(scaled, state_refs[b][:, cols], 1, 1)
                o_ref[here, cols] = total

    ins = [me, *xs, wq, wl, total_q, total_l, k, v, dcol, drow, *spans, *states]
    wide = shape((rows, width), BF16)
    outs = [shape((rows, width), F32), wide, wide, shape(total_l.shape, F32)]
    flops = 2 * rows * wq.shape[1] * width + 4 * rows * rows * width
    return call(kernel, ins, outs, flops, smem=1)[:2]


def finish(local, scaled, state, cuts, head_size, after=()):
    width = local.shape[1]

    def kernel(o_ref, q_ref, s_ref, *outs):
        for rows, n_ref in zip(cuts, outs):
            for c in range(0, width, head_size):
                cols = slice(c, c + head_size)
                total = o_ref[rows, cols] + dot_dims(q_ref[rows, cols], s_ref[:, cols], 1, 1)
                mean = jnp.mean(total * total, axis=-1, keepdims=True)
                n_ref[:, cols] = (total * lax.rsqrt(mean + 1e-05)).astype(BF16)

    outs = [shape((cut.stop - cut.start, width), BF16) for cut in cuts]
    return call(kernel, [local, scaled, state], outs, 0, after)


def out_block(pairs, w0, w1, dtype, after=()):
    columns = w1.shape[1]
    count = len(pairs)
    rows = sum(own.shape[0] for own, _ in pairs)
    tile = min(columns, 512)

    def kernel(*refs):
        w0_ref, w1_ref, o_ref = refs[2 * count :]
        start = 0
        for i in range(count):
            a_ref, b_ref = refs[2 * i], refs[2 * i + 1]
            here = slice(start, start + a_ref.shape[0])
            start = here.stop
            for c in range(0, columns, tile):
                cols = slice(c, c + tile)
                o_ref[here, cols] = (
                    dot(a_ref[...], w0_ref[:, cols]) + dot(b_ref[...], w1_ref[:, cols])
                ).astype(dtype)

    ins = [x for pair in pairs for x in pair] + [w0, w1]
    return call(kernel, ins, [shape((rows, columns), dtype)], 0, after)[0]


def add_rows(here, arrived, out, start, unit):
    rows, columns = arrived.shape

    def kernel(h_ref, a_ref, *refs):
        place = pl.ds(pl.multiple_of(start + pl.program_id(0) * unit, unit), unit)
        refs[-1][...] = (h_ref[place, :] + a_ref[...].astype(F32)).astype(BF16)

    block = (unit, columns)
    ins, specs, aliases = [here, arrived], [VMEM, pl.BlockSpec(block, lambda s: (s, 0))], {}
    if out is not None:
        ins, specs, aliases = ins + [out], specs + [ANY], {2: 0}
    return pl.pallas_call(
        kernel,
        grid=(rows // unit,),
        in_specs=specs,
        out_specs=pl.BlockSpec(block, lambda s: (start // unit + s, 0)),
        out_shape=shape(here.shape, BF16),
        input_output_aliases=aliases,
        compiler_params=pltpu.CompilerParams(vmem_limit_bytes=8 * 1024 * 1024),
        cost_estimate=pl.CostEstimate(flops=0, bytes_accessed=rows * columns * 8, transcendentals=0),
    )(*ins)


def body(tokens, log_decay, w_query, w_key, w_value, w_level, w_out):
    rows, shard = tokens.shape
    heads = log_decay.shape[1]
    head_size = w_out.shape[0] // heads
    level_count = w_level.shape[1] // heads
    seq_size = lax.axis_size("seq")
    seq_bits = seq_size.bit_length() - 1
    me = jnp.full((1,), lax.axis_index("tp"), jnp.int32)
    slab = jnp.full((1,), lax.axis_index("seq"), jnp.int32)

    def swap_tp(x, bit):
        return lax.ppermute(x, "tp", [(i, i ^ bit) for i in range(4)])

    def swap_seq(x, bit):
        return lax.ppermute(x, "seq", [(i, i ^ bit) for i in range(seq_size)])

    far = swap_tp(tokens, 2)
    near = swap_tp(tokens, 1)

    weights = (w_query, w_key, w_value, w_level.T)
    totals, ws, (drow, dcol, keep, total, span), blocks = begin(
        me, slab, tokens, near, log_decay.T, weights, w_out, head_size
    )
    w_here_own, w_here_send, w_far_own, w_far_send = blocks
    w_here, w_far = swap_tp(w_here_send, 1), swap_tp(w_far_send, 1)

    spans, factors, before = [span], [], None
    for b in range(seq_bits - 1):
        total, before, own, other, span = link(slab, b, total, swap_seq(total, 1 << b), before)
        spans.append(span)
        factors.append((own, other))

    wq, wkv, wkv_send, wl = ws
    wkv_near = swap_tp(wkv_send, 1)
    arrived = far
    for_near = partial(arrived, wkv_near, (total, w_far, w_here))
    from_near = swap_tp(for_near, 1)
    total_q, total_kv, total_l = totals
    total_kv = add_product(arrived, wkv, total_kv, (for_near,))
    k, v, state = project_state(total_kv, from_near, keep, head_size)
    total_q, total_l = project(me, 2, arrived, wq, wl, total_q, total_l, (k,))
    arrived_near = [swap_tp(x, 1) for x in split(arrived, 4, (total_l,))]

    earlier = []
    for b in range(seq_bits):
        other = swap_seq(state, 1 << b)
        earlier.append(other)
        if b < seq_bits - 1:
            after = () if b else (total_l,)
            state = combine(state, other, *factors[b], after)

    local, scaled = attend(
        me, 3, arrived_near, wq, wl, total_q, total_l, k, v, dcol, drow, spans, earlier[:-1], head_size, level_count
    )

    unit = rows // 8
    ends = (0, 2, 4, 6, 7, 8)
    cuts = [slice(start * unit, stop * unit) for start, stop in zip(ends, ends[1:])]
    pairs = [(x, swap_tp(x, 1)) for x in finish(local, scaled, earlier[-1], cuts, head_size)]
    crossing = [out_block([pair], w_far_own, w_far, BF16) for pair in pairs]
    own_block = out_block(pairs, w_here_own, w_here, F32, (crossing[-1],))
    out = None
    for cut, x in zip(cuts, crossing):
        out = add_rows(own_block, swap_tp(x, 2), out, cut.start, unit)
    return out


def solution(mesh):
    in_specs = (
        P("seq", "tp"),
        P("seq", "tp"),
        P(None, "tp"),
        P(None, "tp"),
        P(None, "tp"),
        P(None, "tp"),
        P("tp", None),
    )
    out_specs = P("seq", "tp")
    return jax.shard_map(body, mesh=mesh, in_specs=in_specs, out_specs=out_specs, check_vma=False)
```

```python
import functools

import jax
import jax.numpy as jnp
from jax import lax
from jax.experimental import pallas as pl
from jax.experimental.pallas import tpu as pltpu
from jax.sharding import PartitionSpec as P

BLOCK = 128
F32 = jnp.float32
BF16 = jnp.bfloat16
VMEM = pl.BlockSpec(memory_space=pltpu.VMEM)
SMEM = pl.BlockSpec(memory_space=pltpu.SMEM)
ANY = pl.BlockSpec(memory_space=pl.ANY)
HBM = pl.BlockSpec(memory_space=pltpu.HBM)


def dot(a, b):
    return jnp.dot(a, b, preferred_element_type=F32)


def dot_dims(a, b, left, right):
    return lax.dot_general(a, b, (((left,), (right,)), ((), ())), preferred_element_type=F32)


def shape(dims, dtype):
    return jax.ShapeDtypeStruct(dims, dtype)


def call(kernel, ins, outs, flops, after=(), smem=0, hbm=0, aliases=None, scratch=(), megabytes=8):
    count = len(ins)
    ins = list(ins)
    for i in range(smem, smem + hbm):
        ins[i] = pltpu.with_memory_space_constraint(ins[i], pltpu.HBM)

    def run(*refs):
        kernel(*refs[:count], *refs[count + len(after) :])

    nbytes = sum(x.size * x.dtype.itemsize for x in (*ins, *outs)) if flops else 0
    return pl.pallas_call(
        run,
        in_specs=[SMEM] * smem + [HBM] * hbm + [VMEM] * (count - smem - hbm) + [ANY] * len(after),
        out_specs=[VMEM] * len(outs),
        out_shape=list(outs),
        input_output_aliases=aliases or {},
        scratch_shapes=list(scratch),
        compiler_params=pltpu.CompilerParams(vmem_limit_bytes=megabytes * 1024 * 1024),
        cost_estimate=pl.CostEstimate(flops=flops, bytes_accessed=nbytes, transcendentals=0),
    )(*ins, *after)


def gate(x, *after):
    def run(*refs):
        pass

    return pl.pallas_call(
        run,
        in_specs=[ANY] * (1 + len(after)),
        out_specs=ANY,
        out_shape=shape(x.shape, x.dtype),
        input_output_aliases={0: 0},
        compiler_params=pltpu.CompilerParams(vmem_limit_bytes=1024 * 1024),
        cost_estimate=pl.CostEstimate(flops=0, bytes_accessed=0, transcendentals=0),
    )(x, *after)


def copies(pairs, sems):
    started = [pltpu.make_async_copy(src, dst, sems.at[i]) for i, (src, dst) in enumerate(pairs)]
    for copy in started:
        copy.start()
    return started


def upper_half(slab_ref, bit):
    return ((slab_ref[0] >> bit) & 1) == 1


def decays(slab_ref, x_ref, row_ref, col_ref, keep_ref, total_ref, span_ref):
    heads, rows = x_ref.shape
    head_size = total_ref.shape[1] // heads
    x = x_ref[...]
    x = jnp.concatenate([x, jnp.zeros((-heads % 8, rows), F32)], axis=0) if heads % 8 else x
    place = lax.broadcasted_iota(jnp.int32, x.shape, 1)
    shift = 1
    while shift < rows:
        x = x + jnp.where(place >= shift, pltpu.roll(x, shift, 1), 0.0)
        shift *= 2
    total = x[:, rows - 1 : rows]
    row_ref[...] = x[:heads]
    col_ref[...] = jnp.transpose(x)[:, :heads]
    keep_ref[...] = jnp.transpose(jnp.exp(total - x))[:, :heads]
    for h in range(heads):
        total_ref[:, h * head_size : (h + 1) * head_size] = jnp.broadcast_to(
            total[h : h + 1], (8, head_size)
        )
    span_ref[...] = jnp.full(span_ref.shape, jnp.where(upper_half(slab_ref, 0), 0.0, -jnp.inf), F32)


def link(slab, bit, total, other, before):
    def kernel(slab_ref, *refs):
        total_ref, other_ref = refs[:2]
        total_out, before_out, own_out, other_out, span_out = refs[-5:]
        upper = upper_half(slab_ref, bit)
        here, there = total_ref[...], other_ref[...]
        total_out[...] = here + there
        so_far = jnp.where(upper, there, 0.0)
        if before is not None:
            so_far = so_far + refs[2][...]
        before_out[...] = so_far
        own_out[...] = jnp.where(upper, 1.0, jnp.exp(there))
        other_out[...] = jnp.where(upper, jnp.exp(here), 1.0)
        span_out[...] = jnp.where(upper_half(slab_ref, bit + 1), so_far, -jnp.inf)

    ins = [slab, total, other] + ([] if before is None else [before])
    return call(kernel, ins, [shape(total.shape, F32)] * 5, 0, smem=1)


def combine(state, other, own_factor, other_factor, which):
    cols = slice(which * state.shape[1], (which + 1) * state.shape[1])

    def kernel(s_ref, o_ref, a_ref, b_ref, out_ref):
        out_ref[...] = (
            a_ref[0:1, cols] * s_ref[...].astype(F32) + b_ref[0:1, cols] * o_ref[...].astype(F32)
        ).astype(BF16)

    return call(kernel, [state, other, own_factor, other_factor], [shape(state.shape, BF16)], 0)[0]


def begin(me, slab, tokens, near, log_decay_rows, ws, w_out, head_size):
    wq, wk, wv, wl = ws
    rows, shard = near.shape
    q_width, kv_width = wq.shape[1], wk.shape[1]
    heads = log_decay_rows.shape[0]
    block = w_out.shape[1] // 4

    def kernel(me_ref, slab_ref, t_ref, wq_ref, wk_ref, wv_ref, wl_ref, wo_ref, near_ref, decay_ref, *refs):
        total_q, total_kv, total_l, far_q, far_kv, send_kv, all_l = refs[:7]
        decay_outs, blocks, (own_x, own_q, own_kv, sems) = refs[7:12], refs[12:16], refs[16:]

        def pairs(i, q_dst, kv_dst):
            here = pl.ds(pl.multiple_of((me_ref[0] ^ i) * shard, 128), shard)
            return [
                (wk_ref.at[here, :], kv_dst.at[:, :kv_width]),
                (wv_ref.at[here, :], kv_dst.at[:, kv_width:]),
                (wq_ref.at[here, :], q_dst),
            ]

        def columns(i):
            return wo_ref.at[:, pl.ds(pl.multiple_of((me_ref[0] ^ i) * block, 128), block)]

        moves = pairs(0, own_q.at[0], own_kv.at[0]) + [(wl_ref, all_l), (t_ref, own_x)]
        moves += pairs(1, own_q.at[1], own_kv.at[1])
        moves += pairs(2, far_q.at[0], far_kv) + pairs(3, far_q.at[1], send_kv)
        moves += [(columns(i), blocks[i]) for i in range(4)]
        started = copies(moves, sems)
        decays(slab_ref, decay_ref, *decay_outs)
        for copy in started[:5]:
            copy.wait()
        lanes = pl.ds(pl.multiple_of(me_ref[0] * shard, 128), shard)
        own = own_x[...]
        total_kv[...] = dot(own, own_kv[0])
        total_q[...] = dot(own, own_q[0])
        total_l[...] = dot_dims(own, all_l[:, lanes], 1, 1)
        for copy in started[5:8]:
            copy.wait()
        lanes = pl.ds(pl.multiple_of((me_ref[0] ^ 1) * shard, 128), shard)
        total_kv[...] += dot(near_ref[...], own_kv[1])
        total_q[...] += dot(near_ref[...], own_q[1])
        total_l[...] += dot_dims(near_ref[...], all_l[:, lanes], 1, 1)
        for copy in started[8:]:
            copy.wait()

    wide = shape((8, heads * head_size), F32)
    outs = [
        shape((rows, q_width), F32),
        shape((rows, 2 * kv_width), F32),
        shape((rows, wl.shape[0]), F32),
        shape((2, shard, q_width), BF16),
        shape((shard, 2 * kv_width), BF16),
        shape((shard, 2 * kv_width), BF16),
        shape(wl.shape, BF16),
        shape((heads, rows), F32),
        shape((rows, heads), F32),
        shape((rows, heads), F32),
        wide,
        wide,
    ] + [shape((w_out.shape[0], block), BF16)] * 4
    scratch = [
        pltpu.VMEM((rows, shard), BF16),
        pltpu.VMEM((2, shard, q_width), BF16),
        pltpu.VMEM((2, shard, 2 * kv_width), BF16),
        pltpu.SemaphoreType.DMA((18,)),
    ]
    ins = [me, slab, tokens, wq, wk, wv, wl, w_out, near, log_decay_rows]
    outs = call(kernel, ins, outs, 0, smem=2, hbm=6, scratch=scratch, megabytes=14)
    return outs[:3], outs[3:7], outs[7:12], outs[12:]


def add_levels(me_ref, place, x, wl_ref):
    shard = wl_ref.shape[1] // 4
    start = pl.multiple_of((me_ref[0] ^ place) * shard, 128)
    return dot_dims(x, wl_ref[:, pl.ds(start, shard)], 1, 1)


def project(me, place, x, wq, wkv, wl, totals, after=()):
    def kernel(me_ref, x_ref, q_ref, kv_ref, l_ref, *refs):
        ins, outs = refs[:3], refs[3:]
        outs[1][...] = ins[1][...] + dot(x_ref[...], kv_ref[...])
        outs[0][...] = ins[0][...] + dot(x_ref[...], q_ref[place - 2])
        outs[2][...] = ins[2][...] + add_levels(me_ref, place, x_ref[...], l_ref)

    outs = [shape(t.shape, F32) for t in totals]
    return call(kernel, [me, x, wq, wkv, wl, *totals], outs, 0, after, smem=1, aliases={5: 0, 6: 1, 7: 2})


def partial(x, w, after):
    def kernel(x_ref, w_ref, o_ref):
        o_ref[...] = dot(x_ref[...], w_ref[...]).astype(BF16)

    return call(kernel, [x, w], [shape((x.shape[0], w.shape[1]), BF16)], 0, after)[0]


def project_state(total_kv, from_near, keep, head_size):
    rows = total_kv.shape[0]
    heads = keep.shape[1]
    kv_width = total_kv.shape[1] // 2
    group = heads // (kv_width // head_size)

    half = heads // 2 * head_size

    def kernel(total_ref, near_ref, keep_ref, k_out, v_out, *s_outs):
        total = total_ref[...] + near_ref[...].astype(F32)
        keys = total[:, :kv_width].astype(BF16)
        values = total[:, kv_width:].astype(BF16)
        k_out[...] = keys
        v_out[...] = values
        for g in range(kv_width // head_size):
            cols = slice(g * head_size, (g + 1) * head_size)
            kf = keys[:, cols].astype(F32)
            weighted = jnp.concatenate(
                [(kf * keep_ref[:, h : h + 1]).astype(BF16) for h in range(g * group, (g + 1) * group)],
                axis=1,
            )
            states = dot_dims(values[:, cols], weighted, 0, 0).astype(BF16)
            for i in range(group):
                start = (g * group + i) * head_size
                s_outs[start // half][:, start % half : start % half + head_size] = states[
                    :, i * head_size : (i + 1) * head_size
                ]

    outs = [
        shape((rows, kv_width), BF16),
        shape((rows, kv_width), BF16),
        shape((head_size, half), BF16),
        shape((head_size, half), BF16),
    ]
    return call(kernel, [total_kv, from_near, keep], outs, 0)


def attend(me, place, x, wq, wl, total_q, total_l, k, v, dcol, drow, spans, states, head_size, level_count):
    rows, width = total_q.shape
    bits = len(spans)
    heads = width // head_size
    group = heads // (k.shape[1] // head_size)
    own_levels = level_count - bits

    half = width // 2

    def kernel(me_ref, x_ref, wq_ref, wl_ref, *refs):
        x = x_ref[...]
        tq_ref, tl_ref, k_ref, v_ref, dcol_ref, drow_ref = refs[:6]
        span_refs, state_refs = refs[6 : 6 + bits], refs[6 + bits : 6 + bits + len(states)]
        o_ref, s_ref, q_ref, l_ref = refs[-4:]
        raw = tl_ref[...] + add_levels(me_ref, place, x, wl_ref)
        l_ref[...] = jnp.maximum(raw, 0.0) + jnp.log1p(jnp.exp(-jnp.abs(raw)))
        q_ref[...] = (tq_ref[...] + dot(x, wq_ref[place - 2])).astype(BF16)
        row_id = lax.broadcasted_iota(jnp.int32, (BLOCK, BLOCK), 0)
        col_id = lax.broadcasted_iota(jnp.int32, (BLOCK, BLOCK), 1)
        causal = row_id >= col_id
        for h in range(heads):
            g = h // group
            cols = slice(h * head_size, (h + 1) * head_size)
            kv = slice(g * head_size, (g + 1) * head_size)
            for i in range(rows // BLOCK):
                here = slice(i * BLOCK, (i + 1) * BLOCK)
                span = (i + 1) * BLOCK
                query = q_ref[here, cols]
                scores = dot_dims(query, k_ref[:span, kv], 1, 1)
                d_here = jnp.broadcast_to(dcol_ref[here, h : h + 1], (BLOCK, BLOCK))

                def weight(level):
                    column = h * level_count + level
                    return jnp.broadcast_to(l_ref[here, column : column + 1], (BLOCK, BLOCK))

                weights = {}
                mixed = []
                for j in range(i + 1):
                    level = (i ^ j).bit_length()
                    if level not in weights:
                        weights[level] = weight(level)
                    there = slice(j * BLOCK, (j + 1) * BLOCK)
                    gap = d_here - drow_ref[h : h + 1, there]
                    if i == j:
                        gap = jnp.where(causal, gap, -jnp.inf)
                    mixed.append((weights[level] * jnp.exp(gap) * scores[:, there]).astype(BF16))
                mixing = mixed[0] if i == 0 else jnp.concatenate(mixed, axis=1)
                total = dot(mixing, v_ref[:span, kv])
                wide = query.astype(F32)
                for b in range(bits):
                    factor = weight(own_levels + b) * jnp.exp(d_here + span_refs[b][0:1, cols])
                    scaled = (wide * factor).astype(BF16)
                    if b == bits - 1:
                        s_ref[here, cols] = scaled
                    else:
                        state_ref = state_refs[2 * b + cols.start // half]
                        at = cols.start % half
                        total = total + dot_dims(scaled, state_ref[:, at : at + head_size], 1, 1)
                o_ref[here, cols] = total

    ins = [me, x, wq, wl, total_q, total_l, k, v, dcol, drow, *spans, *states]
    wide = shape((rows, width), BF16)
    outs = [shape((rows, width), F32), wide, wide, shape(total_l.shape, F32)]
    flops = 2 * rows * wq.shape[1] * width + 4 * rows * rows * width
    return call(kernel, ins, outs, flops, smem=1)[:2]


def finish(local, scaled, state, which, cuts, head_size, flops, after=()):
    width = state.shape[1]
    offset = which * width

    def kernel(o_ref, q_ref, s_ref, *outs):
        for rows, n_ref in zip(cuts, outs):
            for c in range(0, width, head_size):
                cols = slice(offset + c, offset + c + head_size)
                here = slice(c, c + head_size)
                total = o_ref[rows, cols] + dot_dims(q_ref[rows, cols], s_ref[:, here], 1, 1)
                mean = jnp.mean(total * total, axis=-1, keepdims=True)
                n_ref[:, here] = (total * lax.rsqrt(mean + 1e-05)).astype(BF16)

    outs = [shape((cut.stop - cut.start, width), BF16) for cut in cuts]
    return call(kernel, [local, scaled, state], outs, flops, after)


def out_block(first, second, places, w0, w1, dtype, after=()):
    columns = w1.shape[1]
    rows = sum(cut.stop - cut.start for _, cut in places)
    tile = min(columns, 512)

    def kernel(*refs):
        f_refs, s_refs = refs[: 2 * len(first)], refs[2 * len(first) : -3]
        w0_ref, w1_ref, o_ref = refs[-3:]
        start = 0
        for i, (which, cut) in enumerate(places):
            here = slice(start, start + cut.stop - cut.start)
            start = here.stop
            own = jnp.concatenate([f_refs[2 * which][cut, :], s_refs[2 * i][...]], axis=1)
            near = jnp.concatenate([f_refs[2 * which + 1][cut, :], s_refs[2 * i + 1][...]], axis=1)
            for c in range(0, columns, tile):
                cols = slice(c, c + tile)
                o_ref[here, cols] = (dot(own, w0_ref[:, cols]) + dot(near, w1_ref[:, cols])).astype(dtype)

    ins = [x for pair in (*first, *second) for x in pair] + [w0, w1]
    return call(kernel, ins, [shape((rows, columns), dtype)], 0, after)[0]


def add_rows(here, arrived, out, start, unit):
    rows, columns = arrived.shape

    def kernel(h_ref, a_ref, *refs):
        place = pl.ds(pl.multiple_of(start + pl.program_id(0) * unit, unit), unit)
        refs[-1][...] = (h_ref[place, :] + a_ref[...].astype(F32)).astype(BF16)

    block = (unit, columns)
    ins, specs, aliases = [here, arrived], [VMEM, pl.BlockSpec(block, lambda s: (s, 0))], {}
    if out is not None:
        ins, specs, aliases = ins + [out], specs + [ANY], {2: 0}
    return pl.pallas_call(
        kernel,
        grid=(rows // unit,),
        in_specs=specs,
        out_specs=pl.BlockSpec(block, lambda s: (start // unit + s, 0)),
        out_shape=shape(here.shape, BF16),
        input_output_aliases=aliases,
        compiler_params=pltpu.CompilerParams(vmem_limit_bytes=8 * 1024 * 1024),
        cost_estimate=pl.CostEstimate(flops=0, bytes_accessed=rows * columns * 8, transcendentals=0),
    )(*ins)


def body(tokens, log_decay, w_query, w_key, w_value, w_level, w_out):
    rows, shard = tokens.shape
    heads = log_decay.shape[1]
    head_size = w_out.shape[0] // heads
    level_count = w_level.shape[1] // heads
    seq_size = lax.axis_size("seq")
    seq_bits = seq_size.bit_length() - 1
    me = jnp.full((1,), lax.axis_index("tp"), jnp.int32)
    slab = jnp.full((1,), lax.axis_index("seq"), jnp.int32)

    def swap_tp(x, bit):
        return lax.ppermute(x, "tp", [(i, i ^ bit) for i in range(4)])

    def swap_seq(x, bit):
        return lax.ppermute(x, "seq", [(i, i ^ bit) for i in range(seq_size)])

    far = swap_tp(tokens, 2)
    near = swap_tp(tokens, 1)

    weights = (w_query, w_key, w_value, w_level.T)
    totals, ws, (drow, dcol, keep, total, span), blocks = begin(
        me, slab, tokens, near, log_decay.T, weights, w_out, head_size
    )
    w_here_own, w_here_send, w_far_own, w_far_send = blocks
    w_here, w_far = swap_tp(w_here_send, 1), swap_tp(w_far_send, 1)

    spans, factors, before = [span], [], None
    for b in range(seq_bits - 1):
        total, before, own, other, span = link(slab, b, total, swap_seq(total, 1 << b), before)
        spans.append(span)
        factors.append((own, other))

    wq, wkv, wkv_send, wl = ws
    wkv_near = swap_tp(wkv_send, 1)
    for_near = partial(far, wkv_near, (total, w_far, w_here))
    from_near = swap_tp(for_near, 1)
    totals = project(me, 2, far, wq, wkv, wl, totals, (for_near,))
    total_q, total_kv, total_l = totals
    far_near = swap_tp(gate(far, total_q, from_near), 1)
    k, v, *states = project_state(total_kv, from_near, keep, head_size)

    earlier = []
    for b in range(seq_bits):
        others = [swap_seq(state, 1 << b) for state in states]
        earlier.append(others)
        if b < seq_bits - 1:
            states = [combine(*pair, *factors[b], i) for i, pair in enumerate(zip(states, others))]

    before_last = [state for others in earlier[:-1] for state in others]
    local, scaled = attend(
        me, 3, far_near, wq, wl, total_q, total_l, k, v, dcol, drow, spans, before_last, head_size, level_count
    )

    unit = rows // 8
    ends = (0, 2, 4, 6, 7, 8)
    cuts = [slice(start * unit, stop * unit) for start, stop in zip(ends, ends[1:])]
    middle = rows // 2
    tops = finish(local, scaled, earlier[-1][0], 0, [slice(0, middle), slice(middle, rows)], head_size, 10**8)
    first = [(x, swap_tp(x, 1)) for x in tops]
    second = finish(local, scaled, earlier[-1][1], 1, cuts, head_size, 0, tops)
    second = [(x, swap_tp(x, 1)) for x in second]
    crossing = []
    for pair, cut in zip(second, cuts):
        i = cut.start // middle
        here = slice(cut.start - i * middle, cut.stop - i * middle)
        crossing.append(out_block([first[i]], [pair], [(0, here)], w_far_own, w_far, BF16))
    places = [(c.start // middle, slice(c.start % middle, c.start % middle + c.stop - c.start)) for c in cuts]
    own_block = out_block(first, second, places, w_here_own, w_here, F32, (crossing[-1],))
    out = None
    for cut, x in zip(cuts, crossing):
        out = add_rows(own_block, swap_tp(x, 2), out, cut.start, unit)
    return out


def solution(mesh):
    in_specs = (
        P("seq", "tp"),
        P("seq", "tp"),
        P(None, "tp"),
        P(None, "tp"),
        P(None, "tp"),
        P(None, "tp"),
        P("tp", None),
    )
    out_specs = P("seq", "tp")
    return jax.shard_map(body, mesh=mesh, in_specs=in_specs, out_specs=out_specs, check_vma=False)
```

```python
import functools

import jax
import jax.numpy as jnp
from jax import lax
from jax.experimental import pallas as pl
from jax.experimental.pallas import tpu as pltpu
from jax.sharding import PartitionSpec as P

BLOCK = 128
F32 = jnp.float32
BF16 = jnp.bfloat16
VMEM = pl.BlockSpec(memory_space=pltpu.VMEM)
SMEM = pl.BlockSpec(memory_space=pltpu.SMEM)
ANY = pl.BlockSpec(memory_space=pl.ANY)
HBM = pl.BlockSpec(memory_space=pltpu.HBM)


def dot(a, b):
    return jnp.dot(a, b, preferred_element_type=F32)


def dot_dims(a, b, left, right):
    return lax.dot_general(a, b, (((left,), (right,)), ((), ())), preferred_element_type=F32)


def shape(dims, dtype):
    return jax.ShapeDtypeStruct(dims, dtype)


def call(kernel, ins, outs, flops, after=(), smem=0, hbm=0, aliases=None, scratch=(), megabytes=8):
    count = len(ins)
    ins = list(ins)
    for i in range(smem, smem + hbm):
        ins[i] = pltpu.with_memory_space_constraint(ins[i], pltpu.HBM)

    def run(*refs):
        kernel(*refs[:count], *refs[count + len(after) :])

    nbytes = sum(x.size * x.dtype.itemsize for x in (*ins, *outs)) if flops else 0
    return pl.pallas_call(
        run,
        in_specs=[SMEM] * smem + [HBM] * hbm + [VMEM] * (count - smem - hbm) + [ANY] * len(after),
        out_specs=[VMEM] * len(outs),
        out_shape=list(outs),
        input_output_aliases=aliases or {},
        scratch_shapes=list(scratch),
        compiler_params=pltpu.CompilerParams(vmem_limit_bytes=megabytes * 1024 * 1024),
        cost_estimate=pl.CostEstimate(flops=flops, bytes_accessed=nbytes, transcendentals=0),
    )(*ins, *after)


def gate(x, *after):
    def run(*refs):
        pass

    return pl.pallas_call(
        run,
        in_specs=[ANY] * (1 + len(after)),
        out_specs=ANY,
        out_shape=shape(x.shape, x.dtype),
        input_output_aliases={0: 0},
        compiler_params=pltpu.CompilerParams(vmem_limit_bytes=1024 * 1024),
        cost_estimate=pl.CostEstimate(flops=0, bytes_accessed=0, transcendentals=0),
    )(x, *after)


def copies(pairs, sems):
    started = [pltpu.make_async_copy(src, dst, sems.at[i]) for i, (src, dst) in enumerate(pairs)]
    for copy in started:
        copy.start()
    return started


def upper_half(slab_ref, bit):
    return ((slab_ref[0] >> bit) & 1) == 1


def decays(slab_ref, x_ref, row_ref, col_ref, keep_ref, total_ref, span_ref):
    heads, rows = x_ref.shape
    head_size = total_ref.shape[1] // heads
    x = x_ref[...]
    x = jnp.concatenate([x, jnp.zeros((-heads % 8, rows), F32)], axis=0) if heads % 8 else x
    place = lax.broadcasted_iota(jnp.int32, x.shape, 1)
    shift = 1
    while shift < rows:
        x = x + jnp.where(place >= shift, pltpu.roll(x, shift, 1), 0.0)
        shift *= 2
    total = x[:, rows - 1 : rows]
    row_ref[...] = x[:heads]
    col_ref[...] = jnp.transpose(x)[:, :heads]
    keep_ref[...] = jnp.transpose(jnp.exp(total - x))[:, :heads]
    for h in range(heads):
        total_ref[:, h * head_size : (h + 1) * head_size] = jnp.broadcast_to(
            total[h : h + 1], (8, head_size)
        )
    span_ref[...] = jnp.full(span_ref.shape, jnp.where(upper_half(slab_ref, 0), 0.0, -jnp.inf), F32)


def link(slab, bit, total, other, before):
    def kernel(slab_ref, *refs):
        total_ref, other_ref = refs[:2]
        total_out, before_out, own_out, other_out, span_out = refs[-5:]
        upper = upper_half(slab_ref, bit)
        here, there = total_ref[...], other_ref[...]
        total_out[...] = here + there
        so_far = jnp.where(upper, there, 0.0)
        if before is not None:
            so_far = so_far + refs[2][...]
        before_out[...] = so_far
        own_out[...] = jnp.where(upper, 1.0, jnp.exp(there))
        other_out[...] = jnp.where(upper, jnp.exp(here), 1.0)
        span_out[...] = jnp.where(upper_half(slab_ref, bit + 1), so_far, -jnp.inf)

    ins = [slab, total, other] + ([] if before is None else [before])
    return call(kernel, ins, [shape(total.shape, F32)] * 5, 0, smem=1)


def combine(state, other, own_factor, other_factor, which, after):
    cols = slice(which * state.shape[1], (which + 1) * state.shape[1])

    def kernel(s_ref, o_ref, a_ref, b_ref, out_ref):
        out_ref[...] = (
            a_ref[0:1, cols] * s_ref[...].astype(F32) + b_ref[0:1, cols] * o_ref[...].astype(F32)
        ).astype(BF16)

    return call(kernel, [state, other, own_factor, other_factor], [shape(state.shape, BF16)], 0, after)[0]


def begin(me, slab, tokens, near, log_decay_rows, ws, w_out, head_size):
    wq, wk, wv, wl = ws
    rows, shard = near.shape
    q_width, kv_width = wq.shape[1], wk.shape[1]
    heads = log_decay_rows.shape[0]
    block = w_out.shape[1] // 4

    def kernel(me_ref, slab_ref, t_ref, wq_ref, wk_ref, wv_ref, wl_ref, wo_ref, near_ref, decay_ref, *refs):
        total_q, total_kv, total_l, far_q, far_kv, send_kv, all_l = refs[:7]
        decay_outs, blocks, (own_x, own_q, own_kv, sems) = refs[7:12], refs[12:16], refs[16:]

        def pairs(i, q_dst, kv_dst):
            here = pl.ds(pl.multiple_of((me_ref[0] ^ i) * shard, 128), shard)
            return [
                (wk_ref.at[here, :], kv_dst.at[:, :kv_width]),
                (wv_ref.at[here, :], kv_dst.at[:, kv_width:]),
                (wq_ref.at[here, :], q_dst),
            ]

        def columns(i):
            return wo_ref.at[:, pl.ds(pl.multiple_of((me_ref[0] ^ i) * block, 128), block)]

        moves = pairs(0, own_q.at[0], own_kv.at[0]) + [(wl_ref, all_l), (t_ref, own_x)]
        moves += pairs(1, own_q.at[1], own_kv.at[1])
        moves += pairs(2, far_q.at[0], far_kv) + pairs(3, far_q.at[1], send_kv)
        moves += [(columns(i), blocks[i]) for i in range(4)]
        started = copies(moves, sems)
        decays(slab_ref, decay_ref, *decay_outs)
        for copy in started[:5]:
            copy.wait()
        lanes = pl.ds(pl.multiple_of(me_ref[0] * shard, 128), shard)
        own = own_x[...]
        total_kv[...] = dot(own, own_kv[0])
        total_q[...] = dot(own, own_q[0])
        total_l[...] = dot_dims(own, all_l[:, lanes], 1, 1)
        for copy in started[5:8]:
            copy.wait()
        lanes = pl.ds(pl.multiple_of((me_ref[0] ^ 1) * shard, 128), shard)
        total_kv[...] += dot(near_ref[...], own_kv[1])
        total_q[...] += dot(near_ref[...], own_q[1])
        total_l[...] += dot_dims(near_ref[...], all_l[:, lanes], 1, 1)
        for copy in started[8:]:
            copy.wait()

    wide = shape((8, heads * head_size), F32)
    outs = [
        shape((rows, q_width), F32),
        shape((rows, 2 * kv_width), F32),
        shape((rows, wl.shape[0]), F32),
        shape((2, shard, q_width), BF16),
        shape((shard, 2 * kv_width), BF16),
        shape((shard, 2 * kv_width), BF16),
        shape(wl.shape, BF16),
        shape((heads, rows), F32),
        shape((rows, heads), F32),
        shape((rows, heads), F32),
        wide,
        wide,
    ] + [shape((w_out.shape[0], block), BF16)] * 4
    scratch = [
        pltpu.VMEM((rows, shard), BF16),
        pltpu.VMEM((2, shard, q_width), BF16),
        pltpu.VMEM((2, shard, 2 * kv_width), BF16),
        pltpu.SemaphoreType.DMA((18,)),
    ]
    ins = [me, slab, tokens, wq, wk, wv, wl, w_out, near, log_decay_rows]
    outs = call(kernel, ins, outs, 0, smem=2, hbm=6, scratch=scratch, megabytes=14)
    return outs[:3], outs[3:7], outs[7:12], outs[12:]


def add_levels(me_ref, place, x, wl_ref):
    shard = wl_ref.shape[1] // 4
    start = pl.multiple_of((me_ref[0] ^ place) * shard, 128)
    return dot_dims(x, wl_ref[:, pl.ds(start, shard)], 1, 1)


def project(me, place, x, wq, wkv, wl, totals, after=()):
    def kernel(me_ref, x_ref, q_ref, kv_ref, l_ref, *refs):
        ins, outs = refs[:3], refs[3:]
        outs[1][...] = ins[1][...] + dot(x_ref[...], kv_ref[...])
        outs[0][...] = ins[0][...] + dot(x_ref[...], q_ref[place - 2])
        outs[2][...] = ins[2][...] + add_levels(me_ref, place, x_ref[...], l_ref)

    outs = [shape(t.shape, F32) for t in totals]
    return call(kernel, [me, x, wq, wkv, wl, *totals], outs, 0, after, smem=1, aliases={5: 0, 6: 1, 7: 2})


def partial(x, w, after):
    def kernel(x_ref, w_ref, o_ref):
        o_ref[...] = dot(x_ref[...], w_ref[...]).astype(BF16)

    return call(kernel, [x, w], [shape((x.shape[0], w.shape[1]), BF16)], 0, after)[0]


def project_state(total_kv, from_near, keep, head_size):
    rows = total_kv.shape[0]
    heads = keep.shape[1]
    kv_width = total_kv.shape[1] // 2
    group = heads // (kv_width // head_size)

    half = heads // 2 * head_size

    def kernel(total_ref, near_ref, keep_ref, k_out, v_out, *s_outs):
        total = total_ref[...] + near_ref[...].astype(F32)
        keys = total[:, :kv_width].astype(BF16)
        values = total[:, kv_width:].astype(BF16)
        k_out[...] = keys
        v_out[...] = values
        for g in range(kv_width // head_size):
            cols = slice(g * head_size, (g + 1) * head_size)
            kf = keys[:, cols].astype(F32)
            weighted = jnp.concatenate(
                [(kf * keep_ref[:, h : h + 1]).astype(BF16) for h in range(g * group, (g + 1) * group)],
                axis=1,
            )
            states = dot_dims(values[:, cols], weighted, 0, 0).astype(BF16)
            for i in range(group):
                start = (g * group + i) * head_size
                s_outs[start // half][:, start % half : start % half + head_size] = states[
                    :, i * head_size : (i + 1) * head_size
                ]

    outs = [
        shape((rows, kv_width), BF16),
        shape((rows, kv_width), BF16),
        shape((head_size, half), BF16),
        shape((head_size, half), BF16),
    ]
    return call(kernel, [total_kv, from_near, keep], outs, 0)


def queries(me, place, x, wq, wl, total_q, total_l):
    def kernel(me_ref, x_ref, wq_ref, wl_ref, tq_ref, tl_ref, q_ref, l_ref):
        raw = tl_ref[...] + add_levels(me_ref, place, x_ref[...], wl_ref)
        l_ref[...] = jnp.maximum(raw, 0.0) + jnp.log1p(jnp.exp(-jnp.abs(raw)))
        q_ref[...] = (tq_ref[...] + dot(x_ref[...], wq_ref[place - 2])).astype(BF16)

    outs = [shape(total_q.shape, BF16), shape(total_l.shape, F32)]
    return call(kernel, [me, x, wq, wl, total_q, total_l], outs, 0, smem=1)


def column(ref, rows, place):
    return jnp.broadcast_to(ref[rows, place : place + 1], (BLOCK, BLOCK))


def attend(q, level, k, v, dcol, drow, which, head_size, level_count):
    rows, width = q.shape
    heads = width // head_size
    group = heads // (k.shape[1] // head_size)
    first = which * heads // 2

    def kernel(q_ref, l_ref, k_ref, v_ref, dcol_ref, drow_ref, o_ref):
        row_id = lax.broadcasted_iota(jnp.int32, (BLOCK, BLOCK), 0)
        col_id = lax.broadcasted_iota(jnp.int32, (BLOCK, BLOCK), 1)
        causal = row_id >= col_id
        for h in range(first, first + heads // 2):
            cols = slice(h * head_size, (h + 1) * head_size)
            kv = slice(h // group * head_size, (h // group + 1) * head_size)
            for i in range(rows // BLOCK):
                here = slice(i * BLOCK, (i + 1) * BLOCK)
                span = (i + 1) * BLOCK
                scores = dot_dims(q_ref[here, cols], k_ref[:span, kv], 1, 1)
                d_here = column(dcol_ref, here, h)
                weights = {}
                mixed = []
                for j in range(i + 1):
                    step = (i ^ j).bit_length()
                    if step not in weights:
                        weights[step] = column(l_ref, here, h * level_count + step)
                    there = slice(j * BLOCK, (j + 1) * BLOCK)
                    gap = d_here - drow_ref[h : h + 1, there]
                    if i == j:
                        gap = jnp.where(causal, gap, -jnp.inf)
                    mixed.append((weights[step] * jnp.exp(gap) * scores[:, there]).astype(BF16))
                mixing = mixed[0] if i == 0 else jnp.concatenate(mixed, axis=1)
                out = slice((h - first) * head_size, (h - first + 1) * head_size)
                o_ref[here, out] = dot(mixing, v_ref[:span, kv])

    ins = [q, level, k, v, dcol, drow]
    return call(kernel, ins, [shape((rows, width // 2), F32)], 0)[0]


def attend_earlier(locals_, q, level, dcol, spans, states, head_size, level_count):
    rows, width = q.shape
    bits = len(spans)
    half = width // 2
    own_levels = level_count - bits

    def kernel(a_ref, b_ref, q_ref, l_ref, dcol_ref, *refs):
        span_refs, state_refs = refs[:bits], refs[bits : bits + len(states)]
        outs = refs[-4:]
        for h in range(width // head_size):
            cols = slice(h * head_size, (h + 1) * head_size)
            which, at = divmod(h * head_size, half)
            out = slice(at, at + head_size)
            for i in range(rows // BLOCK):
                here = slice(i * BLOCK, (i + 1) * BLOCK)
                query = q_ref[here, cols].astype(F32)
                d_here = column(dcol_ref, here, h)
                total = (a_ref, b_ref)[which][here, out]
                for b in range(bits):
                    factor = column(l_ref, here, h * level_count + own_levels + b)
                    factor = factor * jnp.exp(d_here + span_refs[b][0:1, cols])
                    scaled = (query * factor).astype(BF16)
                    if b == bits - 1:
                        outs[2 + which][here, out] = scaled
                    else:
                        total = total + dot_dims(scaled, state_refs[2 * b + which][:, out], 1, 1)
                outs[which][here, out] = total

    ins = [*locals_, q, level, dcol, *spans, *states]
    outs = [shape((rows, half), F32)] * 2 + [shape((rows, half), BF16)] * 2
    outs = call(kernel, ins, outs, 0)
    return list(zip(outs[:2], outs[2:]))


def finish(local, scaled, state, cuts, head_size, flops, after=()):
    width = state.shape[1]

    def kernel(o_ref, q_ref, s_ref, *outs):
        for rows, n_ref in zip(cuts, outs):
            for c in range(0, width, head_size):
                cols = slice(c, c + head_size)
                total = o_ref[rows, cols] + dot_dims(q_ref[rows, cols], s_ref[:, cols], 1, 1)
                mean = jnp.mean(total * total, axis=-1, keepdims=True)
                n_ref[:, cols] = (total * lax.rsqrt(mean + 1e-05)).astype(BF16)

    outs = [shape((cut.stop - cut.start, width), BF16) for cut in cuts]
    return call(kernel, [local, scaled, state], outs, flops, after)


def out_block(first, second, places, w0, w1, dtype, after=()):
    columns = w1.shape[1]
    rows = sum(cut.stop - cut.start for _, cut in places)
    tile = min(columns, 512)

    def kernel(*refs):
        f_refs, s_refs = refs[: 2 * len(first)], refs[2 * len(first) : -3]
        w0_ref, w1_ref, o_ref = refs[-3:]
        start = 0
        for i, (which, cut) in enumerate(places):
            here = slice(start, start + cut.stop - cut.start)
            start = here.stop
            own = jnp.concatenate([f_refs[2 * which][cut, :], s_refs[2 * i][...]], axis=1)
            near = jnp.concatenate([f_refs[2 * which + 1][cut, :], s_refs[2 * i + 1][...]], axis=1)
            for c in range(0, columns, tile):
                cols = slice(c, c + tile)
                o_ref[here, cols] = (dot(own, w0_ref[:, cols]) + dot(near, w1_ref[:, cols])).astype(dtype)

    ins = [x for pair in (*first, *second) for x in pair] + [w0, w1]
    return call(kernel, ins, [shape((rows, columns), dtype)], 0, after)[0]


def add_rows(here, arrived, out, start, unit):
    rows, columns = arrived.shape

    def kernel(h_ref, a_ref, *refs):
        place = pl.ds(pl.multiple_of(start + pl.program_id(0) * unit, unit), unit)
        refs[-1][...] = (h_ref[place, :] + a_ref[...].astype(F32)).astype(BF16)

    block = (unit, columns)
    ins, specs, aliases = [here, arrived], [VMEM, pl.BlockSpec(block, lambda s: (s, 0))], {}
    if out is not None:
        ins, specs, aliases = ins + [out], specs + [ANY], {2: 0}
    return pl.pallas_call(
        kernel,
        grid=(rows // unit,),
        in_specs=specs,
        out_specs=pl.BlockSpec(block, lambda s: (start // unit + s, 0)),
        out_shape=shape(here.shape, BF16),
        input_output_aliases=aliases,
        compiler_params=pltpu.CompilerParams(vmem_limit_bytes=8 * 1024 * 1024),
        cost_estimate=pl.CostEstimate(flops=0, bytes_accessed=rows * columns * 8, transcendentals=0),
    )(*ins)


def body(tokens, log_decay, w_query, w_key, w_value, w_level, w_out):
    rows, shard = tokens.shape
    heads = log_decay.shape[1]
    head_size = w_out.shape[0] // heads
    level_count = w_level.shape[1] // heads
    seq_size = lax.axis_size("seq")
    seq_bits = seq_size.bit_length() - 1
    me = jnp.full((1,), lax.axis_index("tp"), jnp.int32)
    slab = jnp.full((1,), lax.axis_index("seq"), jnp.int32)

    def swap_tp(x, bit):
        return lax.ppermute(x, "tp", [(i, i ^ bit) for i in range(4)])

    def swap_seq(x, bit):
        return lax.ppermute(x, "seq", [(i, i ^ bit) for i in range(seq_size)])

    far = swap_tp(tokens, 2)
    near = swap_tp(tokens, 1)

    weights = (w_query, w_key, w_value, w_level.T)
    totals, ws, (drow, dcol, keep, total, span), blocks = begin(
        me, slab, tokens, near, log_decay.T, weights, w_out, head_size
    )
    w_here_own, w_here_send, w_far_own, w_far_send = blocks
    w_here, w_far = swap_tp(w_here_send, 1), swap_tp(w_far_send, 1)

    spans, factors, before = [span], [], None
    for b in range(seq_bits - 1):
        total, before, own, other, span = link(slab, b, total, swap_seq(total, 1 << b), before)
        spans.append(span)
        factors.append((own, other))

    wq, wkv, wkv_send, wl = ws
    wkv_near = swap_tp(wkv_send, 1)
    for_near = partial(far, wkv_near, (total, w_far, w_here))
    from_near = swap_tp(for_near, 1)
    totals = project(me, 2, far, wq, wkv, wl, totals, (for_near,))
    total_q, total_kv, total_l = totals
    far_near = swap_tp(gate(far, total_q, from_near), 1)
    k, v, *states = project_state(total_kv, from_near, keep, head_size)

    q, level = queries(me, 3, far_near, wq, wl, total_q, total_l)
    locals_ = [attend(q, level, k, v, dcol, drow, i, head_size, level_count) for i in range(2)]
    earlier = []
    for b in range(seq_bits):
        others = [swap_seq(state, 1 << b) for state in states]
        earlier.append(others)
        if b < seq_bits - 1:
            afters = (locals_[b : b + 1], ())
            states = [
                combine(state, other, *factors[b], i, after)
                for i, (state, other, after) in enumerate(zip(states, others, afters))
            ]
    before_last = [state for others in earlier[:-1] for state in others]
    halves = attend_earlier(locals_, q, level, dcol, spans, before_last, head_size, level_count)

    unit = rows // 8
    ends = (0, 2, 4, 6, 7, 8)
    cuts = [slice(start * unit, stop * unit) for start, stop in zip(ends, ends[1:])]
    middle = rows // 2
    tops = finish(*halves[0], earlier[-1][0], [slice(0, middle), slice(middle, rows)], head_size, 10**8)
    first = [(x, swap_tp(x, 1)) for x in tops]
    second = finish(*halves[1], earlier[-1][1], cuts, head_size, 0, tops)
    second = [(x, swap_tp(x, 1)) for x in second]
    crossing = []
    for pair, cut in zip(second, cuts):
        i = cut.start // middle
        here = slice(cut.start - i * middle, cut.stop - i * middle)
        crossing.append(out_block([first[i]], [pair], [(0, here)], w_far_own, w_far, BF16))
    places = [(c.start // middle, slice(c.start % middle, c.start % middle + c.stop - c.start)) for c in cuts]
    own_block = out_block(first, second, places, w_here_own, w_here, F32, (crossing[-1],))
    out = None
    for cut, x in zip(cuts, crossing):
        out = add_rows(own_block, swap_tp(x, 2), out, cut.start, unit)
    return out


def solution(mesh):
    in_specs = (
        P("seq", "tp"),
        P("seq", "tp"),
        P(None, "tp"),
        P(None, "tp"),
        P(None, "tp"),
        P(None, "tp"),
        P("tp", None),
    )
    out_specs = P("seq", "tp")
    return jax.shard_map(body, mesh=mesh, in_specs=in_specs, out_specs=out_specs, check_vma=False)
```

```python
import functools

import jax
import jax.numpy as jnp
from jax import lax
from jax.experimental import pallas as pl
from jax.experimental.pallas import tpu as pltpu
from jax.sharding import PartitionSpec as P

BLOCK = 128
F32 = jnp.float32
BF16 = jnp.bfloat16
VMEM = pl.BlockSpec(memory_space=pltpu.VMEM)
SMEM = pl.BlockSpec(memory_space=pltpu.SMEM)
ANY = pl.BlockSpec(memory_space=pl.ANY)
HBM = pl.BlockSpec(memory_space=pltpu.HBM)


def dot(a, b):
    return jnp.dot(a, b, preferred_element_type=F32)


def dot_dims(a, b, left, right):
    return lax.dot_general(a, b, (((left,), (right,)), ((), ())), preferred_element_type=F32)


def shape(dims, dtype):
    return jax.ShapeDtypeStruct(dims, dtype)


def call(kernel, ins, outs, flops, after=(), smem=0, hbm=0, aliases=None, scratch=(), megabytes=8):
    count = len(ins)
    ins = list(ins)
    for i in range(smem, smem + hbm):
        ins[i] = pltpu.with_memory_space_constraint(ins[i], pltpu.HBM)

    def run(*refs):
        kernel(*refs[:count], *refs[count + len(after) :])

    nbytes = sum(x.size * x.dtype.itemsize for x in (*ins, *outs)) if flops else 0
    return pl.pallas_call(
        run,
        in_specs=[SMEM] * smem + [HBM] * hbm + [VMEM] * (count - smem - hbm) + [ANY] * len(after),
        out_specs=[VMEM] * len(outs),
        out_shape=list(outs),
        input_output_aliases=aliases or {},
        scratch_shapes=list(scratch),
        compiler_params=pltpu.CompilerParams(vmem_limit_bytes=megabytes * 1024 * 1024),
        cost_estimate=pl.CostEstimate(flops=flops, bytes_accessed=nbytes, transcendentals=0),
    )(*ins, *after)


def gate(x, *after):
    def run(*refs):
        pass

    return pl.pallas_call(
        run,
        in_specs=[ANY] * (1 + len(after)),
        out_specs=ANY,
        out_shape=shape(x.shape, x.dtype),
        input_output_aliases={0: 0},
        compiler_params=pltpu.CompilerParams(vmem_limit_bytes=1024 * 1024),
        cost_estimate=pl.CostEstimate(flops=0, bytes_accessed=0, transcendentals=0),
    )(x, *after)


def copies(pairs, sems):
    started = [pltpu.make_async_copy(src, dst, sems.at[i]) for i, (src, dst) in enumerate(pairs)]
    for copy in started:
        copy.start()
    return started


def upper_half(slab_ref, bit):
    return ((slab_ref[0] >> bit) & 1) == 1


def decays(slab_ref, x_ref, row_ref, col_ref, keep_ref, total_ref, span_ref):
    heads, rows = x_ref.shape
    head_size = total_ref.shape[1] // heads
    x = x_ref[...]
    x = jnp.concatenate([x, jnp.zeros((-heads % 8, rows), F32)], axis=0) if heads % 8 else x
    place = lax.broadcasted_iota(jnp.int32, x.shape, 1)
    shift = 1
    while shift < rows:
        x = x + jnp.where(place >= shift, pltpu.roll(x, shift, 1), 0.0)
        shift *= 2
    total = x[:, rows - 1 : rows]
    row_ref[...] = x[:heads]
    col_ref[...] = jnp.transpose(x)[:, :heads]
    keep_ref[...] = jnp.transpose(jnp.exp(total - x))[:, :heads]
    for h in range(heads):
        total_ref[:, h * head_size : (h + 1) * head_size] = jnp.broadcast_to(
            total[h : h + 1], (8, head_size)
        )
    span_ref[...] = jnp.full(span_ref.shape, jnp.where(upper_half(slab_ref, 0), 0.0, -jnp.inf), F32)


def link(slab, bit, total, other, before):
    def kernel(slab_ref, *refs):
        total_ref, other_ref = refs[:2]
        total_out, before_out, own_out, other_out, span_out = refs[-5:]
        upper = upper_half(slab_ref, bit)
        here, there = total_ref[...], other_ref[...]
        total_out[...] = here + there
        so_far = jnp.where(upper, there, 0.0)
        if before is not None:
            so_far = so_far + refs[2][...]
        before_out[...] = so_far
        own_out[...] = jnp.where(upper, 1.0, jnp.exp(there))
        other_out[...] = jnp.where(upper, jnp.exp(here), 1.0)
        span_out[...] = jnp.where(upper_half(slab_ref, bit + 1), so_far, -jnp.inf)

    ins = [slab, total, other] + ([] if before is None else [before])
    return call(kernel, ins, [shape(total.shape, F32)] * 5, 0, smem=1)


def combine(state, other, own_factor, other_factor, which, after):
    cols = slice(which * state.shape[1], (which + 1) * state.shape[1])

    def kernel(s_ref, o_ref, a_ref, b_ref, out_ref):
        out_ref[...] = (
            a_ref[0:1, cols] * s_ref[...].astype(F32) + b_ref[0:1, cols] * o_ref[...].astype(F32)
        ).astype(BF16)

    return call(kernel, [state, other, own_factor, other_factor], [shape(state.shape, BF16)], 0, after)[0]


def begin(me, slab, tokens, near, log_decay_rows, ws, w_out, head_size):
    wq, wk, wv, wl = ws
    rows, shard = near.shape
    q_width, kv_width = wq.shape[1], wk.shape[1]
    heads = log_decay_rows.shape[0]
    block = w_out.shape[1] // 4

    def kernel(me_ref, slab_ref, t_ref, wq_ref, wk_ref, wv_ref, wl_ref, wo_ref, near_ref, decay_ref, *refs):
        total_q, total_kv, total_l, far_q, far_kv, send_kv, all_l = refs[:7]
        decay_outs, blocks, (own_x, own_q, own_kv, sems) = refs[7:12], refs[12:16], refs[16:]

        def pairs(i, q_dst, kv_dst):
            here = pl.ds(pl.multiple_of((me_ref[0] ^ i) * shard, 128), shard)
            return [
                (wk_ref.at[here, :], kv_dst.at[:, :kv_width]),
                (wv_ref.at[here, :], kv_dst.at[:, kv_width:]),
                (wq_ref.at[here, :], q_dst),
            ]

        def columns(i):
            return wo_ref.at[:, pl.ds(pl.multiple_of((me_ref[0] ^ i) * block, 128), block)]

        moves = pairs(0, own_q.at[0], own_kv.at[0]) + [(wl_ref, all_l), (t_ref, own_x)]
        moves += pairs(1, own_q.at[1], own_kv.at[1])
        moves += pairs(2, far_q.at[0], far_kv) + pairs(3, far_q.at[1], send_kv)
        moves += [(columns(i), blocks[i]) for i in range(4)]
        started = copies(moves, sems)
        decays(slab_ref, decay_ref, *decay_outs)
        for copy in started[:5]:
            copy.wait()
        lanes = pl.ds(pl.multiple_of(me_ref[0] * shard, 128), shard)
        own = own_x[...]
        total_kv[...] = dot(own, own_kv[0])
        total_q[...] = dot(own, own_q[0])
        total_l[...] = dot_dims(own, all_l[:, lanes], 1, 1)
        for copy in started[5:8]:
            copy.wait()
        lanes = pl.ds(pl.multiple_of((me_ref[0] ^ 1) * shard, 128), shard)
        total_kv[...] += dot(near_ref[...], own_kv[1])
        total_q[...] += dot(near_ref[...], own_q[1])
        total_l[...] += dot_dims(near_ref[...], all_l[:, lanes], 1, 1)
        for copy in started[8:]:
            copy.wait()

    wide = shape((8, heads * head_size), F32)
    outs = [
        shape((rows, q_width), F32),
        shape((rows, 2 * kv_width), F32),
        shape((rows, wl.shape[0]), F32),
        shape((2, shard, q_width), BF16),
        shape((shard, 2 * kv_width), BF16),
        shape((shard, 2 * kv_width), BF16),
        shape(wl.shape, BF16),
        shape((heads, rows), F32),
        shape((rows, heads), F32),
        shape((rows, heads), F32),
        wide,
        wide,
    ] + [shape((w_out.shape[0], block), BF16)] * 4
    scratch = [
        pltpu.VMEM((rows, shard), BF16),
        pltpu.VMEM((2, shard, q_width), BF16),
        pltpu.VMEM((2, shard, 2 * kv_width), BF16),
        pltpu.SemaphoreType.DMA((18,)),
    ]
    ins = [me, slab, tokens, wq, wk, wv, wl, w_out, near, log_decay_rows]
    outs = call(kernel, ins, outs, 0, smem=2, hbm=6, scratch=scratch, megabytes=14)
    return outs[:3], outs[3:7], outs[7:12], outs[12:]


def add_levels(me_ref, place, x, wl_ref):
    shard = wl_ref.shape[1] // 4
    start = pl.multiple_of((me_ref[0] ^ place) * shard, 128)
    return dot_dims(x, wl_ref[:, pl.ds(start, shard)], 1, 1)


def project(me, place, x, wq, wkv, wl, totals, after=()):
    def kernel(me_ref, x_ref, q_ref, kv_ref, l_ref, *refs):
        ins, outs = refs[:3], refs[3:]
        outs[1][...] = ins[1][...] + dot(x_ref[...], kv_ref[...])
        outs[0][...] = ins[0][...] + dot(x_ref[...], q_ref[place - 2])
        outs[2][...] = ins[2][...] + add_levels(me_ref, place, x_ref[...], l_ref)

    outs = [shape(t.shape, F32) for t in totals]
    return call(kernel, [me, x, wq, wkv, wl, *totals], outs, 0, after, smem=1, aliases={5: 0, 6: 1, 7: 2})


def partial(x, w, after):
    def kernel(x_ref, w_ref, o_ref):
        o_ref[...] = dot(x_ref[...], w_ref[...]).astype(BF16)

    return call(kernel, [x, w], [shape((x.shape[0], w.shape[1]), BF16)], 0, after)[0]


def project_state(total_kv, from_near, keep, head_size):
    rows = total_kv.shape[0]
    heads = keep.shape[1]
    kv_width = total_kv.shape[1] // 2
    group = heads // (kv_width // head_size)

    half = heads // 2 * head_size

    def kernel(total_ref, near_ref, keep_ref, k_out, v_out, *s_outs):
        total = total_ref[...] + near_ref[...].astype(F32)
        keys = total[:, :kv_width].astype(BF16)
        values = total[:, kv_width:].astype(BF16)
        k_out[...] = keys
        v_out[...] = values
        for g in range(kv_width // head_size):
            cols = slice(g * head_size, (g + 1) * head_size)
            kf = keys[:, cols].astype(F32)
            weighted = jnp.concatenate(
                [(kf * keep_ref[:, h : h + 1]).astype(BF16) for h in range(g * group, (g + 1) * group)],
                axis=1,
            )
            states = dot_dims(values[:, cols], weighted, 0, 0).astype(BF16)
            for i in range(group):
                start = (g * group + i) * head_size
                s_outs[start // half][:, start % half : start % half + head_size] = states[
                    :, i * head_size : (i + 1) * head_size
                ]

    outs = [
        shape((rows, kv_width), BF16),
        shape((rows, kv_width), BF16),
        shape((head_size, half), BF16),
        shape((head_size, half), BF16),
    ]
    return call(kernel, [total_kv, from_near, keep], outs, 0)


def queries(me, place, x, wq, wl, total_q, total_l):
    def kernel(me_ref, x_ref, wq_ref, wl_ref, tq_ref, tl_ref, q_ref, l_ref):
        raw = tl_ref[...] + add_levels(me_ref, place, x_ref[...], wl_ref)
        l_ref[...] = jnp.maximum(raw, 0.0) + jnp.log1p(jnp.exp(-jnp.abs(raw)))
        q_ref[...] = (tq_ref[...] + dot(x_ref[...], wq_ref[place - 2])).astype(BF16)

    outs = [shape(total_q.shape, BF16), shape(total_l.shape, F32)]
    return call(kernel, [me, x, wq, wl, total_q, total_l], outs, 0, smem=1)


def column(ref, rows, place):
    return jnp.broadcast_to(ref[rows, place : place + 1], (BLOCK, BLOCK))


def attend(q, level, k, v, dcol, drow, which, head_size, level_count):
    rows, width = q.shape
    heads = width // head_size
    group = heads // (k.shape[1] // head_size)
    first = which * heads // 2

    def kernel(q_ref, l_ref, k_ref, v_ref, dcol_ref, drow_ref, o_ref):
        row_id = lax.broadcasted_iota(jnp.int32, (BLOCK, BLOCK), 0)
        col_id = lax.broadcasted_iota(jnp.int32, (BLOCK, BLOCK), 1)
        causal = row_id >= col_id
        for h in range(first, first + heads // 2):
            cols = slice(h * head_size, (h + 1) * head_size)
            kv = slice(h // group * head_size, (h // group + 1) * head_size)
            for i in range(rows // BLOCK):
                here = slice(i * BLOCK, (i + 1) * BLOCK)
                span = (i + 1) * BLOCK
                scores = dot_dims(q_ref[here, cols], k_ref[:span, kv], 1, 1)
                d_here = column(dcol_ref, here, h)
                weights = {}
                mixed = []
                for j in range(i + 1):
                    step = (i ^ j).bit_length()
                    if step not in weights:
                        weights[step] = column(l_ref, here, h * level_count + step)
                    there = slice(j * BLOCK, (j + 1) * BLOCK)
                    gap = d_here - drow_ref[h : h + 1, there]
                    if i == j:
                        gap = jnp.where(causal, gap, -jnp.inf)
                    mixed.append((weights[step] * jnp.exp(gap) * scores[:, there]).astype(BF16))
                mixing = mixed[0] if i == 0 else jnp.concatenate(mixed, axis=1)
                out = slice((h - first) * head_size, (h - first + 1) * head_size)
                o_ref[here, out] = dot(mixing, v_ref[:span, kv])

    ins = [q, level, k, v, dcol, drow]
    return call(kernel, ins, [shape((rows, width // 2), F32)], 0)[0]


def attend_earlier(locals_, q, level, dcol, spans, states, head_size, level_count):
    rows, width = q.shape
    bits = len(spans)
    half = width // 2
    own_levels = level_count - bits

    def kernel(a_ref, b_ref, q_ref, l_ref, dcol_ref, *refs):
        span_refs, state_refs = refs[:bits], refs[bits : bits + len(states)]
        outs = refs[-4:]
        for h in range(width // head_size):
            cols = slice(h * head_size, (h + 1) * head_size)
            which, at = divmod(h * head_size, half)
            out = slice(at, at + head_size)
            for i in range(rows // BLOCK):
                here = slice(i * BLOCK, (i + 1) * BLOCK)
                query = q_ref[here, cols].astype(F32)
                d_here = column(dcol_ref, here, h)
                total = (a_ref, b_ref)[which][here, out]
                for b in range(bits):
                    factor = column(l_ref, here, h * level_count + own_levels + b)
                    factor = factor * jnp.exp(d_here + span_refs[b][0:1, cols])
                    scaled = (query * factor).astype(BF16)
                    if b == bits - 1:
                        outs[2 + which][here, out] = scaled
                    else:
                        total = total + dot_dims(scaled, state_refs[2 * b + which][:, out], 1, 1)
                outs[which][here, out] = total

    ins = [*locals_, q, level, dcol, *spans, *states]
    outs = [shape((rows, half), F32)] * 2 + [shape((rows, half), BF16)] * 2
    outs = call(kernel, ins, outs, 0)
    return list(zip(outs[:2], outs[2:]))


def finish(local, scaled, state, cuts, head_size, flops, after=()):
    width = state.shape[1]

    def kernel(o_ref, q_ref, s_ref, *outs):
        for rows, n_ref in zip(cuts, outs):
            for c in range(0, width, head_size):
                cols = slice(c, c + head_size)
                total = o_ref[rows, cols] + dot_dims(q_ref[rows, cols], s_ref[:, cols], 1, 1)
                mean = jnp.mean(total * total, axis=-1, keepdims=True)
                n_ref[:, cols] = (total * lax.rsqrt(mean + 1e-05)).astype(BF16)

    outs = [shape((cut.stop - cut.start, width), BF16) for cut in cuts]
    return call(kernel, [local, scaled, state], outs, flops, after)


def out_block(first, second, places, w0, w1, dtype, after=()):
    columns = w1.shape[1]
    rows = sum(cut.stop - cut.start for _, cut in places)
    tile = min(columns, 512)

    def kernel(*refs):
        f_refs, s_refs = refs[: 2 * len(first)], refs[2 * len(first) : -3]
        w0_ref, w1_ref, o_ref = refs[-3:]
        start = 0
        for i, (which, cut) in enumerate(places):
            here = slice(start, start + cut.stop - cut.start)
            start = here.stop
            own = jnp.concatenate([f_refs[2 * which][cut, :], s_refs[2 * i][...]], axis=1)
            near = jnp.concatenate([f_refs[2 * which + 1][cut, :], s_refs[2 * i + 1][...]], axis=1)
            for c in range(0, columns, tile):
                cols = slice(c, c + tile)
                o_ref[here, cols] = (dot(own, w0_ref[:, cols]) + dot(near, w1_ref[:, cols])).astype(dtype)

    ins = [x for pair in (*first, *second) for x in pair] + [w0, w1]
    return call(kernel, ins, [shape((rows, columns), dtype)], 0, after)[0]


def add_rows(here, arrived, out, start, unit):
    rows, columns = arrived.shape

    def kernel(h_ref, a_ref, *refs):
        place = pl.ds(pl.multiple_of(start + pl.program_id(0) * unit, unit), unit)
        refs[-1][...] = (h_ref[place, :] + a_ref[...].astype(F32)).astype(BF16)

    block = (unit, columns)
    ins, specs, aliases = [here, arrived], [VMEM, pl.BlockSpec(block, lambda s: (s, 0))], {}
    if out is not None:
        ins, specs, aliases = ins + [out], specs + [ANY], {2: 0}
    return pl.pallas_call(
        kernel,
        grid=(rows // unit,),
        in_specs=specs,
        out_specs=pl.BlockSpec(block, lambda s: (start // unit + s, 0)),
        out_shape=shape(here.shape, BF16),
        input_output_aliases=aliases,
        compiler_params=pltpu.CompilerParams(vmem_limit_bytes=8 * 1024 * 1024),
        cost_estimate=pl.CostEstimate(flops=0, bytes_accessed=rows * columns * 8, transcendentals=0),
    )(*ins)


def body(tokens, log_decay, w_query, w_key, w_value, w_level, w_out):
    rows, shard = tokens.shape
    heads = log_decay.shape[1]
    head_size = w_out.shape[0] // heads
    level_count = w_level.shape[1] // heads
    seq_size = lax.axis_size("seq")
    seq_bits = seq_size.bit_length() - 1
    me = jnp.full((1,), lax.axis_index("tp"), jnp.int32)
    slab = jnp.full((1,), lax.axis_index("seq"), jnp.int32)

    def swap_tp(x, bit):
        return lax.ppermute(x, "tp", [(i, i ^ bit) for i in range(4)])

    def swap_seq(x, bit):
        one_way = 2 * bit == seq_size
        return lax.ppermute(x, "seq", [(i, i ^ bit) for i in range(seq_size) if not (one_way and i & bit)])

    far = swap_tp(tokens, 2)
    near = swap_tp(tokens, 1)

    weights = (w_query, w_key, w_value, w_level.T)
    totals, ws, (drow, dcol, keep, total, span), blocks = begin(
        me, slab, tokens, near, log_decay.T, weights, w_out, head_size
    )
    w_here_own, w_here_send, w_far_own, w_far_send = blocks
    w_here, w_far = swap_tp(w_here_send, 1), swap_tp(w_far_send, 1)

    spans, factors, before = [span], [], None
    for b in range(seq_bits - 1):
        total, before, own, other, span = link(slab, b, total, swap_seq(total, 1 << b), before)
        spans.append(span)
        factors.append((own, other))

    wq, wkv, wkv_send, wl = ws
    wkv_near = swap_tp(wkv_send, 1)
    for_near = partial(far, wkv_near, (total, w_far, w_here))
    from_near = swap_tp(for_near, 1)
    totals = project(me, 2, far, wq, wkv, wl, totals, (for_near,))
    total_q, total_kv, total_l = totals
    far_near = swap_tp(gate(far, total_q, from_near), 1)
    k, v, *states = project_state(total_kv, from_near, keep, head_size)

    q, level = queries(me, 3, far_near, wq, wl, total_q, total_l)
    locals_ = [attend(q, level, k, v, dcol, drow, i, head_size, level_count) for i in range(2)]
    earlier = []
    for b in range(seq_bits):
        others = [swap_seq(state, 1 << b) for state in states]
        earlier.append(others)
        if b < seq_bits - 1:
            afters = (locals_[b : b + 1], ())
            states = [
                combine(state, other, *factors[b], i, after)
                for i, (state, other, after) in enumerate(zip(states, others, afters))
            ]
    before_last = [state for others in earlier[:-1] for state in others]
    halves = attend_earlier(locals_, q, level, dcol, spans, before_last, head_size, level_count)

    unit = rows // 8
    ends = (0, 2, 4, 6, 7, 8)
    cuts = [slice(start * unit, stop * unit) for start, stop in zip(ends, ends[1:])]
    middle = rows // 2
    tops = finish(*halves[0], earlier[-1][0], [slice(0, middle), slice(middle, rows)], head_size, 10**8)
    first = [(x, swap_tp(x, 1)) for x in tops]
    second = finish(*halves[1], earlier[-1][1], cuts, head_size, 0, tops)
    second = [(x, swap_tp(x, 1)) for x in second]
    crossing = []
    for pair, cut in zip(second, cuts):
        i = cut.start // middle
        here = slice(cut.start - i * middle, cut.stop - i * middle)
        crossing.append(out_block([first[i]], [pair], [(0, here)], w_far_own, w_far, BF16))
    places = [(c.start // middle, slice(c.start % middle, c.start % middle + c.stop - c.start)) for c in cuts]
    own_block = out_block(first, second, places, w_here_own, w_here, F32, (crossing[-1],))
    out = None
    for cut, x in zip(cuts, crossing):
        out = add_rows(own_block, swap_tp(x, 2), out, cut.start, unit)
    return out


def solution(mesh):
    in_specs = (
        P("seq", "tp"),
        P("seq", "tp"),
        P(None, "tp"),
        P(None, "tp"),
        P(None, "tp"),
        P(None, "tp"),
        P("tp", None),
    )
    out_specs = P("seq", "tp")
    return jax.shard_map(body, mesh=mesh, in_specs=in_specs, out_specs=out_specs, check_vma=False)
```

```python
import functools

import jax
import jax.numpy as jnp
from jax import lax
from jax.experimental import pallas as pl
from jax.experimental.pallas import tpu as pltpu
from jax.sharding import PartitionSpec as P

BLOCK = 128
F32 = jnp.float32
BF16 = jnp.bfloat16
VMEM = pl.BlockSpec(memory_space=pltpu.VMEM)
SMEM = pl.BlockSpec(memory_space=pltpu.SMEM)
ANY = pl.BlockSpec(memory_space=pl.ANY)
HBM = pl.BlockSpec(memory_space=pltpu.HBM)


def dot(a, b):
    return jnp.dot(a, b, preferred_element_type=F32)


def dot_dims(a, b, left, right):
    return lax.dot_general(a, b, (((left,), (right,)), ((), ())), preferred_element_type=F32)


def shape(dims, dtype):
    return jax.ShapeDtypeStruct(dims, dtype)


def call(kernel, ins, outs, flops, after=(), smem=0, hbm=0, aliases=None, scratch=(), megabytes=8):
    count = len(ins)
    ins = list(ins)
    for i in range(smem, smem + hbm):
        ins[i] = pltpu.with_memory_space_constraint(ins[i], pltpu.HBM)

    def run(*refs):
        kernel(*refs[:count], *refs[count + len(after) :])

    nbytes = sum(x.size * x.dtype.itemsize for x in (*ins, *outs)) if flops else 0
    return pl.pallas_call(
        run,
        in_specs=[SMEM] * smem + [HBM] * hbm + [VMEM] * (count - smem - hbm) + [ANY] * len(after),
        out_specs=[VMEM] * len(outs),
        out_shape=list(outs),
        input_output_aliases=aliases or {},
        scratch_shapes=list(scratch),
        compiler_params=pltpu.CompilerParams(vmem_limit_bytes=megabytes * 1024 * 1024),
        cost_estimate=pl.CostEstimate(flops=flops, bytes_accessed=nbytes, transcendentals=0),
    )(*ins, *after)


def gate(x, *after):
    def run(*refs):
        pass

    return pl.pallas_call(
        run,
        in_specs=[ANY] * (1 + len(after)),
        out_specs=ANY,
        out_shape=shape(x.shape, x.dtype),
        input_output_aliases={0: 0},
        compiler_params=pltpu.CompilerParams(vmem_limit_bytes=1024 * 1024),
        cost_estimate=pl.CostEstimate(flops=0, bytes_accessed=0, transcendentals=0),
    )(x, *after)


def copies(pairs, sems):
    started = [pltpu.make_async_copy(src, dst, sems.at[i]) for i, (src, dst) in enumerate(pairs)]
    for copy in started:
        copy.start()
    return started


def upper_half(slab_ref, bit):
    return ((slab_ref[0] >> bit) & 1) == 1


def decays(slab_ref, x_ref, row_ref, col_ref, keep_ref, total_ref, span_ref):
    heads, rows = x_ref.shape
    head_size = total_ref.shape[1] // heads
    x = x_ref[...]
    x = jnp.concatenate([x, jnp.zeros((-heads % 8, rows), F32)], axis=0) if heads % 8 else x
    place = lax.broadcasted_iota(jnp.int32, x.shape, 1)
    shift = 1
    while shift < rows:
        x = x + jnp.where(place >= shift, pltpu.roll(x, shift, 1), 0.0)
        shift *= 2
    total = x[:, rows - 1 : rows]
    row_ref[...] = x[:heads]
    col_ref[...] = jnp.transpose(x)[:, :heads]
    keep_ref[...] = jnp.transpose(jnp.exp(total - x))[:, :heads]
    for h in range(heads):
        total_ref[:, h * head_size : (h + 1) * head_size] = jnp.broadcast_to(
            total[h : h + 1], (8, head_size)
        )
    span_ref[...] = jnp.full(span_ref.shape, jnp.where(upper_half(slab_ref, 0), 0.0, -jnp.inf), F32)


def link(slab, bit, total, other, before):
    def kernel(slab_ref, *refs):
        total_ref, other_ref = refs[:2]
        total_out, before_out, own_out, other_out, span_out = refs[-5:]
        upper = upper_half(slab_ref, bit)
        here, there = total_ref[...], other_ref[...]
        total_out[...] = here + there
        so_far = jnp.where(upper, there, 0.0)
        if before is not None:
            so_far = so_far + refs[2][...]
        before_out[...] = so_far
        own_out[...] = jnp.where(upper, 1.0, jnp.exp(there))
        other_out[...] = jnp.where(upper, jnp.exp(here), 1.0)
        span_out[...] = jnp.where(upper_half(slab_ref, bit + 1), so_far, -jnp.inf)

    ins = [slab, total, other] + ([] if before is None else [before])
    return call(kernel, ins, [shape(total.shape, F32)] * 5, 0, smem=1)


def combine(state, other, own_factor, other_factor, which, after):
    cols = slice(which * state.shape[1], (which + 1) * state.shape[1])

    def kernel(s_ref, o_ref, a_ref, b_ref, out_ref):
        out_ref[...] = (
            a_ref[0:1, cols] * s_ref[...].astype(F32) + b_ref[0:1, cols] * o_ref[...].astype(F32)
        ).astype(BF16)

    return call(kernel, [state, other, own_factor, other_factor], [shape(state.shape, BF16)], 0, after)[0]


def begin(me, slab, tokens, near, log_decay_rows, ws, w_out, head_size):
    wq, wk, wv, wl = ws
    rows, shard = near.shape
    q_width, kv_width = wq.shape[1], wk.shape[1]
    heads = log_decay_rows.shape[0]
    block = w_out.shape[1] // 4

    def kernel(me_ref, slab_ref, t_ref, wq_ref, wk_ref, wv_ref, wl_ref, wo_ref, near_ref, decay_ref, *refs):
        total_q, total_kv, total_l, far_q, far_kv, send_kv, all_l = refs[:7]
        decay_outs, blocks, (own_x, own_q, own_kv, sems) = refs[7:12], refs[12:16], refs[16:]

        def pairs(i, q_dst, kv_dst):
            here = pl.ds(pl.multiple_of((me_ref[0] ^ i) * shard, 128), shard)
            return [
                (wk_ref.at[here, :], kv_dst.at[:, :kv_width]),
                (wv_ref.at[here, :], kv_dst.at[:, kv_width:]),
                (wq_ref.at[here, :], q_dst),
            ]

        def columns(i):
            return wo_ref.at[:, pl.ds(pl.multiple_of((me_ref[0] ^ i) * block, 128), block)]

        moves = pairs(0, own_q.at[0], own_kv.at[0]) + [(wl_ref, all_l), (t_ref, own_x)]
        moves += pairs(1, own_q.at[1], own_kv.at[1])
        moves += pairs(2, far_q.at[0], far_kv) + pairs(3, far_q.at[1], send_kv)
        moves += [(columns(i), blocks[i]) for i in range(4)]
        started = copies(moves, sems)
        decays(slab_ref, decay_ref, *decay_outs)
        for copy in started[:5]:
            copy.wait()
        lanes = pl.ds(pl.multiple_of(me_ref[0] * shard, 128), shard)
        own = own_x[...]
        total_kv[...] = dot(own, own_kv[0])
        total_q[...] = dot(own, own_q[0])
        total_l[...] = dot_dims(own, all_l[:, lanes], 1, 1)
        for copy in started[5:8]:
            copy.wait()
        lanes = pl.ds(pl.multiple_of((me_ref[0] ^ 1) * shard, 128), shard)
        total_kv[...] += dot(near_ref[...], own_kv[1])
        total_q[...] += dot(near_ref[...], own_q[1])
        total_l[...] += dot_dims(near_ref[...], all_l[:, lanes], 1, 1)
        for copy in started[8:]:
            copy.wait()

    wide = shape((8, heads * head_size), F32)
    outs = [
        shape((rows, q_width), F32),
        shape((rows, 2 * kv_width), F32),
        shape((rows, wl.shape[0]), F32),
        shape((2, shard, q_width), BF16),
        shape((shard, 2 * kv_width), BF16),
        shape((shard, 2 * kv_width), BF16),
        shape(wl.shape, BF16),
        shape((heads, rows), F32),
        shape((rows, heads), F32),
        shape((rows, heads), F32),
        wide,
        wide,
    ] + [shape((w_out.shape[0], block), BF16)] * 4
    scratch = [
        pltpu.VMEM((rows, shard), BF16),
        pltpu.VMEM((2, shard, q_width), BF16),
        pltpu.VMEM((2, shard, 2 * kv_width), BF16),
        pltpu.SemaphoreType.DMA((18,)),
    ]
    ins = [me, slab, tokens, wq, wk, wv, wl, w_out, near, log_decay_rows]
    outs = call(kernel, ins, outs, 0, smem=2, hbm=6, scratch=scratch, megabytes=14)
    return outs[:3], outs[3:7], outs[7:12], outs[12:]


def add_levels(me_ref, place, x, wl_ref):
    shard = wl_ref.shape[1] // 4
    start = pl.multiple_of((me_ref[0] ^ place) * shard, 128)
    return dot_dims(x, wl_ref[:, pl.ds(start, shard)], 1, 1)


def project(me, place, x, wq, wkv, wl, totals, after=()):
    def kernel(me_ref, x_ref, q_ref, kv_ref, l_ref, *refs):
        ins, outs = refs[:3], refs[3:]
        outs[1][...] = ins[1][...] + dot(x_ref[...], kv_ref[...])
        outs[0][...] = ins[0][...] + dot(x_ref[...], q_ref[place - 2])
        outs[2][...] = ins[2][...] + add_levels(me_ref, place, x_ref[...], l_ref)

    outs = [shape(t.shape, F32) for t in totals]
    return call(kernel, [me, x, wq, wkv, wl, *totals], outs, 0, after, smem=1, aliases={5: 0, 6: 1, 7: 2})


def partial(x, w, after):
    def kernel(x_ref, w_ref, o_ref):
        o_ref[...] = dot(x_ref[...], w_ref[...]).astype(BF16)

    return call(kernel, [x, w], [shape((x.shape[0], w.shape[1]), BF16)], 0, after)[0]


def project_state(total_kv, from_near, keep, head_size):
    rows = total_kv.shape[0]
    heads = keep.shape[1]
    kv_width = total_kv.shape[1] // 2
    group = heads // (kv_width // head_size)

    half = heads // 2 * head_size

    def kernel(total_ref, near_ref, keep_ref, k_out, v_out, *s_outs):
        total = total_ref[...] + near_ref[...].astype(F32)
        keys = total[:, :kv_width].astype(BF16)
        values = total[:, kv_width:].astype(BF16)
        k_out[...] = keys
        v_out[...] = values
        for g in range(kv_width // head_size):
            cols = slice(g * head_size, (g + 1) * head_size)
            kf = keys[:, cols].astype(F32)
            weighted = jnp.concatenate(
                [(kf * keep_ref[:, h : h + 1]).astype(BF16) for h in range(g * group, (g + 1) * group)],
                axis=1,
            )
            states = dot_dims(values[:, cols], weighted, 0, 0).astype(BF16)
            for i in range(group):
                start = (g * group + i) * head_size
                s_outs[start // half][:, start % half : start % half + head_size] = states[
                    :, i * head_size : (i + 1) * head_size
                ]

    outs = [
        shape((rows, kv_width), BF16),
        shape((rows, kv_width), BF16),
        shape((head_size, half), BF16),
        shape((head_size, half), BF16),
    ]
    return call(kernel, [total_kv, from_near, keep], outs, 0)


def queries(me, place, x, wq, wl, total_q, total_l):
    def kernel(me_ref, x_ref, wq_ref, wl_ref, tq_ref, tl_ref, q_ref, l_ref):
        raw = tl_ref[...] + add_levels(me_ref, place, x_ref[...], wl_ref)
        l_ref[...] = jnp.maximum(raw, 0.0) + jnp.log1p(jnp.exp(-jnp.abs(raw)))
        q_ref[...] = (tq_ref[...] + dot(x_ref[...], wq_ref[place - 2])).astype(BF16)

    outs = [shape(total_q.shape, BF16), shape(total_l.shape, F32)]
    return call(kernel, [me, x, wq, wl, total_q, total_l], outs, 0, smem=1)


def column(ref, rows, place):
    return jnp.broadcast_to(ref[rows, place : place + 1], (BLOCK, BLOCK))


def attend(q, level, k, v, dcol, drow, which, head_size, level_count):
    rows, width = q.shape
    heads = width // head_size
    group = heads // (k.shape[1] // head_size)
    first = which * heads // 2

    def kernel(q_ref, l_ref, k_ref, v_ref, dcol_ref, drow_ref, o_ref):
        row_id = lax.broadcasted_iota(jnp.int32, (BLOCK, BLOCK), 0)
        col_id = lax.broadcasted_iota(jnp.int32, (BLOCK, BLOCK), 1)
        causal = row_id >= col_id
        for h in range(first, first + heads // 2):
            cols = slice(h * head_size, (h + 1) * head_size)
            kv = slice(h // group * head_size, (h // group + 1) * head_size)
            for i in range(rows // BLOCK):
                here = slice(i * BLOCK, (i + 1) * BLOCK)
                span = (i + 1) * BLOCK
                scores = dot_dims(q_ref[here, cols], k_ref[:span, kv], 1, 1)
                d_here = column(dcol_ref, here, h)
                weights = {}
                mixed = []
                for j in range(i + 1):
                    step = (i ^ j).bit_length()
                    if step not in weights:
                        weights[step] = column(l_ref, here, h * level_count + step)
                    there = slice(j * BLOCK, (j + 1) * BLOCK)
                    gap = d_here - drow_ref[h : h + 1, there]
                    if i == j:
                        gap = jnp.where(causal, gap, -jnp.inf)
                    mixed.append((weights[step] * jnp.exp(gap) * scores[:, there]).astype(BF16))
                mixing = mixed[0] if i == 0 else jnp.concatenate(mixed, axis=1)
                out = slice((h - first) * head_size, (h - first + 1) * head_size)
                o_ref[here, out] = dot(mixing, v_ref[:span, kv])

    ins = [q, level, k, v, dcol, drow]
    return call(kernel, ins, [shape((rows, width // 2), F32)], 0)[0]


def attend_earlier(locals_, q, level, dcol, spans, states, head_size, level_count):
    rows, width = q.shape
    bits = len(spans)
    half = width // 2
    own_levels = level_count - bits

    def kernel(a_ref, b_ref, q_ref, l_ref, dcol_ref, *refs):
        span_refs, state_refs = refs[:bits], refs[bits : bits + len(states)]
        outs = refs[-4:]
        for h in range(width // head_size):
            cols = slice(h * head_size, (h + 1) * head_size)
            which, at = divmod(h * head_size, half)
            out = slice(at, at + head_size)
            for i in range(rows // BLOCK):
                here = slice(i * BLOCK, (i + 1) * BLOCK)
                query = q_ref[here, cols].astype(F32)
                d_here = column(dcol_ref, here, h)
                total = (a_ref, b_ref)[which][here, out]
                for b in range(bits):
                    factor = column(l_ref, here, h * level_count + own_levels + b)
                    factor = factor * jnp.exp(d_here + span_refs[b][0:1, cols])
                    scaled = (query * factor).astype(BF16)
                    if b == bits - 1:
                        outs[2 + which][here, out] = scaled
                    else:
                        total = total + dot_dims(scaled, state_refs[2 * b + which][:, out], 1, 1)
                outs[which][here, out] = total

    ins = [*locals_, q, level, dcol, *spans, *states]
    outs = [shape((rows, half), F32)] * 2 + [shape((rows, half), BF16)] * 2
    outs = call(kernel, ins, outs, 0)
    return list(zip(outs[:2], outs[2:]))


def finish(slab, bit, local, scaled, states, cuts, head_size, flops, after=()):
    width = local.shape[1]

    def kernel(slab_ref, o_ref, q_ref, s0_ref, s1_ref, *outs):
        s_ref = jnp.where(upper_half(slab_ref, bit), s1_ref[...].astype(F32), s0_ref[...].astype(F32))
        s_ref = s_ref.astype(BF16)
        for rows, n_ref in zip(cuts, outs):
            for c in range(0, width, head_size):
                cols = slice(c, c + head_size)
                total = o_ref[rows, cols] + dot_dims(q_ref[rows, cols], s_ref[:, cols], 1, 1)
                mean = jnp.mean(total * total, axis=-1, keepdims=True)
                n_ref[:, cols] = (total * lax.rsqrt(mean + 1e-05)).astype(BF16)

    outs = [shape((cut.stop - cut.start, width), BF16) for cut in cuts]
    return call(kernel, [slab, local, scaled, *states], outs, flops, after, smem=1)


def out_block(first, second, places, w0, w1, dtype, after=()):
    columns = w1.shape[1]
    rows = sum(cut.stop - cut.start for _, cut in places)
    tile = min(columns, 512)

    def kernel(*refs):
        f_refs, s_refs = refs[: 2 * len(first)], refs[2 * len(first) : -3]
        w0_ref, w1_ref, o_ref = refs[-3:]
        start = 0
        for i, (which, cut) in enumerate(places):
            here = slice(start, start + cut.stop - cut.start)
            start = here.stop
            own = jnp.concatenate([f_refs[2 * which][cut, :], s_refs[2 * i][...]], axis=1)
            near = jnp.concatenate([f_refs[2 * which + 1][cut, :], s_refs[2 * i + 1][...]], axis=1)
            for c in range(0, columns, tile):
                cols = slice(c, c + tile)
                o_ref[here, cols] = (dot(own, w0_ref[:, cols]) + dot(near, w1_ref[:, cols])).astype(dtype)

    ins = [x for pair in (*first, *second) for x in pair] + [w0, w1]
    return call(kernel, ins, [shape((rows, columns), dtype)], 0, after)[0]


def add_rows(here, arrived, out, start, unit):
    rows, columns = arrived.shape

    def kernel(h_ref, a_ref, *refs):
        place = pl.ds(pl.multiple_of(start + pl.program_id(0) * unit, unit), unit)
        refs[-1][...] = (h_ref[place, :] + a_ref[...].astype(F32)).astype(BF16)

    block = (unit, columns)
    ins, specs, aliases = [here, arrived], [VMEM, pl.BlockSpec(block, lambda s: (s, 0))], {}
    if out is not None:
        ins, specs, aliases = ins + [out], specs + [ANY], {2: 0}
    return pl.pallas_call(
        kernel,
        grid=(rows // unit,),
        in_specs=specs,
        out_specs=pl.BlockSpec(block, lambda s: (start // unit + s, 0)),
        out_shape=shape(here.shape, BF16),
        input_output_aliases=aliases,
        compiler_params=pltpu.CompilerParams(vmem_limit_bytes=8 * 1024 * 1024),
        cost_estimate=pl.CostEstimate(flops=0, bytes_accessed=rows * columns * 8, transcendentals=0),
    )(*ins)


def body(tokens, log_decay, w_query, w_key, w_value, w_level, w_out):
    rows, shard = tokens.shape
    heads = log_decay.shape[1]
    head_size = w_out.shape[0] // heads
    level_count = w_level.shape[1] // heads
    seq_size = lax.axis_size("seq")
    seq_bits = seq_size.bit_length() - 1
    me = jnp.full((1,), lax.axis_index("tp"), jnp.int32)
    slab = jnp.full((1,), lax.axis_index("seq"), jnp.int32)

    def swap_tp(x, bit):
        return lax.ppermute(x, "tp", [(i, i ^ bit) for i in range(4)])

    def swap_seq(x, bit):
        return lax.ppermute(x, "seq", [(i, i ^ bit) for i in range(seq_size)])

    def from_second_quarter(x, bits):
        quarter = seq_size // 4
        pairs = {i: i for i in range(seq_size)}
        for i in range(quarter, 2 * quarter):
            pairs[i], pairs[i ^ bits] = i ^ bits, i
        return lax.ppermute(x, "seq", list(pairs.items()))

    far = swap_tp(tokens, 2)
    near = swap_tp(tokens, 1)

    weights = (w_query, w_key, w_value, w_level.T)
    totals, ws, (drow, dcol, keep, total, span), blocks = begin(
        me, slab, tokens, near, log_decay.T, weights, w_out, head_size
    )
    w_here_own, w_here_send, w_far_own, w_far_send = blocks
    w_here, w_far = swap_tp(w_here_send, 1), swap_tp(w_far_send, 1)

    spans, factors, before = [span], [], None
    for b in range(seq_bits - 1):
        total, before, own, other, span = link(slab, b, total, swap_seq(total, 1 << b), before)
        spans.append(span)
        factors.append((own, other))

    wq, wkv, wkv_send, wl = ws
    wkv_near = swap_tp(wkv_send, 1)
    for_near = partial(far, wkv_near, (total, w_far, w_here))
    from_near = swap_tp(for_near, 1)
    totals = project(me, 2, far, wq, wkv, wl, totals, (for_near,))
    total_q, total_kv, total_l = totals
    far_near = swap_tp(gate(far, total_q, from_near), 1)
    k, v, *states = project_state(total_kv, from_near, keep, head_size)

    q, level = queries(me, 3, far_near, wq, wl, total_q, total_l)
    locals_ = [attend(q, level, k, v, dcol, drow, i, head_size, level_count) for i in range(2)]
    earlier = []
    for b in range(seq_bits):
        if b == seq_bits - 1:
            last = [
                (from_second_quarter(x, 3 << (b - 1)), from_second_quarter(x, 1 << b)) for x in states
            ]
            break
        others = [swap_seq(state, 1 << b) for state in states]
        earlier.append(others)
        afters = (locals_[b : b + 1], ())
        states = [
            combine(state, other, *factors[b], i, after)
            for i, (state, other, after) in enumerate(zip(states, others, afters))
        ]
    before_last = [state for others in earlier for state in others]
    halves = attend_earlier(locals_, q, level, dcol, spans, before_last, head_size, level_count)

    unit = rows // 8
    ends = (0, 2, 4, 6, 7, 8)
    cuts = [slice(start * unit, stop * unit) for start, stop in zip(ends, ends[1:])]
    middle = rows // 2
    tops = finish(
        slab, seq_bits - 2, *halves[0], last[0], [slice(0, middle), slice(middle, rows)], head_size, 10**8
    )
    first = [(x, swap_tp(x, 1)) for x in tops]
    second = finish(slab, seq_bits - 2, *halves[1], last[1], cuts, head_size, 0, tops)
    second = [(x, swap_tp(x, 1)) for x in second]
    crossing = []
    for pair, cut in zip(second, cuts):
        i = cut.start // middle
        here = slice(cut.start - i * middle, cut.stop - i * middle)
        crossing.append(out_block([first[i]], [pair], [(0, here)], w_far_own, w_far, BF16))
    places = [(c.start // middle, slice(c.start % middle, c.start % middle + c.stop - c.start)) for c in cuts]
    own_block = out_block(first, second, places, w_here_own, w_here, F32, (crossing[-1],))
    out = None
    for cut, x in zip(cuts, crossing):
        out = add_rows(own_block, swap_tp(x, 2), out, cut.start, unit)
    return out


def solution(mesh):
    in_specs = (
        P("seq", "tp"),
        P("seq", "tp"),
        P(None, "tp"),
        P(None, "tp"),
        P(None, "tp"),
        P(None, "tp"),
        P("tp", None),
    )
    out_specs = P("seq", "tp")
    return jax.shard_map(body, mesh=mesh, in_specs=in_specs, out_specs=out_specs, check_vma=False)
```

```python
import functools

import jax
import jax.numpy as jnp
from jax import lax
from jax.experimental import pallas as pl
from jax.experimental.pallas import tpu as pltpu
from jax.sharding import PartitionSpec as P

BLOCK = 128
F32 = jnp.float32
BF16 = jnp.bfloat16
VMEM = pl.BlockSpec(memory_space=pltpu.VMEM)
SMEM = pl.BlockSpec(memory_space=pltpu.SMEM)
ANY = pl.BlockSpec(memory_space=pl.ANY)
HBM = pl.BlockSpec(memory_space=pltpu.HBM)


def dot(a, b):
    return jnp.dot(a, b, preferred_element_type=F32)


def dot_dims(a, b, left, right):
    return lax.dot_general(a, b, (((left,), (right,)), ((), ())), preferred_element_type=F32)


def shape(dims, dtype):
    return jax.ShapeDtypeStruct(dims, dtype)


def call(kernel, ins, outs, flops, after=(), smem=0, hbm=0, aliases=None, scratch=(), megabytes=8):
    count = len(ins)
    ins = list(ins)
    for i in range(smem, smem + hbm):
        ins[i] = pltpu.with_memory_space_constraint(ins[i], pltpu.HBM)

    def run(*refs):
        kernel(*refs[:count], *refs[count + len(after) :])

    nbytes = sum(x.size * x.dtype.itemsize for x in (*ins, *outs)) if flops else 0
    return pl.pallas_call(
        run,
        in_specs=[SMEM] * smem + [HBM] * hbm + [VMEM] * (count - smem - hbm) + [ANY] * len(after),
        out_specs=[VMEM] * len(outs),
        out_shape=list(outs),
        input_output_aliases=aliases or {},
        scratch_shapes=list(scratch),
        compiler_params=pltpu.CompilerParams(vmem_limit_bytes=megabytes * 1024 * 1024),
        cost_estimate=pl.CostEstimate(flops=flops, bytes_accessed=nbytes, transcendentals=0),
    )(*ins, *after)


def gate(x, *after):
    def run(*refs):
        pass

    return pl.pallas_call(
        run,
        in_specs=[ANY] * (1 + len(after)),
        out_specs=ANY,
        out_shape=shape(x.shape, x.dtype),
        input_output_aliases={0: 0},
        compiler_params=pltpu.CompilerParams(vmem_limit_bytes=1024 * 1024),
        cost_estimate=pl.CostEstimate(flops=0, bytes_accessed=0, transcendentals=0),
    )(x, *after)


def copies(pairs, sems):
    started = [pltpu.make_async_copy(src, dst, sems.at[i]) for i, (src, dst) in enumerate(pairs)]
    for copy in started:
        copy.start()
    return started


def upper_half(slab_ref, bit):
    return ((slab_ref[0] >> bit) & 1) == 1


def decays(slab_ref, x_ref, row_ref, col_ref, keep_ref, total_ref, span_ref):
    heads, rows = x_ref.shape
    head_size = total_ref.shape[1] // heads
    x = x_ref[...]
    x = jnp.concatenate([x, jnp.zeros((-heads % 8, rows), F32)], axis=0) if heads % 8 else x
    place = lax.broadcasted_iota(jnp.int32, x.shape, 1)
    shift = 1
    while shift < rows:
        x = x + jnp.where(place >= shift, pltpu.roll(x, shift, 1), 0.0)
        shift *= 2
    total = x[:, rows - 1 : rows]
    row_ref[...] = x[:heads]
    col_ref[...] = jnp.transpose(x)[:, :heads]
    keep_ref[...] = jnp.transpose(jnp.exp(total - x))[:, :heads]
    for h in range(heads):
        total_ref[:, h * head_size : (h + 1) * head_size] = jnp.broadcast_to(
            total[h : h + 1], (8, head_size)
        )
    span_ref[...] = jnp.full(span_ref.shape, jnp.where(upper_half(slab_ref, 0), 0.0, -jnp.inf), F32)


def link(slab, bit, total, other, before):
    def kernel(slab_ref, *refs):
        total_ref, other_ref = refs[:2]
        total_out, before_out, own_out, other_out, span_out = refs[-5:]
        upper = upper_half(slab_ref, bit)
        here, there = total_ref[...], other_ref[...]
        total_out[...] = here + there
        so_far = jnp.where(upper, there, 0.0)
        if before is not None:
            so_far = so_far + refs[2][...]
        before_out[...] = so_far
        own_out[...] = jnp.where(upper, 1.0, jnp.exp(there))
        other_out[...] = jnp.where(upper, jnp.exp(here), 1.0)
        span_out[...] = jnp.where(upper_half(slab_ref, bit + 1), so_far, -jnp.inf)

    ins = [slab, total, other] + ([] if before is None else [before])
    return call(kernel, ins, [shape(total.shape, F32)] * 5, 0, smem=1)


def combine(state, other, own_factor, other_factor, after):
    def kernel(s_ref, o_ref, a_ref, b_ref, out_ref):
        out_ref[...] = (
            a_ref[0:1, :] * s_ref[...].astype(F32) + b_ref[0:1, :] * o_ref[...].astype(F32)
        ).astype(BF16)

    return call(kernel, [state, other, own_factor, other_factor], [shape(state.shape, BF16)], 0, after)[0]


def begin(me, slab, tokens, near, log_decay_rows, ws, w_out, head_size):
    wq, wk, wv, wl = ws
    rows, shard = near.shape
    q_width, kv_width = wq.shape[1], wk.shape[1]
    heads = log_decay_rows.shape[0]
    block = w_out.shape[1] // 4

    def kernel(me_ref, slab_ref, t_ref, wq_ref, wk_ref, wv_ref, wl_ref, wo_ref, near_ref, decay_ref, *refs):
        total_q, total_kv, total_l, far_q, far_kv, send_kv, all_l = refs[:7]
        decay_outs, blocks, (own_x, own_q, own_kv, sems) = refs[7:12], refs[12:16], refs[16:]

        def pairs(i, q_dst, kv_dst):
            here = pl.ds(pl.multiple_of((me_ref[0] ^ i) * shard, 128), shard)
            return [
                (wk_ref.at[here, :], kv_dst.at[:, :kv_width]),
                (wv_ref.at[here, :], kv_dst.at[:, kv_width:]),
                (wq_ref.at[here, :], q_dst),
            ]

        def columns(i):
            return wo_ref.at[:, pl.ds(pl.multiple_of((me_ref[0] ^ i) * block, 128), block)]

        moves = pairs(0, own_q.at[0], own_kv.at[0]) + [(wl_ref, all_l), (t_ref, own_x)]
        moves += pairs(1, own_q.at[1], own_kv.at[1])
        moves += pairs(2, far_q.at[0], far_kv) + pairs(3, far_q.at[1], send_kv)
        moves += [(columns(i), blocks[i]) for i in range(4)]
        started = copies(moves, sems)
        decays(slab_ref, decay_ref, *decay_outs)
        for copy in started[:5]:
            copy.wait()
        lanes = pl.ds(pl.multiple_of(me_ref[0] * shard, 128), shard)
        own = own_x[...]
        total_kv[...] = dot(own, own_kv[0])
        total_q[...] = dot(own, own_q[0])
        total_l[...] = dot_dims(own, all_l[:, lanes], 1, 1)
        for copy in started[5:8]:
            copy.wait()
        lanes = pl.ds(pl.multiple_of((me_ref[0] ^ 1) * shard, 128), shard)
        total_kv[...] += dot(near_ref[...], own_kv[1])
        total_q[...] += dot(near_ref[...], own_q[1])
        total_l[...] += dot_dims(near_ref[...], all_l[:, lanes], 1, 1)
        for copy in started[8:]:
            copy.wait()

    wide = shape((8, heads * head_size), F32)
    outs = [
        shape((rows, q_width), F32),
        shape((rows, 2 * kv_width), F32),
        shape((rows, wl.shape[0]), F32),
        shape((2, shard, q_width), BF16),
        shape((shard, 2 * kv_width), BF16),
        shape((shard, 2 * kv_width), BF16),
        shape(wl.shape, BF16),
        shape((heads, rows), F32),
        shape((rows, heads), F32),
        shape((rows, heads), F32),
        wide,
        wide,
    ] + [shape((w_out.shape[0], block), BF16)] * 4
    scratch = [
        pltpu.VMEM((rows, shard), BF16),
        pltpu.VMEM((2, shard, q_width), BF16),
        pltpu.VMEM((2, shard, 2 * kv_width), BF16),
        pltpu.SemaphoreType.DMA((18,)),
    ]
    ins = [me, slab, tokens, wq, wk, wv, wl, w_out, near, log_decay_rows]
    outs = call(kernel, ins, outs, 0, smem=2, hbm=6, scratch=scratch, megabytes=14)
    return outs[:3], outs[3:7], outs[7:12], outs[12:]


def add_levels(me_ref, place, x, wl_ref):
    shard = wl_ref.shape[1] // 4
    start = pl.multiple_of((me_ref[0] ^ place) * shard, 128)
    return dot_dims(x, wl_ref[:, pl.ds(start, shard)], 1, 1)


def project(me, place, x, wq, wl, total_q, total_l, after):
    def kernel(me_ref, x_ref, wq_ref, wl_ref, q_ref, l_ref, q_out, l_out):
        q_out[...] = q_ref[...] + dot(x_ref[...], wq_ref[place - 2])
        l_out[...] = l_ref[...] + add_levels(me_ref, place, x_ref[...], wl_ref)

    outs = [shape(t.shape, F32) for t in (total_q, total_l)]
    flops = 2 * x.size * (total_q.shape[1] + total_l.shape[1])
    return call(kernel, [me, x, wq, wl, total_q, total_l], outs, flops, after, smem=1, aliases={4: 0, 5: 1})


def split(x, ways, after):
    rows, columns = x.shape
    part = columns // ways

    def kernel(x_ref, *outs):
        for i, o_ref in enumerate(outs):
            o_ref[...] = x_ref[:, i * part : (i + 1) * part]

    return call(kernel, [x], [shape((rows, part), x.dtype)] * ways, 0, after)


def partial(x, w, after):
    def kernel(x_ref, w_ref, o_ref):
        o_ref[...] = dot(x_ref[...], w_ref[...]).astype(BF16)

    return call(kernel, [x, w], [shape((x.shape[0], w.shape[1]), BF16)], 0, after)[0]


def add_product(x, w, total, after):
    def kernel(x_ref, w_ref, t_ref, o_ref):
        o_ref[...] = t_ref[...] + dot(x_ref[...], w_ref[...])

    return call(kernel, [x, w, total], [shape(total.shape, F32)], 0, after, aliases={2: 0})[0]


def project_state(total_kv, from_near, keep, head_size):
    rows = total_kv.shape[0]
    heads = keep.shape[1]
    kv_width = total_kv.shape[1] // 2
    group = heads // (kv_width // head_size)

    def kernel(total_ref, near_ref, keep_ref, k_out, v_out, s_out):
        total = total_ref[...] + near_ref[...].astype(F32)
        keys = total[:, :kv_width].astype(BF16)
        values = total[:, kv_width:].astype(BF16)
        k_out[...] = keys
        v_out[...] = values
        for g in range(kv_width // head_size):
            cols = slice(g * head_size, (g + 1) * head_size)
            kf = keys[:, cols].astype(F32)
            weighted = jnp.concatenate(
                [(kf * keep_ref[:, h : h + 1]).astype(BF16) for h in range(g * group, (g + 1) * group)],
                axis=1,
            )
            wide = slice(g * group * head_size, (g + 1) * group * head_size)
            s_out[:, wide] = dot_dims(values[:, cols], weighted, 0, 0).astype(BF16)

    outs = [
        shape((rows, kv_width), BF16),
        shape((rows, kv_width), BF16),
        shape((head_size, heads * head_size), BF16),
    ]
    return call(kernel, [total_kv, from_near, keep], outs, 0)


def attend(me, place, xs, wq, wl, total_q, total_l, k, v, dcol, drow, spans, states, head_size, level_count):
    rows, width = total_q.shape
    bits = len(spans)
    heads = width // head_size
    group = heads // (k.shape[1] // head_size)
    own_levels = level_count - bits

    def kernel(me_ref, *refs):
        x = jnp.concatenate([x_ref[...] for x_ref in refs[: len(xs)]], axis=1)
        refs = refs[len(xs) :]
        wq_ref, wl_ref, tq_ref, tl_ref, k_ref, v_ref, dcol_ref, drow_ref = refs[:8]
        span_refs, state_refs = refs[8 : 8 + bits], refs[8 + bits : 7 + 2 * bits]
        o_ref, s_ref, q_ref, l_ref = refs[-4:]
        raw = tl_ref[...] + add_levels(me_ref, place, x, wl_ref)
        l_ref[...] = jnp.maximum(raw, 0.0) + jnp.log1p(jnp.exp(-jnp.abs(raw)))
        q_ref[...] = (tq_ref[...] + dot(x, wq_ref[place - 2])).astype(BF16)
        row_id = lax.broadcasted_iota(jnp.int32, (BLOCK, BLOCK), 0)
        col_id = lax.broadcasted_iota(jnp.int32, (BLOCK, BLOCK), 1)
        causal = row_id >= col_id
        for h in range(heads):
            g = h // group
            cols = slice(h * head_size, (h + 1) * head_size)
            kv = slice(g * head_size, (g + 1) * head_size)
            for i in range(rows // BLOCK):
                here = slice(i * BLOCK, (i + 1) * BLOCK)
                span = (i + 1) * BLOCK
                query = q_ref[here, cols]
                scores = dot_dims(query, k_ref[:span, kv], 1, 1)
                d_here = jnp.broadcast_to(dcol_ref[here, h : h + 1], (BLOCK, BLOCK))

                def weight(level):
                    column = h * level_count + level
                    return jnp.broadcast_to(l_ref[here, column : column + 1], (BLOCK, BLOCK))

                weights = {}
                mixed = []
                for j in range(i + 1):
                    level = (i ^ j).bit_length()
                    if level not in weights:
                        weights[level] = weight(level)
                    there = slice(j * BLOCK, (j + 1) * BLOCK)
                    gap = d_here - drow_ref[h : h + 1, there]
                    if i == j:
                        gap = jnp.where(causal, gap, -jnp.inf)
                    mixed.append((weights[level] * jnp.exp(gap) * scores[:, there]).astype(BF16))
                mixing = mixed[0] if i == 0 else jnp.concatenate(mixed, axis=1)
                total = dot(mixing, v_ref[:span, kv])
                wide = query.astype(F32)
                for b in range(bits):
                    factor = weight(own_levels + b) * jnp.exp(d_here + span_refs[b][0:1, cols])
                    scaled = (wide * factor).astype(BF16)
                    if b == bits - 1:
                        s_ref[here, cols] = scaled
                    else:
                        total = total + dot_dims(scaled, state_refs[b][:, cols], 1, 1)
                o_ref[here, cols] = total

    ins = [me, *xs, wq, wl, total_q, total_l, k, v, dcol, drow, *spans, *states]
    wide = shape((rows, width), BF16)
    outs = [shape((rows, width), F32), wide, wide, shape(total_l.shape, F32)]
    flops = 2 * rows * wq.shape[1] * width + 4 * rows * rows * width
    return call(kernel, ins, outs, flops, smem=1)[:2]


def finish(local, scaled, state, cuts, head_size, after=()):
    width = local.shape[1]

    def kernel(o_ref, q_ref, s_ref, *outs):
        for rows, n_ref in zip(cuts, outs):
            for c in range(0, width, head_size):
                cols = slice(c, c + head_size)
                total = o_ref[rows, cols] + dot_dims(q_ref[rows, cols], s_ref[:, cols], 1, 1)
                mean = jnp.mean(total * total, axis=-1, keepdims=True)
                n_ref[:, cols] = (total * lax.rsqrt(mean + 1e-05)).astype(BF16)

    outs = [shape((cut.stop - cut.start, width), BF16) for cut in cuts]
    return call(kernel, [local, scaled, state], outs, 0, after)


def out_block(pairs, w0, w1, dtype, after=()):
    columns = w1.shape[1]
    count = len(pairs)
    rows = sum(own.shape[0] for own, _ in pairs)
    tile = min(columns, 512)

    def kernel(*refs):
        w0_ref, w1_ref, o_ref = refs[2 * count :]
        start = 0
        for i in range(count):
            a_ref, b_ref = refs[2 * i], refs[2 * i + 1]
            here = slice(start, start + a_ref.shape[0])
            start = here.stop
            for c in range(0, columns, tile):
                cols = slice(c, c + tile)
                o_ref[here, cols] = (
                    dot(a_ref[...], w0_ref[:, cols]) + dot(b_ref[...], w1_ref[:, cols])
                ).astype(dtype)

    ins = [x for pair in pairs for x in pair] + [w0, w1]
    return call(kernel, ins, [shape((rows, columns), dtype)], 0, after)[0]


def add_rows(here, arrived, out, start):
    rows, columns = arrived.shape
    half = rows // 2

    def kernel(h_ref, a_ref, *refs):
        o_ref, sums, sems = refs[-3:]
        moves = []
        for i in range(2):
            part = slice(i * half, (i + 1) * half)
            place = slice(start + part.start, start + part.stop)
            sums[part, :] = (h_ref[place, :] + a_ref[part, :].astype(F32)).astype(BF16)
            moves.append(pltpu.make_async_copy(sums.at[part, :], o_ref.at[place, :], sems.at[i]))
            moves[-1].start()
        for move in moves:
            move.wait()

    ins, specs, aliases = [here, arrived], [VMEM, VMEM], {}
    if out is not None:
        ins, specs, aliases = ins + [out], specs + [ANY], {2: 0}
    return pl.pallas_call(
        kernel,
        in_specs=specs,
        out_specs=ANY,
        out_shape=shape(here.shape, BF16),
        input_output_aliases=aliases,
        scratch_shapes=[pltpu.VMEM((rows, columns), BF16), pltpu.SemaphoreType.DMA((2,))],
        compiler_params=pltpu.CompilerParams(vmem_limit_bytes=4 * 1024 * 1024),
        cost_estimate=pl.CostEstimate(flops=0, bytes_accessed=rows * columns * 8, transcendentals=0),
    )(*ins)


def body(tokens, log_decay, w_query, w_key, w_value, w_level, w_out):
    rows, shard = tokens.shape
    heads = log_decay.shape[1]
    head_size = w_out.shape[0] // heads
    level_count = w_level.shape[1] // heads
    seq_size = lax.axis_size("seq")
    seq_bits = seq_size.bit_length() - 1
    me = jnp.full((1,), lax.axis_index("tp"), jnp.int32)
    slab = jnp.full((1,), lax.axis_index("seq"), jnp.int32)

    def swap_tp(x, bit):
        return lax.ppermute(x, "tp", [(i, i ^ bit) for i in range(4)])

    def swap_seq(x, bit):
        return lax.ppermute(x, "seq", [(i, i ^ bit) for i in range(seq_size)])

    far = swap_tp(tokens, 2)
    near = swap_tp(tokens, 1)

    weights = (w_query, w_key, w_value, w_level.T)
    totals, ws, (drow, dcol, keep, total, span), blocks = begin(
        me, slab, tokens, near, log_decay.T, weights, w_out, head_size
    )
    w_here_own, w_here_send, w_far_own, w_far_send = blocks
    w_here, w_far = swap_tp(w_here_send, 1), swap_tp(w_far_send, 1)

    spans, factors, before = [span], [], None
    for b in range(seq_bits - 1):
        total, before, own, other, span = link(slab, b, total, swap_seq(total, 1 << b), before)
        spans.append(span)
        factors.append((own, other))

    wq, wkv, wkv_send, wl = ws
    wkv_near = swap_tp(wkv_send, 1)
    arrived = far
    for_near = partial(arrived, wkv_near, (total, w_far, w_here))
    from_near = swap_tp(for_near, 1)
    total_q, total_kv, total_l = totals
    total_kv = add_product(arrived, wkv, total_kv, (for_near,))
    k, v, state = project_state(total_kv, from_near, keep, head_size)
    total_q, total_l = project(me, 2, arrived, wq, wl, total_q, total_l, (k,))
    arrived_near = [swap_tp(x, 1) for x in split(arrived, 4, (total_l,))]

    earlier = []
    for b in range(seq_bits):
        other = swap_seq(state, 1 << b)
        earlier.append(other)
        if b < seq_bits - 1:
            after = () if b else (total_l,)
            state = combine(state, other, *factors[b], after)

    local, scaled = attend(
        me, 3, arrived_near, wq, wl, total_q, total_l, k, v, dcol, drow, spans, earlier[:-1], head_size, level_count
    )

    unit = rows // 8
    ends = (0, 2, 4, 6, 7, 8)
    cuts = [slice(start * unit, stop * unit) for start, stop in zip(ends, ends[1:])]
    pieces = finish(local, scaled, earlier[-1], cuts[:1], head_size)
    pieces += finish(local, scaled, earlier[-1], cuts[1:], head_size, pieces)
    pairs = [(x, swap_tp(x, 1)) for x in pieces]
    crossing = [out_block([pair], w_far_own, w_far, BF16) for pair in pairs]
    own_block = out_block(pairs, w_here_own, w_here, F32, (crossing[-1],))
    out = None
    for cut, x in zip(cuts, crossing):
        out = add_rows(own_block, swap_tp(x, 2), out, cut.start)
    return out


def solution(mesh):
    in_specs = (
        P("seq", "tp"),
        P("seq", "tp"),
        P(None, "tp"),
        P(None, "tp"),
        P(None, "tp"),
        P(None, "tp"),
        P("tp", None),
    )
    out_specs = P("seq", "tp")
    return jax.shard_map(body, mesh=mesh, in_specs=in_specs, out_specs=out_specs, check_vma=False)
```

```python
import functools

import jax
import jax.numpy as jnp
from jax import lax
from jax.experimental import pallas as pl
from jax.experimental.pallas import tpu as pltpu
from jax.sharding import PartitionSpec as P

BLOCK = 128
F32 = jnp.float32
BF16 = jnp.bfloat16
VMEM = pl.BlockSpec(memory_space=pltpu.VMEM)
SMEM = pl.BlockSpec(memory_space=pltpu.SMEM)
ANY = pl.BlockSpec(memory_space=pl.ANY)
HBM = pl.BlockSpec(memory_space=pltpu.HBM)


def dot(a, b):
    return jnp.dot(a, b, preferred_element_type=F32)


def dot_dims(a, b, left, right):
    return lax.dot_general(a, b, (((left,), (right,)), ((), ())), preferred_element_type=F32)


def shape(dims, dtype):
    return jax.ShapeDtypeStruct(dims, dtype)


def call(kernel, ins, outs, flops, after=(), smem=0, hbm=0, aliases=None, scratch=(), megabytes=8):
    count = len(ins)
    ins = list(ins)
    for i in range(smem, smem + hbm):
        ins[i] = pltpu.with_memory_space_constraint(ins[i], pltpu.HBM)

    def run(*refs):
        kernel(*refs[:count], *refs[count + len(after) :])

    nbytes = sum(x.size * x.dtype.itemsize for x in (*ins, *outs)) if flops else 0
    return pl.pallas_call(
        run,
        in_specs=[SMEM] * smem + [HBM] * hbm + [VMEM] * (count - smem - hbm) + [ANY] * len(after),
        out_specs=[VMEM] * len(outs),
        out_shape=list(outs),
        input_output_aliases=aliases or {},
        scratch_shapes=list(scratch),
        compiler_params=pltpu.CompilerParams(vmem_limit_bytes=megabytes * 1024 * 1024),
        cost_estimate=pl.CostEstimate(flops=flops, bytes_accessed=nbytes, transcendentals=0),
    )(*ins, *after)


def gate(x, *after):
    def run(*refs):
        pass

    return pl.pallas_call(
        run,
        in_specs=[ANY] * (1 + len(after)),
        out_specs=ANY,
        out_shape=shape(x.shape, x.dtype),
        input_output_aliases={0: 0},
        compiler_params=pltpu.CompilerParams(vmem_limit_bytes=1024 * 1024),
        cost_estimate=pl.CostEstimate(flops=0, bytes_accessed=0, transcendentals=0),
    )(x, *after)


def copies(pairs, sems):
    started = [pltpu.make_async_copy(src, dst, sems.at[i]) for i, (src, dst) in enumerate(pairs)]
    for copy in started:
        copy.start()
    return started


def upper_half(slab_ref, bit):
    return ((slab_ref[0] >> bit) & 1) == 1


def decays(slab_ref, x_ref, row_ref, col_ref, keep_ref, total_ref, span_ref):
    heads, rows = x_ref.shape
    head_size = total_ref.shape[1] // heads
    x = x_ref[...]
    x = jnp.concatenate([x, jnp.zeros((-heads % 8, rows), F32)], axis=0) if heads % 8 else x
    place = lax.broadcasted_iota(jnp.int32, x.shape, 1)
    shift = 1
    while shift < rows:
        x = x + jnp.where(place >= shift, pltpu.roll(x, shift, 1), 0.0)
        shift *= 2
    total = x[:, rows - 1 : rows]
    row_ref[...] = x[:heads]
    col_ref[...] = jnp.transpose(x)[:, :heads]
    keep_ref[...] = jnp.transpose(jnp.exp(total - x))[:, :heads]
    for h in range(heads):
        total_ref[:, h * head_size : (h + 1) * head_size] = jnp.broadcast_to(
            total[h : h + 1], (8, head_size)
        )
    span_ref[...] = jnp.full(span_ref.shape, jnp.where(upper_half(slab_ref, 0), 0.0, -jnp.inf), F32)


def link(slab, bit, total, other, before):
    def kernel(slab_ref, *refs):
        total_ref, other_ref = refs[:2]
        total_out, before_out, own_out, other_out, span_out = refs[-5:]
        upper = upper_half(slab_ref, bit)
        here, there = total_ref[...], other_ref[...]
        total_out[...] = here + there
        so_far = jnp.where(upper, there, 0.0)
        if before is not None:
            so_far = so_far + refs[2][...]
        before_out[...] = so_far
        own_out[...] = jnp.where(upper, 1.0, jnp.exp(there))
        other_out[...] = jnp.where(upper, jnp.exp(here), 1.0)
        span_out[...] = jnp.where(upper_half(slab_ref, bit + 1), so_far, -jnp.inf)

    ins = [slab, total, other] + ([] if before is None else [before])
    return call(kernel, ins, [shape(total.shape, F32)] * 5, 0, smem=1)


def combine(state, other, own_factor, other_factor, which, after):
    cols = slice(which * state.shape[1], (which + 1) * state.shape[1])

    def kernel(s_ref, o_ref, a_ref, b_ref, out_ref):
        out_ref[...] = (
            a_ref[0:1, cols] * s_ref[...].astype(F32) + b_ref[0:1, cols] * o_ref[...].astype(F32)
        ).astype(BF16)

    return call(kernel, [state, other, own_factor, other_factor], [shape(state.shape, BF16)], 0, after)[0]


def begin(me, slab, tokens, near, log_decay_rows, ws, w_out, head_size):
    wq, wk, wv, wl = ws
    rows, shard = near.shape
    q_width, kv_width = wq.shape[1], wk.shape[1]
    heads = log_decay_rows.shape[0]
    block = w_out.shape[1] // 4

    def kernel(me_ref, slab_ref, t_ref, wq_ref, wk_ref, wv_ref, wl_ref, wo_ref, near_ref, decay_ref, *refs):
        total_q, total_kv, total_l, far_q, far_kv, send_kv, all_l = refs[:7]
        decay_outs, blocks, (own_x, own_q, own_kv, sems) = refs[7:12], refs[12:16], refs[16:]

        def pairs(i, q_dst, kv_dst):
            here = pl.ds(pl.multiple_of((me_ref[0] ^ i) * shard, 128), shard)
            return [
                (wk_ref.at[here, :], kv_dst.at[:, :kv_width]),
                (wv_ref.at[here, :], kv_dst.at[:, kv_width:]),
                (wq_ref.at[here, :], q_dst),
            ]

        def columns(i):
            return wo_ref.at[:, pl.ds(pl.multiple_of((me_ref[0] ^ i) * block, 128), block)]

        moves = pairs(0, own_q.at[0], own_kv.at[0]) + [(wl_ref, all_l), (t_ref, own_x)]
        moves += pairs(1, own_q.at[1], own_kv.at[1])
        moves += pairs(2, far_q.at[0], far_kv) + pairs(3, far_q.at[1], send_kv)
        moves += [(columns(i), blocks[i]) for i in range(4)]
        started = copies(moves, sems)
        decays(slab_ref, decay_ref, *decay_outs)
        for copy in started[:5]:
            copy.wait()
        lanes = pl.ds(pl.multiple_of(me_ref[0] * shard, 128), shard)
        own = own_x[...]
        total_kv[...] = dot(own, own_kv[0])
        total_q[...] = dot(own, own_q[0])
        total_l[...] = dot_dims(own, all_l[:, lanes], 1, 1)
        for copy in started[5:8]:
            copy.wait()
        lanes = pl.ds(pl.multiple_of((me_ref[0] ^ 1) * shard, 128), shard)
        total_kv[...] += dot(near_ref[...], own_kv[1])
        total_q[...] += dot(near_ref[...], own_q[1])
        total_l[...] += dot_dims(near_ref[...], all_l[:, lanes], 1, 1)
        for copy in started[8:]:
            copy.wait()

    wide = shape((8, heads * head_size), F32)
    outs = [
        shape((rows, q_width), F32),
        shape((rows, 2 * kv_width), F32),
        shape((rows, wl.shape[0]), F32),
        shape((2, shard, q_width), BF16),
        shape((shard, 2 * kv_width), BF16),
        shape((shard, 2 * kv_width), BF16),
        shape(wl.shape, BF16),
        shape((heads, rows), F32),
        shape((rows, heads), F32),
        shape((rows, heads), F32),
        wide,
        wide,
    ] + [shape((w_out.shape[0], block), BF16)] * 4
    scratch = [
        pltpu.VMEM((rows, shard), BF16),
        pltpu.VMEM((2, shard, q_width), BF16),
        pltpu.VMEM((2, shard, 2 * kv_width), BF16),
        pltpu.SemaphoreType.DMA((18,)),
    ]
    ins = [me, slab, tokens, wq, wk, wv, wl, w_out, near, log_decay_rows]
    outs = call(kernel, ins, outs, 0, smem=2, hbm=6, scratch=scratch, megabytes=14)
    return outs[:3], outs[3:7], outs[7:12], outs[12:]


def add_levels(me_ref, place, x, wl_ref):
    shard = wl_ref.shape[1] // 4
    start = pl.multiple_of((me_ref[0] ^ place) * shard, 128)
    return dot_dims(x, wl_ref[:, pl.ds(start, shard)], 1, 1)


def project(me, place, x, wq, wkv, wl, totals, after=()):
    def kernel(me_ref, x_ref, q_ref, kv_ref, l_ref, *refs):
        ins, outs = refs[:3], refs[3:]
        outs[1][...] = ins[1][...] + dot(x_ref[...], kv_ref[...])
        outs[0][...] = ins[0][...] + dot(x_ref[...], q_ref[place - 2])
        outs[2][...] = ins[2][...] + add_levels(me_ref, place, x_ref[...], l_ref)

    outs = [shape(t.shape, F32) for t in totals]
    return call(kernel, [me, x, wq, wkv, wl, *totals], outs, 0, after, smem=1, aliases={5: 0, 6: 1, 7: 2})


def partial(x, w, after):
    def kernel(x_ref, w_ref, o_ref):
        o_ref[...] = dot(x_ref[...], w_ref[...]).astype(BF16)

    return call(kernel, [x, w], [shape((x.shape[0], w.shape[1]), BF16)], 0, after)[0]


def project_state(total_kv, from_near, keep, head_size):
    rows = total_kv.shape[0]
    heads = keep.shape[1]
    kv_width = total_kv.shape[1] // 2
    group = heads // (kv_width // head_size)

    half = heads // 2 * head_size

    def kernel(total_ref, near_ref, keep_ref, k_out, v_out, *s_outs):
        total = total_ref[...] + near_ref[...].astype(F32)
        keys = total[:, :kv_width].astype(BF16)
        values = total[:, kv_width:].astype(BF16)
        k_out[...] = keys
        v_out[...] = values
        for g in range(kv_width // head_size):
            cols = slice(g * head_size, (g + 1) * head_size)
            kf = keys[:, cols].astype(F32)
            weighted = jnp.concatenate(
                [(kf * keep_ref[:, h : h + 1]).astype(BF16) for h in range(g * group, (g + 1) * group)],
                axis=1,
            )
            states = dot_dims(values[:, cols], weighted, 0, 0).astype(BF16)
            for i in range(group):
                start = (g * group + i) * head_size
                s_outs[start // half][:, start % half : start % half + head_size] = states[
                    :, i * head_size : (i + 1) * head_size
                ]

    outs = [
        shape((rows, kv_width), BF16),
        shape((rows, kv_width), BF16),
        shape((head_size, half), BF16),
        shape((head_size, half), BF16),
    ]
    return call(kernel, [total_kv, from_near, keep], outs, 0)


def queries(me, place, x, wq, wl, total_q, total_l):
    def kernel(me_ref, x_ref, wq_ref, wl_ref, tq_ref, tl_ref, q_ref, l_ref):
        raw = tl_ref[...] + add_levels(me_ref, place, x_ref[...], wl_ref)
        l_ref[...] = jnp.maximum(raw, 0.0) + jnp.log1p(jnp.exp(-jnp.abs(raw)))
        q_ref[...] = (tq_ref[...] + dot(x_ref[...], wq_ref[place - 2])).astype(BF16)

    outs = [shape(total_q.shape, BF16), shape(total_l.shape, F32)]
    return call(kernel, [me, x, wq, wl, total_q, total_l], outs, 0, smem=1)


def column(ref, rows, place):
    return jnp.broadcast_to(ref[rows, place : place + 1], (BLOCK, BLOCK))


def attend(q, level, k, v, dcol, drow, which, head_size, level_count):
    rows, width = q.shape
    heads = width // head_size
    group = heads // (k.shape[1] // head_size)
    first = which * heads // 2

    def kernel(q_ref, l_ref, k_ref, v_ref, dcol_ref, drow_ref, o_ref):
        row_id = lax.broadcasted_iota(jnp.int32, (BLOCK, BLOCK), 0)
        col_id = lax.broadcasted_iota(jnp.int32, (BLOCK, BLOCK), 1)
        causal = row_id >= col_id
        for h in range(first, first + heads // 2):
            cols = slice(h * head_size, (h + 1) * head_size)
            kv = slice(h // group * head_size, (h // group + 1) * head_size)
            for i in range(rows // BLOCK):
                here = slice(i * BLOCK, (i + 1) * BLOCK)
                span = (i + 1) * BLOCK
                scores = dot_dims(q_ref[here, cols], k_ref[:span, kv], 1, 1)
                d_here = column(dcol_ref, here, h)
                weights = {}
                mixed = []
                for j in range(i + 1):
                    step = (i ^ j).bit_length()
                    if step not in weights:
                        weights[step] = column(l_ref, here, h * level_count + step)
                    there = slice(j * BLOCK, (j + 1) * BLOCK)
                    gap = d_here - drow_ref[h : h + 1, there]
                    if i == j:
                        gap = jnp.where(causal, gap, -jnp.inf)
                    mixed.append((weights[step] * jnp.exp(gap) * scores[:, there]).astype(BF16))
                mixing = mixed[0] if i == 0 else jnp.concatenate(mixed, axis=1)
                out = slice((h - first) * head_size, (h - first + 1) * head_size)
                o_ref[here, out] = dot(mixing, v_ref[:span, kv])

    ins = [q, level, k, v, dcol, drow]
    return call(kernel, ins, [shape((rows, width // 2), F32)], 0)[0]


def attend_earlier(locals_, q, level, dcol, spans, states, head_size, level_count):
    rows, width = q.shape
    bits = len(spans)
    half = width // 2
    own_levels = level_count - bits

    def kernel(a_ref, b_ref, q_ref, l_ref, dcol_ref, *refs):
        span_refs, state_refs = refs[:bits], refs[bits : bits + len(states)]
        outs = refs[-4:]
        for h in range(width // head_size):
            cols = slice(h * head_size, (h + 1) * head_size)
            which, at = divmod(h * head_size, half)
            out = slice(at, at + head_size)
            for i in range(rows // BLOCK):
                here = slice(i * BLOCK, (i + 1) * BLOCK)
                query = q_ref[here, cols].astype(F32)
                d_here = column(dcol_ref, here, h)
                total = (a_ref, b_ref)[which][here, out]
                for b in range(bits):
                    factor = column(l_ref, here, h * level_count + own_levels + b)
                    factor = factor * jnp.exp(d_here + span_refs[b][0:1, cols])
                    scaled = (query * factor).astype(BF16)
                    if b == bits - 1:
                        outs[2 + which][here, out] = scaled
                    else:
                        total = total + dot_dims(scaled, state_refs[2 * b + which][:, out], 1, 1)
                outs[which][here, out] = total

    ins = [*locals_, q, level, dcol, *spans, *states]
    outs = [shape((rows, half), F32)] * 2 + [shape((rows, half), BF16)] * 2
    outs = call(kernel, ins, outs, 0)
    return list(zip(outs[:2], outs[2:]))


def finish(local, scaled, state, cuts, head_size, flops, after=()):
    width = state.shape[1]

    def kernel(o_ref, q_ref, s_ref, *outs):
        for rows, n_ref in zip(cuts, outs):
            for c in range(0, width, head_size):
                cols = slice(c, c + head_size)
                total = o_ref[rows, cols] + dot_dims(q_ref[rows, cols], s_ref[:, cols], 1, 1)
                mean = jnp.mean(total * total, axis=-1, keepdims=True)
                n_ref[:, cols] = (total * lax.rsqrt(mean + 1e-05)).astype(BF16)

    outs = [shape((cut.stop - cut.start, width), BF16) for cut in cuts]
    return call(kernel, [local, scaled, state], outs, flops, after)


def out_block(first, second, places, w0, w1, dtype, after=()):
    columns = w1.shape[1]
    rows = sum(cut.stop - cut.start for _, cut in places)
    tile = min(columns, 512)

    def kernel(*refs):
        f_refs, s_refs = refs[: 2 * len(first)], refs[2 * len(first) : -3]
        w0_ref, w1_ref, o_ref = refs[-3:]
        start = 0
        for i, (which, cut) in enumerate(places):
            here = slice(start, start + cut.stop - cut.start)
            start = here.stop
            own = jnp.concatenate([f_refs[2 * which][cut, :], s_refs[2 * i][...]], axis=1)
            near = jnp.concatenate([f_refs[2 * which + 1][cut, :], s_refs[2 * i + 1][...]], axis=1)
            for c in range(0, columns, tile):
                cols = slice(c, c + tile)
                o_ref[here, cols] = (dot(own, w0_ref[:, cols]) + dot(near, w1_ref[:, cols])).astype(dtype)

    ins = [x for pair in (*first, *second) for x in pair] + [w0, w1]
    return call(kernel, ins, [shape((rows, columns), dtype)], 0, after)[0]


def add_rows(here, arrived, out, start, unit):
    rows, columns = arrived.shape

    def kernel(h_ref, a_ref, *refs):
        place = pl.ds(pl.multiple_of(start + pl.program_id(0) * unit, unit), unit)
        refs[-1][...] = (h_ref[place, :] + a_ref[...].astype(F32)).astype(BF16)

    block = (unit, columns)
    ins, specs, aliases = [here, arrived], [VMEM, pl.BlockSpec(block, lambda s: (s, 0))], {}
    if out is not None:
        ins, specs, aliases = ins + [out], specs + [ANY], {2: 0}
    return pl.pallas_call(
        kernel,
        grid=(rows // unit,),
        in_specs=specs,
        out_specs=pl.BlockSpec(block, lambda s: (start // unit + s, 0)),
        out_shape=shape(here.shape, BF16),
        input_output_aliases=aliases,
        compiler_params=pltpu.CompilerParams(vmem_limit_bytes=8 * 1024 * 1024),
        cost_estimate=pl.CostEstimate(flops=0, bytes_accessed=rows * columns * 8, transcendentals=0),
    )(*ins)


def body(tokens, log_decay, w_query, w_key, w_value, w_level, w_out):
    rows, shard = tokens.shape
    heads = log_decay.shape[1]
    head_size = w_out.shape[0] // heads
    level_count = w_level.shape[1] // heads
    seq_size = lax.axis_size("seq")
    seq_bits = seq_size.bit_length() - 1
    me = jnp.full((1,), lax.axis_index("tp"), jnp.int32)
    slab = jnp.full((1,), lax.axis_index("seq"), jnp.int32)

    def swap_tp(x, bit):
        return lax.ppermute(x, "tp", [(i, i ^ bit) for i in range(4)])

    def swap_seq(x, bit, both=True):
        return lax.ppermute(x, "seq", [(i, i ^ bit) for i in range(seq_size) if both or not i & bit])

    far = swap_tp(tokens, 2)
    near = swap_tp(tokens, 1)

    weights = (w_query, w_key, w_value, w_level.T)
    totals, ws, (drow, dcol, keep, total, span), blocks = begin(
        me, slab, tokens, near, log_decay.T, weights, w_out, head_size
    )
    w_here_own, w_here_send, w_far_own, w_far_send = blocks
    w_here, w_far = swap_tp(w_here_send, 1), swap_tp(w_far_send, 1)

    spans, factors, before = [span], [], None
    for b in range(seq_bits - 1):
        total, before, own, other, span = link(slab, b, total, swap_seq(total, 1 << b), before)
        spans.append(span)
        factors.append((own, other))

    wq, wkv, wkv_send, wl = ws
    wkv_near = swap_tp(wkv_send, 1)
    for_near = partial(far, wkv_near, (total, w_far, w_here))
    from_near = swap_tp(for_near, 1)
    totals = project(me, 2, far, wq, wkv, wl, totals, (for_near,))
    total_q, total_kv, total_l = totals
    far_near = swap_tp(gate(far, total_q, from_near), 1)
    k, v, *states = project_state(total_kv, from_near, keep, head_size)

    q, level = queries(me, 3, far_near, wq, wl, total_q, total_l)
    locals_ = [attend(q, level, k, v, dcol, drow, i, head_size, level_count) for i in range(2)]
    earlier = []
    for b in range(seq_bits):
        others = [swap_seq(state, 1 << b, b < seq_bits - 1 or i == 0) for i, state in enumerate(states)]
        earlier.append(others)
        if b < seq_bits - 1:
            afters = (locals_[b : b + 1], ())
            states = [
                combine(state, other, *factors[b], i, after)
                for i, (state, other, after) in enumerate(zip(states, others, afters))
            ]
    before_last = [state for others in earlier[:-1] for state in others]
    halves = attend_earlier(locals_, q, level, dcol, spans, before_last, head_size, level_count)

    unit = rows // 8
    ends = (0, 2, 4, 6, 7, 8)
    cuts = [slice(start * unit, stop * unit) for start, stop in zip(ends, ends[1:])]
    middle = rows // 2
    tops = finish(*halves[0], earlier[-1][0], [slice(0, middle), slice(middle, rows)], head_size, 10**8)
    first = [(x, swap_tp(x, 1)) for x in tops]
    second = finish(*halves[1], earlier[-1][1], cuts, head_size, 0, tops)
    second = [(x, swap_tp(x, 1)) for x in second]
    crossing = []
    for pair, cut in zip(second, cuts):
        i = cut.start // middle
        here = slice(cut.start - i * middle, cut.stop - i * middle)
        crossing.append(out_block([first[i]], [pair], [(0, here)], w_far_own, w_far, BF16))
    places = [(c.start // middle, slice(c.start % middle, c.start % middle + c.stop - c.start)) for c in cuts]
    own_block = out_block(first, second, places, w_here_own, w_here, F32, (crossing[-1],))
    out = None
    for cut, x in zip(cuts, crossing):
        out = add_rows(own_block, swap_tp(x, 2), out, cut.start, unit)
    return out


def solution(mesh):
    in_specs = (
        P("seq", "tp"),
        P("seq", "tp"),
        P(None, "tp"),
        P(None, "tp"),
        P(None, "tp"),
        P(None, "tp"),
        P("tp", None),
    )
    out_specs = P("seq", "tp")
    return jax.shard_map(body, mesh=mesh, in_specs=in_specs, out_specs=out_specs, check_vma=False)
```

```python
import functools

import jax
import jax.numpy as jnp
from jax import lax
from jax.experimental import pallas as pl
from jax.experimental.pallas import tpu as pltpu
from jax.sharding import PartitionSpec as P

BLOCK = 128
F32 = jnp.float32
BF16 = jnp.bfloat16
VMEM = pl.BlockSpec(memory_space=pltpu.VMEM)
SMEM = pl.BlockSpec(memory_space=pltpu.SMEM)
ANY = pl.BlockSpec(memory_space=pl.ANY)
HBM = pl.BlockSpec(memory_space=pltpu.HBM)


def dot(a, b):
    return jnp.dot(a, b, preferred_element_type=F32)


def dot_dims(a, b, left, right):
    return lax.dot_general(a, b, (((left,), (right,)), ((), ())), preferred_element_type=F32)


def shape(dims, dtype):
    return jax.ShapeDtypeStruct(dims, dtype)


def call(kernel, ins, outs, flops, after=(), smem=0, hbm=0, aliases=None, scratch=(), megabytes=8):
    count = len(ins)
    ins = list(ins)
    for i in range(smem, smem + hbm):
        ins[i] = pltpu.with_memory_space_constraint(ins[i], pltpu.HBM)

    def run(*refs):
        kernel(*refs[:count], *refs[count + len(after) :])

    nbytes = sum(x.size * x.dtype.itemsize for x in (*ins, *outs)) if flops else 0
    return pl.pallas_call(
        run,
        in_specs=[SMEM] * smem + [HBM] * hbm + [VMEM] * (count - smem - hbm) + [ANY] * len(after),
        out_specs=[VMEM] * len(outs),
        out_shape=list(outs),
        input_output_aliases=aliases or {},
        scratch_shapes=list(scratch),
        compiler_params=pltpu.CompilerParams(vmem_limit_bytes=megabytes * 1024 * 1024),
        cost_estimate=pl.CostEstimate(flops=flops, bytes_accessed=nbytes, transcendentals=0),
    )(*ins, *after)


def gate(x, *after):
    def run(*refs):
        pass

    return pl.pallas_call(
        run,
        in_specs=[ANY] * (1 + len(after)),
        out_specs=ANY,
        out_shape=shape(x.shape, x.dtype),
        input_output_aliases={0: 0},
        compiler_params=pltpu.CompilerParams(vmem_limit_bytes=1024 * 1024),
        cost_estimate=pl.CostEstimate(flops=0, bytes_accessed=0, transcendentals=0),
    )(x, *after)


def copies(pairs, sems):
    started = [pltpu.make_async_copy(src, dst, sems.at[i]) for i, (src, dst) in enumerate(pairs)]
    for copy in started:
        copy.start()
    return started


def upper_half(slab_ref, bit):
    return ((slab_ref[0] >> bit) & 1) == 1


def decays(slab_ref, x_ref, row_ref, col_ref, keep_ref, total_ref, span_ref):
    heads, rows = x_ref.shape
    head_size = total_ref.shape[1] // heads
    x = x_ref[...]
    x = jnp.concatenate([x, jnp.zeros((-heads % 8, rows), F32)], axis=0) if heads % 8 else x
    place = lax.broadcasted_iota(jnp.int32, x.shape, 1)
    shift = 1
    while shift < rows:
        x = x + jnp.where(place >= shift, pltpu.roll(x, shift, 1), 0.0)
        shift *= 2
    total = x[:, rows - 1 : rows]
    row_ref[...] = x[:heads]
    col_ref[...] = jnp.transpose(x)[:, :heads]
    keep_ref[...] = jnp.transpose(jnp.exp(total - x))[:, :heads]
    for h in range(heads):
        total_ref[:, h * head_size : (h + 1) * head_size] = jnp.broadcast_to(
            total[h : h + 1], (8, head_size)
        )
    span_ref[...] = jnp.full(span_ref.shape, jnp.where(upper_half(slab_ref, 0), 0.0, -jnp.inf), F32)


def link(slab, bit, total, other, before):
    def kernel(slab_ref, *refs):
        total_ref, other_ref = refs[:2]
        total_out, before_out, own_out, other_out, span_out = refs[-5:]
        upper = upper_half(slab_ref, bit)
        here, there = total_ref[...], other_ref[...]
        total_out[...] = here + there
        so_far = jnp.where(upper, there, 0.0)
        if before is not None:
            so_far = so_far + refs[2][...]
        before_out[...] = so_far
        own_out[...] = jnp.where(upper, 1.0, jnp.exp(there))
        other_out[...] = jnp.where(upper, jnp.exp(here), 1.0)
        span_out[...] = jnp.where(upper_half(slab_ref, bit + 1), so_far, -jnp.inf)

    ins = [slab, total, other] + ([] if before is None else [before])
    return call(kernel, ins, [shape(total.shape, F32)] * 5, 0, smem=1)


def combine(state, other, own_factor, other_factor, after):
    def kernel(s_ref, o_ref, a_ref, b_ref, out_ref):
        out_ref[...] = (
            a_ref[0:1, :] * s_ref[...].astype(F32) + b_ref[0:1, :] * o_ref[...].astype(F32)
        ).astype(BF16)

    return call(kernel, [state, other, own_factor, other_factor], [shape(state.shape, BF16)], 0, after)[0]


def begin(me, slab, tokens, near, log_decay_rows, ws, w_out, head_size):
    wq, wk, wv, wl = ws
    rows, shard = near.shape
    q_width, kv_width = wq.shape[1], wk.shape[1]
    heads = log_decay_rows.shape[0]
    block = w_out.shape[1] // 4

    def kernel(me_ref, slab_ref, t_ref, wq_ref, wk_ref, wv_ref, wl_ref, wo_ref, near_ref, decay_ref, *refs):
        total_q, total_kv, total_l, far_q, far_kv, send_kv, all_l = refs[:7]
        decay_outs, blocks, (own_x, own_q, own_kv, sems) = refs[7:12], refs[12:16], refs[16:]

        def pairs(i, q_dst, kv_dst):
            here = pl.ds(pl.multiple_of((me_ref[0] ^ i) * shard, 128), shard)
            return [
                (wk_ref.at[here, :], kv_dst.at[:, :kv_width]),
                (wv_ref.at[here, :], kv_dst.at[:, kv_width:]),
                (wq_ref.at[here, :], q_dst),
            ]

        def columns(i):
            return wo_ref.at[:, pl.ds(pl.multiple_of((me_ref[0] ^ i) * block, 128), block)]

        moves = pairs(0, own_q.at[0], own_kv.at[0]) + [(wl_ref, all_l), (t_ref, own_x)]
        moves += pairs(1, own_q.at[1], own_kv.at[1])
        moves += pairs(2, far_q.at[0], far_kv) + pairs(3, far_q.at[1], send_kv)
        moves += [(columns(i), blocks[i]) for i in range(4)]
        started = copies(moves, sems)
        decays(slab_ref, decay_ref, *decay_outs)
        for copy in started[:5]:
            copy.wait()
        lanes = pl.ds(pl.multiple_of(me_ref[0] * shard, 128), shard)
        own = own_x[...]
        total_kv[...] = dot(own, own_kv[0])
        total_q[...] = dot(own, own_q[0])
        total_l[...] = dot_dims(own, all_l[:, lanes], 1, 1)
        for copy in started[5:8]:
            copy.wait()
        lanes = pl.ds(pl.multiple_of((me_ref[0] ^ 1) * shard, 128), shard)
        total_kv[...] += dot(near_ref[...], own_kv[1])
        total_q[...] += dot(near_ref[...], own_q[1])
        total_l[...] += dot_dims(near_ref[...], all_l[:, lanes], 1, 1)
        for copy in started[8:]:
            copy.wait()

    wide = shape((8, heads * head_size), F32)
    outs = [
        shape((rows, q_width), F32),
        shape((rows, 2 * kv_width), F32),
        shape((rows, wl.shape[0]), F32),
        shape((2, shard, q_width), BF16),
        shape((shard, 2 * kv_width), BF16),
        shape((shard, 2 * kv_width), BF16),
        shape(wl.shape, BF16),
        shape((heads, rows), F32),
        shape((rows, heads), F32),
        shape((rows, heads), F32),
        wide,
        wide,
    ] + [shape((w_out.shape[0], block), BF16)] * 4
    scratch = [
        pltpu.VMEM((rows, shard), BF16),
        pltpu.VMEM((2, shard, q_width), BF16),
        pltpu.VMEM((2, shard, 2 * kv_width), BF16),
        pltpu.SemaphoreType.DMA((18,)),
    ]
    ins = [me, slab, tokens, wq, wk, wv, wl, w_out, near, log_decay_rows]
    outs = call(kernel, ins, outs, 0, smem=2, hbm=6, scratch=scratch, megabytes=14)
    return outs[:3], outs[3:7], outs[7:12], outs[12:]


def add_levels(me_ref, place, x, wl_ref):
    shard = wl_ref.shape[1] // 4
    start = pl.multiple_of((me_ref[0] ^ place) * shard, 128)
    return dot_dims(x, wl_ref[:, pl.ds(start, shard)], 1, 1)


def project(me, place, x, wq, wl, total_q, total_l, after):
    def kernel(me_ref, x_ref, wq_ref, wl_ref, q_ref, l_ref, q_out, l_out):
        q_out[...] = q_ref[...] + dot(x_ref[...], wq_ref[place - 2])
        l_out[...] = l_ref[...] + add_levels(me_ref, place, x_ref[...], wl_ref)

    outs = [shape(t.shape, F32) for t in (total_q, total_l)]
    flops = 2 * x.size * (total_q.shape[1] + total_l.shape[1])
    return call(kernel, [me, x, wq, wl, total_q, total_l], outs, flops, after, smem=1, aliases={4: 0, 5: 1})


def split(x, ways, after):
    rows, columns = x.shape
    part = columns // ways

    def kernel(x_ref, *outs):
        for i, o_ref in enumerate(outs):
            o_ref[...] = x_ref[:, i * part : (i + 1) * part]

    return call(kernel, [x], [shape((rows, part), x.dtype)] * ways, 0, after)


def partial(x, w, after):
    def kernel(x_ref, w_ref, o_ref):
        o_ref[...] = dot(x_ref[...], w_ref[...]).astype(BF16)

    return call(kernel, [x, w], [shape((x.shape[0], w.shape[1]), BF16)], 0, after)[0]


def add_product(x, w, total, after):
    def kernel(x_ref, w_ref, t_ref, o_ref):
        o_ref[...] = t_ref[...] + dot(x_ref[...], w_ref[...])

    return call(kernel, [x, w, total], [shape(total.shape, F32)], 0, after, aliases={2: 0})[0]


def project_state(total_kv, from_near, keep, head_size):
    rows = total_kv.shape[0]
    heads = keep.shape[1]
    kv_width = total_kv.shape[1] // 2
    group = heads // (kv_width // head_size)

    def kernel(total_ref, near_ref, keep_ref, k_out, v_out, s_out):
        total = total_ref[...] + near_ref[...].astype(F32)
        keys = total[:, :kv_width].astype(BF16)
        values = total[:, kv_width:].astype(BF16)
        k_out[...] = keys
        v_out[...] = values
        for g in range(kv_width // head_size):
            cols = slice(g * head_size, (g + 1) * head_size)
            kf = keys[:, cols].astype(F32)
            weighted = jnp.concatenate(
                [(kf * keep_ref[:, h : h + 1]).astype(BF16) for h in range(g * group, (g + 1) * group)],
                axis=1,
            )
            wide = slice(g * group * head_size, (g + 1) * group * head_size)
            s_out[:, wide] = dot_dims(values[:, cols], weighted, 0, 0).astype(BF16)

    outs = [
        shape((rows, kv_width), BF16),
        shape((rows, kv_width), BF16),
        shape((head_size, heads * head_size), BF16),
    ]
    return call(kernel, [total_kv, from_near, keep], outs, 0)


def attend(me, place, xs, wq, wl, total_q, total_l, k, v, dcol, drow, spans, states, head_size, level_count):
    rows, width = total_q.shape
    bits = len(spans)
    heads = width // head_size
    group = heads // (k.shape[1] // head_size)
    own_levels = level_count - bits

    def kernel(me_ref, *refs):
        x = jnp.concatenate([x_ref[...] for x_ref in refs[: len(xs)]], axis=1)
        refs = refs[len(xs) :]
        wq_ref, wl_ref, tq_ref, tl_ref, k_ref, v_ref, dcol_ref, drow_ref = refs[:8]
        span_refs, state_refs = refs[8 : 8 + bits], refs[8 + bits : 7 + 2 * bits]
        o_ref, s_ref, q_ref, l_ref = refs[-4:]
        raw = tl_ref[...] + add_levels(me_ref, place, x, wl_ref)
        l_ref[...] = jnp.maximum(raw, 0.0) + jnp.log1p(jnp.exp(-jnp.abs(raw)))
        q_ref[...] = (tq_ref[...] + dot(x, wq_ref[place - 2])).astype(BF16)
        row_id = lax.broadcasted_iota(jnp.int32, (BLOCK, BLOCK), 0)
        col_id = lax.broadcasted_iota(jnp.int32, (BLOCK, BLOCK), 1)
        causal = row_id >= col_id
        for h in range(heads):
            g = h // group
            cols = slice(h * head_size, (h + 1) * head_size)
            kv = slice(g * head_size, (g + 1) * head_size)
            for i in range(rows // BLOCK):
                here = slice(i * BLOCK, (i + 1) * BLOCK)
                span = (i + 1) * BLOCK
                query = q_ref[here, cols]
                scores = dot_dims(query, k_ref[:span, kv], 1, 1)
                d_here = jnp.broadcast_to(dcol_ref[here, h : h + 1], (BLOCK, BLOCK))

                def weight(level):
                    column = h * level_count + level
                    return jnp.broadcast_to(l_ref[here, column : column + 1], (BLOCK, BLOCK))

                weights = {}
                mixed = []
                for j in range(i + 1):
                    level = (i ^ j).bit_length()
                    if level not in weights:
                        weights[level] = weight(level)
                    there = slice(j * BLOCK, (j + 1) * BLOCK)
                    gap = d_here - drow_ref[h : h + 1, there]
                    if i == j:
                        gap = jnp.where(causal, gap, -jnp.inf)
                    mixed.append((weights[level] * jnp.exp(gap) * scores[:, there]).astype(BF16))
                mixing = mixed[0] if i == 0 else jnp.concatenate(mixed, axis=1)
                total = dot(mixing, v_ref[:span, kv])
                wide = query.astype(F32)
                for b in range(bits):
                    factor = weight(own_levels + b) * jnp.exp(d_here + span_refs[b][0:1, cols])
                    scaled = (wide * factor).astype(BF16)
                    if b == bits - 1:
                        s_ref[here, cols] = scaled
                    else:
                        total = total + dot_dims(scaled, state_refs[b][:, cols], 1, 1)
                o_ref[here, cols] = total

    ins = [me, *xs, wq, wl, total_q, total_l, k, v, dcol, drow, *spans, *states]
    wide = shape((rows, width), BF16)
    outs = [shape((rows, width), F32), wide, wide, shape(total_l.shape, F32)]
    flops = 2 * rows * wq.shape[1] * width + 4 * rows * rows * width
    return call(kernel, ins, outs, flops, smem=1)[:2]


def finish(local, scaled, state, cuts, head_size, after=()):
    width = local.shape[1]

    def kernel(o_ref, q_ref, s_ref, *outs):
        for rows, n_ref in zip(cuts, outs):
            for c in range(0, width, head_size):
                cols = slice(c, c + head_size)
                total = o_ref[rows, cols] + dot_dims(q_ref[rows, cols], s_ref[:, cols], 1, 1)
                mean = jnp.mean(total * total, axis=-1, keepdims=True)
                n_ref[:, cols] = (total * lax.rsqrt(mean + 1e-05)).astype(BF16)

    outs = [shape((cut.stop - cut.start, width), BF16) for cut in cuts]
    return call(kernel, [local, scaled, state], outs, 0, after)


def out_block(pairs, w0, w1, dtype, after=()):
    columns = w1.shape[1]
    count = len(pairs)
    rows = sum(own.shape[0] for own, _ in pairs)
    tile = min(columns, 512)

    def kernel(*refs):
        w0_ref, w1_ref, o_ref = refs[2 * count :]
        start = 0
        for i in range(count):
            a_ref, b_ref = refs[2 * i], refs[2 * i + 1]
            here = slice(start, start + a_ref.shape[0])
            start = here.stop
            for c in range(0, columns, tile):
                cols = slice(c, c + tile)
                o_ref[here, cols] = (
                    dot(a_ref[...], w0_ref[:, cols]) + dot(b_ref[...], w1_ref[:, cols])
                ).astype(dtype)

    ins = [x for pair in pairs for x in pair] + [w0, w1]
    return call(kernel, ins, [shape((rows, columns), dtype)], 0, after)[0]


def add_rows(here, arrived, out, start, unit):
    rows, columns = arrived.shape

    def kernel(h_ref, a_ref, *refs):
        place = pl.ds(pl.multiple_of(start + pl.program_id(0) * unit, unit), unit)
        refs[-1][...] = (h_ref[place, :] + a_ref[...].astype(F32)).astype(BF16)

    block = (unit, columns)
    ins, specs, aliases = [here, arrived], [VMEM, pl.BlockSpec(block, lambda s: (s, 0))], {}
    if out is not None:
        ins, specs, aliases = ins + [out], specs + [ANY], {2: 0}
    return pl.pallas_call(
        kernel,
        grid=(rows // unit,),
        in_specs=specs,
        out_specs=pl.BlockSpec(block, lambda s: (start // unit + s, 0)),
        out_shape=shape(here.shape, BF16),
        input_output_aliases=aliases,
        compiler_params=pltpu.CompilerParams(vmem_limit_bytes=8 * 1024 * 1024),
        cost_estimate=pl.CostEstimate(flops=0, bytes_accessed=rows * columns * 8, transcendentals=0),
    )(*ins)


def body(tokens, log_decay, w_query, w_key, w_value, w_level, w_out):
    rows, shard = tokens.shape
    heads = log_decay.shape[1]
    head_size = w_out.shape[0] // heads
    level_count = w_level.shape[1] // heads
    seq_size = lax.axis_size("seq")
    seq_bits = seq_size.bit_length() - 1
    me = jnp.full((1,), lax.axis_index("tp"), jnp.int32)
    slab = jnp.full((1,), lax.axis_index("seq"), jnp.int32)

    def swap_tp(x, bit):
        return lax.ppermute(x, "tp", [(i, i ^ bit) for i in range(4)])

    def swap_seq(x, bit):
        return lax.ppermute(x, "seq", [(i, i ^ bit) for i in range(seq_size)])

    far = swap_tp(tokens, 2)
    near = swap_tp(tokens, 1)

    weights = (w_query, w_key, w_value, w_level.T)
    totals, ws, (drow, dcol, keep, total, span), blocks = begin(
        me, slab, tokens, near, log_decay.T, weights, w_out, head_size
    )
    w_here_own, w_here_send, w_far_own, w_far_send = blocks
    w_here, w_far = swap_tp(w_here_send, 1), swap_tp(w_far_send, 1)

    spans, factors, before = [span], [], None
    for b in range(seq_bits - 1):
        total, before, own, other, span = link(slab, b, total, swap_seq(total, 1 << b), before)
        spans.append(span)
        factors.append((own, other))

    wq, wkv, wkv_send, wl = ws
    wkv_near = swap_tp(wkv_send, 1)
    arrived = far
    for_near = partial(arrived, wkv_near, (total, w_far, w_here))
    from_near = swap_tp(for_near, 1)
    total_q, total_kv, total_l = totals
    total_kv = add_product(arrived, wkv, total_kv, (for_near,))
    k, v, state = project_state(total_kv, from_near, keep, head_size)
    total_q, total_l = project(me, 2, arrived, wq, wl, total_q, total_l, (k,))
    arrived_near = [swap_tp(x, 1) for x in split(arrived, 4, (total_l,))]

    earlier = []
    for b in range(seq_bits):
        other = swap_seq(state, 1 << b)
        earlier.append(other)
        if b < seq_bits - 1:
            after = () if b else (total_l,)
            state = combine(state, other, *factors[b], after)

    local, scaled = attend(
        me, 3, arrived_near, wq, wl, total_q, total_l, k, v, dcol, drow, spans, earlier[:-1], head_size, level_count
    )

    unit = rows // 8
    ends = (0, 2, 4, 6, 7, 8)
    cuts = [slice(start * unit, stop * unit) for start, stop in zip(ends, ends[1:])]
    pieces = finish(local, scaled, earlier[-1], cuts[:1], head_size)
    pieces += finish(local, scaled, earlier[-1], cuts[1:], head_size, pieces)
    pairs = [(x, swap_tp(x, 1)) for x in pieces]
    crossing = [out_block([pair], w_far_own, w_far, BF16) for pair in pairs]
    own_block = out_block(pairs, w_here_own, w_here, F32, (crossing[-1],))
    out = None
    for cut, x in zip(cuts[:-1], crossing):
        out = add_rows(own_block, swap_tp(x, 2), out, cut.start, unit)
    last = own_block[cuts[-1]] + swap_tp(crossing[-1], 2).astype(F32)
    return lax.dynamic_update_slice_in_dim(out, last.astype(BF16), cuts[-1].start, 0)


def solution(mesh):
    in_specs = (
        P("seq", "tp"),
        P("seq", "tp"),
        P(None, "tp"),
        P(None, "tp"),
        P(None, "tp"),
        P(None, "tp"),
        P("tp", None),
    )
    out_specs = P("seq", "tp")
    return jax.shard_map(body, mesh=mesh, in_specs=in_specs, out_specs=out_specs, check_vma=False)
```

```python
import functools

import jax
import jax.numpy as jnp
from jax import lax
from jax.experimental import pallas as pl
from jax.experimental.pallas import tpu as pltpu
from jax.sharding import PartitionSpec as P

BLOCK = 128
F32 = jnp.float32
BF16 = jnp.bfloat16
VMEM = pl.BlockSpec(memory_space=pltpu.VMEM)
SMEM = pl.BlockSpec(memory_space=pltpu.SMEM)
ANY = pl.BlockSpec(memory_space=pl.ANY)
HBM = pl.BlockSpec(memory_space=pltpu.HBM)


def dot(a, b):
    return jnp.dot(a, b, preferred_element_type=F32)


def dot_dims(a, b, left, right):
    return lax.dot_general(a, b, (((left,), (right,)), ((), ())), preferred_element_type=F32)


def shape(dims, dtype):
    return jax.ShapeDtypeStruct(dims, dtype)


def call(kernel, ins, outs, flops, after=(), smem=0, hbm=0, aliases=None, scratch=(), megabytes=8):
    count = len(ins)
    ins = list(ins)
    for i in range(smem, smem + hbm):
        ins[i] = pltpu.with_memory_space_constraint(ins[i], pltpu.HBM)

    def run(*refs):
        kernel(*refs[:count], *refs[count + len(after) :])

    nbytes = sum(x.size * x.dtype.itemsize for x in (*ins, *outs)) if flops else 0
    return pl.pallas_call(
        run,
        in_specs=[SMEM] * smem + [HBM] * hbm + [VMEM] * (count - smem - hbm) + [ANY] * len(after),
        out_specs=[VMEM] * len(outs),
        out_shape=list(outs),
        input_output_aliases=aliases or {},
        scratch_shapes=list(scratch),
        compiler_params=pltpu.CompilerParams(vmem_limit_bytes=megabytes * 1024 * 1024),
        cost_estimate=pl.CostEstimate(flops=flops, bytes_accessed=nbytes, transcendentals=0),
    )(*ins, *after)


def copies(pairs, sems):
    started = [pltpu.make_async_copy(src, dst, sems.at[i]) for i, (src, dst) in enumerate(pairs)]
    for copy in started:
        copy.start()
    return started


def upper_half(slab_ref, bit):
    return ((slab_ref[0] >> bit) & 1) == 1


def decays(slab_ref, x_ref, row_ref, col_ref, keep_ref, total_ref, span_ref):
    heads, rows = x_ref.shape
    head_size = total_ref.shape[1] // heads
    x = x_ref[...]
    x = jnp.concatenate([x, jnp.zeros((-heads % 8, rows), F32)], axis=0) if heads % 8 else x
    place = lax.broadcasted_iota(jnp.int32, x.shape, 1)
    shift = 1
    while shift < rows:
        x = x + jnp.where(place >= shift, pltpu.roll(x, shift, 1), 0.0)
        shift *= 2
    total = x[:, rows - 1 : rows]
    row_ref[...] = x[:heads]
    col_ref[...] = jnp.transpose(x)[:, :heads]
    keep_ref[...] = jnp.transpose(jnp.exp(total - x))[:, :heads]
    for h in range(heads):
        total_ref[:, h * head_size : (h + 1) * head_size] = jnp.broadcast_to(
            total[h : h + 1], (8, head_size)
        )
    span_ref[...] = jnp.full(span_ref.shape, jnp.where(upper_half(slab_ref, 0), 0.0, -jnp.inf), F32)


def link(slab, bit, total, other, before):
    def kernel(slab_ref, *refs):
        total_ref, other_ref = refs[:2]
        total_out, before_out, own_out, other_out, span_out = refs[-5:]
        upper = upper_half(slab_ref, bit)
        here, there = total_ref[...], other_ref[...]
        total_out[...] = here + there
        so_far = jnp.where(upper, there, 0.0)
        if before is not None:
            so_far = so_far + refs[2][...]
        before_out[...] = so_far
        own_out[...] = jnp.where(upper, 1.0, jnp.exp(there))
        other_out[...] = jnp.where(upper, jnp.exp(here), 1.0)
        span_out[...] = jnp.where(upper_half(slab_ref, bit + 1), so_far, -jnp.inf)

    ins = [slab, total, other] + ([] if before is None else [before])
    return call(kernel, ins, [shape(total.shape, F32)] * 5, 0, smem=1)


def combine(state, other, own_factor, other_factor, after):
    def kernel(s_ref, o_ref, a_ref, b_ref, out_ref):
        out_ref[...] = (
            a_ref[0:1, :] * s_ref[...].astype(F32) + b_ref[0:1, :] * o_ref[...].astype(F32)
        ).astype(BF16)

    return call(kernel, [state, other, own_factor, other_factor], [shape(state.shape, BF16)], 0, after)[0]


def begin(me, slab, tokens, near, log_decay_rows, ws, w_out, head_size):
    wq, wk, wv, wl = ws
    rows, shard = near.shape
    q_width, kv_width = wq.shape[1], wk.shape[1]
    heads = log_decay_rows.shape[0]
    block = w_out.shape[1] // 4

    def kernel(me_ref, slab_ref, t_ref, wq_ref, wk_ref, wv_ref, wo_ref, wl_ref, near_ref, decay_ref, *refs):
        total_q, total_kv, total_l, far_q, far_kv, send_kv, all_l = refs[:7]
        decay_outs, blocks, (own_x, own_q, own_kv, sems) = refs[7:12], refs[12:16], refs[16:]

        def pairs(i, q_dst, kv_dst):
            here = pl.ds(pl.multiple_of((me_ref[0] ^ i) * shard, 128), shard)
            return [
                (wk_ref.at[here, :], kv_dst.at[:, :kv_width]),
                (wv_ref.at[here, :], kv_dst.at[:, kv_width:]),
                (wq_ref.at[here, :], q_dst),
            ]

        def columns(i):
            return wo_ref.at[:, pl.ds(pl.multiple_of((me_ref[0] ^ i) * block, 128), block)]

        moves = pairs(0, own_q.at[0], own_kv.at[0]) + [(t_ref, own_x)]
        moves += pairs(1, own_q.at[1], own_kv.at[1])
        moves += pairs(2, far_q.at[0], far_kv) + pairs(3, far_q.at[1], send_kv)
        moves += [(columns(i), blocks[i]) for i in range(4)]
        started = copies(moves, sems)
        decays(slab_ref, decay_ref, *decay_outs)
        all_l[...] = wl_ref[...]
        for copy in started[:4]:
            copy.wait()
        lanes = pl.ds(pl.multiple_of(me_ref[0] * shard, 128), shard)
        own = own_x[...]
        total_kv[...] = dot(own, own_kv[0])
        total_q[...] = dot(own, own_q[0])
        total_l[...] = dot_dims(own, all_l[:, lanes], 1, 1)
        for copy in started[4:7]:
            copy.wait()
        lanes = pl.ds(pl.multiple_of((me_ref[0] ^ 1) * shard, 128), shard)
        total_kv[...] += dot(near_ref[...], own_kv[1])
        total_q[...] += dot(near_ref[...], own_q[1])
        total_l[...] += dot_dims(near_ref[...], all_l[:, lanes], 1, 1)
        for copy in started[7:]:
            copy.wait()

    wide = shape((8, heads * head_size), F32)
    outs = [
        shape((rows, q_width), F32),
        shape((rows, 2 * kv_width), F32),
        shape((rows, wl.shape[0]), F32),
        shape((2, shard, q_width), BF16),
        shape((shard, 2 * kv_width), BF16),
        shape((shard, 2 * kv_width), BF16),
        shape(wl.shape, BF16),
        shape((heads, rows), F32),
        shape((rows, heads), F32),
        shape((rows, heads), F32),
        wide,
        wide,
    ] + [shape((w_out.shape[0], block), BF16)] * 4
    scratch = [
        pltpu.VMEM((rows, shard), BF16),
        pltpu.VMEM((2, shard, q_width), BF16),
        pltpu.VMEM((2, shard, 2 * kv_width), BF16),
        pltpu.SemaphoreType.DMA((17,)),
    ]
    ins = [me, slab, tokens, wq, wk, wv, w_out, wl, near, log_decay_rows]
    outs = call(kernel, ins, outs, 0, smem=2, hbm=5, scratch=scratch, megabytes=14)
    return outs[:3], outs[3:7], outs[7:12], outs[12:]


def add_levels(me_ref, place, x, wl_ref):
    shard = wl_ref.shape[1] // 4
    start = pl.multiple_of((me_ref[0] ^ place) * shard, 128)
    return dot_dims(x, wl_ref[:, pl.ds(start, shard)], 1, 1)


def project(me, place, x, wq, wl, total_q, total_l, after):
    def kernel(me_ref, x_ref, wq_ref, wl_ref, q_ref, l_ref, q_out, l_out):
        q_out[...] = q_ref[...] + dot(x_ref[...], wq_ref[place - 2])
        l_out[...] = l_ref[...] + add_levels(me_ref, place, x_ref[...], wl_ref)

    outs = [shape(t.shape, F32) for t in (total_q, total_l)]
    flops = 2 * x.size * (total_q.shape[1] + total_l.shape[1])
    return call(kernel, [me, x, wq, wl, total_q, total_l], outs, flops, after, smem=1, aliases={4: 0, 5: 1})


def split(x, ways, after):
    rows, columns = x.shape
    part = columns // ways

    def kernel(x_ref, *outs):
        for i, o_ref in enumerate(outs):
            o_ref[...] = x_ref[:, i * part : (i + 1) * part]

    return call(kernel, [x], [shape((rows, part), x.dtype)] * ways, 0, after)


def partial(x, w, after):
    def kernel(x_ref, w_ref, o_ref):
        o_ref[...] = dot(x_ref[...], w_ref[...]).astype(BF16)

    return call(kernel, [x, w], [shape((x.shape[0], w.shape[1]), BF16)], 0, after)[0]


def add_product(x, w, total, after):
    def kernel(x_ref, w_ref, t_ref, o_ref):
        o_ref[...] = t_ref[...] + dot(x_ref[...], w_ref[...])

    return call(kernel, [x, w, total], [shape(total.shape, F32)], 0, after, aliases={2: 0})[0]


def project_state(total_kv, from_near, keep, head_size):
    rows = total_kv.shape[0]
    heads = keep.shape[1]
    kv_width = total_kv.shape[1] // 2
    group = heads // (kv_width // head_size)

    def kernel(total_ref, near_ref, keep_ref, k_out, v_out, s_out):
        total = total_ref[...] + near_ref[...].astype(F32)
        keys = total[:, :kv_width].astype(BF16)
        values = total[:, kv_width:].astype(BF16)
        k_out[...] = keys
        v_out[...] = values
        for g in range(kv_width // head_size):
            cols = slice(g * head_size, (g + 1) * head_size)
            kf = keys[:, cols].astype(F32)
            weighted = jnp.concatenate(
                [(kf * keep_ref[:, h : h + 1]).astype(BF16) for h in range(g * group, (g + 1) * group)],
                axis=1,
            )
            wide = slice(g * group * head_size, (g + 1) * group * head_size)
            s_out[:, wide] = dot_dims(values[:, cols], weighted, 0, 0).astype(BF16)

    outs = [
        shape((rows, kv_width), BF16),
        shape((rows, kv_width), BF16),
        shape((head_size, heads * head_size), BF16),
    ]
    return call(kernel, [total_kv, from_near, keep], outs, 0)


def attend(me, place, xs, wq, wl, total_q, total_l, k, v, dcol, drow, spans, states, head_size, level_count):
    rows, width = total_q.shape
    bits = len(spans)
    heads = width // head_size
    group = heads // (k.shape[1] // head_size)
    own_levels = level_count - bits

    def kernel(me_ref, *refs):
        x = jnp.concatenate([x_ref[...] for x_ref in refs[: len(xs)]], axis=1)
        refs = refs[len(xs) :]
        wq_ref, wl_ref, tq_ref, tl_ref, k_ref, v_ref, dcol_ref, drow_ref = refs[:8]
        span_refs, state_refs = refs[8 : 8 + bits], refs[8 + bits : 7 + 2 * bits]
        o_ref, s_ref, q_ref, l_ref = refs[-4:]
        raw = tl_ref[...] + add_levels(me_ref, place, x, wl_ref)
        l_ref[...] = jnp.maximum(raw, 0.0) + jnp.log1p(jnp.exp(-jnp.abs(raw)))
        q_ref[...] = (tq_ref[...] + dot(x, wq_ref[place - 2])).astype(BF16)
        row_id = lax.broadcasted_iota(jnp.int32, (BLOCK, BLOCK), 0)
        col_id = lax.broadcasted_iota(jnp.int32, (BLOCK, BLOCK), 1)
        causal = row_id >= col_id
        for h in range(heads):
            g = h // group
            cols = slice(h * head_size, (h + 1) * head_size)
            kv = slice(g * head_size, (g + 1) * head_size)
            for i in range(rows // BLOCK):
                here = slice(i * BLOCK, (i + 1) * BLOCK)
                span = (i + 1) * BLOCK
                query = q_ref[here, cols]
                scores = dot_dims(query, k_ref[:span, kv], 1, 1)
                d_here = jnp.broadcast_to(dcol_ref[here, h : h + 1], (BLOCK, BLOCK))

                def weight(level):
                    column = h * level_count + level
                    return jnp.broadcast_to(l_ref[here, column : column + 1], (BLOCK, BLOCK))

                weights = {}
                mixed = []
                for j in range(i + 1):
                    level = (i ^ j).bit_length()
                    if level not in weights:
                        weights[level] = weight(level)
                    there = slice(j * BLOCK, (j + 1) * BLOCK)
                    gap = d_here - drow_ref[h : h + 1, there]
                    if i == j:
                        gap = jnp.where(causal, gap, -jnp.inf)
                    mixed.append((weights[level] * jnp.exp(gap) * scores[:, there]).astype(BF16))
                mixing = mixed[0] if i == 0 else jnp.concatenate(mixed, axis=1)
                total = dot(mixing, v_ref[:span, kv])
                wide = query.astype(F32)
                for b in range(bits):
                    factor = weight(own_levels + b) * jnp.exp(d_here + span_refs[b][0:1, cols])
                    scaled = (wide * factor).astype(BF16)
                    if b == bits - 1:
                        s_ref[here, cols] = scaled
                    else:
                        total = total + dot_dims(scaled, state_refs[b][:, cols], 1, 1)
                o_ref[here, cols] = total

    ins = [me, *xs, wq, wl, total_q, total_l, k, v, dcol, drow, *spans, *states]
    wide = shape((rows, width), BF16)
    outs = [shape((rows, width), F32), wide, wide, shape(total_l.shape, F32)]
    flops = 2 * rows * wq.shape[1] * width + 4 * rows * rows * width
    return call(kernel, ins, outs, flops, smem=1)[:2]


def finish(local, scaled, state, cuts, head_size, after=()):
    width = local.shape[1]

    def kernel(o_ref, q_ref, s_ref, *outs):
        for rows, n_ref in zip(cuts, outs):
            for c in range(0, width, head_size):
                cols = slice(c, c + head_size)
                total = o_ref[rows, cols] + dot_dims(q_ref[rows, cols], s_ref[:, cols], 1, 1)
                mean = jnp.mean(total * total, axis=-1, keepdims=True)
                n_ref[:, cols] = (total * lax.rsqrt(mean + 1e-05)).astype(BF16)

    outs = [shape((cut.stop - cut.start, width), BF16) for cut in cuts]
    return call(kernel, [local, scaled, state], outs, 0, after)


def out_block(pairs, w0, w1, dtype, after=()):
    columns = w1.shape[1]
    count = len(pairs)
    rows = sum(own.shape[0] for own, _ in pairs)
    tile = min(columns, 512)

    def kernel(*refs):
        w0_ref, w1_ref, o_ref = refs[2 * count :]
        start = 0
        for i in range(count):
            a_ref, b_ref = refs[2 * i], refs[2 * i + 1]
            here = slice(start, start + a_ref.shape[0])
            start = here.stop
            for c in range(0, columns, tile):
                cols = slice(c, c + tile)
                o_ref[here, cols] = (
                    dot(a_ref[...], w0_ref[:, cols]) + dot(b_ref[...], w1_ref[:, cols])
                ).astype(dtype)

    ins = [x for pair in pairs for x in pair] + [w0, w1]
    return call(kernel, ins, [shape((rows, columns), dtype)], 0, after)[0]


def add_rows(here, arrived, out, start, unit):
    rows, columns = arrived.shape

    def kernel(h_ref, a_ref, *refs):
        place = pl.ds(pl.multiple_of(start + pl.program_id(0) * unit, unit), unit)
        refs[-1][...] = (h_ref[place, :] + a_ref[...].astype(F32)).astype(BF16)

    block = (unit, columns)
    ins, specs, aliases = [here, arrived], [VMEM, pl.BlockSpec(block, lambda s: (s, 0))], {}
    if out is not None:
        ins, specs, aliases = ins + [out], specs + [ANY], {2: 0}
    return pl.pallas_call(
        kernel,
        grid=(rows // unit,),
        in_specs=specs,
        out_specs=pl.BlockSpec(block, lambda s: (start // unit + s, 0)),
        out_shape=shape(here.shape, BF16),
        input_output_aliases=aliases,
        compiler_params=pltpu.CompilerParams(vmem_limit_bytes=8 * 1024 * 1024),
        cost_estimate=pl.CostEstimate(flops=0, bytes_accessed=rows * columns * 8, transcendentals=0),
    )(*ins)


def body(tokens, log_decay, w_query, w_key, w_value, w_level, w_out):
    rows, shard = tokens.shape
    heads = log_decay.shape[1]
    head_size = w_out.shape[0] // heads
    level_count = w_level.shape[1] // heads
    seq_size = lax.axis_size("seq")
    seq_bits = seq_size.bit_length() - 1
    me = jnp.full((1,), lax.axis_index("tp"), jnp.int32)
    slab = jnp.full((1,), lax.axis_index("seq"), jnp.int32)

    def swap_tp(x, bit):
        return lax.ppermute(x, "tp", [(i, i ^ bit) for i in range(4)])

    def swap_seq(x, bit):
        return lax.ppermute(x, "seq", [(i, i ^ bit) for i in range(seq_size)])

    far = swap_tp(tokens, 2)
    near = swap_tp(tokens, 1)

    weights = (w_query, w_key, w_value, w_level.T)
    totals, ws, (drow, dcol, keep, total, span), blocks = begin(
        me, slab, tokens, near, log_decay.T, weights, w_out, head_size
    )
    w_here_own, w_here_send, w_far_own, w_far_send = blocks
    w_here, w_far = swap_tp(w_here_send, 1), swap_tp(w_far_send, 1)

    spans, factors, before = [span], [], None
    for b in range(seq_bits - 1):
        total, before, own, other, span = link(slab, b, total, swap_seq(total, 1 << b), before)
        spans.append(span)
        factors.append((own, other))

    wq, wkv, wkv_send, wl = ws
    wkv_near = swap_tp(wkv_send, 1)
    arrived = far
    for_near = partial(arrived, wkv_near, (total, w_far, w_here))
    from_near = swap_tp(for_near, 1)
    total_q, total_kv, total_l = totals
    total_kv = add_product(arrived, wkv, total_kv, (for_near,))
    k, v, state = project_state(total_kv, from_near, keep, head_size)
    total_q, total_l = project(me, 2, arrived, wq, wl, total_q, total_l, (k,))
    arrived_near = [swap_tp(x, 1) for x in split(arrived, 4, (total_l,))]

    earlier = []
    for b in range(seq_bits):
        other = swap_seq(state, 1 << b)
        earlier.append(other)
        if b < seq_bits - 1:
            after = () if b else (total_l,)
            state = combine(state, other, *factors[b], after)

    local, scaled = attend(
        me, 3, arrived_near, wq, wl, total_q, total_l, k, v, dcol, drow, spans, earlier[:-1], head_size, level_count
    )

    unit = rows // 8
    ends = (0, 2, 4, 6, 7, 8)
    cuts = [slice(start * unit, stop * unit) for start, stop in zip(ends, ends[1:])]
    pieces = finish(local, scaled, earlier[-1], cuts[:1], head_size)
    pieces += finish(local, scaled, earlier[-1], cuts[1:], head_size, pieces)
    pairs = [(x, swap_tp(x, 1)) for x in pieces]
    crossing = [out_block([pair], w_far_own, w_far, BF16) for pair in pairs]
    own_block = out_block(pairs, w_here_own, w_here, F32, (crossing[-1],))
    out = None
    for cut, x in zip(cuts[:-1], crossing):
        out = add_rows(own_block, swap_tp(x, 2), out, cut.start, unit)
    last = own_block[cuts[-1]] + swap_tp(crossing[-1], 2).astype(F32)
    return lax.dynamic_update_slice_in_dim(out, last.astype(BF16), cuts[-1].start, 0)


def solution(mesh):
    in_specs = (
        P("seq", "tp"),
        P("seq", "tp"),
        P(None, "tp"),
        P(None, "tp"),
        P(None, "tp"),
        P(None, "tp"),
        P("tp", None),
    )
    out_specs = P("seq", "tp")
    return jax.shard_map(body, mesh=mesh, in_specs=in_specs, out_specs=out_specs, check_vma=False)
```

```python
import functools

import jax
import jax.numpy as jnp
from jax import lax
from jax.experimental import pallas as pl
from jax.experimental.pallas import tpu as pltpu
from jax.sharding import PartitionSpec as P

BLOCK = 128
F32 = jnp.float32
BF16 = jnp.bfloat16
VMEM = pl.BlockSpec(memory_space=pltpu.VMEM)
SMEM = pl.BlockSpec(memory_space=pltpu.SMEM)
ANY = pl.BlockSpec(memory_space=pl.ANY)
HBM = pl.BlockSpec(memory_space=pltpu.HBM)


def dot(a, b):
    return jnp.dot(a, b, preferred_element_type=F32)


def dot_dims(a, b, left, right):
    return lax.dot_general(a, b, (((left,), (right,)), ((), ())), preferred_element_type=F32)


def shape(dims, dtype):
    return jax.ShapeDtypeStruct(dims, dtype)


def call(kernel, ins, outs, flops, after=(), smem=0, hbm=0, aliases=None, scratch=(), megabytes=8):
    count = len(ins)
    ins = list(ins)
    for i in range(smem, smem + hbm):
        ins[i] = pltpu.with_memory_space_constraint(ins[i], pltpu.HBM)

    def run(*refs):
        kernel(*refs[:count], *refs[count + len(after) :])

    nbytes = sum(x.size * x.dtype.itemsize for x in (*ins, *outs)) if flops else 0
    return pl.pallas_call(
        run,
        in_specs=[SMEM] * smem + [HBM] * hbm + [VMEM] * (count - smem - hbm) + [ANY] * len(after),
        out_specs=[VMEM] * len(outs),
        out_shape=list(outs),
        input_output_aliases=aliases or {},
        scratch_shapes=list(scratch),
        compiler_params=pltpu.CompilerParams(vmem_limit_bytes=megabytes * 1024 * 1024),
        cost_estimate=pl.CostEstimate(flops=flops, bytes_accessed=nbytes, transcendentals=0),
    )(*ins, *after)


def gate(x, *after):
    def run(*refs):
        pass

    return pl.pallas_call(
        run,
        in_specs=[ANY] * (1 + len(after)),
        out_specs=ANY,
        out_shape=shape(x.shape, x.dtype),
        input_output_aliases={0: 0},
        compiler_params=pltpu.CompilerParams(vmem_limit_bytes=1024 * 1024),
        cost_estimate=pl.CostEstimate(flops=0, bytes_accessed=0, transcendentals=0),
    )(x, *after)


def copies(pairs, sems):
    started = [pltpu.make_async_copy(src, dst, sems.at[i]) for i, (src, dst) in enumerate(pairs)]
    for copy in started:
        copy.start()
    return started


def upper_half(slab_ref, bit):
    return ((slab_ref[0] >> bit) & 1) == 1


def decays(slab_ref, x_ref, row_ref, col_ref, keep_ref, total_ref, span_ref):
    heads, rows = x_ref.shape
    head_size = total_ref.shape[1] // heads
    x = x_ref[...]
    x = jnp.concatenate([x, jnp.zeros((-heads % 8, rows), F32)], axis=0) if heads % 8 else x
    place = lax.broadcasted_iota(jnp.int32, x.shape, 1)
    shift = 1
    while shift < rows:
        x = x + jnp.where(place >= shift, pltpu.roll(x, shift, 1), 0.0)
        shift *= 2
    total = x[:, rows - 1 : rows]
    row_ref[...] = x[:heads]
    col_ref[...] = jnp.transpose(x)[:, :heads]
    keep_ref[...] = jnp.transpose(jnp.exp(total - x))[:, :heads]
    for h in range(heads):
        total_ref[:, h * head_size : (h + 1) * head_size] = jnp.broadcast_to(
            total[h : h + 1], (8, head_size)
        )
    span_ref[...] = jnp.full(span_ref.shape, jnp.where(upper_half(slab_ref, 0), 0.0, -jnp.inf), F32)


def link(slab, bit, total, other, before):
    def kernel(slab_ref, *refs):
        total_ref, other_ref = refs[:2]
        total_out, before_out, own_out, other_out, span_out = refs[-5:]
        upper = upper_half(slab_ref, bit)
        here, there = total_ref[...], other_ref[...]
        total_out[...] = here + there
        so_far = jnp.where(upper, there, 0.0)
        if before is not None:
            so_far = so_far + refs[2][...]
        before_out[...] = so_far
        own_out[...] = jnp.where(upper, 1.0, jnp.exp(there))
        other_out[...] = jnp.where(upper, jnp.exp(here), 1.0)
        span_out[...] = jnp.where(upper_half(slab_ref, bit + 1), so_far, -jnp.inf)

    ins = [slab, total, other] + ([] if before is None else [before])
    return call(kernel, ins, [shape(total.shape, F32)] * 5, 0, smem=1)


def combine(state, other, own_factor, other_factor):
    def kernel(s_ref, o_ref, a_ref, b_ref, out_ref):
        out_ref[...] = (
            a_ref[0:1, :] * s_ref[...].astype(F32) + b_ref[0:1, :] * o_ref[...].astype(F32)
        ).astype(BF16)

    return call(kernel, [state, other, own_factor, other_factor], [shape(state.shape, BF16)], 0)[0]


def begin(me, slab, tokens, near, log_decay_rows, ws, w_out, head_size):
    wq, wk, wv, wl = ws
    rows, shard = near.shape
    q_width, kv_width = wq.shape[1], wk.shape[1]
    heads = log_decay_rows.shape[0]
    block = w_out.shape[1] // 4

    def kernel(me_ref, slab_ref, t_ref, wq_ref, wk_ref, wv_ref, wo_ref, wl_ref, near_ref, decay_ref, *refs):
        total_q, total_kv, total_l, far_q, far_kv, send_kv, all_l = refs[:7]
        decay_outs, blocks, (own_x, own_q, own_kv, sems) = refs[7:12], refs[12:16], refs[16:]

        def pairs(i, q_dst, kv_dst):
            here = pl.ds(pl.multiple_of((me_ref[0] ^ i) * shard, 128), shard)
            return [
                (wk_ref.at[here, :], kv_dst.at[:, :kv_width]),
                (wv_ref.at[here, :], kv_dst.at[:, kv_width:]),
                (wq_ref.at[here, :], q_dst),
            ]

        def columns(i):
            return wo_ref.at[:, pl.ds(pl.multiple_of((me_ref[0] ^ i) * block, 128), block)]

        moves = pairs(0, own_q.at[0], own_kv.at[0]) + [(t_ref, own_x)]
        moves += pairs(1, own_q.at[1], own_kv.at[1])
        moves += pairs(2, far_q.at[0], far_kv) + pairs(3, far_q.at[1], send_kv)
        moves += [(columns(i), blocks[i]) for i in range(4)]
        started = copies(moves, sems)
        decays(slab_ref, decay_ref, *decay_outs)
        all_l[...] = wl_ref[...]
        for copy in started[:4]:
            copy.wait()
        lanes = pl.ds(pl.multiple_of(me_ref[0] * shard, 128), shard)
        own = own_x[...]
        total_kv[...] = dot(own, own_kv[0])
        total_q[...] = dot(own, own_q[0])
        total_l[...] = dot_dims(own, all_l[:, lanes], 1, 1)
        for copy in started[4:7]:
            copy.wait()
        lanes = pl.ds(pl.multiple_of((me_ref[0] ^ 1) * shard, 128), shard)
        total_kv[...] += dot(near_ref[...], own_kv[1])
        total_q[...] += dot(near_ref[...], own_q[1])
        total_l[...] += dot_dims(near_ref[...], all_l[:, lanes], 1, 1)
        for copy in started[7:]:
            copy.wait()

    wide = shape((8, heads * head_size), F32)
    outs = [
        shape((rows, q_width), F32),
        shape((rows, 2 * kv_width), F32),
        shape((rows, wl.shape[0]), F32),
        shape((2, shard, q_width), BF16),
        shape((shard, 2 * kv_width), BF16),
        shape((shard, 2 * kv_width), BF16),
        shape(wl.shape, BF16),
        shape((heads, rows), F32),
        shape((rows, heads), F32),
        shape((rows, heads), F32),
        wide,
        wide,
    ] + [shape((w_out.shape[0], block), BF16)] * 4
    scratch = [
        pltpu.VMEM((rows, shard), BF16),
        pltpu.VMEM((2, shard, q_width), BF16),
        pltpu.VMEM((2, shard, 2 * kv_width), BF16),
        pltpu.SemaphoreType.DMA((17,)),
    ]
    ins = [me, slab, tokens, wq, wk, wv, w_out, wl, near, log_decay_rows]
    outs = call(kernel, ins, outs, 0, smem=2, hbm=5, scratch=scratch, megabytes=14)
    return outs[:3], outs[3:7], outs[7:12], outs[12:]


def add_levels(me_ref, place, x, wl_ref):
    shard = wl_ref.shape[1] // 4
    start = pl.multiple_of((me_ref[0] ^ place) * shard, 128)
    return dot_dims(x, wl_ref[:, pl.ds(start, shard)], 1, 1)


def project(me, place, x, wq, wkv, wl, totals, after=()):
    def kernel(me_ref, x_ref, q_ref, kv_ref, l_ref, *refs):
        ins, outs = refs[:3], refs[3:]
        outs[1][...] = ins[1][...] + dot(x_ref[...], kv_ref[...])
        outs[0][...] = ins[0][...] + dot(x_ref[...], q_ref[place - 2])
        outs[2][...] = ins[2][...] + add_levels(me_ref, place, x_ref[...], l_ref)

    outs = [shape(t.shape, F32) for t in totals]
    return call(kernel, [me, x, wq, wkv, wl, *totals], outs, 0, after, smem=1, aliases={5: 0, 6: 1, 7: 2})


def partial(x, w, after):
    def kernel(x_ref, w_ref, o_ref):
        o_ref[...] = dot(x_ref[...], w_ref[...]).astype(BF16)

    return call(kernel, [x, w], [shape((x.shape[0], w.shape[1]), BF16)], 0, after)[0]


def project_state(total_kv, from_near, keep, head_size):
    rows = total_kv.shape[0]
    heads = keep.shape[1]
    kv_width = total_kv.shape[1] // 2
    group = heads // (kv_width // head_size)

    def kernel(total_ref, near_ref, keep_ref, k_out, v_out, s_out):
        total = total_ref[...] + near_ref[...].astype(F32)
        keys = total[:, :kv_width].astype(BF16)
        values = total[:, kv_width:].astype(BF16)
        k_out[...] = keys
        v_out[...] = values
        for g in range(kv_width // head_size):
            cols = slice(g * head_size, (g + 1) * head_size)
            kf = keys[:, cols].astype(F32)
            weighted = jnp.concatenate(
                [(kf * keep_ref[:, h : h + 1]).astype(BF16) for h in range(g * group, (g + 1) * group)],
                axis=1,
            )
            wide = slice(g * group * head_size, (g + 1) * group * head_size)
            s_out[:, wide] = dot_dims(values[:, cols], weighted, 0, 0).astype(BF16)

    outs = [
        shape((rows, kv_width), BF16),
        shape((rows, kv_width), BF16),
        shape((head_size, heads * head_size), BF16),
    ]
    return call(kernel, [total_kv, from_near, keep], outs, 0)


def attend(me, place, xs, wq, wl, total_q, total_l, k, v, dcol, drow, spans, states, head_size, level_count):
    rows, width = total_q.shape
    bits = len(spans)
    heads = width // head_size
    group = heads // (k.shape[1] // head_size)
    own_levels = level_count - bits

    def kernel(me_ref, *refs):
        x = jnp.concatenate([x_ref[...] for x_ref in refs[: len(xs)]], axis=1)
        refs = refs[len(xs) :]
        wq_ref, wl_ref, tq_ref, tl_ref, k_ref, v_ref, dcol_ref, drow_ref = refs[:8]
        span_refs, state_refs = refs[8 : 8 + bits], refs[8 + bits : 7 + 2 * bits]
        o_ref, s_ref, q_ref, l_ref = refs[-4:]
        raw = tl_ref[...] + add_levels(me_ref, place, x, wl_ref)
        l_ref[...] = jnp.maximum(raw, 0.0) + jnp.log1p(jnp.exp(-jnp.abs(raw)))
        q_ref[...] = (tq_ref[...] + dot(x, wq_ref[place - 2])).astype(BF16)
        row_id = lax.broadcasted_iota(jnp.int32, (BLOCK, BLOCK), 0)
        col_id = lax.broadcasted_iota(jnp.int32, (BLOCK, BLOCK), 1)
        causal = row_id >= col_id
        for h in range(heads):
            g = h // group
            cols = slice(h * head_size, (h + 1) * head_size)
            kv = slice(g * head_size, (g + 1) * head_size)
            for i in range(rows // BLOCK):
                here = slice(i * BLOCK, (i + 1) * BLOCK)
                span = (i + 1) * BLOCK
                query = q_ref[here, cols]
                scores = dot_dims(query, k_ref[:span, kv], 1, 1)
                d_here = jnp.broadcast_to(dcol_ref[here, h : h + 1], (BLOCK, BLOCK))

                def weight(level):
                    column = h * level_count + level
                    return jnp.broadcast_to(l_ref[here, column : column + 1], (BLOCK, BLOCK))

                weights = {}
                mixed = []
                for j in range(i + 1):
                    level = (i ^ j).bit_length()
                    if level not in weights:
                        weights[level] = weight(level)
                    there = slice(j * BLOCK, (j + 1) * BLOCK)
                    gap = d_here - drow_ref[h : h + 1, there]
                    if i == j:
                        gap = jnp.where(causal, gap, -jnp.inf)
                    mixed.append((weights[level] * jnp.exp(gap) * scores[:, there]).astype(BF16))
                mixing = mixed[0] if i == 0 else jnp.concatenate(mixed, axis=1)
                total = dot(mixing, v_ref[:span, kv])
                wide = query.astype(F32)
                for b in range(bits):
                    factor = weight(own_levels + b) * jnp.exp(d_here + span_refs[b][0:1, cols])
                    scaled = (wide * factor).astype(BF16)
                    if b == bits - 1:
                        s_ref[here, cols] = scaled
                    else:
                        total = total + dot_dims(scaled, state_refs[b][:, cols], 1, 1)
                o_ref[here, cols] = total

    ins = [me, *xs, wq, wl, total_q, total_l, k, v, dcol, drow, *spans, *states]
    wide = shape((rows, width), BF16)
    outs = [shape((rows, width), F32), wide, wide, shape(total_l.shape, F32)]
    flops = 2 * rows * wq.shape[1] * width + 4 * rows * rows * width
    return call(kernel, ins, outs, flops, smem=1)[:2]


def finish(local, scaled, state, cuts, head_size, after=()):
    width = local.shape[1]

    def kernel(o_ref, q_ref, s_ref, *outs):
        for rows, n_ref in zip(cuts, outs):
            for c in range(0, width, head_size):
                cols = slice(c, c + head_size)
                total = o_ref[rows, cols] + dot_dims(q_ref[rows, cols], s_ref[:, cols], 1, 1)
                mean = jnp.mean(total * total, axis=-1, keepdims=True)
                n_ref[:, cols] = (total * lax.rsqrt(mean + 1e-05)).astype(BF16)

    outs = [shape((cut.stop - cut.start, width), BF16) for cut in cuts]
    return call(kernel, [local, scaled, state], outs, 0, after)


def out_block(pairs, w0, w1, dtype, after=()):
    columns = w1.shape[1]
    count = len(pairs)
    rows = sum(own.shape[0] for own, _ in pairs)
    tile = min(columns, 512)

    def kernel(*refs):
        w0_ref, w1_ref, o_ref = refs[2 * count :]
        start = 0
        for i in range(count):
            a_ref, b_ref = refs[2 * i], refs[2 * i + 1]
            here = slice(start, start + a_ref.shape[0])
            start = here.stop
            for c in range(0, columns, tile):
                cols = slice(c, c + tile)
                o_ref[here, cols] = (
                    dot(a_ref[...], w0_ref[:, cols]) + dot(b_ref[...], w1_ref[:, cols])
                ).astype(dtype)

    ins = [x for pair in pairs for x in pair] + [w0, w1]
    return call(kernel, ins, [shape((rows, columns), dtype)], 0, after)[0]


def add_rows(here, arrived, out, start, unit):
    rows, columns = arrived.shape

    def kernel(h_ref, a_ref, *refs):
        place = pl.ds(pl.multiple_of(start + pl.program_id(0) * unit, unit), unit)
        refs[-1][...] = (h_ref[place, :] + a_ref[...].astype(F32)).astype(BF16)

    block = (unit, columns)
    ins, specs, aliases = [here, arrived], [VMEM, pl.BlockSpec(block, lambda s: (s, 0))], {}
    if out is not None:
        ins, specs, aliases = ins + [out], specs + [ANY], {2: 0}
    return pl.pallas_call(
        kernel,
        grid=(rows // unit,),
        in_specs=specs,
        out_specs=pl.BlockSpec(block, lambda s: (start // unit + s, 0)),
        out_shape=shape(here.shape, BF16),
        input_output_aliases=aliases,
        compiler_params=pltpu.CompilerParams(vmem_limit_bytes=8 * 1024 * 1024),
        cost_estimate=pl.CostEstimate(flops=0, bytes_accessed=rows * columns * 8, transcendentals=0),
    )(*ins)


def body(tokens, log_decay, w_query, w_key, w_value, w_level, w_out):
    rows, shard = tokens.shape
    heads = log_decay.shape[1]
    head_size = w_out.shape[0] // heads
    level_count = w_level.shape[1] // heads
    seq_size = lax.axis_size("seq")
    seq_bits = seq_size.bit_length() - 1
    me = jnp.full((1,), lax.axis_index("tp"), jnp.int32)
    slab = jnp.full((1,), lax.axis_index("seq"), jnp.int32)

    def swap_tp(x, bit):
        return lax.ppermute(x, "tp", [(i, i ^ bit) for i in range(4)])

    def swap_seq(x, bit):
        return lax.ppermute(x, "seq", [(i, i ^ bit) for i in range(seq_size)])

    far = swap_tp(tokens, 2)
    near = swap_tp(tokens, 1)

    weights = (w_query, w_key, w_value, w_level.T)
    totals, ws, (drow, dcol, keep, total, span), blocks = begin(
        me, slab, tokens, near, log_decay.T, weights, w_out, head_size
    )
    w_here_own, w_here_send, w_far_own, w_far_send = blocks
    w_here, w_far = swap_tp(w_here_send, 1), swap_tp(w_far_send, 1)

    spans, factors, before = [span], [], None
    for b in range(seq_bits - 1):
        total, before, own, other, span = link(slab, b, total, swap_seq(total, 1 << b), before)
        spans.append(span)
        factors.append((own, other))

    wq, wkv, wkv_send, wl = ws
    wkv_near = swap_tp(wkv_send, 1)
    for_near = partial(far, wkv_near, (total, w_far, w_here))
    from_near = swap_tp(for_near, 1)
    total_q, total_kv, total_l = project(me, 2, far, wq, wkv, wl, totals, (for_near,))
    far_near = swap_tp(gate(far, total_q, from_near), 1)
    k, v, state = project_state(total_kv, from_near, keep, head_size)

    earlier = []
    for b in range(seq_bits):
        other = swap_seq(state, 1 << b)
        earlier.append(other)
        if b < seq_bits - 1:
            state = combine(state, other, *factors[b])

    local, scaled = attend(
        me, 3, [far_near], wq, wl, total_q, total_l, k, v, dcol, drow, spans, earlier[:-1], head_size, level_count
    )

    unit = rows // 8
    ends = (0, 2, 4, 6, 7, 8)
    cuts = [slice(start * unit, stop * unit) for start, stop in zip(ends, ends[1:])]
    pieces = finish(local, scaled, earlier[-1], cuts[:1], head_size)
    pieces += finish(local, scaled, earlier[-1], cuts[1:], head_size, pieces)
    pairs = [(x, swap_tp(x, 1)) for x in pieces]
    crossing = [out_block([pair], w_far_own, w_far, BF16) for pair in pairs]
    own_block = out_block(pairs, w_here_own, w_here, F32, (crossing[-1],))
    out = None
    for cut, x in zip(cuts[:-1], crossing):
        out = add_rows(own_block, swap_tp(x, 2), out, cut.start, unit)
    last = own_block[cuts[-1]] + swap_tp(crossing[-1], 2).astype(F32)
    return lax.dynamic_update_slice_in_dim(out, last.astype(BF16), cuts[-1].start, 0)


def solution(mesh):
    in_specs = (
        P("seq", "tp"),
        P("seq", "tp"),
        P(None, "tp"),
        P(None, "tp"),
        P(None, "tp"),
        P(None, "tp"),
        P("tp", None),
    )
    out_specs = P("seq", "tp")
    return jax.shard_map(body, mesh=mesh, in_specs=in_specs, out_specs=out_specs, check_vma=False)
```

```python
import functools

import jax
import jax.numpy as jnp
from jax import lax
from jax.experimental import pallas as pl
from jax.experimental.pallas import tpu as pltpu
from jax.sharding import PartitionSpec as P

BLOCK = 128
F32 = jnp.float32
BF16 = jnp.bfloat16
VMEM = pl.BlockSpec(memory_space=pltpu.VMEM)
SMEM = pl.BlockSpec(memory_space=pltpu.SMEM)
ANY = pl.BlockSpec(memory_space=pl.ANY)
HBM = pl.BlockSpec(memory_space=pltpu.HBM)


def dot(a, b):
    return jnp.dot(a, b, preferred_element_type=F32)


def dot_dims(a, b, left, right):
    return lax.dot_general(a, b, (((left,), (right,)), ((), ())), preferred_element_type=F32)


def shape(dims, dtype):
    return jax.ShapeDtypeStruct(dims, dtype)


def call(kernel, ins, outs, flops, after=(), smem=0, hbm=0, aliases=None, scratch=(), megabytes=8):
    count = len(ins)
    ins = list(ins)
    for i in range(smem, smem + hbm):
        ins[i] = pltpu.with_memory_space_constraint(ins[i], pltpu.HBM)

    def run(*refs):
        kernel(*refs[:count], *refs[count + len(after) :])

    nbytes = sum(x.size * x.dtype.itemsize for x in (*ins, *outs)) if flops else 0
    return pl.pallas_call(
        run,
        in_specs=[SMEM] * smem + [HBM] * hbm + [VMEM] * (count - smem - hbm) + [ANY] * len(after),
        out_specs=[VMEM] * len(outs),
        out_shape=list(outs),
        input_output_aliases=aliases or {},
        scratch_shapes=list(scratch),
        compiler_params=pltpu.CompilerParams(vmem_limit_bytes=megabytes * 1024 * 1024),
        cost_estimate=pl.CostEstimate(flops=flops, bytes_accessed=nbytes, transcendentals=0),
    )(*ins, *after)


def copies(pairs, sems):
    started = [pltpu.make_async_copy(src, dst, sems.at[i]) for i, (src, dst) in enumerate(pairs)]
    for copy in started:
        copy.start()
    return started


def upper_half(slab_ref, bit):
    return ((slab_ref[0] >> bit) & 1) == 1


def decays(slab_ref, x_ref, row_ref, col_ref, keep_ref, total_ref, span_ref):
    heads, rows = x_ref.shape
    head_size = total_ref.shape[1] // heads
    x = x_ref[...]
    x = jnp.concatenate([x, jnp.zeros((-heads % 8, rows), F32)], axis=0) if heads % 8 else x
    place = lax.broadcasted_iota(jnp.int32, x.shape, 1)
    shift = 1
    while shift < rows:
        x = x + jnp.where(place >= shift, pltpu.roll(x, shift, 1), 0.0)
        shift *= 2
    total = x[:, rows - 1 : rows]
    row_ref[...] = x[:heads]
    col_ref[...] = jnp.transpose(x)[:, :heads]
    keep_ref[...] = jnp.transpose(jnp.exp(total - x))[:, :heads]
    for h in range(heads):
        total_ref[:, h * head_size : (h + 1) * head_size] = jnp.broadcast_to(
            total[h : h + 1], (8, head_size)
        )
    span_ref[...] = jnp.full(span_ref.shape, jnp.where(upper_half(slab_ref, 0), 0.0, -jnp.inf), F32)


def link(slab, bit, total, other, before):
    def kernel(slab_ref, *refs):
        total_ref, other_ref = refs[:2]
        total_out, before_out, own_out, other_out, span_out = refs[-5:]
        upper = upper_half(slab_ref, bit)
        here, there = total_ref[...], other_ref[...]
        total_out[...] = here + there
        so_far = jnp.where(upper, there, 0.0)
        if before is not None:
            so_far = so_far + refs[2][...]
        before_out[...] = so_far
        own_out[...] = jnp.where(upper, 1.0, jnp.exp(there))
        other_out[...] = jnp.where(upper, jnp.exp(here), 1.0)
        span_out[...] = jnp.where(upper_half(slab_ref, bit + 1), so_far, -jnp.inf)

    ins = [slab, total, other] + ([] if before is None else [before])
    return call(kernel, ins, [shape(total.shape, F32)] * 5, 0, smem=1)


def combine(state, other, own_factor, other_factor, after):
    def kernel(s_ref, o_ref, a_ref, b_ref, out_ref):
        out_ref[...] = (
            a_ref[0:1, :] * s_ref[...].astype(F32) + b_ref[0:1, :] * o_ref[...].astype(F32)
        ).astype(BF16)

    return call(kernel, [state, other, own_factor, other_factor], [shape(state.shape, BF16)], 0, after)[0]


def begin(me, slab, tokens, near, log_decay_rows, ws, w_out, head_size):
    wq, wk, wv, wl = ws
    rows, shard = near.shape
    q_width, kv_width = wq.shape[1], wk.shape[1]
    heads = log_decay_rows.shape[0]
    block = w_out.shape[1] // 4

    def kernel(me_ref, slab_ref, t_ref, wq_ref, wk_ref, wv_ref, wo_ref, wl_ref, near_ref, decay_ref, *refs):
        total_q, total_kv, total_l, far_q, far_kv, send_kv, all_l = refs[:7]
        decay_outs, blocks, (own_x, own_q, own_kv, sems) = refs[7:12], refs[12:16], refs[16:]

        def pairs(i, q_dst, kv_dst):
            here = pl.ds(pl.multiple_of((me_ref[0] ^ i) * shard, 128), shard)
            return [
                (wk_ref.at[here, :], kv_dst.at[:, :kv_width]),
                (wv_ref.at[here, :], kv_dst.at[:, kv_width:]),
                (wq_ref.at[here, :], q_dst),
            ]

        def columns(i):
            return wo_ref.at[:, pl.ds(pl.multiple_of((me_ref[0] ^ i) * block, 128), block)]

        moves = pairs(0, own_q.at[0], own_kv.at[0]) + [(t_ref, own_x)]
        moves += pairs(1, own_q.at[1], own_kv.at[1])
        moves += pairs(2, far_q.at[0], far_kv) + pairs(3, far_q.at[1], send_kv)
        moves += [(columns(i), blocks[i]) for i in range(4)]
        started = copies(moves, sems)
        decays(slab_ref, decay_ref, *decay_outs)
        all_l[...] = wl_ref[...]
        for copy in started[:4]:
            copy.wait()
        lanes = pl.ds(pl.multiple_of(me_ref[0] * shard, 128), shard)
        own = own_x[...]
        total_kv[...] = dot(own, own_kv[0])
        total_q[...] = dot(own, own_q[0])
        total_l[...] = dot_dims(own, all_l[:, lanes], 1, 1)
        for copy in started[4:7]:
            copy.wait()
        lanes = pl.ds(pl.multiple_of((me_ref[0] ^ 1) * shard, 128), shard)
        total_kv[...] += dot(near_ref[...], own_kv[1])
        total_q[...] += dot(near_ref[...], own_q[1])
        total_l[...] += dot_dims(near_ref[...], all_l[:, lanes], 1, 1)
        for copy in started[7:]:
            copy.wait()

    wide = shape((8, heads * head_size), F32)
    outs = [
        shape((rows, q_width), F32),
        shape((rows, 2 * kv_width), F32),
        shape((rows, wl.shape[0]), F32),
        shape((2, shard, q_width), BF16),
        shape((shard, 2 * kv_width), BF16),
        shape((shard, 2 * kv_width), BF16),
        shape(wl.shape, BF16),
        shape((heads, rows), F32),
        shape((rows, heads), F32),
        shape((rows, heads), F32),
        wide,
        wide,
    ] + [shape((w_out.shape[0], block), BF16)] * 4
    scratch = [
        pltpu.VMEM((rows, shard), BF16),
        pltpu.VMEM((2, shard, q_width), BF16),
        pltpu.VMEM((2, shard, 2 * kv_width), BF16),
        pltpu.SemaphoreType.DMA((17,)),
    ]
    ins = [me, slab, tokens, wq, wk, wv, w_out, wl, near, log_decay_rows]
    outs = call(kernel, ins, outs, 0, smem=2, hbm=5, scratch=scratch, megabytes=14)
    return outs[:3], outs[3:7], outs[7:12], outs[12:]


def add_levels(me_ref, place, x, wl_ref):
    shard = wl_ref.shape[1] // 4
    start = pl.multiple_of((me_ref[0] ^ place) * shard, 128)
    return dot_dims(x, wl_ref[:, pl.ds(start, shard)], 1, 1)


def project(me, place, x, wq, wl, total_q, total_l, after):
    def kernel(me_ref, x_ref, wq_ref, wl_ref, q_ref, l_ref, q_out, l_out):
        q_out[...] = q_ref[...] + dot(x_ref[...], wq_ref[place - 2])
        l_out[...] = l_ref[...] + add_levels(me_ref, place, x_ref[...], wl_ref)

    outs = [shape(t.shape, F32) for t in (total_q, total_l)]
    flops = 2 * x.size * (total_q.shape[1] + total_l.shape[1])
    return call(kernel, [me, x, wq, wl, total_q, total_l], outs, flops, after, smem=1, aliases={4: 0, 5: 1})


def split(x, ways, after):
    rows, columns = x.shape
    part = columns // ways

    def kernel(x_ref, *outs):
        for i, o_ref in enumerate(outs):
            o_ref[...] = x_ref[:, i * part : (i + 1) * part]

    return call(kernel, [x], [shape((rows, part), x.dtype)] * ways, 0, after)


def partial(x, w, after):
    def kernel(x_ref, w_ref, o_ref):
        o_ref[...] = dot(x_ref[...], w_ref[...]).astype(BF16)

    return call(kernel, [x, w], [shape((x.shape[0], w.shape[1]), BF16)], 0, after)[0]


def add_product(x, w, total, after):
    def kernel(x_ref, w_ref, t_ref, o_ref):
        o_ref[...] = t_ref[...] + dot(x_ref[...], w_ref[...])

    return call(kernel, [x, w, total], [shape(total.shape, F32)], 0, after, aliases={2: 0})[0]


def project_state(total_kv, from_near, keep, head_size):
    rows = total_kv.shape[0]
    heads = keep.shape[1]
    kv_width = total_kv.shape[1] // 2
    group = heads // (kv_width // head_size)

    def kernel(total_ref, near_ref, keep_ref, k_out, v_out, s_out):
        total = total_ref[...] + near_ref[...].astype(F32)
        keys = total[:, :kv_width].astype(BF16)
        values = total[:, kv_width:].astype(BF16)
        k_out[...] = keys
        v_out[...] = values
        for g in range(kv_width // head_size):
            cols = slice(g * head_size, (g + 1) * head_size)
            kf = keys[:, cols].astype(F32)
            weighted = jnp.concatenate(
                [(kf * keep_ref[:, h : h + 1]).astype(BF16) for h in range(g * group, (g + 1) * group)],
                axis=1,
            )
            wide = slice(g * group * head_size, (g + 1) * group * head_size)
            s_out[:, wide] = dot_dims(values[:, cols], weighted, 0, 0).astype(BF16)

    outs = [
        shape((rows, kv_width), BF16),
        shape((rows, kv_width), BF16),
        shape((head_size, heads * head_size), BF16),
    ]
    return call(kernel, [total_kv, from_near, keep], outs, 0)


def attend(me, place, xs, wq, wl, total_q, total_l, k, v, dcol, drow, spans, states, head_size, level_count):
    rows, width = total_q.shape
    bits = len(spans)
    heads = width // head_size
    group = heads // (k.shape[1] // head_size)
    own_levels = level_count - bits

    def kernel(me_ref, *refs):
        x = jnp.concatenate([x_ref[...] for x_ref in refs[: len(xs)]], axis=1)
        refs = refs[len(xs) :]
        wq_ref, wl_ref, tq_ref, tl_ref, k_ref, v_ref, dcol_ref, drow_ref = refs[:8]
        span_refs, state_refs = refs[8 : 8 + bits], refs[8 + bits : 7 + 2 * bits]
        o_ref, s_ref, q_ref, l_ref = refs[-4:]
        raw = tl_ref[...] + add_levels(me_ref, place, x, wl_ref)
        l_ref[...] = jnp.maximum(raw, 0.0) + jnp.log1p(jnp.exp(-jnp.abs(raw)))
        q_ref[...] = (tq_ref[...] + dot(x, wq_ref[place - 2])).astype(BF16)
        row_id = lax.broadcasted_iota(jnp.int32, (BLOCK, BLOCK), 0)
        col_id = lax.broadcasted_iota(jnp.int32, (BLOCK, BLOCK), 1)
        causal = row_id >= col_id
        for h in range(heads):
            g = h // group
            cols = slice(h * head_size, (h + 1) * head_size)
            kv = slice(g * head_size, (g + 1) * head_size)
            for i in range(rows // BLOCK):
                here = slice(i * BLOCK, (i + 1) * BLOCK)
                span = (i + 1) * BLOCK
                query = q_ref[here, cols]
                scores = dot_dims(query, k_ref[:span, kv], 1, 1)
                d_here = jnp.broadcast_to(dcol_ref[here, h : h + 1], (BLOCK, BLOCK))

                def weight(level):
                    column = h * level_count + level
                    return jnp.broadcast_to(l_ref[here, column : column + 1], (BLOCK, BLOCK))

                weights = {}
                mixed = []
                for j in range(i + 1):
                    level = (i ^ j).bit_length()
                    if level not in weights:
                        weights[level] = weight(level)
                    there = slice(j * BLOCK, (j + 1) * BLOCK)
                    gap = d_here - drow_ref[h : h + 1, there]
                    if i == j:
                        gap = jnp.where(causal, gap, -jnp.inf)
                    mixed.append((weights[level] * jnp.exp(gap) * scores[:, there]).astype(BF16))
                mixing = mixed[0] if i == 0 else jnp.concatenate(mixed, axis=1)
                total = dot(mixing, v_ref[:span, kv])
                wide = query.astype(F32)
                for b in range(bits):
                    factor = weight(own_levels + b) * jnp.exp(d_here + span_refs[b][0:1, cols])
                    scaled = (wide * factor).astype(BF16)
                    if b == bits - 1:
                        s_ref[here, cols] = scaled
                    else:
                        total = total + dot_dims(scaled, state_refs[b][:, cols], 1, 1)
                o_ref[here, cols] = total

    ins = [me, *xs, wq, wl, total_q, total_l, k, v, dcol, drow, *spans, *states]
    wide = shape((rows, width), BF16)
    outs = [shape((rows, width), F32), wide, wide, shape(total_l.shape, F32)]
    flops = 2 * rows * wq.shape[1] * width + 4 * rows * rows * width
    return call(kernel, ins, outs, flops, smem=1)[:2]


def finish(local, scaled, state, cuts, head_size, after=()):
    width = local.shape[1]

    def kernel(o_ref, q_ref, s_ref, *outs):
        for rows, n_ref in zip(cuts, outs):
            for c in range(0, width, head_size):
                cols = slice(c, c + head_size)
                total = o_ref[rows, cols] + dot_dims(q_ref[rows, cols], s_ref[:, cols], 1, 1)
                mean = jnp.mean(total * total, axis=-1, keepdims=True)
                n_ref[:, cols] = (total * lax.rsqrt(mean + 1e-05)).astype(BF16)

    outs = [shape((cut.stop - cut.start, width), BF16) for cut in cuts]
    return call(kernel, [local, scaled, state], outs, 0, after)


def out_block(pairs, w0, w1, dtype, after=()):
    columns = w1.shape[1]
    count = len(pairs)
    rows = sum(own.shape[0] for own, _ in pairs)
    tile = min(columns, 512)

    def kernel(*refs):
        w0_ref, w1_ref, o_ref = refs[2 * count :]
        start = 0
        for i in range(count):
            a_ref, b_ref = refs[2 * i], refs[2 * i + 1]
            here = slice(start, start + a_ref.shape[0])
            start = here.stop
            for c in range(0, columns, tile):
                cols = slice(c, c + tile)
                o_ref[here, cols] = (
                    dot(a_ref[...], w0_ref[:, cols]) + dot(b_ref[...], w1_ref[:, cols])
                ).astype(dtype)

    ins = [x for pair in pairs for x in pair] + [w0, w1]
    return call(kernel, ins, [shape((rows, columns), dtype)], 0, after)[0]


def add_rows(here, arrived, out, start, unit):
    rows, columns = arrived.shape

    def kernel(h_ref, a_ref, *refs):
        place = pl.ds(pl.multiple_of(start + pl.program_id(0) * unit, unit), unit)
        refs[-1][...] = (h_ref[place, :] + a_ref[...].astype(F32)).astype(BF16)

    block = (unit, columns)
    ins, specs, aliases = [here, arrived], [VMEM, pl.BlockSpec(block, lambda s: (s, 0))], {}
    if out is not None:
        ins, specs, aliases = ins + [out], specs + [ANY], {2: 0}
    return pl.pallas_call(
        kernel,
        grid=(rows // unit,),
        in_specs=specs,
        out_specs=pl.BlockSpec(block, lambda s: (start // unit + s, 0)),
        out_shape=shape(here.shape, BF16),
        input_output_aliases=aliases,
        compiler_params=pltpu.CompilerParams(vmem_limit_bytes=8 * 1024 * 1024),
        cost_estimate=pl.CostEstimate(flops=0, bytes_accessed=rows * columns * 8, transcendentals=0),
    )(*ins)


def body(tokens, log_decay, w_query, w_key, w_value, w_level, w_out):
    rows, shard = tokens.shape
    heads = log_decay.shape[1]
    head_size = w_out.shape[0] // heads
    level_count = w_level.shape[1] // heads
    seq_size = lax.axis_size("seq")
    seq_bits = seq_size.bit_length() - 1
    me = jnp.full((1,), lax.axis_index("tp"), jnp.int32)
    slab = jnp.full((1,), lax.axis_index("seq"), jnp.int32)

    def swap_tp(x, bit):
        return lax.ppermute(x, "tp", [(i, i ^ bit) for i in range(4)])

    def swap_seq(x, bit):
        return lax.ppermute(x, "seq", [(i, i ^ bit) for i in range(seq_size)])

    far = swap_tp(tokens, 2)
    near = swap_tp(tokens, 1)

    weights = (w_query, w_key, w_value, w_level.T)
    totals, ws, (drow, dcol, keep, total, span), blocks = begin(
        me, slab, tokens, near, log_decay.T, weights, w_out, head_size
    )
    w_here_own, w_here_send, w_far_own, w_far_send = blocks
    w_here, w_far = swap_tp(w_here_send, 1), swap_tp(w_far_send, 1)

    spans, factors, before = [span], [], None
    for b in range(seq_bits - 1):
        total, before, own, other, span = link(slab, b, total, swap_seq(total, 1 << b), before)
        spans.append(span)
        factors.append((own, other))

    wq, wkv, wkv_send, wl = ws
    wkv_near = swap_tp(wkv_send, 1)
    arrived = far
    for_near = partial(arrived, wkv_near, (total, w_far, w_here))
    from_near = swap_tp(for_near, 1)
    total_q, total_kv, total_l = totals
    total_kv = add_product(arrived, wkv, total_kv, (for_near,))
    k, v, state = project_state(total_kv, from_near, keep, head_size)
    total_q, total_l = project(me, 2, arrived, wq, wl, total_q, total_l, (k,))
    arrived_near = [swap_tp(x, 1) for x in split(arrived, 4, (total_l,))]

    earlier = []
    for b in range(seq_bits):
        other = swap_seq(state, 1 << b)
        earlier.append(other)
        if b < seq_bits - 1:
            after = () if b else (total_l,)
            state = combine(state, other, *factors[b], after)

    local, scaled = attend(
        me, 3, arrived_near, wq, wl, total_q, total_l, k, v, dcol, drow, spans, earlier[:-1], head_size, level_count
    )

    unit = rows // 8
    ends = (0, 3, 5, 7, 8)
    cuts = [slice(start * unit, stop * unit) for start, stop in zip(ends, ends[1:])]
    pieces = finish(local, scaled, earlier[-1], cuts[:1], head_size)
    pieces += finish(local, scaled, earlier[-1], cuts[1:], head_size, pieces)
    pairs = [(x, swap_tp(x, 1)) for x in pieces]
    crossing = [out_block([pair], w_far_own, w_far, BF16) for pair in pairs]
    own_block = out_block(pairs, w_here_own, w_here, F32, (crossing[-1],))
    out = None
    for cut, x in zip(cuts[:-1], crossing):
        out = add_rows(own_block, swap_tp(x, 2), out, cut.start, unit)
    last = own_block[cuts[-1]] + swap_tp(crossing[-1], 2).astype(F32)
    return lax.dynamic_update_slice_in_dim(out, last.astype(BF16), cuts[-1].start, 0)


def solution(mesh):
    in_specs = (
        P("seq", "tp"),
        P("seq", "tp"),
        P(None, "tp"),
        P(None, "tp"),
        P(None, "tp"),
        P(None, "tp"),
        P("tp", None),
    )
    out_specs = P("seq", "tp")
    return jax.shard_map(body, mesh=mesh, in_specs=in_specs, out_specs=out_specs, check_vma=False)
```

```python
import functools

import jax
import jax.numpy as jnp
from jax import lax
from jax.experimental import pallas as pl
from jax.experimental.pallas import tpu as pltpu
from jax.sharding import PartitionSpec as P

BLOCK = 128
F32 = jnp.float32
BF16 = jnp.bfloat16
VMEM = pl.BlockSpec(memory_space=pltpu.VMEM)
SMEM = pl.BlockSpec(memory_space=pltpu.SMEM)
ANY = pl.BlockSpec(memory_space=pl.ANY)
HBM = pl.BlockSpec(memory_space=pltpu.HBM)


def dot(a, b):
    return jnp.dot(a, b, preferred_element_type=F32)


def dot_dims(a, b, left, right):
    return lax.dot_general(a, b, (((left,), (right,)), ((), ())), preferred_element_type=F32)


def shape(dims, dtype):
    return jax.ShapeDtypeStruct(dims, dtype)


def call(kernel, ins, outs, flops, after=(), smem=0, hbm=0, aliases=None, scratch=(), megabytes=8):
    count = len(ins)
    ins = list(ins)
    for i in range(smem, smem + hbm):
        ins[i] = pltpu.with_memory_space_constraint(ins[i], pltpu.HBM)

    def run(*refs):
        kernel(*refs[:count], *refs[count + len(after) :])

    nbytes = sum(x.size * x.dtype.itemsize for x in (*ins, *outs)) if flops else 0
    return pl.pallas_call(
        run,
        in_specs=[SMEM] * smem + [HBM] * hbm + [VMEM] * (count - smem - hbm) + [ANY] * len(after),
        out_specs=[VMEM] * len(outs),
        out_shape=list(outs),
        input_output_aliases=aliases or {},
        scratch_shapes=list(scratch),
        compiler_params=pltpu.CompilerParams(vmem_limit_bytes=megabytes * 1024 * 1024),
        cost_estimate=pl.CostEstimate(flops=flops, bytes_accessed=nbytes, transcendentals=0),
    )(*ins, *after)


def gate(x, *after):
    def run(*refs):
        pass

    return pl.pallas_call(
        run,
        in_specs=[ANY] * (1 + len(after)),
        out_specs=ANY,
        out_shape=shape(x.shape, x.dtype),
        input_output_aliases={0: 0},
        compiler_params=pltpu.CompilerParams(vmem_limit_bytes=1024 * 1024),
        cost_estimate=pl.CostEstimate(flops=0, bytes_accessed=0, transcendentals=0),
    )(x, *after)


def copies(pairs, sems):
    started = [pltpu.make_async_copy(src, dst, sems.at[i]) for i, (src, dst) in enumerate(pairs)]
    for copy in started:
        copy.start()
    return started


def upper_half(slab_ref, bit):
    return ((slab_ref[0] >> bit) & 1) == 1


def decays(slab_ref, x_ref, row_ref, col_ref, keep_ref, total_ref, span_ref):
    heads, rows = x_ref.shape
    head_size = total_ref.shape[1] // heads
    x = x_ref[...]
    x = jnp.concatenate([x, jnp.zeros((-heads % 8, rows), F32)], axis=0) if heads % 8 else x
    place = lax.broadcasted_iota(jnp.int32, x.shape, 1)
    shift = 1
    while shift < rows:
        x = x + jnp.where(place >= shift, pltpu.roll(x, shift, 1), 0.0)
        shift *= 2
    total = x[:, rows - 1 : rows]
    row_ref[...] = x[:heads]
    col_ref[...] = jnp.transpose(x)[:, :heads]
    keep_ref[...] = jnp.transpose(jnp.exp(total - x))[:, :heads]
    for h in range(heads):
        total_ref[:, h * head_size : (h + 1) * head_size] = jnp.broadcast_to(
            total[h : h + 1], (8, head_size)
        )
    span_ref[...] = jnp.full(span_ref.shape, jnp.where(upper_half(slab_ref, 0), 0.0, -jnp.inf), F32)


def link(slab, bit, total, other, before):
    def kernel(slab_ref, *refs):
        total_ref, other_ref = refs[:2]
        total_out, before_out, own_out, other_out, span_out = refs[-5:]
        upper = upper_half(slab_ref, bit)
        here, there = total_ref[...], other_ref[...]
        total_out[...] = here + there
        so_far = jnp.where(upper, there, 0.0)
        if before is not None:
            so_far = so_far + refs[2][...]
        before_out[...] = so_far
        own_out[...] = jnp.where(upper, 1.0, jnp.exp(there))
        other_out[...] = jnp.where(upper, jnp.exp(here), 1.0)
        span_out[...] = jnp.where(upper_half(slab_ref, bit + 1), so_far, -jnp.inf)

    ins = [slab, total, other] + ([] if before is None else [before])
    return call(kernel, ins, [shape(total.shape, F32)] * 5, 0, smem=1)


def combine(state, other, own_factor, other_factor, which, after):
    cols = slice(which * state.shape[1], (which + 1) * state.shape[1])

    def kernel(s_ref, o_ref, a_ref, b_ref, out_ref):
        out_ref[...] = (
            a_ref[0:1, cols] * s_ref[...].astype(F32) + b_ref[0:1, cols] * o_ref[...].astype(F32)
        ).astype(BF16)

    return call(kernel, [state, other, own_factor, other_factor], [shape(state.shape, BF16)], 0, after)[0]


def combine_both(states, others, own_factor, other_factor, after):
    rows, half = states[0].shape

    def kernel(s0_ref, s1_ref, o0_ref, o1_ref, a_ref, b_ref, out_ref):
        for i, (s_ref, o_ref) in enumerate(((s0_ref, o0_ref), (s1_ref, o1_ref))):
            cols = slice(i * half, (i + 1) * half)
            out_ref[:, cols] = (
                a_ref[0:1, cols] * s_ref[...].astype(F32) + b_ref[0:1, cols] * o_ref[...].astype(F32)
            ).astype(BF16)

    return call(kernel, [*states, *others, own_factor, other_factor], [shape((rows, 2 * half), BF16)], 0, after)[0]


def begin(me, slab, tokens, near, log_decay_rows, ws, w_out, head_size):
    wq, wk, wv, wl = ws
    rows, shard = near.shape
    q_width, kv_width = wq.shape[1], wk.shape[1]
    heads = log_decay_rows.shape[0]
    block = w_out.shape[1] // 4

    def kernel(me_ref, slab_ref, t_ref, wq_ref, wk_ref, wv_ref, wo_ref, wl_ref, near_ref, decay_ref, *refs):
        total_q, total_kv, total_l, far_q, far_kv, send_kv, all_l = refs[:7]
        decay_outs, blocks, (own_x, own_q, own_kv, sems) = refs[7:12], refs[12:16], refs[16:]

        def pairs(i, q_dst, kv_dst):
            here = pl.ds(pl.multiple_of((me_ref[0] ^ i) * shard, 128), shard)
            return [
                (wk_ref.at[here, :], kv_dst.at[:, :kv_width]),
                (wv_ref.at[here, :], kv_dst.at[:, kv_width:]),
                (wq_ref.at[here, :], q_dst),
            ]

        def columns(i):
            return wo_ref.at[:, pl.ds(pl.multiple_of((me_ref[0] ^ i) * block, 128), block)]

        moves = pairs(0, own_q.at[0], own_kv.at[0]) + [(t_ref, own_x)]
        moves += pairs(1, own_q.at[1], own_kv.at[1])
        moves += pairs(2, far_q.at[0], far_kv) + pairs(3, far_q.at[1], send_kv)
        moves += [(columns(i), blocks[i]) for i in range(4)]
        started = copies(moves, sems)
        decays(slab_ref, decay_ref, *decay_outs)
        all_l[...] = wl_ref[...]
        for copy in started[:4]:
            copy.wait()
        lanes = pl.ds(pl.multiple_of(me_ref[0] * shard, 128), shard)
        own = own_x[...]
        total_kv[...] = dot(own, own_kv[0])
        total_q[...] = dot(own, own_q[0])
        total_l[...] = dot_dims(own, all_l[:, lanes], 1, 1)
        for copy in started[4:7]:
            copy.wait()
        lanes = pl.ds(pl.multiple_of((me_ref[0] ^ 1) * shard, 128), shard)
        total_kv[...] += dot(near_ref[...], own_kv[1])
        total_q[...] += dot(near_ref[...], own_q[1])
        total_l[...] += dot_dims(near_ref[...], all_l[:, lanes], 1, 1)
        for copy in started[7:]:
            copy.wait()

    wide = shape((8, heads * head_size), F32)
    outs = [
        shape((rows, q_width), F32),
        shape((rows, 2 * kv_width), F32),
        shape((rows, wl.shape[0]), F32),
        shape((2, shard, q_width), BF16),
        shape((shard, 2 * kv_width), BF16),
        shape((shard, 2 * kv_width), BF16),
        shape(wl.shape, BF16),
        shape((heads, rows), F32),
        shape((rows, heads), F32),
        shape((rows, heads), F32),
        wide,
        wide,
    ] + [shape((w_out.shape[0], block), BF16)] * 4
    scratch = [
        pltpu.VMEM((rows, shard), BF16),
        pltpu.VMEM((2, shard, q_width), BF16),
        pltpu.VMEM((2, shard, 2 * kv_width), BF16),
        pltpu.SemaphoreType.DMA((17,)),
    ]
    ins = [me, slab, tokens, wq, wk, wv, w_out, wl, near, log_decay_rows]
    outs = call(kernel, ins, outs, 0, smem=2, hbm=5, scratch=scratch, megabytes=14)
    return outs[:3], outs[3:7], outs[7:12], outs[12:]


def add_levels(me_ref, place, x, wl_ref):
    shard = wl_ref.shape[1] // 4
    start = pl.multiple_of((me_ref[0] ^ place) * shard, 128)
    return dot_dims(x, wl_ref[:, pl.ds(start, shard)], 1, 1)


def project(me, place, x, wq, wkv, wl, totals, after=()):
    def kernel(me_ref, x_ref, q_ref, kv_ref, l_ref, *refs):
        ins, outs = refs[:3], refs[3:]
        outs[1][...] = ins[1][...] + dot(x_ref[...], kv_ref[...])
        outs[0][...] = ins[0][...] + dot(x_ref[...], q_ref[place - 2])
        outs[2][...] = ins[2][...] + add_levels(me_ref, place, x_ref[...], l_ref)

    outs = [shape(t.shape, F32) for t in totals]
    return call(kernel, [me, x, wq, wkv, wl, *totals], outs, 0, after, smem=1, aliases={5: 0, 6: 1, 7: 2})


def partial(x, w, after):
    def kernel(x_ref, w_ref, o_ref):
        o_ref[...] = dot(x_ref[...], w_ref[...]).astype(BF16)

    return call(kernel, [x, w], [shape((x.shape[0], w.shape[1]), BF16)], 0, after)[0]


def project_state(total_kv, from_near, keep, head_size):
    rows = total_kv.shape[0]
    heads = keep.shape[1]
    kv_width = total_kv.shape[1] // 2
    group = heads // (kv_width // head_size)

    half = heads // 2 * head_size

    def kernel(total_ref, near_ref, keep_ref, k_out, v_out, *s_outs):
        total = total_ref[...] + near_ref[...].astype(F32)
        keys = total[:, :kv_width].astype(BF16)
        values = total[:, kv_width:].astype(BF16)
        k_out[...] = keys
        v_out[...] = values
        for g in range(kv_width // head_size):
            cols = slice(g * head_size, (g + 1) * head_size)
            kf = keys[:, cols].astype(F32)
            weighted = jnp.concatenate(
                [(kf * keep_ref[:, h : h + 1]).astype(BF16) for h in range(g * group, (g + 1) * group)],
                axis=1,
            )
            states = dot_dims(values[:, cols], weighted, 0, 0).astype(BF16)
            for i in range(group):
                start = (g * group + i) * head_size
                s_outs[start // half][:, start % half : start % half + head_size] = states[
                    :, i * head_size : (i + 1) * head_size
                ]

    outs = [
        shape((rows, kv_width), BF16),
        shape((rows, kv_width), BF16),
        shape((head_size, half), BF16),
        shape((head_size, half), BF16),
    ]
    return call(kernel, [total_kv, from_near, keep], outs, 0)


def queries(me, place, x, wq, wl, total_q, total_l):
    def kernel(me_ref, x_ref, wq_ref, wl_ref, tq_ref, tl_ref, q_ref, l_ref):
        raw = tl_ref[...] + add_levels(me_ref, place, x_ref[...], wl_ref)
        l_ref[...] = jnp.maximum(raw, 0.0) + jnp.log1p(jnp.exp(-jnp.abs(raw)))
        q_ref[...] = (tq_ref[...] + dot(x_ref[...], wq_ref[place - 2])).astype(BF16)

    outs = [shape(total_q.shape, BF16), shape(total_l.shape, F32)]
    return call(kernel, [me, x, wq, wl, total_q, total_l], outs, 0, smem=1)


def column(ref, rows, place):
    return jnp.broadcast_to(ref[rows, place : place + 1], (BLOCK, BLOCK))


def attend(q, level, k, v, dcol, drow, which, head_size, level_count):
    rows, width = q.shape
    heads = width // head_size
    group = heads // (k.shape[1] // head_size)
    first = which * heads // 2

    def kernel(q_ref, l_ref, k_ref, v_ref, dcol_ref, drow_ref, o_ref):
        row_id = lax.broadcasted_iota(jnp.int32, (BLOCK, BLOCK), 0)
        col_id = lax.broadcasted_iota(jnp.int32, (BLOCK, BLOCK), 1)
        causal = row_id >= col_id
        for h in range(first, first + heads // 2):
            cols = slice(h * head_size, (h + 1) * head_size)
            kv = slice(h // group * head_size, (h // group + 1) * head_size)
            for i in range(rows // BLOCK):
                here = slice(i * BLOCK, (i + 1) * BLOCK)
                span = (i + 1) * BLOCK
                scores = dot_dims(q_ref[here, cols], k_ref[:span, kv], 1, 1)
                d_here = column(dcol_ref, here, h)
                weights = {}
                mixed = []
                for j in range(i + 1):
                    step = (i ^ j).bit_length()
                    if step not in weights:
                        weights[step] = column(l_ref, here, h * level_count + step)
                    there = slice(j * BLOCK, (j + 1) * BLOCK)
                    gap = d_here - drow_ref[h : h + 1, there]
                    if i == j:
                        gap = jnp.where(causal, gap, -jnp.inf)
                    mixed.append((weights[step] * jnp.exp(gap) * scores[:, there]).astype(BF16))
                mixing = mixed[0] if i == 0 else jnp.concatenate(mixed, axis=1)
                out = slice((h - first) * head_size, (h - first + 1) * head_size)
                o_ref[here, out] = dot(mixing, v_ref[:span, kv])

    ins = [q, level, k, v, dcol, drow]
    return call(kernel, ins, [shape((rows, width // 2), F32)], 0)[0]


def attend_earlier(locals_, q, level, dcol, spans, states, head_size, level_count):
    rows, width = q.shape
    bits = len(spans)
    half = width // 2
    own_levels = level_count - bits

    def kernel(a_ref, b_ref, q_ref, l_ref, dcol_ref, *refs):
        span_refs, state_refs = refs[:bits], refs[bits : bits + len(states)]
        outs = refs[-4:]
        for h in range(width // head_size):
            cols = slice(h * head_size, (h + 1) * head_size)
            which, at = divmod(h * head_size, half)
            out = slice(at, at + head_size)
            for i in range(rows // BLOCK):
                here = slice(i * BLOCK, (i + 1) * BLOCK)
                query = q_ref[here, cols].astype(F32)
                d_here = column(dcol_ref, here, h)
                total = (a_ref, b_ref)[which][here, out]
                for b in range(bits):
                    factor = column(l_ref, here, h * level_count + own_levels + b)
                    factor = factor * jnp.exp(d_here + span_refs[b][0:1, cols])
                    scaled = (query * factor).astype(BF16)
                    if b == bits - 1:
                        outs[2 + which][here, out] = scaled
                    else:
                        total = total + dot_dims(scaled, state_refs[2 * b + which][:, out], 1, 1)
                outs[which][here, out] = total

    ins = [*locals_, q, level, dcol, *spans, *states]
    outs = [shape((rows, half), F32)] * 2 + [shape((rows, half), BF16)] * 2
    outs = call(kernel, ins, outs, 0)
    return list(zip(outs[:2], outs[2:]))


def finish(halves, state, cuts, head_size, after=()):
    half = halves[0][0].shape[1]

    def kernel(o0_ref, q0_ref, o1_ref, q1_ref, s_ref, *outs):
        for rows, n_ref in zip(cuts, outs):
            for c in range(0, 2 * half, head_size):
                cols = slice(c, c + head_size)
                here = slice(c % half, c % half + head_size)
                o_ref, q_ref = (o0_ref, q0_ref) if c < half else (o1_ref, q1_ref)
                total = o_ref[rows, here] + dot_dims(q_ref[rows, here], s_ref[:, cols], 1, 1)
                mean = jnp.mean(total * total, axis=-1, keepdims=True)
                n_ref[:, cols] = (total * lax.rsqrt(mean + 1e-05)).astype(BF16)

    outs = [shape((cut.stop - cut.start, 2 * half), BF16) for cut in cuts]
    return call(kernel, [*halves[0], *halves[1], state], outs, 0, after)


def out_block(pairs, w0, w1, dtype, after=()):
    columns = w1.shape[1]
    count = len(pairs)
    rows = sum(own.shape[0] for own, _ in pairs)
    tile = min(columns, 512)

    def kernel(*refs):
        w0_ref, w1_ref, o_ref = refs[2 * count :]
        start = 0
        for i in range(count):
            a_ref, b_ref = refs[2 * i], refs[2 * i + 1]
            here = slice(start, start + a_ref.shape[0])
            start = here.stop
            for c in range(0, columns, tile):
                cols = slice(c, c + tile)
                o_ref[here, cols] = (
                    dot(a_ref[...], w0_ref[:, cols]) + dot(b_ref[...], w1_ref[:, cols])
                ).astype(dtype)

    ins = [x for pair in pairs for x in pair] + [w0, w1]
    return call(kernel, ins, [shape((rows, columns), dtype)], 0, after)[0]


def add_rows(here, arrived, out, start, unit):
    rows, columns = arrived.shape

    def kernel(h_ref, a_ref, *refs):
        place = pl.ds(pl.multiple_of(start + pl.program_id(0) * unit, unit), unit)
        refs[-1][...] = (h_ref[place, :] + a_ref[...].astype(F32)).astype(BF16)

    block = (unit, columns)
    ins, specs, aliases = [here, arrived], [VMEM, pl.BlockSpec(block, lambda s: (s, 0))], {}
    if out is not None:
        ins, specs, aliases = ins + [out], specs + [ANY], {2: 0}
    return pl.pallas_call(
        kernel,
        grid=(rows // unit,),
        in_specs=specs,
        out_specs=pl.BlockSpec(block, lambda s: (start // unit + s, 0)),
        out_shape=shape(here.shape, BF16),
        input_output_aliases=aliases,
        compiler_params=pltpu.CompilerParams(vmem_limit_bytes=8 * 1024 * 1024),
        cost_estimate=pl.CostEstimate(flops=0, bytes_accessed=rows * columns * 8, transcendentals=0),
    )(*ins)


def body(tokens, log_decay, w_query, w_key, w_value, w_level, w_out):
    rows, shard = tokens.shape
    heads = log_decay.shape[1]
    head_size = w_out.shape[0] // heads
    level_count = w_level.shape[1] // heads
    seq_size = lax.axis_size("seq")
    seq_bits = seq_size.bit_length() - 1
    me = jnp.full((1,), lax.axis_index("tp"), jnp.int32)
    slab = jnp.full((1,), lax.axis_index("seq"), jnp.int32)

    def swap_tp(x, bit):
        return lax.ppermute(x, "tp", [(i, i ^ bit) for i in range(4)])

    def swap_seq(x, bit):
        return lax.ppermute(x, "seq", [(i, i ^ bit) for i in range(seq_size)])

    far = swap_tp(tokens, 2)
    near = swap_tp(tokens, 1)

    weights = (w_query, w_key, w_value, w_level.T)
    totals, ws, (drow, dcol, keep, total, span), blocks = begin(
        me, slab, tokens, near, log_decay.T, weights, w_out, head_size
    )
    w_here_own, w_here_send, w_far_own, w_far_send = blocks
    w_here, w_far = swap_tp(w_here_send, 1), swap_tp(w_far_send, 1)

    spans, factors, before = [span], [], None
    for b in range(seq_bits - 1):
        total, before, own, other, span = link(slab, b, total, swap_seq(total, 1 << b), before)
        spans.append(span)
        factors.append((own, other))

    wq, wkv, wkv_send, wl = ws
    wkv_near = swap_tp(wkv_send, 1)
    for_near = partial(far, wkv_near, (total, w_far, w_here))
    from_near = swap_tp(for_near, 1)
    totals = project(me, 2, far, wq, wkv, wl, totals, (for_near,))
    total_q, total_kv, total_l = totals
    far_near = swap_tp(gate(far, total_q, from_near), 1)
    k, v, *states = project_state(total_kv, from_near, keep, head_size)

    q, level = queries(me, 3, far_near, wq, wl, total_q, total_l)
    locals_ = [attend(q, level, k, v, dcol, drow, i, head_size, level_count) for i in range(2)]
    earlier = []
    for b in range(seq_bits - 1):
        others = [swap_seq(state, 1 << b) for state in states]
        earlier.append(others)
        if b < seq_bits - 2:
            states = [
                combine(state, other, *factors[b], i, ())
                for i, (state, other) in enumerate(zip(states, others))
            ]
    last = swap_seq(combine_both(states, others, *factors[seq_bits - 2], (level,)), 1 << (seq_bits - 1))
    before_last = [state for others in earlier for state in others]
    halves = attend_earlier(locals_, q, level, dcol, spans, before_last, head_size, level_count)

    unit = rows // 8
    ends = (0, 2, 4, 6, 7, 8)
    cuts = [slice(start * unit, stop * unit) for start, stop in zip(ends, ends[1:])]
    pieces = finish(halves, last, cuts[:1], head_size)
    pieces += finish(halves, last, cuts[1:], head_size, pieces)
    pairs = [(x, swap_tp(x, 1)) for x in pieces]
    crossing = [out_block([pair], w_far_own, w_far, BF16) for pair in pairs]
    own_block = out_block(pairs, w_here_own, w_here, F32, (crossing[-1],))
    out = None
    for cut, x in zip(cuts[:-1], crossing):
        out = add_rows(own_block, swap_tp(x, 2), out, cut.start, unit)
    last = own_block[cuts[-1]] + swap_tp(crossing[-1], 2).astype(F32)
    return lax.dynamic_update_slice_in_dim(out, last.astype(BF16), cuts[-1].start, 0)


def solution(mesh):
    in_specs = (
        P("seq", "tp"),
        P("seq", "tp"),
        P(None, "tp"),
        P(None, "tp"),
        P(None, "tp"),
        P(None, "tp"),
        P("tp", None),
    )
    out_specs = P("seq", "tp")
    return jax.shard_map(body, mesh=mesh, in_specs=in_specs, out_specs=out_specs, check_vma=False)
```

```python
import functools

import jax
import jax.numpy as jnp
from jax import lax
from jax.experimental import pallas as pl
from jax.experimental.pallas import tpu as pltpu
from jax.sharding import PartitionSpec as P

BLOCK = 128
F32 = jnp.float32
BF16 = jnp.bfloat16
VMEM = pl.BlockSpec(memory_space=pltpu.VMEM)
SMEM = pl.BlockSpec(memory_space=pltpu.SMEM)
ANY = pl.BlockSpec(memory_space=pl.ANY)
HBM = pl.BlockSpec(memory_space=pltpu.HBM)


def dot(a, b):
    return jnp.dot(a, b, preferred_element_type=F32)


def dot_dims(a, b, left, right):
    return lax.dot_general(a, b, (((left,), (right,)), ((), ())), preferred_element_type=F32)


def shape(dims, dtype):
    return jax.ShapeDtypeStruct(dims, dtype)


def call(kernel, ins, outs, flops, after=(), smem=0, hbm=0, aliases=None, scratch=(), megabytes=8):
    count = len(ins)
    ins = list(ins)
    for i in range(smem, smem + hbm):
        ins[i] = pltpu.with_memory_space_constraint(ins[i], pltpu.HBM)

    def run(*refs):
        kernel(*refs[:count], *refs[count + len(after) :])

    nbytes = sum(x.size * x.dtype.itemsize for x in (*ins, *outs)) if flops else 0
    return pl.pallas_call(
        run,
        in_specs=[SMEM] * smem + [HBM] * hbm + [VMEM] * (count - smem - hbm) + [ANY] * len(after),
        out_specs=[VMEM] * len(outs),
        out_shape=list(outs),
        input_output_aliases=aliases or {},
        scratch_shapes=list(scratch),
        compiler_params=pltpu.CompilerParams(vmem_limit_bytes=megabytes * 1024 * 1024),
        cost_estimate=pl.CostEstimate(flops=flops, bytes_accessed=nbytes, transcendentals=0),
    )(*ins, *after)


def copies(pairs, sems):
    started = [pltpu.make_async_copy(src, dst, sems.at[i]) for i, (src, dst) in enumerate(pairs)]
    for copy in started:
        copy.start()
    return started


def upper_half(slab_ref, bit):
    return ((slab_ref[0] >> bit) & 1) == 1


def decays(slab_ref, x_ref, row_ref, col_ref, keep_ref, total_ref, span_ref):
    heads, rows = x_ref.shape
    head_size = total_ref.shape[1] // heads
    x = x_ref[...]
    x = jnp.concatenate([x, jnp.zeros((-heads % 8, rows), F32)], axis=0) if heads % 8 else x
    place = lax.broadcasted_iota(jnp.int32, x.shape, 1)
    shift = 1
    while shift < rows:
        x = x + jnp.where(place >= shift, pltpu.roll(x, shift, 1), 0.0)
        shift *= 2
    total = x[:, rows - 1 : rows]
    row_ref[...] = x[:heads]
    col_ref[...] = jnp.transpose(x)[:, :heads]
    keep_ref[...] = jnp.transpose(jnp.exp(total - x))[:, :heads]
    for h in range(heads):
        total_ref[:, h * head_size : (h + 1) * head_size] = jnp.broadcast_to(
            total[h : h + 1], (8, head_size)
        )
    span_ref[...] = jnp.full(span_ref.shape, jnp.where(upper_half(slab_ref, 0), 0.0, -jnp.inf), F32)


def link(slab, bit, total, other, before):
    def kernel(slab_ref, *refs):
        total_ref, other_ref = refs[:2]
        total_out, before_out, own_out, other_out, span_out = refs[-5:]
        upper = upper_half(slab_ref, bit)
        here, there = total_ref[...], other_ref[...]
        total_out[...] = here + there
        so_far = jnp.where(upper, there, 0.0)
        if before is not None:
            so_far = so_far + refs[2][...]
        before_out[...] = so_far
        own_out[...] = jnp.where(upper, 1.0, jnp.exp(there))
        other_out[...] = jnp.where(upper, jnp.exp(here), 1.0)
        span_out[...] = jnp.where(upper_half(slab_ref, bit + 1), so_far, -jnp.inf)

    ins = [slab, total, other] + ([] if before is None else [before])
    return call(kernel, ins, [shape(total.shape, F32)] * 5, 0, smem=1)


def combine(state, other, own_factor, other_factor, after):
    def kernel(s_ref, o_ref, a_ref, b_ref, out_ref):
        out_ref[...] = (
            a_ref[0:1, :] * s_ref[...].astype(F32) + b_ref[0:1, :] * o_ref[...].astype(F32)
        ).astype(BF16)

    return call(kernel, [state, other, own_factor, other_factor], [shape(state.shape, BF16)], 0, after)[0]


def begin(me, slab, tokens, near, log_decay_rows, ws, w_out, head_size):
    wq, wk, wv, wl = ws
    rows, shard = near.shape
    q_width, kv_width = wq.shape[1], wk.shape[1]
    heads = log_decay_rows.shape[0]
    block = w_out.shape[1] // 4

    def kernel(me_ref, slab_ref, t_ref, wq_ref, wk_ref, wv_ref, wo_ref, wl_ref, near_ref, decay_ref, *refs):
        total_q, total_kv, total_l, far_q, far_kv, send_kv, all_l = refs[:7]
        decay_outs, blocks, (own_x, own_q, own_kv, sems) = refs[7:12], refs[12:16], refs[16:]

        def pairs(i, q_dst, kv_dst):
            here = pl.ds(pl.multiple_of((me_ref[0] ^ i) * shard, 128), shard)
            return [
                (wk_ref.at[here, :], kv_dst.at[:, :kv_width]),
                (wv_ref.at[here, :], kv_dst.at[:, kv_width:]),
                (wq_ref.at[here, :], q_dst),
            ]

        def columns(i):
            return wo_ref.at[:, pl.ds(pl.multiple_of((me_ref[0] ^ i) * block, 128), block)]

        moves = pairs(0, own_q.at[0], own_kv.at[0]) + [(t_ref, own_x)]
        moves += pairs(1, own_q.at[1], own_kv.at[1])
        moves += pairs(2, far_q.at[0], far_kv) + pairs(3, far_q.at[1], send_kv)
        moves += [(columns(i), blocks[i]) for i in range(4)]
        started = copies(moves, sems)
        decays(slab_ref, decay_ref, *decay_outs)
        all_l[...] = wl_ref[...]
        for copy in started[:4]:
            copy.wait()
        lanes = pl.ds(pl.multiple_of(me_ref[0] * shard, 128), shard)
        own = own_x[...]
        total_kv[...] = dot(own, own_kv[0])
        total_q[...] = dot(own, own_q[0])
        total_l[...] = dot_dims(own, all_l[:, lanes], 1, 1)
        for copy in started[4:7]:
            copy.wait()
        lanes = pl.ds(pl.multiple_of((me_ref[0] ^ 1) * shard, 128), shard)
        total_kv[...] += dot(near_ref[...], own_kv[1])
        total_q[...] += dot(near_ref[...], own_q[1])
        total_l[...] += dot_dims(near_ref[...], all_l[:, lanes], 1, 1)
        for copy in started[7:]:
            copy.wait()

    wide = shape((8, heads * head_size), F32)
    outs = [
        shape((rows, q_width), F32),
        shape((rows, 2 * kv_width), F32),
        shape((rows, wl.shape[0]), F32),
        shape((2, shard, q_width), BF16),
        shape((shard, 2 * kv_width), BF16),
        shape((shard, 2 * kv_width), BF16),
        shape(wl.shape, BF16),
        shape((heads, rows), F32),
        shape((rows, heads), F32),
        shape((rows, heads), F32),
        wide,
        wide,
    ] + [shape((w_out.shape[0], block), BF16)] * 4
    scratch = [
        pltpu.VMEM((rows, shard), BF16),
        pltpu.VMEM((2, shard, q_width), BF16),
        pltpu.VMEM((2, shard, 2 * kv_width), BF16),
        pltpu.SemaphoreType.DMA((17,)),
    ]
    ins = [me, slab, tokens, wq, wk, wv, w_out, wl, near, log_decay_rows]
    outs = call(kernel, ins, outs, 0, smem=2, hbm=5, scratch=scratch, megabytes=14)
    return outs[:3], outs[3:7], outs[7:12], outs[12:]


def add_levels(me_ref, place, x, wl_ref):
    shard = wl_ref.shape[1] // 4
    start = pl.multiple_of((me_ref[0] ^ place) * shard, 128)
    return dot_dims(x, wl_ref[:, pl.ds(start, shard)], 1, 1)


def project(me, place, x, wq, wl, total_q, total_l, after):
    def kernel(me_ref, x_ref, wq_ref, wl_ref, q_ref, l_ref, q_out, l_out):
        q_out[...] = q_ref[...] + dot(x_ref[...], wq_ref[place - 2])
        l_out[...] = l_ref[...] + add_levels(me_ref, place, x_ref[...], wl_ref)

    outs = [shape(t.shape, F32) for t in (total_q, total_l)]
    flops = 2 * x.size * (total_q.shape[1] + total_l.shape[1])
    return call(kernel, [me, x, wq, wl, total_q, total_l], outs, flops, after, smem=1, aliases={4: 0, 5: 1})


def split(x, ways, after):
    rows, columns = x.shape
    part = columns // ways

    def kernel(x_ref, *outs):
        for i, o_ref in enumerate(outs):
            o_ref[...] = x_ref[:, i * part : (i + 1) * part]

    return call(kernel, [x], [shape((rows, part), x.dtype)] * ways, 0, after)


def partial(x, w, after):
    def kernel(x_ref, w_ref, o_ref):
        o_ref[...] = dot(x_ref[...], w_ref[...]).astype(BF16)

    return call(kernel, [x, w], [shape((x.shape[0], w.shape[1]), BF16)], 0, after)[0]


def add_product(x, w, total, after):
    def kernel(x_ref, w_ref, t_ref, o_ref):
        o_ref[...] = t_ref[...] + dot(x_ref[...], w_ref[...])

    return call(kernel, [x, w, total], [shape(total.shape, F32)], 0, after, aliases={2: 0})[0]


def project_state(total_kv, from_near, keep, head_size):
    rows = total_kv.shape[0]
    heads = keep.shape[1]
    kv_width = total_kv.shape[1] // 2
    group = heads // (kv_width // head_size)

    def kernel(total_ref, near_ref, keep_ref, k_out, v_out, s_out):
        total = total_ref[...] + near_ref[...].astype(F32)
        keys = total[:, :kv_width].astype(BF16)
        values = total[:, kv_width:].astype(BF16)
        k_out[...] = keys
        v_out[...] = values
        for g in range(kv_width // head_size):
            cols = slice(g * head_size, (g + 1) * head_size)
            kf = keys[:, cols].astype(F32)
            weighted = jnp.concatenate(
                [(kf * keep_ref[:, h : h + 1]).astype(BF16) for h in range(g * group, (g + 1) * group)],
                axis=1,
            )
            wide = slice(g * group * head_size, (g + 1) * group * head_size)
            s_out[:, wide] = dot_dims(values[:, cols], weighted, 0, 0).astype(BF16)

    outs = [
        shape((rows, kv_width), BF16),
        shape((rows, kv_width), BF16),
        shape((head_size, heads * head_size), BF16),
    ]
    return call(kernel, [total_kv, from_near, keep], outs, 0)


def attend(me, place, xs, wq, wl, total_q, total_l, k, v, dcol, drow, spans, states, head_size, level_count):
    rows, width = total_q.shape
    bits = len(spans)
    heads = width // head_size
    group = heads // (k.shape[1] // head_size)
    own_levels = level_count - bits

    def kernel(me_ref, *refs):
        x = jnp.concatenate([x_ref[...] for x_ref in refs[: len(xs)]], axis=1)
        refs = refs[len(xs) :]
        wq_ref, wl_ref, tq_ref, tl_ref, k_ref, v_ref, dcol_ref, drow_ref = refs[:8]
        span_refs, state_refs = refs[8 : 8 + bits], refs[8 + bits : 7 + 2 * bits]
        o_ref, s_ref, q_ref, l_ref = refs[-4:]
        raw = tl_ref[...] + add_levels(me_ref, place, x, wl_ref)
        l_ref[...] = jnp.maximum(raw, 0.0) + jnp.log1p(jnp.exp(-jnp.abs(raw)))
        q_ref[...] = (tq_ref[...] + dot(x, wq_ref[place - 2])).astype(BF16)
        row_id = lax.broadcasted_iota(jnp.int32, (BLOCK, BLOCK), 0)
        col_id = lax.broadcasted_iota(jnp.int32, (BLOCK, BLOCK), 1)
        causal = row_id >= col_id
        for h in range(heads):
            g = h // group
            cols = slice(h * head_size, (h + 1) * head_size)
            kv = slice(g * head_size, (g + 1) * head_size)
            for i in range(rows // BLOCK):
                here = slice(i * BLOCK, (i + 1) * BLOCK)
                span = (i + 1) * BLOCK
                query = q_ref[here, cols]
                scores = dot_dims(query, k_ref[:span, kv], 1, 1)
                d_here = jnp.broadcast_to(dcol_ref[here, h : h + 1], (BLOCK, BLOCK))

                def weight(level):
                    column = h * level_count + level
                    return jnp.broadcast_to(l_ref[here, column : column + 1], (BLOCK, BLOCK))

                weights = {}
                mixed = []
                for j in range(i + 1):
                    level = (i ^ j).bit_length()
                    if level not in weights:
                        weights[level] = weight(level)
                    there = slice(j * BLOCK, (j + 1) * BLOCK)
                    gap = d_here - drow_ref[h : h + 1, there]
                    if i == j:
                        gap = jnp.where(causal, gap, -jnp.inf)
                    mixed.append((weights[level] * jnp.exp(gap) * scores[:, there]).astype(BF16))
                mixing = mixed[0] if i == 0 else jnp.concatenate(mixed, axis=1)
                total = dot(mixing, v_ref[:span, kv])
                wide = query.astype(F32)
                for b in range(bits):
                    factor = weight(own_levels + b) * jnp.exp(d_here + span_refs[b][0:1, cols])
                    scaled = (wide * factor).astype(BF16)
                    if b == bits - 1:
                        s_ref[here, cols] = scaled
                    else:
                        total = total + dot_dims(scaled, state_refs[b][:, cols], 1, 1)
                o_ref[here, cols] = total

    ins = [me, *xs, wq, wl, total_q, total_l, k, v, dcol, drow, *spans, *states]
    wide = shape((rows, width), BF16)
    outs = [shape((rows, width), F32), wide, wide, shape(total_l.shape, F32)]
    flops = 2 * rows * wq.shape[1] * width + 4 * rows * rows * width
    return call(kernel, ins, outs, flops, smem=1)[:2]


def finish(local, scaled, state, cuts, head_size, after=()):
    width = local.shape[1]

    def kernel(o_ref, q_ref, s_ref, *outs):
        for rows, n_ref in zip(cuts, outs):
            for c in range(0, width, head_size):
                cols = slice(c, c + head_size)
                total = o_ref[rows, cols] + dot_dims(q_ref[rows, cols], s_ref[:, cols], 1, 1)
                mean = jnp.mean(total * total, axis=-1, keepdims=True)
                n_ref[:, cols] = (total * lax.rsqrt(mean + 1e-05)).astype(BF16)

    outs = [shape((cut.stop - cut.start, width), BF16) for cut in cuts]
    return call(kernel, [local, scaled, state], outs, 0, after)


def out_block(pairs, w0, w1, dtype, after=()):
    columns = w1.shape[1]
    count = len(pairs)
    rows = sum(own.shape[0] for own, _ in pairs)
    tile = min(columns, 512)

    def kernel(*refs):
        w0_ref, w1_ref, o_ref = refs[2 * count :]
        start = 0
        for i in range(count):
            a_ref, b_ref = refs[2 * i], refs[2 * i + 1]
            here = slice(start, start + a_ref.shape[0])
            start = here.stop
            for c in range(0, columns, tile):
                cols = slice(c, c + tile)
                o_ref[here, cols] = (
                    dot(a_ref[...], w0_ref[:, cols]) + dot(b_ref[...], w1_ref[:, cols])
                ).astype(dtype)

    ins = [x for pair in pairs for x in pair] + [w0, w1]
    return call(kernel, ins, [shape((rows, columns), dtype)], 0, after)[0]


def add_rows(here, arrived, out, start, unit):
    rows, columns = arrived.shape

    def kernel(h_ref, a_ref, *refs):
        place = pl.ds(pl.multiple_of(start + pl.program_id(0) * unit, unit), unit)
        refs[-1][...] = (h_ref[place, :] + a_ref[...].astype(F32)).astype(BF16)

    block = (unit, columns)
    ins, specs, aliases = [here, arrived], [VMEM, pl.BlockSpec(block, lambda s: (s, 0))], {}
    if out is not None:
        ins, specs, aliases = ins + [out], specs + [ANY], {2: 0}
    return pl.pallas_call(
        kernel,
        grid=(rows // unit,),
        in_specs=specs,
        out_specs=pl.BlockSpec(block, lambda s: (start // unit + s, 0)),
        out_shape=shape(here.shape, BF16),
        input_output_aliases=aliases,
        compiler_params=pltpu.CompilerParams(vmem_limit_bytes=8 * 1024 * 1024),
        cost_estimate=pl.CostEstimate(flops=0, bytes_accessed=rows * columns * 8, transcendentals=0),
    )(*ins)


def body(tokens, log_decay, w_query, w_key, w_value, w_level, w_out):
    rows, shard = tokens.shape
    heads = log_decay.shape[1]
    head_size = w_out.shape[0] // heads
    level_count = w_level.shape[1] // heads
    seq_size = lax.axis_size("seq")
    seq_bits = seq_size.bit_length() - 1
    me = jnp.full((1,), lax.axis_index("tp"), jnp.int32)
    slab = jnp.full((1,), lax.axis_index("seq"), jnp.int32)

    def swap_tp(x, bit):
        return lax.ppermute(x, "tp", [(i, i ^ bit) for i in range(4)])

    def swap_seq(x, bit):
        return lax.ppermute(x, "seq", [(i, i ^ bit) for i in range(seq_size)])

    far = swap_tp(tokens, 2)
    near = swap_tp(tokens, 1)

    weights = (w_query, w_key, w_value, w_level.T)
    totals, ws, (drow, dcol, keep, total, span), blocks = begin(
        me, slab, tokens, near, log_decay.T, weights, w_out, head_size
    )
    w_here_own, w_here_send, w_far_own, w_far_send = blocks
    w_here, w_far = swap_tp(w_here_send, 1), swap_tp(w_far_send, 1)

    spans, factors, before = [span], [], None
    for b in range(seq_bits - 1):
        total, before, own, other, span = link(slab, b, total, swap_seq(total, 1 << b), before)
        spans.append(span)
        factors.append((own, other))

    wq, wkv, wkv_send, wl = ws
    wkv_near = swap_tp(wkv_send, 1)
    arrived = far
    for_near = partial(arrived, wkv_near, (total, w_far, w_here))
    from_near = swap_tp(for_near, 1)
    total_q, total_kv, total_l = totals
    total_kv = add_product(arrived, wkv, total_kv, (for_near,))
    k, v, state = project_state(total_kv, from_near, keep, head_size)
    total_q, total_l = project(me, 2, arrived, wq, wl, total_q, total_l, (k,))
    arrived_near = [swap_tp(x, 1) for x in split(arrived, 4, (total_l,))]

    earlier = []
    for b in range(seq_bits):
        other = swap_seq(state, 1 << b)
        earlier.append(other)
        if b < seq_bits - 1:
            after = () if b else (total_l,)
            state = combine(state, other, *factors[b], after)

    local, scaled = attend(
        me, 3, arrived_near, wq, wl, total_q, total_l, k, v, dcol, drow, spans, earlier[:-1], head_size, level_count
    )

    unit = rows // 8
    ends = (0, 2, 4, 6, 8)
    cuts = [slice(start * unit, stop * unit) for start, stop in zip(ends, ends[1:])]
    pieces = finish(local, scaled, earlier[-1], cuts[:1], head_size)
    pieces += finish(local, scaled, earlier[-1], cuts[1:], head_size, pieces)
    pairs = [(x, swap_tp(x, 1)) for x in pieces]
    crossing = [out_block([pair], w_far_own, w_far, BF16) for pair in pairs]
    own_block = out_block(pairs, w_here_own, w_here, F32, (crossing[-1],))
    out = None
    for cut, x in zip(cuts[:-1], crossing):
        out = add_rows(own_block, swap_tp(x, 2), out, cut.start, unit)
    last = own_block[cuts[-1]] + swap_tp(crossing[-1], 2).astype(F32)
    return lax.dynamic_update_slice_in_dim(out, last.astype(BF16), cuts[-1].start, 0)


def solution(mesh):
    in_specs = (
        P("seq", "tp"),
        P("seq", "tp"),
        P(None, "tp"),
        P(None, "tp"),
        P(None, "tp"),
        P(None, "tp"),
        P("tp", None),
    )
    out_specs = P("seq", "tp")
    return jax.shard_map(body, mesh=mesh, in_specs=in_specs, out_specs=out_specs, check_vma=False)
```

```python
import functools

import jax
import jax.numpy as jnp
from jax import lax
from jax.experimental import pallas as pl
from jax.experimental.pallas import tpu as pltpu
from jax.sharding import PartitionSpec as P

BLOCK = 128
F32 = jnp.float32
BF16 = jnp.bfloat16
VMEM = pl.BlockSpec(memory_space=pltpu.VMEM)
SMEM = pl.BlockSpec(memory_space=pltpu.SMEM)
ANY = pl.BlockSpec(memory_space=pl.ANY)
HBM = pl.BlockSpec(memory_space=pltpu.HBM)


def dot(a, b):
    return jnp.dot(a, b, preferred_element_type=F32)


def dot_dims(a, b, left, right):
    return lax.dot_general(a, b, (((left,), (right,)), ((), ())), preferred_element_type=F32)


def shape(dims, dtype):
    return jax.ShapeDtypeStruct(dims, dtype)


def call(kernel, ins, outs, flops, after=(), smem=0, hbm=0, aliases=None, scratch=(), megabytes=8):
    count = len(ins)
    ins = list(ins)
    for i in range(smem, smem + hbm):
        ins[i] = pltpu.with_memory_space_constraint(ins[i], pltpu.HBM)

    def run(*refs):
        kernel(*refs[:count], *refs[count + len(after) :])

    nbytes = sum(x.size * x.dtype.itemsize for x in (*ins, *outs)) if flops else 0
    return pl.pallas_call(
        run,
        in_specs=[SMEM] * smem + [HBM] * hbm + [VMEM] * (count - smem - hbm) + [ANY] * len(after),
        out_specs=[VMEM] * len(outs),
        out_shape=list(outs),
        input_output_aliases=aliases or {},
        scratch_shapes=list(scratch),
        compiler_params=pltpu.CompilerParams(vmem_limit_bytes=megabytes * 1024 * 1024),
        cost_estimate=pl.CostEstimate(flops=flops, bytes_accessed=nbytes, transcendentals=0),
    )(*ins, *after)


def copies(pairs, sems):
    started = [pltpu.make_async_copy(src, dst, sems.at[i]) for i, (src, dst) in enumerate(pairs)]
    for copy in started:
        copy.start()
    return started


def upper_half(slab_ref, bit):
    return ((slab_ref[0] >> bit) & 1) == 1


def decays(slab_ref, x_ref, row_ref, col_ref, keep_ref, total_ref, span_ref):
    heads, rows = x_ref.shape
    head_size = total_ref.shape[1] // heads
    x = x_ref[...]
    x = jnp.concatenate([x, jnp.zeros((-heads % 8, rows), F32)], axis=0) if heads % 8 else x
    place = lax.broadcasted_iota(jnp.int32, x.shape, 1)
    shift = 1
    while shift < rows:
        x = x + jnp.where(place >= shift, pltpu.roll(x, shift, 1), 0.0)
        shift *= 2
    total = x[:, rows - 1 : rows]
    row_ref[...] = x[:heads]
    col_ref[...] = jnp.transpose(x)[:, :heads]
    keep_ref[...] = jnp.transpose(jnp.exp(total - x))[:, :heads]
    for h in range(heads):
        total_ref[:, h * head_size : (h + 1) * head_size] = jnp.broadcast_to(
            total[h : h + 1], (8, head_size)
        )
    span_ref[...] = jnp.full(span_ref.shape, jnp.where(upper_half(slab_ref, 0), 0.0, -jnp.inf), F32)


def link(slab, bit, total, other, before):
    def kernel(slab_ref, *refs):
        total_ref, other_ref = refs[:2]
        total_out, before_out, own_out, other_out, span_out = refs[-5:]
        upper = upper_half(slab_ref, bit)
        here, there = total_ref[...], other_ref[...]
        total_out[...] = here + there
        so_far = jnp.where(upper, there, 0.0)
        if before is not None:
            so_far = so_far + refs[2][...]
        before_out[...] = so_far
        own_out[...] = jnp.where(upper, 1.0, jnp.exp(there))
        other_out[...] = jnp.where(upper, jnp.exp(here), 1.0)
        span_out[...] = jnp.where(upper_half(slab_ref, bit + 1), so_far, -jnp.inf)

    ins = [slab, total, other] + ([] if before is None else [before])
    return call(kernel, ins, [shape(total.shape, F32)] * 5, 0, smem=1)


def combine(state, other, own_factor, other_factor, after):
    def kernel(s_ref, o_ref, a_ref, b_ref, out_ref):
        out_ref[...] = (
            a_ref[0:1, :] * s_ref[...].astype(F32) + b_ref[0:1, :] * o_ref[...].astype(F32)
        ).astype(BF16)

    return call(kernel, [state, other, own_factor, other_factor], [shape(state.shape, BF16)], 0, after)[0]


def begin(me, slab, tokens, near, log_decay_rows, ws, w_out, head_size):
    wq, wk, wv, wl = ws
    rows, shard = near.shape
    q_width, kv_width = wq.shape[1], wk.shape[1]
    heads = log_decay_rows.shape[0]
    block = w_out.shape[1] // 4

    def kernel(me_ref, slab_ref, t_ref, wq_ref, wk_ref, wv_ref, wo_ref, wl_ref, near_ref, decay_ref, *refs):
        total_q, total_kv, total_l, far_q, far_kv, send_kv, all_l = refs[:7]
        decay_outs, blocks, (own_x, own_q, own_kv, sems) = refs[7:12], refs[12:16], refs[16:]

        def pairs(i, q_dst, kv_dst):
            here = pl.ds(pl.multiple_of((me_ref[0] ^ i) * shard, 128), shard)
            return [
                (wk_ref.at[here, :], kv_dst.at[:, :kv_width]),
                (wv_ref.at[here, :], kv_dst.at[:, kv_width:]),
                (wq_ref.at[here, :], q_dst),
            ]

        def columns(i):
            return wo_ref.at[:, pl.ds(pl.multiple_of((me_ref[0] ^ i) * block, 128), block)]

        moves = pairs(0, own_q.at[0], own_kv.at[0]) + [(t_ref, own_x)]
        moves += pairs(1, own_q.at[1], own_kv.at[1])
        moves += pairs(2, far_q.at[0], far_kv) + pairs(3, far_q.at[1], send_kv)
        moves += [(columns(i), blocks[i]) for i in range(4)]
        started = copies(moves, sems)
        decays(slab_ref, decay_ref, *decay_outs)
        all_l[...] = wl_ref[...]
        for copy in started[:4]:
            copy.wait()
        lanes = pl.ds(pl.multiple_of(me_ref[0] * shard, 128), shard)
        own = own_x[...]
        total_kv[...] = dot(own, own_kv[0])
        total_q[...] = dot(own, own_q[0])
        total_l[...] = dot_dims(own, all_l[:, lanes], 1, 1)
        for copy in started[4:7]:
            copy.wait()
        lanes = pl.ds(pl.multiple_of((me_ref[0] ^ 1) * shard, 128), shard)
        total_kv[...] += dot(near_ref[...], own_kv[1])
        total_q[...] += dot(near_ref[...], own_q[1])
        total_l[...] += dot_dims(near_ref[...], all_l[:, lanes], 1, 1)
        for copy in started[7:]:
            copy.wait()

    wide = shape((8, heads * head_size), F32)
    outs = [
        shape((rows, q_width), F32),
        shape((rows, 2 * kv_width), F32),
        shape((rows, wl.shape[0]), F32),
        shape((2, shard, q_width), BF16),
        shape((shard, 2 * kv_width), BF16),
        shape((shard, 2 * kv_width), BF16),
        shape(wl.shape, BF16),
        shape((heads, rows), F32),
        shape((rows, heads), F32),
        shape((rows, heads), F32),
        wide,
        wide,
    ] + [shape((w_out.shape[0], block), BF16)] * 4
    scratch = [
        pltpu.VMEM((rows, shard), BF16),
        pltpu.VMEM((2, shard, q_width), BF16),
        pltpu.VMEM((2, shard, 2 * kv_width), BF16),
        pltpu.SemaphoreType.DMA((17,)),
    ]
    ins = [me, slab, tokens, wq, wk, wv, w_out, wl, near, log_decay_rows]
    outs = call(kernel, ins, outs, 0, smem=2, hbm=5, scratch=scratch, megabytes=14)
    return outs[:3], outs[3:7], outs[7:12], outs[12:]


def add_levels(me_ref, place, x, wl_ref):
    shard = wl_ref.shape[1] // 4
    start = pl.multiple_of((me_ref[0] ^ place) * shard, 128)
    return dot_dims(x, wl_ref[:, pl.ds(start, shard)], 1, 1)


def project(me, place, x, wq, wl, total_q, total_l, after):
    def kernel(me_ref, x_ref, wq_ref, wl_ref, q_ref, l_ref, q_out, l_out):
        q_out[...] = q_ref[...] + dot(x_ref[...], wq_ref[place - 2])
        l_out[...] = l_ref[...] + add_levels(me_ref, place, x_ref[...], wl_ref)

    outs = [shape(t.shape, F32) for t in (total_q, total_l)]
    flops = 2 * x.size * (total_q.shape[1] + total_l.shape[1])
    return call(kernel, [me, x, wq, wl, total_q, total_l], outs, flops, after, smem=1, aliases={4: 0, 5: 1})


def split(x, ways, after):
    rows, columns = x.shape
    part = columns // ways

    def kernel(x_ref, *outs):
        for i, o_ref in enumerate(outs):
            o_ref[...] = x_ref[:, i * part : (i + 1) * part]

    return call(kernel, [x], [shape((rows, part), x.dtype)] * ways, 0, after)


def partial(x, w, after):
    def kernel(x_ref, w_ref, o_ref):
        o_ref[...] = dot(x_ref[...], w_ref[...]).astype(BF16)

    return call(kernel, [x, w], [shape((x.shape[0], w.shape[1]), BF16)], 0, after)[0]


def add_product(x, w, total, after):
    def kernel(x_ref, w_ref, t_ref, o_ref):
        o_ref[...] = t_ref[...] + dot(x_ref[...], w_ref[...])

    return call(kernel, [x, w, total], [shape(total.shape, F32)], 0, after, aliases={2: 0})[0]


def project_state(total_kv, from_near, keep, head_size):
    rows = total_kv.shape[0]
    heads = keep.shape[1]
    kv_width = total_kv.shape[1] // 2
    group = heads // (kv_width // head_size)

    def kernel(total_ref, near_ref, keep_ref, k_out, v_out, s_out):
        total = total_ref[...] + near_ref[...].astype(F32)
        keys = total[:, :kv_width].astype(BF16)
        values = total[:, kv_width:].astype(BF16)
        k_out[...] = keys
        v_out[...] = values
        for g in range(kv_width // head_size):
            cols = slice(g * head_size, (g + 1) * head_size)
            kf = keys[:, cols].astype(F32)
            weighted = jnp.concatenate(
                [(kf * keep_ref[:, h : h + 1]).astype(BF16) for h in range(g * group, (g + 1) * group)],
                axis=1,
            )
            wide = slice(g * group * head_size, (g + 1) * group * head_size)
            s_out[:, wide] = dot_dims(values[:, cols], weighted, 0, 0).astype(BF16)

    outs = [
        shape((rows, kv_width), BF16),
        shape((rows, kv_width), BF16),
        shape((head_size, heads * head_size), BF16),
    ]
    return call(kernel, [total_kv, from_near, keep], outs, 0)


def attend(me, place, xs, wq, wl, total_q, total_l, k, v, dcol, drow, spans, states, head_size, level_count):
    rows, width = total_q.shape
    bits = len(spans)
    heads = width // head_size
    group = heads // (k.shape[1] // head_size)
    own_levels = level_count - bits

    def kernel(me_ref, *refs):
        x = jnp.concatenate([x_ref[...] for x_ref in refs[: len(xs)]], axis=1)
        refs = refs[len(xs) :]
        wq_ref, wl_ref, tq_ref, tl_ref, k_ref, v_ref, dcol_ref, drow_ref = refs[:8]
        span_refs, state_refs = refs[8 : 8 + bits], refs[8 + bits : 7 + 2 * bits]
        o_ref, s_ref, q_ref, l_ref = refs[-4:]
        raw = tl_ref[...] + add_levels(me_ref, place, x, wl_ref)
        l_ref[...] = jnp.maximum(raw, 0.0) + jnp.log1p(jnp.exp(-jnp.abs(raw)))
        q_ref[...] = (tq_ref[...] + dot(x, wq_ref[place - 2])).astype(BF16)
        row_id = lax.broadcasted_iota(jnp.int32, (BLOCK, BLOCK), 0)
        col_id = lax.broadcasted_iota(jnp.int32, (BLOCK, BLOCK), 1)
        causal = row_id >= col_id
        for h in range(heads):
            g = h // group
            cols = slice(h * head_size, (h + 1) * head_size)
            kv = slice(g * head_size, (g + 1) * head_size)
            for i in range(rows // BLOCK):
                here = slice(i * BLOCK, (i + 1) * BLOCK)
                span = (i + 1) * BLOCK
                query = q_ref[here, cols]
                scores = dot_dims(query, k_ref[:span, kv], 1, 1)
                d_here = jnp.broadcast_to(dcol_ref[here, h : h + 1], (BLOCK, BLOCK))

                def weight(level):
                    column = h * level_count + level
                    return jnp.broadcast_to(l_ref[here, column : column + 1], (BLOCK, BLOCK))

                weights = {}
                mixed = []
                for j in range(i + 1):
                    level = (i ^ j).bit_length()
                    if level not in weights:
                        weights[level] = weight(level)
                    there = slice(j * BLOCK, (j + 1) * BLOCK)
                    gap = d_here - drow_ref[h : h + 1, there]
                    if i == j:
                        gap = jnp.where(causal, gap, -jnp.inf)
                    mixed.append((weights[level] * jnp.exp(gap) * scores[:, there]).astype(BF16))
                mixing = mixed[0] if i == 0 else jnp.concatenate(mixed, axis=1)
                total = dot(mixing, v_ref[:span, kv])
                wide = query.astype(F32)
                for b in range(bits):
                    factor = weight(own_levels + b) * jnp.exp(d_here + span_refs[b][0:1, cols])
                    scaled = (wide * factor).astype(BF16)
                    if b == bits - 1:
                        s_ref[here, cols] = scaled
                    else:
                        total = total + dot_dims(scaled, state_refs[b][:, cols], 1, 1)
                o_ref[here, cols] = total

    ins = [me, *xs, wq, wl, total_q, total_l, k, v, dcol, drow, *spans, *states]
    wide = shape((rows, width), BF16)
    outs = [shape((rows, width), F32), wide, wide, shape(total_l.shape, F32)]
    flops = 2 * rows * wq.shape[1] * width + 4 * rows * rows * width
    return call(kernel, ins, outs, flops, smem=1)[:2]


def finish(local, scaled, state, cuts, head_size, after=()):
    width = local.shape[1]

    def kernel(o_ref, q_ref, s_ref, *outs):
        for rows, n_ref in zip(cuts, outs):
            for c in range(0, width, head_size):
                cols = slice(c, c + head_size)
                total = o_ref[rows, cols] + dot_dims(q_ref[rows, cols], s_ref[:, cols], 1, 1)
                mean = jnp.mean(total * total, axis=-1, keepdims=True)
                n_ref[:, cols] = (total * lax.rsqrt(mean + 1e-05)).astype(BF16)

    outs = [shape((cut.stop - cut.start, width), BF16) for cut in cuts]
    return call(kernel, [local, scaled, state], outs, 0, after)


def out_block(pairs, w0, w1, dtype, after=()):
    columns = w1.shape[1]
    count = len(pairs)
    rows = sum(own.shape[0] for own, _ in pairs)
    tile = min(columns, 512)

    def kernel(*refs):
        w0_ref, w1_ref, o_ref = refs[2 * count :]
        start = 0
        for i in range(count):
            a_ref, b_ref = refs[2 * i], refs[2 * i + 1]
            here = slice(start, start + a_ref.shape[0])
            start = here.stop
            for c in range(0, columns, tile):
                cols = slice(c, c + tile)
                o_ref[here, cols] = (
                    dot(a_ref[...], w0_ref[:, cols]) + dot(b_ref[...], w1_ref[:, cols])
                ).astype(dtype)

    ins = [x for pair in pairs for x in pair] + [w0, w1]
    return call(kernel, ins, [shape((rows, columns), dtype)], 0, after)[0]


def add_rows(here, arrived, out, start, unit):
    rows, columns = arrived.shape

    def kernel(h_ref, a_ref, *refs):
        place = pl.ds(pl.multiple_of(start + pl.program_id(0) * unit, unit), unit)
        refs[-1][...] = (h_ref[place, :] + a_ref[...].astype(F32)).astype(BF16)

    block = (unit, columns)
    ins, specs, aliases = [here, arrived], [VMEM, pl.BlockSpec(block, lambda s: (s, 0))], {}
    if out is not None:
        ins, specs, aliases = ins + [out], specs + [ANY], {2: 0}
    return pl.pallas_call(
        kernel,
        grid=(rows // unit,),
        in_specs=specs,
        out_specs=pl.BlockSpec(block, lambda s: (start // unit + s, 0)),
        out_shape=shape(here.shape, BF16),
        input_output_aliases=aliases,
        compiler_params=pltpu.CompilerParams(vmem_limit_bytes=8 * 1024 * 1024),
        cost_estimate=pl.CostEstimate(flops=0, bytes_accessed=rows * columns * 8, transcendentals=0),
    )(*ins)


def body(tokens, log_decay, w_query, w_key, w_value, w_level, w_out):
    rows, shard = tokens.shape
    heads = log_decay.shape[1]
    head_size = w_out.shape[0] // heads
    level_count = w_level.shape[1] // heads
    seq_size = lax.axis_size("seq")
    seq_bits = seq_size.bit_length() - 1
    me = jnp.full((1,), lax.axis_index("tp"), jnp.int32)
    slab = jnp.full((1,), lax.axis_index("seq"), jnp.int32)

    def swap_tp(x, bit):
        return lax.ppermute(x, "tp", [(i, i ^ bit) for i in range(4)])

    def swap_seq(x, bit):
        return lax.ppermute(x, "seq", [(i, i ^ bit) for i in range(seq_size)])

    far = swap_tp(tokens, 2)
    near = swap_tp(tokens, 1)

    weights = (w_query, w_key, w_value, w_level.T)
    totals, ws, (drow, dcol, keep, total, span), blocks = begin(
        me, slab, tokens, near, log_decay.T, weights, w_out, head_size
    )
    w_here_own, w_here_send, w_far_own, w_far_send = blocks
    w_here, w_far = swap_tp(w_here_send, 1), swap_tp(w_far_send, 1)

    spans, factors, before = [span], [], None
    for b in range(seq_bits - 1):
        total, before, own, other, span = link(slab, b, total, swap_seq(total, 1 << b), before)
        spans.append(span)
        factors.append((own, other))

    wq, wkv, wkv_send, wl = ws
    wkv_near = swap_tp(wkv_send, 1)
    arrived = far
    for_near = partial(arrived, wkv_near, (total, w_far, w_here))
    from_near = swap_tp(for_near, 1)
    total_q, total_kv, total_l = totals
    total_kv = add_product(arrived, wkv, total_kv, (for_near,))
    k, v, state = project_state(total_kv, from_near, keep, head_size)
    total_q, total_l = project(me, 2, arrived, wq, wl, total_q, total_l, (k,))
    arrived_near = [swap_tp(x, 1) for x in split(arrived, 4, (total_l,))]

    earlier = []
    for b in range(seq_bits):
        other = swap_seq(state, 1 << b)
        earlier.append(other)
        if b < seq_bits - 1:
            after = () if b else (total_l,)
            state = combine(state, other, *factors[b], after)

    local, scaled = attend(
        me, 3, arrived_near, wq, wl, total_q, total_l, k, v, dcol, drow, spans, earlier[:-1], head_size, level_count
    )

    unit = rows // 8
    ends = (0, 3, 6, 8)
    cuts = [slice(start * unit, stop * unit) for start, stop in zip(ends, ends[1:])]
    pieces = finish(local, scaled, earlier[-1], cuts[:1], head_size)
    pieces += finish(local, scaled, earlier[-1], cuts[1:], head_size, pieces)
    pairs = [(x, swap_tp(x, 1)) for x in pieces]
    crossing = [out_block([pair], w_far_own, w_far, BF16) for pair in pairs]
    own_block = out_block(pairs, w_here_own, w_here, F32, (crossing[-1],))
    out = None
    for cut, x in zip(cuts[:-1], crossing):
        out = add_rows(own_block, swap_tp(x, 2), out, cut.start, unit)
    last = own_block[cuts[-1]] + swap_tp(crossing[-1], 2).astype(F32)
    return lax.dynamic_update_slice_in_dim(out, last.astype(BF16), cuts[-1].start, 0)


def solution(mesh):
    in_specs = (
        P("seq", "tp"),
        P("seq", "tp"),
        P(None, "tp"),
        P(None, "tp"),
        P(None, "tp"),
        P(None, "tp"),
        P("tp", None),
    )
    out_specs = P("seq", "tp")
    return jax.shard_map(body, mesh=mesh, in_specs=in_specs, out_specs=out_specs, check_vma=False)
```
